32 devices in a mesh: rep: 4 (over y, x), fsdp: 8 (over z, core).
Axes of the slice: x: 2, y: 2, z: 4, core: 2. Of those that a mesh axis runs over, the one named last changes fastest.
Arguments:
- dec_in: bfloat16 [64, 512, 768], P(('rep', 'fsdp')), may hold values from -6 to 6
- memory: bfloat16 [64, 512, 768], P(('rep', 'fsdp')), may hold values from -6 to 6
- out_grad: bfloat16 [64, 512, 768], P(('rep', 'fsdp')), may hold values from -6 to 6
- dec_len: int32 [64], P(('rep', 'fsdp')), may hold values from 32 to 512, as said below
- enc_len: int32 [64], P(('rep', 'fsdp')), may hold values from 32 to 512, as said below
- buckets: int32 [512], replicated, may hold values from 0 to 31, as said below
- self_weight: float32 [4, 768, 768], P(None, 'fsdp'), as said below
- cross_weight: float32 [4, 768, 768], P(None, 'fsdp'), as said below
- ffn_in: float32 [2, 768, 2048], P(None, 'fsdp'), may hold values from -0.21875 to 0.21875
- ffn_out: float32 [2048, 768], P('fsdp'), may hold values from -0.1875 to 0.1875
- gains: float32 [3, 768], P(None, 'fsdp'), may hold values from 0.5 to 1.5
- table: float32 [32, 12], replicated, may hold values from -4 to 4
- self_rows: float32 [4, 768], P(None, 'fsdp'), as said below
- self_cols: float32 [4, 768], replicated, as said below
- cross_rows: float32 [4, 768], P(None, 'fsdp'), as said below
- cross_cols: float32 [4, 768], replicated, as said below
- in_rows: float32 [2, 768], P(None, 'fsdp'), as said below
- in_cols: float32 [2, 2048], replicated, as said below
- out_rows: float32 [2048], P('fsdp'), as said below
- out_cols: float32 [768], replicated, as said below
- gain_moment: float32 [3, 768], P(None, 'fsdp'), may hold values from 0.01 to 1
- table_moment: float32 [32, 12], replicated, may hold values from 0.01 to 1
Outputs:
- layer_out: bfloat16 [64, 512, 768], P(('rep', 'fsdp'))
- input_grad: float32 [64, 512, 768], P(('rep', 'fsdp'))
- memory_grad: float32 [64, 512, 768], P(('rep', 'fsdp'))
- self_grad: float32 [4, 768, 768], P(None, 'fsdp')
- cross_grad: float32 [4, 768, 768], P(None, 'fsdp')
- ffn_in_grad: float32 [2, 768, 2048], P(None, 'fsdp')
- feedforward_output_gradient: float32 [2048, 768], P('fsdp')
- gains_grad: float32 [3, 768], P(None, 'fsdp')
- table_grad: float32 [32, 12], replicated
- new_self: float32 [4, 768, 768], P(None, 'fsdp')
- new_cross: float32 [4, 768, 768], P(None, 'fsdp')
- new_ffn_in: float32 [2, 768, 2048], P(None, 'fsdp')
- new_ffn_out: float32 [2048, 768], P('fsdp')
- new_gains: float32 [3, 768], P(None, 'fsdp')
- new_table: float32 [32, 12], replicated
- new_self_rows: float32 [4, 768], P(None, 'fsdp')
- new_self_cols: float32 [4, 768], replicated
- new_cross_rows: float32 [4, 768], P(None, 'fsdp')
- new_cross_cols: float32 [4, 768], replicated
- new_in_rows: float32 [2, 768], P(None, 'fsdp')
- new_in_cols: float32 [2, 2048], replicated
- new_out_rows: float32 [2048], P('fsdp')
- new_out_cols: float32 [768], replicated
- new_gain_moment: float32 [3, 768], P(None, 'fsdp')
- new_table_moment: float32 [32, 12], replicated
The draws below stay inside these ranges and needn't reach their ends.
Inputs may be any that keep to these rules, and one draw needn't show every extreme that they name: `dec_len`: a sequence's valid decoder tokens; some sequence has 512. `enc_len`: a sequence's valid memory tokens; some sequence has 512. `buckets`: never falls as the distance grows, is 0 at distance 0 and takes every bucket. `self_weight`: four 768 x 768 projections. `cross_weight`: four 768 x 768 projections. `self_rows`: positive running averages of squared gradients. `self_cols`: positive running averages of squared gradients. `cross_rows`: positive running averages of squared gradients. `cross_cols`: positive running averages of squared gradients. `in_rows`: positive running averages of squared gradients. `in_cols`: positive running averages of squared gradients. `out_rows`: positive running averages of squared gradients. `out_cols`: positive running averages of squared gradients.
All inputs are finite; a program needn't handle non-finite values.
Results may differ from the reference program's by a relative error of at most 0.03.
The reference program's roundings to bfloat16 on the way count: a program that leaves them out, or rounds other values in their place, can miss the bound.
Values may be sent and summed in bfloat16 or wider, within the bound.
No kernel may reach another device: no remote copies, remote signals or barrier semaphores. Data moves between devices by JAX's collectives and lax.ppermute only.
A program may use at most 320 MiB of HBM per device.

```python
import math
import jax
import jax.numpy as jnp
from jax import lax

D = 768
H = 12
DH = 64
FF = 2048
BUCKETS = 32
LEN = 512
MLEN = 512
SHORT = 32
SEQS = 64
TOKENS = 32768


def attention_stacked_heads(key):
    scales = jnp.array([0.25, 1.0, 1.0, 3.0], jnp.float32) / math.sqrt(D)
    base_draw = jax.random.normal(key, (4, D, D), jnp.float32)
    return base_draw * scales[:, None, None]


def draw_self_weight(key, part):
    return attention_stacked_heads(jax.random.fold_in(key, 11))


def draw_cross_weight(key, part):
    return attention_stacked_heads(jax.random.fold_in(key, 12))


def ragged_lengths(key, longest):
    lengths = jax.random.randint(key, (SEQS,), SHORT, longest + 1)
    full_slot = jax.random.randint(jax.random.fold_in(key, 5), (), 0, SEQS)
    return jnp.where(jnp.arange(SEQS) == full_slot, longest, lengths).astype(jnp.int32)


def draw_dec_len(key, part):
    return ragged_lengths(jax.random.fold_in(key, 21), LEN)


def draw_enc_len(key, part):
    return ragged_lengths(jax.random.fold_in(key, 22), MLEN)


def draw_buckets(key, part):
    break_points = jax.random.permutation(jax.random.fold_in(key, 31), LEN - 1)[:BUCKETS - 1] + 1
    distance = jnp.arange(LEN)
    return jnp.sum((distance[:, None] >= break_points[None, :]).astype(jnp.int32), axis=1).astype(jnp.int32)


def statistic_values(key, shape, center):
    lower_end = center / 21.5
    exponent = jax.random.uniform(key, shape, jnp.float32, 0.0, math.log(100.0))
    return lower_end * jnp.exp(exponent)


def draw_self_rows(key, part):
    key = jax.random.fold_in(key, 41)
    return statistic_values(key, (4, D), 6.0)


def draw_self_cols(key, part):
    key = jax.random.fold_in(key, 42)
    return statistic_values(key, (4, D), 6.0)


def draw_cross_rows(key, part):
    key = jax.random.fold_in(key, 43)
    return statistic_values(key, (4, D), 2.0)


def draw_cross_cols(key, part):
    key = jax.random.fold_in(key, 44)
    return statistic_values(key, (4, D), 2.0)


def draw_in_rows(key, part):
    key = jax.random.fold_in(key, 45)
    return statistic_values(key, (2, D), 0.04)


def draw_in_cols(key, part):
    key = jax.random.fold_in(key, 46)
    return statistic_values(key, (2, FF), 0.04)


def draw_out_rows(key, part):
    key = jax.random.fold_in(key, 47)
    return statistic_values(key, (FF,), 0.04)


def draw_out_cols(key, part):
    key = jax.random.fold_in(key, 48)
    return statistic_values(key, (D,), 0.04)


def levels(rng, shape, cuts, least, largest):
    factor_of = 1.0
    for axis_at, parts in cuts:
        draws = jax.random.uniform(jax.random.fold_in(jax.random.fold_in(rng, 6), axis_at), (parts,), jnp.float32, least / len(cuts), largest / len(cuts))
        factor_of = factor_of * jnp.repeat(jnp.exp(draws), shape[axis_at] // parts).reshape((-1,) + (1,) * (len(shape) - 1 - axis_at))
    return factor_of


def noise(own_key, dims, scale, reach, pieces=(), kind=jnp.bfloat16):
    factor_of = levels(own_key, dims, pieces, -0.22, 0.18) if pieces else 1.0
    values = jax.random.normal(own_key, dims, jnp.float32) * scale * factor_of
    return jnp.minimum(jnp.maximum(values, -reach), reach).astype(kind)


def setup_inputs(seed: int = 0) -> dict:
    keys = jax.random.split(jax.random.key(seed), 23)
    return {
        "dec_in": noise(keys[0], (SEQS, LEN, D), 1.0, 6.0, ((0, 32),)),
        "memory": noise(keys[1], (SEQS, MLEN, D), 1.0, 6.0, ((0, 32),)),
        "out_grad": noise(keys[2], (SEQS, LEN, D), 1.0, 6.0, ((0, 32),)),
        "dec_len": draw_dec_len(jax.random.fold_in(keys[22], 71), 0),
        "enc_len": draw_enc_len(jax.random.fold_in(keys[22], 71), 0),
        "buckets": draw_buckets(jax.random.fold_in(keys[22], 71), 0),
        "self_weight": draw_self_weight(jax.random.fold_in(keys[22], 71), 0),
        "cross_weight": draw_cross_weight(jax.random.fold_in(keys[22], 71), 0),
        "ffn_in": noise(keys[8], (2, D, FF), D ** -0.5, 0.21875, ((1, 8),), jnp.float32),
        "ffn_out": noise(keys[9], (FF, D), (FF // 2) ** -0.5, 0.1875, ((0, 8),), jnp.float32),
        "gains": jnp.clip(1.0 + 0.1 * jax.random.normal(keys[10], (3, D), jnp.float32), 0.5, 1.5),
        "table": noise(keys[11], (BUCKETS, H), 1.0, 4.0, (), jnp.float32),
        "self_rows": draw_self_rows(jax.random.fold_in(keys[22], 71), 0),
        "self_cols": draw_self_cols(jax.random.fold_in(keys[22], 71), 0),
        "cross_rows": draw_cross_rows(jax.random.fold_in(keys[22], 71), 0),
        "cross_cols": draw_cross_cols(jax.random.fold_in(keys[22], 71), 0),
        "in_rows": draw_in_rows(jax.random.fold_in(keys[22], 71), 0),
        "in_cols": draw_in_cols(jax.random.fold_in(keys[22], 71), 0),
        "out_rows": draw_out_rows(jax.random.fold_in(keys[22], 71), 0),
        "out_cols": draw_out_cols(jax.random.fold_in(keys[22], 71), 0),
        "gain_moment": jnp.clip(jnp.exp(math.log(1.0) - 4.6051702 * jax.random.uniform(keys[20], (3, D), jnp.float32) ** levels(keys[20], (3, D), ((1, 8),), -0.2, 0.2)), 0.01, 1.0),
        "table_moment": jnp.clip(jnp.exp(jax.random.uniform(keys[21], (BUCKETS, H), jnp.float32, math.log(0.01), math.log(1.0))), 0.01, 1.0),
    }


EXACT_ARITHMETIC = lax.Precision.HIGHEST
MASKED = -1000000000.0
DECAY_RATE = 0.8
STEP_RATE = 0.2
TINY_TERM = 1e-30

@jax.custom_vjp
def low(v):
    return lax.optimization_barrier(v.astype(jnp.bfloat16)).astype(jnp.float32)

@jax.custom_vjp
def low_back(v):
    return v

def low_keep(v):
    return (low(v), None)

def low_pass(kept, grad):
    return (grad,)

def back_keep(v):
    return (v, None)

def back_low(kept, grad):
    return (low(grad),)
low.defvjp(low_keep, low_pass)
low_back.defvjp(back_keep, back_low)

def rms_scale(vector, gain_row):
    return vector * lax.rsqrt(lax.optimization_barrier(jnp.mean(vector * vector, axis=-1, keepdims=True)) + 1e-06) * gain_row

def project(earlier_operand, later_operand):
    return jnp.einsum('afn,nu->afu', earlier_operand, later_operand, precision=EXACT_ARITHMETIC)

def attention(query_rows, key_rows, value_rows, rel_bias, keep_mask):
    query_heads = query_rows.reshape(query_rows.shape[0], query_rows.shape[1], H, DH)
    key_heads = key_rows.reshape(key_rows.shape[0], key_rows.shape[1], H, DH)
    value_heads = value_rows.reshape(value_rows.shape[0], value_rows.shape[1], H, DH)
    scores = jnp.einsum('sqhd,skhd->shqk', query_heads, key_heads, precision=EXACT_ARITHMETIC) + rel_bias
    scores = low_back(scores)
    scores = jnp.where(keep_mask[:, None], scores, MASKED)
    probability = low(jax.nn.softmax(scores, axis=-1))
    mixture = jnp.einsum('shqk,skhd->sqhd', probability, value_heads, precision=EXACT_ARITHMETIC)
    return low_back(low(mixture.reshape(query_rows.shape)))

def layer_forward(dec_rows, mem_rows, w_self, w_cross, w_in, w_out, gain_rows, table, dec_len, enc_len, buckets):
    w_self = low(w_self)
    w_cross = low(w_cross)
    w_in = low(w_in)
    w_out = low(w_out)
    gain_rows = low(gain_rows)
    positions = jnp.arange(LEN)
    distance = positions[:, None] - positions[None, :]
    pair_bucket = buckets[jnp.maximum(distance, 0)]
    rel_bias = jnp.transpose(table[pair_bucket], (2, 0, 1))
    live_rows = positions[None, :] < dec_len[:, None]
    self_mask = (distance >= 0)[None] & live_rows[:, None, :]
    cross_mask = jnp.broadcast_to((jnp.arange(MLEN)[None, :] < enc_len[:, None])[:, None, :], (dec_len.shape[0], LEN, MLEN))
    normed = low(rms_scale(dec_rows, gain_rows[0]))
    query_rows = low_back(low(project(normed, w_self[0])))
    key_rows = low_back(low(project(normed, w_self[1])))
    value_rows = low_back(low(project(normed, w_self[2])))
    mixture = attention(query_rows, key_rows, value_rows, rel_bias, self_mask)
    after_self = dec_rows + low_back(project(mixture, w_self[3]))
    normed = low(rms_scale(after_self, gain_rows[1]))
    query_rows = low_back(low(project(normed, w_cross[0])))
    key_rows = low_back(low(project(mem_rows, w_cross[1])))
    value_rows = low_back(low(project(mem_rows, w_cross[2])))
    mixture = attention(query_rows, key_rows, value_rows, 0.0, cross_mask)
    after_cross = after_self + low_back(project(mixture, w_cross[3]))
    normed = low(rms_scale(after_cross, gain_rows[2]))
    gate_pre = low_back(project(normed, w_in[0]))
    up_pre = low_back(project(normed, w_in[1]))
    hidden = low(jax.nn.gelu(gate_pre, approximate=True) * up_pre)
    result = after_cross + low_back(project(hidden, w_out))
    return result * live_rows[:, :, None].astype(result.dtype)

def apply_optimizer_update(weight, direction):
    step_size = STEP_RATE * jnp.sqrt(jnp.mean(weight * weight) + 1e-06)
    return weight - step_size * direction

def factored(gradient, weight, row_state, col_state):
    squares = gradient * gradient + TINY_TERM
    row_moment = DECAY_RATE * row_state + (1.0 - DECAY_RATE) * lax.optimization_barrier(jnp.mean(squares, axis=1))
    col_moment = DECAY_RATE * col_state + (1.0 - DECAY_RATE) * lax.optimization_barrier(jnp.mean(squares, axis=0))
    direction = gradient * lax.rsqrt(row_moment[:, None] * col_moment[None, :] / jnp.mean(row_moment))
    return (apply_optimizer_update(weight, direction), row_moment, col_moment)

def plain_step(gradient, weight, moment):
    new_moment = DECAY_RATE * moment + (1.0 - DECAY_RATE) * (gradient * gradient + TINY_TERM)
    return (apply_optimizer_update(weight, gradient * lax.rsqrt(new_moment)), new_moment)

def reference(dec_in, memory, out_grad, dec_len, enc_len, buckets, self_weight, cross_weight, ffn_in, ffn_out, gains, table, self_rows, self_cols, cross_rows, cross_cols, in_rows, in_cols, out_rows, out_cols, gain_moment, table_moment):
    grouped_sequences = 4
    group_count = SEQS // grouped_sequences
    params = (self_weight, cross_weight, ffn_in, ffn_out, gains, table)

    def one_group(totals, element):
        dec_rows, mem_rows, grad_rows, dec_group, enc_group = element

        def forward(dec_part, mem_part, w_self, w_cross, w_in, w_out, gain_rows, bias_table):
            return layer_forward(dec_part, mem_part, w_self, w_cross, w_in, w_out, gain_rows, bias_table, dec_group, enc_group, buckets)
        result, pullback = jax.vjp(forward, dec_rows.astype(jnp.float32), mem_rows.astype(jnp.float32), *params)
        grads = pullback(grad_rows.astype(jnp.float32))
        totals = tuple((total + piece for total, piece in zip(totals, grads[2:])))
        return (totals, (result.astype(jnp.bfloat16), grads[0], grads[1]))
    zeros = tuple((jnp.zeros(param.shape, jnp.float32) for param in params))
    element_rows = (dec_in.reshape(group_count, grouped_sequences, LEN, D), memory.reshape(group_count, grouped_sequences, MLEN, D), out_grad.reshape(group_count, grouped_sequences, LEN, D), dec_len.reshape(group_count, grouped_sequences), enc_len.reshape(group_count, grouped_sequences))
    totals, (layer_out, input_grad, memory_grad) = lax.scan(one_group, zeros, element_rows)
    layer_out = layer_out.reshape(SEQS, LEN, D)
    input_grad = input_grad.reshape(SEQS, LEN, D)
    memory_grad = memory_grad.reshape(SEQS, MLEN, D)
    grad_factor = 1.0 / math.sqrt(TOKENS)
    self_grad, cross_grad, ffn_in_grad, feedforward_output_gradient, gains_grad, table_grad = [total * grad_factor for total in totals]
    new_self, new_self_rows, new_self_cols = jax.vmap(factored)(self_grad, self_weight, self_rows, self_cols)
    new_cross, new_cross_rows, new_cross_cols = jax.vmap(factored)(cross_grad, cross_weight, cross_rows, cross_cols)
    new_ffn_in, new_in_rows, new_in_cols = jax.vmap(factored)(ffn_in_grad, ffn_in, in_rows, in_cols)
    new_ffn_out, new_out_rows, new_out_cols = factored(feedforward_output_gradient, ffn_out, out_rows, out_cols)
    new_gains, new_gain_moment = jax.vmap(plain_step)(gains_grad, gains, gain_moment)
    new_table, new_table_moment = plain_step(table_grad, table, table_moment)
    return (layer_out, input_grad, memory_grad, self_grad, cross_grad, ffn_in_grad, feedforward_output_gradient, gains_grad, table_grad, new_self, new_cross, new_ffn_in, new_ffn_out, new_gains, new_table, new_self_rows, new_self_cols, new_cross_rows, new_cross_cols, new_in_rows, new_in_cols, new_out_rows, new_out_cols, new_gain_moment, new_table_moment)
```

```python
import math

import jax
import jax.numpy as jnp
from jax import lax
from jax.sharding import PartitionSpec as P

H = 12
DH = 64
BUCKETS = 32


EXACT_ARITHMETIC = lax.Precision.HIGHEST
MASKED = -1000000000.0
DECAY_RATE = 0.8
STEP_RATE = 0.2
TINY_TERM = 1e-30


def rms_scale(vector, gain_row):
    return vector * lax.rsqrt(jnp.mean(vector * vector, axis=-1, keepdims=True) + 1e-06) * gain_row


def matmul(earlier_operand, later_operand):
    return jnp.dot(earlier_operand, later_operand, preferred_element_type=jnp.float32)


def inner_first(earlier_operand, later_operand):
    return lax.dot_general(
        earlier_operand, later_operand, (((0,), (0,)), ((), ())), preferred_element_type=jnp.float32
    )


def inner_last(earlier_operand, later_operand):
    return lax.dot_general(
        earlier_operand, later_operand, (((1,), (1,)), ((), ())), preferred_element_type=jnp.float32
    )


def split_heads(rows_in):
    return rows_in.reshape(rows_in.shape[0], H, DH)


def score_block(query_rows, key_rows, rel_bias, keep_mask):
    scores = jnp.einsum(
        "qhd,khd->hqk",
        split_heads(query_rows),
        split_heads(key_rows),
        preferred_element_type=jnp.float32,
    )
    if rel_bias is not None:
        scores = scores + rel_bias
    return jnp.where(keep_mask[None], scores, MASKED)


def attend(query_rows, key_rows, value_rows, rel_bias, keep_mask):
    scores = score_block(query_rows, key_rows, rel_bias, keep_mask)
    row_max = jnp.max(scores, axis=2, keepdims=True)
    log_total = row_max + jnp.log(jnp.sum(jnp.exp(scores - row_max), axis=2, keepdims=True))
    probability = jnp.exp(scores - log_total).astype(jnp.bfloat16)
    mixture = jnp.einsum(
        "hqk,khd->qhd", probability, split_heads(value_rows), preferred_element_type=jnp.float32
    )
    return (mixture.reshape(query_rows.shape).astype(jnp.bfloat16), log_total)


def attend_back(query_rows, key_rows, value_rows, grad_mix, log_total, rel_bias, keep_mask):
    scores = score_block(query_rows, key_rows, rel_bias, keep_mask)
    probability = jnp.exp(scores - log_total)
    heads_grad = split_heads(grad_mix)
    grad_prob = jnp.einsum(
        "qhd,khd->hqk", heads_grad, split_heads(value_rows), preferred_element_type=jnp.float32
    )
    grad_value = jnp.einsum(
        "hqk,qhd->khd",
        probability.astype(jnp.bfloat16),
        heads_grad,
        preferred_element_type=jnp.float32,
    )
    grad_score = (
        probability * (grad_prob - jnp.sum(probability * grad_prob, axis=2, keepdims=True))
    ).astype(jnp.bfloat16)
    grad_query = jnp.einsum(
        "hqk,khd->qhd", grad_score, split_heads(key_rows), preferred_element_type=jnp.float32
    )
    grad_key = jnp.einsum(
        "hqk,qhd->khd", grad_score, split_heads(query_rows), preferred_element_type=jnp.float32
    )
    return (
        grad_query.reshape(query_rows.shape).astype(jnp.bfloat16),
        grad_key.reshape(key_rows.shape).astype(jnp.bfloat16),
        grad_value.reshape(key_rows.shape).astype(jnp.bfloat16),
        grad_score,
    )


def gated_unit(gate_pre, up_pre):
    return jax.nn.gelu(gate_pre, approximate=True) * up_pre


def row_parts(gradient, weight, row_state):
    squares = gradient * gradient + TINY_TERM
    row_moment = DECAY_RATE * row_state + (1.0 - DECAY_RATE) * jnp.mean(squares, axis=2)
    return (
        row_moment,
        jnp.sum(squares, axis=1),
        jnp.sum(row_moment, axis=1),
        jnp.sum(weight * weight, axis=(1, 2)),
    )


def column_step(gradient, row_moment, col_state, col_sum, row_sum, whole_rows):
    col_moment = DECAY_RATE * col_state + (1.0 - DECAY_RATE) * col_sum / whole_rows
    row_mean = row_sum / whole_rows
    direction = gradient * lax.rsqrt(
        row_moment[:, :, None] * col_moment[:, None, :] / row_mean[:, None, None]
    )
    return (direction, col_moment)


def apply_optimizer_update(weight, direction, weight_square):
    step_size = STEP_RATE * jnp.sqrt(weight_square + 1e-06)
    ratio = step_size.reshape((-1,) + (1,) * (weight.ndim - 1))
    return weight - ratio * direction


def per_device(
    dec_in,
    memory,
    out_grad,
    dec_len,
    enc_len,
    buckets,
    self_weight,
    cross_weight,
    ffn_in,
    ffn_out,
    gains,
    table,
    self_rows,
    self_cols,
    cross_rows,
    cross_cols,
    in_rows,
    in_cols,
    out_rows,
    out_cols,
    gain_moment,
    table_moment,
):
    seq_count, seq_length, model_width = dec_in.shape
    mem_length = memory.shape[1]
    row_count = seq_count * seq_length
    shards = (
        self_weight.astype(jnp.bfloat16),
        cross_weight.astype(jnp.bfloat16),
        ffn_in.astype(jnp.bfloat16),
        ffn_out.astype(jnp.bfloat16),
        gains.astype(jnp.bfloat16),
    )
    gathered = (
        lax.all_gather(shards[0], "fsdp", axis=1, tiled=True),
        lax.all_gather(shards[1], "fsdp", axis=1, tiled=True),
        lax.all_gather(shards[2], "fsdp", axis=1, tiled=True),
        lax.all_gather(shards[3], "fsdp", axis=0, tiled=True),
        lax.all_gather(shards[4], "fsdp", axis=1, tiled=True),
    )
    col_whole = (self_cols, cross_cols, in_cols, out_cols)
    w_self, w_cross, w_in, w_out, gain_low = gathered
    gain_full = gain_low.astype(jnp.float32)
    positions = jnp.arange(seq_length)
    distance = positions[:, None] - positions[None, :]
    first_distance = jnp.sum(buckets[:, None] < jnp.arange(BUCKETS + 1)[None, :], axis=0)
    pair_distance = jnp.maximum(distance, 0).reshape(-1)[:, None]
    one_hot = (
        (pair_distance >= first_distance[None, :-1]) & (pair_distance < first_distance[None, 1:])
    ).astype(jnp.float32)
    rel_bias = jnp.dot(one_hot, table, precision=EXACT_ARITHMETIC).T.reshape(
        H, seq_length, seq_length
    )
    live_rows = (positions[None, :] < dec_len[:, None]).astype(jnp.float32).reshape(row_count, 1)
    mem_positions = jnp.arange(mem_length)

    def self_keep(seq_len):
        return (distance >= 0) & (positions[None, :] < seq_len)

    def cross_keep(seq_len):
        return jnp.broadcast_to(mem_positions[None, :] < seq_len, (seq_length, mem_length))

    def by_seq(rows_in, length_rows):
        return rows_in.reshape(seq_count, length_rows, model_width)

    residual = dec_in.reshape(row_count, model_width).astype(jnp.float32)
    mem_rows = memory.reshape(seq_count * mem_length, model_width)
    normed_one = rms_scale(residual, gain_full[0]).astype(jnp.bfloat16)
    query_one = matmul(normed_one, w_self[0]).astype(jnp.bfloat16)
    key_one = matmul(normed_one, w_self[1]).astype(jnp.bfloat16)
    value_one = matmul(normed_one, w_self[2]).astype(jnp.bfloat16)

    def self_forward(element):
        return attend(element[0], element[1], element[2], rel_bias, self_keep(element[3]))

    mix_one, total_one = lax.map(
        self_forward,
        (
            by_seq(query_one, seq_length),
            by_seq(key_one, seq_length),
            by_seq(value_one, seq_length),
            dec_len,
        ),
    )
    mix_one = mix_one.reshape(row_count, model_width)
    after_self = residual + matmul(mix_one, w_self[3])
    normed_two = rms_scale(after_self, gain_full[1]).astype(jnp.bfloat16)
    query_two = matmul(normed_two, w_cross[0]).astype(jnp.bfloat16)
    key_two = matmul(mem_rows, w_cross[1]).astype(jnp.bfloat16)
    value_two = matmul(mem_rows, w_cross[2]).astype(jnp.bfloat16)

    def cross_forward(element):
        return attend(element[0], element[1], element[2], None, cross_keep(element[3]))

    mix_two, total_two = lax.map(
        cross_forward,
        (
            by_seq(query_two, seq_length),
            by_seq(key_two, mem_length),
            by_seq(value_two, mem_length),
            enc_len,
        ),
    )
    mix_two = mix_two.reshape(row_count, model_width)
    after_cross = after_self + matmul(mix_two, w_cross[3])
    normed_three = rms_scale(after_cross, gain_full[2]).astype(jnp.bfloat16)
    gate_pre = matmul(normed_three, w_in[0])
    up_pre = matmul(normed_three, w_in[1])
    hidden = gated_unit(gate_pre, up_pre).astype(jnp.bfloat16)
    result = (after_cross + matmul(hidden, w_out)) * live_rows
    layer_out = result.astype(jnp.bfloat16).reshape(seq_count, seq_length, model_width)
    back_weights = (
        lax.all_gather(shards[0], "fsdp", axis=1, tiled=True),
        lax.all_gather(shards[1], "fsdp", axis=1, tiled=True),
        lax.all_gather(shards[2], "fsdp", axis=1, tiled=True),
        lax.all_gather(shards[3], "fsdp", axis=0, tiled=True),
        lax.all_gather(shards[4], "fsdp", axis=1, tiled=True),
    )
    back_self, back_cross, back_in, back_out, back_gain = back_weights
    back_gain = back_gain.astype(jnp.float32)
    grad_out = out_grad.reshape(row_count, model_width).astype(jnp.float32) * live_rows
    down_low = grad_out.astype(jnp.bfloat16)
    grad_down = inner_first(hidden, down_low)
    grad_hidden = inner_last(down_low, back_out)
    _, pullback = jax.vjp(gated_unit, gate_pre, up_pre)
    grad_gate, grad_up = pullback(grad_hidden)
    grad_gate = grad_gate.astype(jnp.bfloat16)
    grad_up = grad_up.astype(jnp.bfloat16)
    grad_inner = jnp.stack(
        [inner_first(normed_three, grad_gate), inner_first(normed_three, grad_up)]
    )
    grad_three = inner_last(grad_gate, back_in[0]) + inner_last(grad_up, back_in[1])
    _, pullback = jax.vjp(rms_scale, after_cross, back_gain[2])
    grad_cross, gain_three = pullback(grad_three)
    grad_cross = grad_out + grad_cross
    branch_two = grad_cross.astype(jnp.bfloat16)
    grad_co = inner_first(mix_two, branch_two)
    grad_mix_two = inner_last(branch_two, back_cross[3]).astype(jnp.bfloat16)

    def cross_backward(element):
        return attend_back(
            element[0], element[1], element[2], element[3], element[4], None, cross_keep(element[5])
        )[:3]

    grad_q_two, grad_k_two, grad_v_two = lax.map(
        cross_backward,
        (
            by_seq(query_two, seq_length),
            by_seq(key_two, mem_length),
            by_seq(value_two, mem_length),
            by_seq(grad_mix_two, seq_length),
            total_two,
            enc_len,
        ),
    )
    grad_q_two = grad_q_two.reshape(row_count, model_width)
    grad_k_two = grad_k_two.reshape(seq_count * mem_length, model_width)
    grad_v_two = grad_v_two.reshape(seq_count * mem_length, model_width)
    grad_cross_weights = jnp.stack(
        [
            inner_first(normed_two, grad_q_two),
            inner_first(mem_rows, grad_k_two),
            inner_first(mem_rows, grad_v_two),
            grad_co,
        ]
    )
    memory_grad = (
        inner_last(grad_k_two, back_cross[1]) + inner_last(grad_v_two, back_cross[2])
    ).reshape(seq_count, mem_length, model_width)
    _, pullback = jax.vjp(rms_scale, after_self, back_gain[1])
    grad_self, gain_two = pullback(inner_last(grad_q_two, back_cross[0]))
    grad_self = grad_cross + grad_self
    branch_one = grad_self.astype(jnp.bfloat16)
    grad_wo = inner_first(mix_one, branch_one)
    grad_mix_one = inner_last(branch_one, back_self[3]).astype(jnp.bfloat16)

    def self_backward(score_total, element):
        grad_query, grad_key, grad_value, grad_score = attend_back(
            element[0],
            element[1],
            element[2],
            element[3],
            element[4],
            rel_bias,
            self_keep(element[5]),
        )
        return (score_total + grad_score.astype(jnp.float32), (grad_query, grad_key, grad_value))

    score_total, (grad_q_one, grad_k_one, grad_v_one) = lax.scan(
        self_backward,
        jnp.zeros((H, seq_length, seq_length), jnp.float32),
        (
            by_seq(query_one, seq_length),
            by_seq(key_one, seq_length),
            by_seq(value_one, seq_length),
            by_seq(grad_mix_one, seq_length),
            total_one,
            dec_len,
        ),
    )
    table_part = jnp.dot(score_total.reshape(H, -1), one_hot, precision=EXACT_ARITHMETIC).T
    grad_q_one = grad_q_one.reshape(row_count, model_width)
    grad_k_one = grad_k_one.reshape(row_count, model_width)
    grad_v_one = grad_v_one.reshape(row_count, model_width)
    grad_self_weights = jnp.stack(
        [
            inner_first(normed_one, grad_q_one),
            inner_first(normed_one, grad_k_one),
            inner_first(normed_one, grad_v_one),
            grad_wo,
        ]
    )
    grad_normed = (
        inner_last(grad_q_one, back_self[0])
        + inner_last(grad_k_one, back_self[1])
        + inner_last(grad_v_one, back_self[2])
    )
    _, pullback = jax.vjp(rms_scale, residual, back_gain[0])
    grad_input, first_norm_gain = pullback(grad_normed)
    input_grad = (grad_self + grad_input).reshape(seq_count, seq_length, model_width)
    grad_gains = jnp.stack([first_norm_gain, gain_two, gain_three])
    owned = (
        lax.psum_scatter(grad_self_weights.astype(jnp.bfloat16), "fsdp", scatter_dimension=1, tiled=True),
        lax.psum_scatter(grad_cross_weights.astype(jnp.bfloat16), "fsdp", scatter_dimension=1, tiled=True),
        lax.psum_scatter(grad_inner.astype(jnp.bfloat16), "fsdp", scatter_dimension=1, tiled=True),
        lax.psum_scatter(grad_down.astype(jnp.bfloat16), "fsdp", scatter_dimension=0, tiled=True),
        lax.psum_scatter(grad_gains, "fsdp", scatter_dimension=1, tiled=True),
    )
    owned = (
        lax.psum(owned[0].astype(jnp.bfloat16), "rep").astype(jnp.float32),
        lax.psum(owned[1].astype(jnp.bfloat16), "rep").astype(jnp.float32),
        lax.psum(owned[2].astype(jnp.bfloat16), "rep").astype(jnp.float32),
        lax.psum(owned[3].astype(jnp.bfloat16), "rep").astype(jnp.float32),
        lax.psum(owned[4].astype(jnp.bfloat16), "rep").astype(jnp.float32),
    )
    table_total = lax.psum(table_part, ("rep", "fsdp"))
    fsdp_count = lax.axis_size("fsdp")
    grad_factor = 1.0 / math.sqrt(row_count * lax.axis_size("rep") * fsdp_count)
    self_grad, cross_grad, ffn_in_grad, feedforward_output_gradient, gains_grad = [
        member * grad_factor for member in owned
    ]
    table_grad = table_total * grad_factor
    batches = [
        (self_grad, self_weight, self_rows, col_whole[0]),
        (cross_grad, cross_weight, cross_rows, col_whole[1]),
        (ffn_in_grad, ffn_in, in_rows, col_whole[2]),
        (feedforward_output_gradient[None], ffn_out[None], out_rows[None], col_whole[3][None]),
    ]
    prepared = [
        row_parts(gradient, weight, row_state) for gradient, weight, row_state, col_state in batches
    ]
    gain_state = DECAY_RATE * gain_moment + (1.0 - DECAY_RATE) * (
        gains_grad * gains_grad + TINY_TERM
    )
    gain_direction = gains_grad * lax.rsqrt(gain_state)
    local_sums = []
    for parts in prepared:
        local_sums = local_sums + [parts[1], parts[2], parts[3]]
    local_sums = local_sums + [jnp.sum(gains * gains, axis=1)]
    totals = lax.psum(tuple(local_sums), "fsdp")
    updated = []
    col_results = []
    for place_index in range(len(batches)):
        gradient, weight, row_state, col_state = batches[place_index]
        whole_rows = weight.shape[1] * fsdp_count
        direction, col_moment = column_step(
            gradient,
            prepared[place_index][0],
            col_state,
            totals[3 * place_index],
            totals[3 * place_index + 1],
            whole_rows,
        )
        count_all = whole_rows * weight.shape[2]
        updated.append(
            apply_optimizer_update(weight, direction, totals[3 * place_index + 2] / count_all)
        )
        col_results.append(col_moment)
    gain_width = gains.shape[1] * fsdp_count
    gain_offset = 3 * len(batches)
    new_gains = apply_optimizer_update(gains, gain_direction, totals[gain_offset] / gain_width)
    table_state = DECAY_RATE * table_moment + (1.0 - DECAY_RATE) * (
        table_grad * table_grad + TINY_TERM
    )
    table_direction = table_grad * lax.rsqrt(table_state)
    new_table = apply_optimizer_update(table, table_direction, jnp.mean(table * table))
    return (
        layer_out,
        input_grad,
        memory_grad,
        self_grad,
        cross_grad,
        ffn_in_grad,
        feedforward_output_gradient,
        gains_grad,
        table_grad,
        updated[0],
        updated[1],
        updated[2],
        updated[3][0],
        new_gains,
        new_table,
        prepared[0][0],
        col_results[0],
        prepared[1][0],
        col_results[1],
        prepared[2][0],
        col_results[2],
        prepared[3][0][0],
        col_results[3][0],
        gain_state,
        table_state,
    )


def solution(mesh):
    placed = (
        P(("rep", "fsdp"), None, None),
        P(("rep", "fsdp"), None, None),
        P(("rep", "fsdp"), None, None),
        P(("rep", "fsdp")),
        P(("rep", "fsdp")),
        P(),
        P(None, "fsdp", None),
        P(None, "fsdp", None),
        P(None, "fsdp", None),
        P("fsdp", None),
        P(None, "fsdp"),
        P(),
        P(None, "fsdp"),
        P(),
        P(None, "fsdp"),
        P(),
        P(None, "fsdp"),
        P(),
        P("fsdp"),
        P(),
        P(None, "fsdp"),
        P(),
    )
    return jax.shard_map(
        per_device,
        mesh=mesh,
        in_specs=placed,
        out_specs=(
            P(("rep", "fsdp"), None, None),
            P(("rep", "fsdp"), None, None),
            P(("rep", "fsdp"), None, None),
            P(None, "fsdp", None),
            P(None, "fsdp", None),
            P(None, "fsdp", None),
            P("fsdp", None),
            P(None, "fsdp"),
            P(),
            P(None, "fsdp", None),
            P(None, "fsdp", None),
            P(None, "fsdp", None),
            P("fsdp", None),
            P(None, "fsdp"),
            P(),
            P(None, "fsdp"),
            P(),
            P(None, "fsdp"),
            P(),
            P(None, "fsdp"),
            P(),
            P("fsdp"),
            P(),
            P(None, "fsdp"),
            P(),
        ),
        check_vma=False,
    )
```

```python
import functools
import math

import jax
import jax.numpy as jnp
from jax import lax
from jax.experimental import pallas as pl
from jax.experimental.pallas import tpu as pltpu
from jax.sharding import PartitionSpec as P

H = 12
DH = 64
BUCKETS = 32
DECAY_RATE = 0.8
STEP_RATE = 0.2
TINY_TERM = 1e-30
EXACT_ARITHMETIC = lax.Precision.HIGHEST
PAIR = 2 * DH
GROUP = 4 * DH
HIDDEN = -1e30
VMEM_BYTES = 60 * 1024 * 1024
LOW = jnp.bfloat16
WIDE = jnp.float32


def nn(left, right):
    return lax.dot_general(left, right, (((1,), (0,)), ((), ())), preferred_element_type=WIDE)


def nt(left, right):
    return lax.dot_general(left, right, (((1,), (1,)), ((), ())), preferred_element_type=WIDE)


def tn(left, right):
    return lax.dot_general(left, right, (((0,), (0,)), ((), ())), preferred_element_type=WIDE)


def rms_rate(rows):
    return lax.rsqrt(jnp.mean(rows * rows, axis=-1, keepdims=True) + 1e-06)


def three_parts(column):
    high = column.astype(LOW)
    rest = column - high.astype(WIDE)
    middle = rest.astype(LOW)
    low = (rest - middle.astype(WIDE)).astype(LOW)
    return high, middle, low


def chunks(total, size):
    return [(at, min(size, total - at)) for at in range(0, total, size)]


def lanes(rows):
    return lax.broadcasted_iota(jnp.int32, (rows, PAIR), 1)


def own_lanes(rows, side):
    lane = lanes(rows)
    return (lane >= DH * side) & (lane < DH * (side + 1))


def key_extras(rows, side, length):
    lane = lanes(rows) - DH * (1 - side)
    dead = lax.broadcasted_iota(jnp.int32, (rows, PAIR), 0) >= length
    mask = jnp.where(dead, HIDDEN, 0.0)
    return jnp.where(
        (lane >= 0) & (lane < 3), 1.0, jnp.where(lane == 3, mask, 0.0)
    ).astype(LOW)


def row_extras(rows, side, column, last):
    lane = lanes(rows) - DH * (1 - side)
    high, middle, low = three_parts(column)
    wide = lambda part: jnp.broadcast_to(part.astype(WIDE), (rows, PAIR))
    return jnp.where(
        lane == 0,
        wide(high),
        jnp.where(
            lane == 1, wide(middle), jnp.where(lane == 2, wide(low), jnp.where(lane == 3, last, 0.0))
        ),
    ).astype(LOW)


def forward_body(causal, seq_count, length_ref, wave_ref, bias_ref, q_ref, k_ref, v_ref, mix_ref, total_ref, group):
    rows = q_ref.shape[0] // seq_count
    keys = k_ref.shape[0] // seq_count
    block = 256
    for pair in range(2):
        at = pair * PAIR
        for side in range(2):
            head = 2 * pair + side
            if causal:
                wave = wave_ref[pl.ds(group * 4 + head, 1), :]
                spread = pltpu.roll(
                    jnp.broadcast_to(wave, (rows, keys)), 0, 1, stride=1, stride_axis=0
                )
                row = lax.broadcasted_iota(jnp.int32, (rows, keys), 0)
                column = lax.broadcasted_iota(jnp.int32, (rows, keys), 1)
                bias_ref[side] = jnp.where(column <= row, spread, HIDDEN)
        for seq in range(seq_count):
            outs = []
            for side in range(2):
                own_q = own_lanes(rows, side)
                own_k = own_lanes(keys, side)
                query = jnp.where(
                    own_q,
                    q_ref[seq * rows : (seq + 1) * rows, at : at + PAIR],
                    (lanes(rows) == DH * (1 - side) + 3).astype(LOW),
                )
                key = jnp.where(
                    own_k,
                    k_ref[seq * keys : (seq + 1) * keys, at : at + PAIR],
                    key_extras(keys, side, length_ref[seq]),
                )
                value = jnp.where(
                    own_k,
                    v_ref[seq * keys : (seq + 1) * keys, at : at + PAIR],
                    jnp.ones((), LOW),
                )
                parts = []
                for start in range(0, rows, block):
                    span = start + block if causal else keys
                    scores = nt(query[start : start + block], key[:span])
                    if causal:
                        scores = scores + bias_ref[side, start : start + block, :span]
                    top = jnp.max(scores, axis=1, keepdims=True)
                    weight = jnp.exp(scores - top)
                    out = nn(weight.astype(LOW), value[:span])
                    total = out[:, DH * (1 - side) : DH * (1 - side) + 1]
                    parts.append(out * (1.0 / total))
                    spot = pl.ds(seq * rows + start, block)
                    lane = lanes(block)
                    seen = total_ref[spot, :] if (pair or side) else jnp.zeros((block, PAIR), WIDE)
                    total_ref[spot, :] = jnp.where(
                        lane == 2 * pair + side, top + jnp.log(total), seen
                    )
                outs.append(jnp.concatenate(parts, axis=0))
            mix_ref[seq * rows : (seq + 1) * rows, at : at + PAIR] = jnp.where(
                own_lanes(rows, 0), outs[0], outs[1]
            ).astype(LOW)


def forward_kernel(
    causal, seq_count, length_ref, x_ref, source_ref, gain_ref, wq_ref, wk_ref, wv_ref, wo_ref, wave_ref,
    q_ref, k_ref, v_ref, mix_ref, total_ref, after_ref, normed, bias,
):
    group = pl.program_id(0)

    @pl.when(group == 0)
    def _():
        for at, size in chunks(x_ref.shape[0], 256):
            rows = x_ref[at : at + size, :].astype(WIDE)
            normed[at : at + size, :] = (rows * rms_rate(rows) * gain_ref[...]).astype(LOW)
            after_ref[at : at + size, :] = rows

    source = normed if causal else source_ref
    q_ref[...] = nn(normed[...], wq_ref[...]).astype(LOW)
    k_ref[...] = nn(source[...], wk_ref[...]).astype(LOW)
    v_ref[...] = nn(source[...], wv_ref[...]).astype(LOW)
    forward_body(causal, seq_count, length_ref, wave_ref, bias, q_ref, k_ref, v_ref, mix_ref, total_ref, group)
    after_ref[...] += nn(mix_ref[...], wo_ref[...])


def weight_specs(width):
    across = lambda at: pl.BlockSpec((None, width, GROUP), lambda g, at=at: (at, 0, g))
    return [across(0), across(1), across(2), pl.BlockSpec((None, GROUP, width), lambda g: (3, g, 0))]


def whole(shape):
    return pl.BlockSpec(shape, lambda g: (0,) * len(shape))


def columns(rows):
    return pl.BlockSpec((rows, GROUP), lambda g: (0, g))


def attention_forward(causal, x, source, lengths, gain, weights, wave):
    row_count, width = x.shape
    seq_count = lengths.shape[0]
    source_rows = row_count if causal else source.shape[0]
    length = row_count // seq_count
    groups = width // GROUP
    low = lambda rows: jax.ShapeDtypeStruct((rows, width), LOW)
    args = [lengths, x, source, gain, weights, weights, weights, weights, wave]
    return pl.pallas_call(
        functools.partial(forward_kernel, causal, seq_count),
        grid=(groups,),
        in_specs=[
            pl.BlockSpec(memory_space=pltpu.SMEM),
            whole(x.shape),
            whole(source.shape),
            whole(gain.shape),
            *weight_specs(width),
            whole(wave.shape),
        ],
        out_specs=[
            columns(row_count),
            columns(source_rows),
            columns(source_rows),
            columns(row_count),
            pl.BlockSpec((None, row_count, PAIR), lambda g: (g, 0, 0)),
            whole((row_count, width)),
        ],
        out_shape=[
            low(row_count),
            low(source_rows),
            low(source_rows),
            low(row_count),
            jax.ShapeDtypeStruct((groups, row_count, PAIR), WIDE),
            jax.ShapeDtypeStruct((row_count, width), WIDE),
        ],
        scratch_shapes=[
            pltpu.VMEM((row_count, width), LOW),
            pltpu.VMEM((2, length, length) if causal else (1, 8, PAIR), WIDE),
        ],
        compiler_params=pltpu.CompilerParams(vmem_limit_bytes=VMEM_BYTES),
        name="self_forward" if causal else "cross_forward",
    )(*args)


def gelu_parts(gate):
    root = 0.7978845608028654
    square = gate * gate
    inner = jnp.tanh(root * gate * (1.0 + 0.044715 * square))
    half = 0.5 * (1.0 + inner)
    value = gate * half
    slope = half + 0.5 * gate * (1.0 - inner * inner) * (root * (1.0 + 3 * 0.044715 * square))
    return value, slope


def rms_back(rows, gain, grad):
    rate = rms_rate(rows)
    scaled = rows * rate
    low = grad * gain
    grad_rows = rate * (low - scaled * jnp.mean(scaled * low, axis=-1, keepdims=True))
    return grad_rows, jnp.sum(grad * scaled, axis=0, keepdims=True)


def feed_kernel(
    seq_count, length_ref, after_ref, out_grad_ref, gain_ref, wg_ref, wu_ref, wd_ref,
    layer_ref, grad_cross_ref, dwg_ref, dwu_ref, dwd_ref, dgain_ref,
    normed, normed_t, down, out_total, grad_total,
):
    step = pl.program_id(0)
    row_count = after_ref.shape[0]
    length = row_count // seq_count

    def live(at, size):
        position = lax.broadcasted_iota(jnp.int32, (size, 1), 0) + (at % length)
        return (position < length_ref[at // length]).astype(WIDE)

    @pl.when(step == 0)
    def _():
        for at, size in chunks(row_count, 256):
            rows = after_ref[at : at + size, :]
            low = (rows * rms_rate(rows) * gain_ref[...]).astype(LOW)
            normed[at : at + size, :] = low
            normed_t[:, at : at + size] = low.T
            down[at : at + size, :] = (
                out_grad_ref[at : at + size, :].astype(WIDE) * live(at, size)
            ).astype(LOW)
            out_total[at : at + size, :] = rows
            grad_total[at : at + size, :] = jnp.zeros((size, rows.shape[1]), WIDE)

    gate = nn(normed[...], wg_ref[...])
    up = nn(normed[...], wu_ref[...])
    value, slope = gelu_parts(gate)
    hidden = (value * up).astype(LOW)
    out_total[...] += nn(hidden, wd_ref[...])
    grad_hidden = nt(down[...], wd_ref[...])
    dwd_ref[...] = tn(hidden, down[...]).astype(LOW)
    grad_gate = (grad_hidden * up * slope).astype(LOW)
    grad_up = (grad_hidden * value).astype(LOW)
    dwg_ref[...] = nn(normed_t[...], grad_gate).astype(LOW)
    dwu_ref[...] = nn(normed_t[...], grad_up).astype(LOW)
    grad_total[...] += nt(grad_gate, wg_ref[...]) + nt(grad_up, wu_ref[...])

    @pl.when(step == pl.num_programs(0) - 1)
    def _():
        dgain = jnp.zeros(dgain_ref.shape, WIDE)
        for at, size in chunks(row_count, 256):
            part = slice(at, at + size)
            layer_ref[part, :] = (out_total[part, :] * live(at, size)).astype(LOW)
            grad_rows, gain_part = rms_back(after_ref[part, :], gain_ref[...], grad_total[part, :])
            dgain = dgain + gain_part
            grad_cross_ref[part, :] = (
                out_grad_ref[part, :].astype(WIDE) * live(at, size) + grad_rows
            )
        dgain_ref[...] = dgain


def feed_forward_both(after, out_grad, lengths, gain, w_in, w_out, block=256):
    row_count, width = after.shape
    hidden = w_out.shape[0]
    seq_count = lengths.shape[0]
    wide = pl.BlockSpec((None, width, block), lambda g: (0, 0, g))
    wide_up = pl.BlockSpec((None, width, block), lambda g: (1, 0, g))
    tall = pl.BlockSpec((block, width), lambda g: (g, 0))
    flat = pl.BlockSpec((width, block), lambda g: (0, g))
    return pl.pallas_call(
        functools.partial(feed_kernel, seq_count),
        grid=(hidden // block,),
        in_specs=[
            pl.BlockSpec(memory_space=pltpu.SMEM),
            whole(after.shape),
            whole(out_grad.shape),
            whole(gain.shape),
            wide,
            wide_up,
            tall,
        ],
        out_specs=[whole(after.shape), whole(after.shape), flat, flat, tall, whole((1, width))],
        out_shape=[
            jax.ShapeDtypeStruct((row_count, width), LOW),
            jax.ShapeDtypeStruct((row_count, width), WIDE),
            jax.ShapeDtypeStruct((width, hidden), LOW),
            jax.ShapeDtypeStruct((width, hidden), LOW),
            jax.ShapeDtypeStruct((hidden, width), LOW),
            jax.ShapeDtypeStruct((1, width), WIDE),
        ],
        scratch_shapes=[
            pltpu.VMEM((row_count, width), LOW),
            pltpu.VMEM((width, row_count), LOW),
            pltpu.VMEM((row_count, width), LOW),
            pltpu.VMEM((row_count, width), WIDE),
            pltpu.VMEM((row_count, width), WIDE),
        ],
        compiler_params=pltpu.CompilerParams(vmem_limit_bytes=VMEM_BYTES),
        name="feed_forward_both",
    )(lengths, after, out_grad, gain, w_in, w_in, w_out)


def backward_kernel(
    causal, seq_count, length_ref, x_ref, source_ref, grad_ref, gain_ref, wq_ref, wk_ref, wv_ref, wo_ref, wave_ref,
    q_ref, k_ref, v_ref, mix_ref, total_ref,
    grad_x_ref, gk_out_ref, gv_out_ref, dwq_ref, dwk_ref, dwv_ref, dwo_ref, dgain_ref, dist_ref,
    normed_t, source_t, branch, grad_mix, gq, bias, score_sum, grad_total,
):
    group = pl.program_id(0)
    row_count = x_ref.shape[0]
    rows = q_ref.shape[0] // seq_count
    keys = k_ref.shape[0] // seq_count
    block = 256

    @pl.when(group == 0)
    def _():
        for at, size in chunks(row_count, 256):
            value = x_ref[at : at + size, :].astype(WIDE)
            low = (value * rms_rate(value) * gain_ref[...]).astype(LOW)
            normed_t[:, at : at + size] = low.T
            branch[at : at + size, :] = grad_ref[at : at + size, :].astype(LOW)
            grad_total[at : at + size, :] = jnp.zeros((size, value.shape[1]), WIDE)
        if not causal:
            for at, size in chunks(source_ref.shape[0], 256):
                source_t[:, at : at + size] = source_ref[at : at + size, :].T

    grad_mix[...] = nt(branch[...], wo_ref[...]).astype(LOW)
    dwo_ref[...] = tn(mix_ref[...], branch[...]).astype(LOW)

    for pair in range(2):
        at = pair * PAIR
        if causal:
            for side in range(2):
                head = 2 * pair + side
                wave = wave_ref[pl.ds(group * 4 + head, 1), :]
                spread = pltpu.roll(
                    jnp.broadcast_to(wave, (keys, rows)), 0, 1, stride=1, stride_axis=0
                )
                row = lax.broadcasted_iota(jnp.int32, (keys, rows), 0)
                column = lax.broadcasted_iota(jnp.int32, (keys, rows), 1)
                bias[side] = jnp.where(column >= row, spread, HIDDEN)
        for seq in range(seq_count):
            span_q = slice(seq * rows, (seq + 1) * rows)
            span_k = slice(seq * keys, (seq + 1) * keys)
            sides = []
            for side in range(2):
                head = 2 * pair + side
                own_q = own_lanes(rows, side)
                own_k = own_lanes(keys, side)
                total = jnp.sum(
                    jnp.where(lanes(rows) == head, total_ref[span_q, :], 0.0), axis=1, keepdims=True
                )
                grad_low = grad_mix[span_q, at : at + PAIR]
                product = grad_low.astype(WIDE) * mix_ref[span_q, at : at + PAIR].astype(WIDE)
                delta = jnp.sum(jnp.where(own_q, product, 0.0), axis=1, keepdims=True)
                query = jnp.where(
                    own_q, q_ref[span_q, at : at + PAIR], row_extras(rows, side, -total, 1.0)
                )
                grad_out = jnp.where(own_q, grad_low, row_extras(rows, side, -delta, 0.0))
                key = jnp.where(
                    own_k,
                    k_ref[span_k, at : at + PAIR],
                    key_extras(keys, side, length_ref[seq]),
                )
                value = jnp.where(own_k, v_ref[span_k, at : at + PAIR], jnp.ones((), LOW))
                grad_query = []
                grad_key = None
                grad_value = None
                for start in range(0, rows, block):
                    span = start + block if causal else keys
                    scores = nt(key[:span], query[start : start + block])
                    if causal:
                        scores = scores + bias[side, :span, start : start + block]
                    weight = jnp.exp(scores)
                    low = weight.astype(LOW)
                    grad_weight = nt(value[:span], grad_out[start : start + block])
                    grad_score = (weight * grad_weight).astype(LOW)
                    if causal:
                        if seq == 0:
                            score_sum[side, :span, start : start + block] = grad_score.astype(WIDE)
                        else:
                            score_sum[side, :span, start : start + block] += grad_score.astype(WIDE)
                    key_part = nn(grad_score, query[start : start + block])
                    value_part = nn(low, grad_out[start : start + block])
                    grad_query.append(tn(grad_score, key[:span]))
                    if causal and start == 0 and rows > block:
                        rest = jnp.zeros((keys - span, PAIR), WIDE)
                        key_part = jnp.concatenate([key_part, rest], axis=0)
                        value_part = jnp.concatenate([value_part, rest], axis=0)
                    grad_key = key_part if grad_key is None else grad_key + key_part
                    grad_value = value_part if grad_value is None else grad_value + value_part
                sides.append((jnp.concatenate(grad_query, axis=0), grad_key, grad_value))
            pick_q = own_lanes(rows, 0)
            pick_k = own_lanes(keys, 0)
            gq[span_q, at : at + PAIR] = jnp.where(pick_q, sides[0][0], sides[1][0]).astype(LOW)
            gk_out_ref[span_k, at : at + PAIR] = jnp.where(pick_k, sides[0][1], sides[1][1]).astype(LOW)
            gv_out_ref[span_k, at : at + PAIR] = jnp.where(pick_k, sides[0][2], sides[1][2]).astype(LOW)
        if causal:
            for side in range(2):
                head = 2 * pair + side
                row = lax.broadcasted_iota(jnp.int32, (keys, rows), 0)
                column = lax.broadcasted_iota(jnp.int32, (keys, rows), 1)
                held = jnp.where(column >= row, score_sum[side], 0.0)
                while held.shape[0] > 1:
                    half = held.shape[0] // 2
                    held = held[:half] + pltpu.roll(held[half:], rows - half, 1)
                dist_ref[pl.ds(group * 4 + head, 1), :] = held

    if causal:
        source_t = normed_t
    dwq_ref[...] = nn(normed_t[...], gq[...]).astype(LOW)
    dwk_ref[...] = nn(source_t[...], gk_out_ref[...]).astype(LOW)
    dwv_ref[...] = nn(source_t[...], gv_out_ref[...]).astype(LOW)
    update = nt(gq[...], wq_ref[...])
    if causal:
        update = update + nt(gk_out_ref[...], wk_ref[...]) + nt(gv_out_ref[...], wv_ref[...])
    grad_total[...] += update

    @pl.when(group == pl.num_programs(0) - 1)
    def _():
        dgain = jnp.zeros(dgain_ref.shape, WIDE)
        for at, size in chunks(row_count, 256):
            part = slice(at, at + size)
            grad_rows, gain_part = rms_back(
                x_ref[part, :].astype(WIDE), gain_ref[...], grad_total[part, :]
            )
            dgain = dgain + gain_part
            grad_x_ref[part, :] = grad_ref[part, :] + grad_rows
        dgain_ref[...] = dgain


def attention_backward(causal, x, source, grad, lengths, gain, weights, wave, kept):
    row_count, width = x.shape
    seq_count = lengths.shape[0]
    source_rows = row_count if causal else source.shape[0]
    length = row_count // seq_count
    groups = width // GROUP
    low = lambda rows: jax.ShapeDtypeStruct((rows, width), LOW)
    grad_columns = pl.BlockSpec((width, GROUP), lambda g: (0, g))
    grad_rows = pl.BlockSpec((GROUP, width), lambda g: (g, 0))
    square = jax.ShapeDtypeStruct((width, width), LOW)
    score = (2, length, length) if causal else (1, 8, PAIR)
    return pl.pallas_call(
        functools.partial(backward_kernel, causal, seq_count),
        grid=(groups,),
        in_specs=[
            pl.BlockSpec(memory_space=pltpu.SMEM),
            whole(x.shape),
            whole(source.shape),
            whole(grad.shape),
            whole(gain.shape),
            *weight_specs(width),
            whole(wave.shape),
            columns(row_count),
            columns(source_rows),
            columns(source_rows),
            columns(row_count),
            pl.BlockSpec((None, row_count, PAIR), lambda g: (g, 0, 0)),
        ],
        out_specs=[
            whole((row_count, width)),
            columns(source_rows),
            columns(source_rows),
            grad_columns,
            grad_columns,
            grad_columns,
            grad_rows,
            whole((1, width)),
            whole(wave.shape),
        ],
        out_shape=[
            jax.ShapeDtypeStruct((row_count, width), WIDE),
            low(source_rows),
            low(source_rows),
            square,
            square,
            square,
            square,
            jax.ShapeDtypeStruct((1, width), WIDE),
            jax.ShapeDtypeStruct(wave.shape, WIDE),
        ],
        scratch_shapes=[
            pltpu.VMEM((width, row_count), LOW),
            pltpu.VMEM((width, source_rows) if not causal else (16, PAIR), LOW),
            pltpu.VMEM((row_count, width), LOW),
            pltpu.VMEM((row_count, GROUP), LOW),
            pltpu.VMEM((row_count, GROUP), LOW),
            pltpu.VMEM(score, WIDE),
            pltpu.VMEM(score, WIDE),
            pltpu.VMEM((row_count, width), WIDE),
        ],
        compiler_params=pltpu.CompilerParams(vmem_limit_bytes=VMEM_BYTES),
        name="self_backward" if causal else "cross_backward",
    )(lengths, x, source, grad, gain, weights, weights, weights, weights, wave, *kept)


def memory_kernel(gk_ref, gv_ref, wk_ref, wv_ref, out_ref):
    out_ref[...] = nt(gk_ref[...], wk_ref[...]) + nt(gv_ref[...], wv_ref[...])


def memory_gradient(grad_key, grad_value, weights):
    rows, width = grad_key.shape
    block = 256
    rowwise = pl.BlockSpec((block, width), lambda g: (g, 0))
    matrix = lambda at: pl.BlockSpec((None, width, width), lambda g: (at, 0, 0))
    return pl.pallas_call(
        memory_kernel,
        grid=(rows // block,),
        in_specs=[rowwise, rowwise, matrix(1), matrix(2)],
        out_specs=rowwise,
        out_shape=jax.ShapeDtypeStruct((rows, width), WIDE),
        compiler_params=pltpu.CompilerParams(vmem_limit_bytes=VMEM_BYTES),
        name="memory_gradient",
    )(grad_key, grad_value, weights, weights)


def row_parts(gradient, weight, row_state):
    squares = gradient * gradient + TINY_TERM
    row_moment = DECAY_RATE * row_state + (1.0 - DECAY_RATE) * jnp.mean(squares, axis=2)
    return (
        row_moment,
        jnp.sum(squares, axis=1),
        jnp.sum(row_moment, axis=1),
        jnp.sum(weight * weight, axis=(1, 2)),
    )


def column_step(gradient, row_moment, col_state, col_sum, row_sum, whole_rows):
    col_moment = DECAY_RATE * col_state + (1.0 - DECAY_RATE) * col_sum / whole_rows
    row_mean = row_sum / whole_rows
    direction = gradient * lax.rsqrt(
        row_moment[:, :, None] * col_moment[:, None, :] / row_mean[:, None, None]
    )
    return (direction, col_moment)


def apply_optimizer_update(weight, direction, weight_square):
    step_size = STEP_RATE * jnp.sqrt(weight_square + 1e-06)
    ratio = step_size.reshape((-1,) + (1,) * (weight.ndim - 1))
    return weight - ratio * direction


def per_device(
    dec_in,
    memory,
    out_grad,
    dec_len,
    enc_len,
    buckets,
    self_weight,
    cross_weight,
    ffn_in,
    ffn_out,
    gains,
    table,
    self_rows,
    self_cols,
    cross_rows,
    cross_cols,
    in_rows,
    in_cols,
    out_rows,
    out_cols,
    gain_moment,
    table_moment,
):
    seq_count, seq_length, model_width = dec_in.shape
    mem_length = memory.shape[1]
    row_count = seq_count * seq_length
    hidden_width = ffn_in.shape[2]
    w_self = lax.all_gather(self_weight.astype(LOW), "fsdp", axis=1, tiled=True)
    gain_full = lax.all_gather(gains.astype(LOW), "fsdp", axis=1, tiled=True).astype(WIDE)
    w_cross = lax.all_gather(cross_weight.astype(LOW), "fsdp", axis=1, tiled=True)
    w_in = lax.all_gather(ffn_in.astype(LOW), "fsdp", axis=1, tiled=True)
    w_out = lax.all_gather(ffn_out.astype(LOW), "fsdp", axis=0, tiled=True)
    col_whole = (self_cols, cross_cols, in_cols, out_cols)

    bucket_mask = (buckets[None, :] == jnp.arange(BUCKETS)[:, None]).astype(WIDE)
    by_distance = jnp.sum(table.T[:, :, None] * bucket_mask[None], axis=1)
    by_distance = jnp.pad(by_distance, ((0, 16 - H), (0, 0)))
    backwards = jnp.roll(by_distance[:, ::-1], 1, axis=1)
    no_bias = jnp.zeros((8, PAIR), WIDE)
    no_source = jnp.zeros((16, PAIR), LOW)

    dec_rows = dec_in.reshape(row_count, model_width)
    mem_rows = memory.reshape(seq_count * mem_length, model_width)
    grad_rows = out_grad.reshape(row_count, model_width)
    *kept_one, after_self = attention_forward(
        True, dec_rows, no_source, dec_len, gain_full[0:1], w_self, backwards
    )
    *kept_two, after_cross = attention_forward(
        False, after_self, mem_rows, enc_len, gain_full[1:2], w_cross, no_bias
    )
    layer_out, grad_cross, grad_wg, grad_wu, grad_wd, gain_three = feed_forward_both(
        after_cross, grad_rows, dec_len, gain_full[2:3], w_in, w_out
    )
    grad_self, grad_k_two, grad_v_two, *cross_parts, gain_two, _ = attention_backward(
        False, after_self, mem_rows, grad_cross, enc_len, gain_full[1:2], w_cross, no_bias, kept_two
    )
    memory_grad = memory_gradient(grad_k_two, grad_v_two, w_cross)
    input_grad, _, _, *self_parts, gain_one, dist_grad = attention_backward(
        True, dec_rows, no_source, grad_self, dec_len, gain_full[0:1], w_self, by_distance, kept_one
    )
    layer_out = layer_out.reshape(dec_in.shape)
    input_grad = input_grad.reshape(dec_in.shape)
    memory_grad = memory_grad.reshape(memory.shape)
    table_part = jnp.sum(bucket_mask[:, None, :] * dist_grad[None, :H, :], axis=2)

    owned = (
        lax.psum_scatter(jnp.stack(self_parts), "fsdp", scatter_dimension=1, tiled=True),
        lax.psum_scatter(jnp.stack(cross_parts), "fsdp", scatter_dimension=1, tiled=True),
        lax.psum_scatter(jnp.stack([grad_wg, grad_wu]), "fsdp", scatter_dimension=1, tiled=True),
        lax.psum_scatter(grad_wd, "fsdp", scatter_dimension=0, tiled=True),
    )
    owned = [lax.psum(member, "rep").astype(WIDE) for member in owned]
    small = jnp.concatenate(
        [gain_one.reshape(-1), gain_two.reshape(-1), gain_three.reshape(-1), table_part.reshape(-1)]
    )
    small = lax.psum(small, ("rep", "fsdp"))
    gain_total = small[: 3 * model_width].reshape(3, model_width)
    gain_mine = lax.dynamic_slice_in_dim(
        gain_total, lax.axis_index("fsdp") * gains.shape[1], gains.shape[1], axis=1
    )
    table_total = small[3 * model_width :].reshape(BUCKETS, H)
    owned.append(gain_mine)
    fsdp_count = lax.axis_size("fsdp")
    grad_factor = 1.0 / math.sqrt(row_count * lax.axis_size("rep") * fsdp_count)
    self_grad, cross_grad, ffn_in_grad, feedforward_output_gradient, gains_grad = [
        member * grad_factor for member in owned
    ]
    table_grad = table_total * grad_factor
    batches = [
        (self_grad, self_weight, self_rows, col_whole[0]),
        (cross_grad, cross_weight, cross_rows, col_whole[1]),
        (ffn_in_grad, ffn_in, in_rows, col_whole[2]),
        (feedforward_output_gradient[None], ffn_out[None], out_rows[None], col_whole[3][None]),
    ]
    prepared = [
        row_parts(gradient, weight, row_state) for gradient, weight, row_state, col_state in batches
    ]
    gain_state = DECAY_RATE * gain_moment + (1.0 - DECAY_RATE) * (
        gains_grad * gains_grad + TINY_TERM
    )
    gain_direction = gains_grad * lax.rsqrt(gain_state)
    local_sums = []
    for parts in prepared:
        local_sums = local_sums + [parts[1], parts[2], parts[3]]
    local_sums = local_sums + [jnp.sum(gains * gains, axis=1)]
    totals = lax.psum(tuple(local_sums), "fsdp")
    updated = []
    col_results = []
    for place_index in range(len(batches)):
        gradient, weight, row_state, col_state = batches[place_index]
        whole_rows = weight.shape[1] * fsdp_count
        direction, col_moment = column_step(
            gradient,
            prepared[place_index][0],
            col_state,
            totals[3 * place_index],
            totals[3 * place_index + 1],
            whole_rows,
        )
        count_all = whole_rows * weight.shape[2]
        updated.append(
            apply_optimizer_update(weight, direction, totals[3 * place_index + 2] / count_all)
        )
        col_results.append(col_moment)
    gain_width = gains.shape[1] * fsdp_count
    gain_offset = 3 * len(batches)
    new_gains = apply_optimizer_update(gains, gain_direction, totals[gain_offset] / gain_width)
    table_state = DECAY_RATE * table_moment + (1.0 - DECAY_RATE) * (
        table_grad * table_grad + TINY_TERM
    )
    table_direction = table_grad * lax.rsqrt(table_state)
    new_table = apply_optimizer_update(table, table_direction, jnp.mean(table * table))
    return (
        layer_out,
        input_grad,
        memory_grad,
        self_grad,
        cross_grad,
        ffn_in_grad,
        feedforward_output_gradient,
        gains_grad,
        table_grad,
        updated[0],
        updated[1],
        updated[2],
        updated[3][0],
        new_gains,
        new_table,
        prepared[0][0],
        col_results[0],
        prepared[1][0],
        col_results[1],
        prepared[2][0],
        col_results[2],
        prepared[3][0][0],
        col_results[3][0],
        gain_state,
        table_state,
    )


def solution(mesh):
    placed = (
        P(("rep", "fsdp"), None, None),
        P(("rep", "fsdp"), None, None),
        P(("rep", "fsdp"), None, None),
        P(("rep", "fsdp")),
        P(("rep", "fsdp")),
        P(),
        P(None, "fsdp", None),
        P(None, "fsdp", None),
        P(None, "fsdp", None),
        P("fsdp", None),
        P(None, "fsdp"),
        P(),
        P(None, "fsdp"),
        P(),
        P(None, "fsdp"),
        P(),
        P(None, "fsdp"),
        P(),
        P("fsdp"),
        P(),
        P(None, "fsdp"),
        P(),
    )
    return jax.shard_map(
        per_device,
        mesh=mesh,
        in_specs=placed,
        out_specs=(
            P(("rep", "fsdp"), None, None),
            P(("rep", "fsdp"), None, None),
            P(("rep", "fsdp"), None, None),
            P(None, "fsdp", None),
            P(None, "fsdp", None),
            P(None, "fsdp", None),
            P("fsdp", None),
            P(None, "fsdp"),
            P(),
            P(None, "fsdp", None),
            P(None, "fsdp", None),
            P(None, "fsdp", None),
            P("fsdp", None),
            P(None, "fsdp"),
            P(),
            P(None, "fsdp"),
            P(),
            P(None, "fsdp"),
            P(),
            P(None, "fsdp"),
            P(),
            P("fsdp"),
            P(),
            P(None, "fsdp"),
            P(),
        ),
        check_vma=False,
    )
```

```python
import functools
import math

import jax
import jax.numpy as jnp
from jax import lax
from jax.experimental import pallas as pl
from jax.experimental.pallas import tpu as pltpu
from jax.sharding import PartitionSpec as P

H = 12
DH = 64
BUCKETS = 32
DECAY_RATE = 0.8
STEP_RATE = 0.2
TINY_TERM = 1e-30
PAIR = 2 * DH
GROUP = 4 * DH
HIDDEN = -1e30
VMEM_BYTES = 60 * 1024 * 1024
PEAK = 1.15e9
LOW = jnp.bfloat16
WIDE = jnp.float32


def nn(left, right):
    return lax.dot_general(left, right, (((1,), (0,)), ((), ())), preferred_element_type=WIDE)


def nt(left, right):
    return lax.dot_general(left, right, (((1,), (1,)), ((), ())), preferred_element_type=WIDE)


def tn(left, right):
    return lax.dot_general(left, right, (((0,), (0,)), ((), ())), preferred_element_type=WIDE)


def rms_rate(rows):
    return lax.rsqrt(jnp.mean(rows * rows, axis=-1, keepdims=True) + 1e-06)


def three_parts(column):
    high = column.astype(LOW)
    rest = column - high.astype(WIDE)
    middle = rest.astype(LOW)
    low = (rest - middle.astype(WIDE)).astype(LOW)
    return high, middle, low


def chunks(total, size):
    return [(at, min(size, total - at)) for at in range(0, total, size)]


def lanes(rows):
    return lax.broadcasted_iota(jnp.int32, (rows, PAIR), 1)


def own_lanes(rows, side):
    lane = lanes(rows)
    return (lane >= DH * side) & (lane < DH * (side + 1))


def key_extras(rows, side, length):
    lane = lanes(rows) - DH * (1 - side)
    dead = lax.broadcasted_iota(jnp.int32, (rows, PAIR), 0) >= length
    mask = jnp.where(dead, HIDDEN, 0.0)
    return jnp.where(
        (lane >= 0) & (lane < 3), 1.0, jnp.where(lane == 3, mask, 0.0)
    ).astype(LOW)


def row_extras(rows, side, column, last):
    lane = lanes(rows) - DH * (1 - side)
    high, middle, low = three_parts(column)
    wide = lambda part: jnp.broadcast_to(part.astype(WIDE), (rows, PAIR))
    return jnp.where(
        lane == 0,
        wide(high),
        jnp.where(
            lane == 1, wide(middle), jnp.where(lane == 2, wide(low), jnp.where(lane == 3, last, 0.0))
        ),
    ).astype(LOW)


def forward_body(causal, seq_count, length_ref, wave_ref, bias_ref, q_ref, k_ref, v_ref, mix_ref, total_ref, group):
    rows = q_ref.shape[0] // seq_count
    keys = k_ref.shape[0] // seq_count
    block = 256
    for pair in range(2):
        at = pair * PAIR
        for side in range(2):
            head = 2 * pair + side
            if causal:
                wave = wave_ref[pl.ds(group * 4 + head, 1), :]
                spread = pltpu.roll(
                    jnp.broadcast_to(wave, (rows, keys)), 0, 1, stride=1, stride_axis=0
                )
                row = lax.broadcasted_iota(jnp.int32, (rows, keys), 0)
                column = lax.broadcasted_iota(jnp.int32, (rows, keys), 1)
                bias_ref[side] = jnp.where(column <= row, spread, HIDDEN)
        for seq in range(seq_count):
            outs = []
            for side in range(2):
                own_q = own_lanes(rows, side)
                own_k = own_lanes(keys, side)
                query = jnp.where(
                    own_q,
                    q_ref[seq * rows : (seq + 1) * rows, at : at + PAIR],
                    (lanes(rows) == DH * (1 - side) + 3).astype(LOW),
                )
                key = jnp.where(
                    own_k,
                    k_ref[seq * keys : (seq + 1) * keys, at : at + PAIR],
                    key_extras(keys, side, length_ref[seq]),
                )
                value = jnp.where(
                    own_k,
                    v_ref[seq * keys : (seq + 1) * keys, at : at + PAIR],
                    jnp.ones((), LOW),
                )
                parts = []
                for start in range(0, rows, block):
                    span = start + block if causal else keys
                    scores = nt(query[start : start + block], key[:span])
                    if causal:
                        scores = scores + bias_ref[side, start : start + block, :span]
                    top = jnp.max(scores, axis=1, keepdims=True)
                    weight = jnp.exp(scores - top)
                    out = nn(weight.astype(LOW), value[:span])
                    total = out[:, DH * (1 - side) : DH * (1 - side) + 1]
                    parts.append(out * (1.0 / total))
                    spot = pl.ds(seq * rows + start, block)
                    lane = lanes(block)
                    seen = total_ref[spot, :] if (pair or side) else jnp.zeros((block, PAIR), WIDE)
                    total_ref[spot, :] = jnp.where(
                        lane == 2 * pair + side, top + jnp.log(total), seen
                    )
                outs.append(jnp.concatenate(parts, axis=0))
            mix_ref[seq * rows : (seq + 1) * rows, at : at + PAIR] = jnp.where(
                own_lanes(rows, 0), outs[0], outs[1]
            ).astype(LOW)


def forward_kernel(
    causal, seq_count, length_ref, x_ref, source_ref, gain_ref, wq_ref, wk_ref, wv_ref, wo_ref, wave_ref,
    q_ref, k_ref, v_ref, mix_ref, total_ref, after_ref, normed, bias,
):
    group = pl.program_id(0)

    @pl.when(group == 0)
    def _():
        for at, size in chunks(x_ref.shape[0], 256):
            rows = x_ref[at : at + size, :].astype(WIDE)
            normed[at : at + size, :] = (rows * rms_rate(rows) * gain_ref[...]).astype(LOW)
            after_ref[at : at + size, :] = rows

    source = normed if causal else source_ref
    q_ref[...] = nn(normed[...], wq_ref[...]).astype(LOW)
    k_ref[...] = nn(source[...], wk_ref[...]).astype(LOW)
    v_ref[...] = nn(source[...], wv_ref[...]).astype(LOW)
    forward_body(causal, seq_count, length_ref, wave_ref, bias, q_ref, k_ref, v_ref, mix_ref, total_ref, group)
    after_ref[...] += nn(mix_ref[...], wo_ref[...])


def weight_specs(width):
    across = lambda at: pl.BlockSpec((None, width, GROUP), lambda g, at=at: (at, 0, g))
    return [across(0), across(1), across(2), pl.BlockSpec((None, GROUP, width), lambda g: (3, g, 0))]


def whole(shape):
    return pl.BlockSpec(shape, lambda g: (0,) * len(shape))


def columns(rows):
    return pl.BlockSpec((rows, GROUP), lambda g: (0, g))


def attention_forward(causal, x, source, lengths, gain, weights, wave):
    row_count, width = x.shape
    seq_count = lengths.shape[0]
    source_rows = row_count if causal else source.shape[0]
    length = row_count // seq_count
    groups = width // GROUP
    low = lambda rows: jax.ShapeDtypeStruct((rows, width), LOW)
    args = [lengths, x, source, gain, weights, weights, weights, weights, wave]
    return pl.pallas_call(
        functools.partial(forward_kernel, causal, seq_count),
        grid=(groups,),
        in_specs=[
            pl.BlockSpec(memory_space=pltpu.SMEM),
            whole(x.shape),
            whole(source.shape),
            whole(gain.shape),
            *weight_specs(width),
            whole(wave.shape),
        ],
        out_specs=[
            columns(row_count),
            columns(source_rows),
            columns(source_rows),
            columns(row_count),
            pl.BlockSpec((None, row_count, PAIR), lambda g: (g, 0, 0)),
            whole((row_count, width)),
        ],
        out_shape=[
            low(row_count),
            low(source_rows),
            low(source_rows),
            low(row_count),
            jax.ShapeDtypeStruct((groups, row_count, PAIR), WIDE),
            jax.ShapeDtypeStruct((row_count, width), WIDE),
        ],
        scratch_shapes=[
            pltpu.VMEM((row_count, width), LOW),
            pltpu.VMEM((2, length, length) if causal else (1, 8, PAIR), WIDE),
        ],
        cost_estimate=pl.CostEstimate(flops=int(27 * PEAK), bytes_accessed=20 << 20, transcendentals=0),
        compiler_params=pltpu.CompilerParams(vmem_limit_bytes=VMEM_BYTES),
        name="self_forward" if causal else "cross_forward",
    )(*args)


def gelu_parts(gate):
    root = 0.7978845608028654
    square = gate * gate
    inner = jnp.tanh(root * gate * (1.0 + 0.044715 * square))
    half = 0.5 * (1.0 + inner)
    value = gate * half
    slope = half + 0.5 * gate * (1.0 - inner * inner) * (root * (1.0 + 3 * 0.044715 * square))
    return value, slope


def rms_back(rows, gain, grad):
    rate = rms_rate(rows)
    scaled = rows * rate
    low = grad * gain
    grad_rows = rate * (low - scaled * jnp.mean(scaled * low, axis=-1, keepdims=True))
    return grad_rows, jnp.sum(grad * scaled, axis=0, keepdims=True)


def feed_kernel(
    seq_count, length_ref, after_ref, out_grad_ref, gain_ref, wg_ref, wu_ref, wd_ref,
    layer_ref, grad_cross_ref, dwi_ref, dwd_ref, dgain_ref,
    normed, normed_t, down, out_total, grad_total,
):
    step = pl.program_id(0)
    row_count = after_ref.shape[0]
    length = row_count // seq_count

    def live(at, size):
        position = lax.broadcasted_iota(jnp.int32, (size, 1), 0) + (at % length)
        return (position < length_ref[at // length]).astype(WIDE)

    @pl.when(step == 0)
    def _():
        for at, size in chunks(row_count, 256):
            rows = after_ref[at : at + size, :]
            low = (rows * rms_rate(rows) * gain_ref[...]).astype(LOW)
            normed[at : at + size, :] = low
            normed_t[:, at : at + size] = low.T
            down[at : at + size, :] = (
                out_grad_ref[at : at + size, :].astype(WIDE) * live(at, size)
            ).astype(LOW)
            out_total[at : at + size, :] = rows
            grad_total[at : at + size, :] = jnp.zeros((size, rows.shape[1]), WIDE)

    gate = nn(normed[...], wg_ref[...])
    up = nn(normed[...], wu_ref[...])
    value, slope = gelu_parts(gate)
    hidden = (value * up).astype(LOW)
    out_total[...] += nn(hidden, wd_ref[...])
    grad_hidden = nt(down[...], wd_ref[...])
    dwd_ref[...] = tn(hidden, down[...]).astype(LOW).reshape(dwd_ref.shape)
    grad_gate = (grad_hidden * up * slope).astype(LOW)
    grad_up = (grad_hidden * value).astype(LOW)
    dwi_ref[0] = nn(normed_t[...], grad_gate).astype(LOW)
    dwi_ref[1] = nn(normed_t[...], grad_up).astype(LOW)
    grad_total[...] += nt(grad_gate, wg_ref[...]) + nt(grad_up, wu_ref[...])

    @pl.when(step == pl.num_programs(0) - 1)
    def _():
        dgain = jnp.zeros(dgain_ref.shape, WIDE)
        for at, size in chunks(row_count, 256):
            part = slice(at, at + size)
            layer_ref[part, :] = (out_total[part, :] * live(at, size)).astype(LOW)
            grad_rows, gain_part = rms_back(after_ref[part, :], gain_ref[...], grad_total[part, :])
            dgain = dgain + gain_part
            grad_cross_ref[part, :] = (
                out_grad_ref[part, :].astype(WIDE) * live(at, size) + grad_rows
            )
        dgain_ref[...] = dgain


def feed_forward_both(after, out_grad, lengths, gain, w_in, w_out, block=256):
    row_count, width = after.shape
    hidden = w_out.shape[0]
    seq_count = lengths.shape[0]
    wide = pl.BlockSpec((None, width, block), lambda g: (0, 0, g))
    wide_up = pl.BlockSpec((None, width, block), lambda g: (1, 0, g))
    tall = pl.BlockSpec((block, width), lambda g: (g, 0))
    both = pl.BlockSpec((2, width, block), lambda g: (0, 0, g))
    quarter = block // 4
    cut = pl.BlockSpec((4, None, quarter, width), lambda g: (0, g, 0, 0))
    return pl.pallas_call(
        functools.partial(feed_kernel, seq_count),
        grid=(hidden // block,),
        in_specs=[
            pl.BlockSpec(memory_space=pltpu.SMEM),
            whole(after.shape),
            whole(out_grad.shape),
            whole(gain.shape),
            wide,
            wide_up,
            tall,
        ],
        out_specs=[whole(after.shape), whole(after.shape), both, cut, whole((1, width))],
        out_shape=[
            jax.ShapeDtypeStruct((row_count, width), LOW),
            jax.ShapeDtypeStruct((row_count, width), WIDE),
            jax.ShapeDtypeStruct((2, width, hidden), LOW),
            jax.ShapeDtypeStruct((4, hidden // block, quarter, width), LOW),
            jax.ShapeDtypeStruct((1, width), WIDE),
        ],
        scratch_shapes=[
            pltpu.VMEM((row_count, width), LOW),
            pltpu.VMEM((width, row_count), LOW),
            pltpu.VMEM((row_count, width), LOW),
            pltpu.VMEM((row_count, width), WIDE),
            pltpu.VMEM((row_count, width), WIDE),
        ],
        cost_estimate=pl.CostEstimate(flops=int(46 * PEAK), bytes_accessed=40 << 20, transcendentals=0),
        compiler_params=pltpu.CompilerParams(vmem_limit_bytes=VMEM_BYTES),
        name="feed_forward_both",
    )(lengths, after, out_grad, gain, w_in, w_in, w_out)


def backward_kernel(
    causal, seq_count, length_ref, x_ref, source_ref, grad_ref, gain_ref, wq_ref, wk_ref, wv_ref, wo_ref, wave_ref,
    q_ref, k_ref, v_ref, mix_ref, total_ref, mix_all_ref,
    grad_x_ref, gk_out_ref, gv_out_ref, dw_ref, dgain_ref, dist_ref,
    normed_t, source_t, mix_t, branch, grad_mix, gq, bias, score_sum, grad_total,
):
    group = pl.program_id(0)
    row_count = x_ref.shape[0]
    rows = q_ref.shape[0] // seq_count
    keys = k_ref.shape[0] // seq_count
    block = 256

    @pl.when(group == 0)
    def _():
        for at, size in chunks(row_count, 256):
            value = x_ref[at : at + size, :].astype(WIDE)
            low = (value * rms_rate(value) * gain_ref[...]).astype(LOW)
            normed_t[:, at : at + size] = low.T
            mix_t[:, at : at + size] = mix_all_ref[at : at + size, :].T
            branch[at : at + size, :] = grad_ref[at : at + size, :].astype(LOW)
            grad_total[at : at + size, :] = jnp.zeros((size, value.shape[1]), WIDE)
        if not causal:
            for at, size in chunks(source_ref.shape[0], 256):
                source_t[:, at : at + size] = source_ref[at : at + size, :].T

    grad_mix[...] = nt(branch[...], wo_ref[...]).astype(LOW)
    across = pl.ds(pl.multiple_of(group * GROUP, GROUP), GROUP)
    dw_ref[3] = nn(mix_t[...], branch[:, across]).astype(LOW)

    for pair in range(2):
        at = pair * PAIR
        if causal:
            for side in range(2):
                head = 2 * pair + side
                wave = wave_ref[pl.ds(group * 4 + head, 1), :]
                spread = pltpu.roll(
                    jnp.broadcast_to(wave, (keys, rows)), 0, 1, stride=1, stride_axis=0
                )
                row = lax.broadcasted_iota(jnp.int32, (keys, rows), 0)
                column = lax.broadcasted_iota(jnp.int32, (keys, rows), 1)
                bias[side] = jnp.where(column >= row, spread, HIDDEN)
        for seq in range(seq_count):
            span_q = slice(seq * rows, (seq + 1) * rows)
            span_k = slice(seq * keys, (seq + 1) * keys)
            sides = []
            for side in range(2):
                head = 2 * pair + side
                own_q = own_lanes(rows, side)
                own_k = own_lanes(keys, side)
                total = jnp.sum(
                    jnp.where(lanes(rows) == head, total_ref[span_q, :], 0.0), axis=1, keepdims=True
                )
                grad_low = grad_mix[span_q, at : at + PAIR]
                product = grad_low.astype(WIDE) * mix_ref[span_q, at : at + PAIR].astype(WIDE)
                delta = jnp.sum(jnp.where(own_q, product, 0.0), axis=1, keepdims=True)
                query = jnp.where(
                    own_q, q_ref[span_q, at : at + PAIR], row_extras(rows, side, -total, 1.0)
                )
                grad_out = jnp.where(own_q, grad_low, row_extras(rows, side, -delta, 0.0))
                key = jnp.where(
                    own_k,
                    k_ref[span_k, at : at + PAIR],
                    key_extras(keys, side, length_ref[seq]),
                )
                value = jnp.where(own_k, v_ref[span_k, at : at + PAIR], jnp.ones((), LOW))
                grad_query = []
                grad_key = None
                grad_value = None
                for start in range(0, rows, block):
                    span = start + block if causal else keys
                    scores = nt(key[:span], query[start : start + block])
                    if causal:
                        scores = scores + bias[side, :span, start : start + block]
                    weight = jnp.exp(scores)
                    low = weight.astype(LOW)
                    grad_weight = nt(value[:span], grad_out[start : start + block])
                    grad_score = (weight * grad_weight).astype(LOW)
                    if causal:
                        if seq == 0:
                            score_sum[side, :span, start : start + block] = grad_score.astype(WIDE)
                        else:
                            score_sum[side, :span, start : start + block] += grad_score.astype(WIDE)
                    key_part = nn(grad_score, query[start : start + block])
                    value_part = nn(low, grad_out[start : start + block])
                    grad_query.append(tn(grad_score, key[:span]))
                    if causal and start == 0 and rows > block:
                        rest = jnp.zeros((keys - span, PAIR), WIDE)
                        key_part = jnp.concatenate([key_part, rest], axis=0)
                        value_part = jnp.concatenate([value_part, rest], axis=0)
                    grad_key = key_part if grad_key is None else grad_key + key_part
                    grad_value = value_part if grad_value is None else grad_value + value_part
                sides.append((jnp.concatenate(grad_query, axis=0), grad_key, grad_value))
            pick_q = own_lanes(rows, 0)
            pick_k = own_lanes(keys, 0)
            gq[span_q, at : at + PAIR] = jnp.where(pick_q, sides[0][0], sides[1][0]).astype(LOW)
            gk_out_ref[span_k, at : at + PAIR] = jnp.where(pick_k, sides[0][1], sides[1][1]).astype(LOW)
            gv_out_ref[span_k, at : at + PAIR] = jnp.where(pick_k, sides[0][2], sides[1][2]).astype(LOW)
        if causal:
            for side in range(2):
                head = 2 * pair + side
                row = lax.broadcasted_iota(jnp.int32, (keys, rows), 0)
                column = lax.broadcasted_iota(jnp.int32, (keys, rows), 1)
                held = jnp.where(column >= row, score_sum[side], 0.0)
                while held.shape[0] > 1:
                    half = held.shape[0] // 2
                    held = held[:half] + pltpu.roll(held[half:], rows - half, 1)
                dist_ref[pl.ds(group * 4 + head, 1), :] = held

    if causal:
        source_t = normed_t
    dw_ref[0] = nn(normed_t[...], gq[...]).astype(LOW)
    dw_ref[1] = nn(source_t[...], gk_out_ref[...]).astype(LOW)
    dw_ref[2] = nn(source_t[...], gv_out_ref[...]).astype(LOW)
    update = nt(gq[...], wq_ref[...])
    if causal:
        update = update + nt(gk_out_ref[...], wk_ref[...]) + nt(gv_out_ref[...], wv_ref[...])
    grad_total[...] += update

    @pl.when(group == pl.num_programs(0) - 1)
    def _():
        dgain = jnp.zeros(dgain_ref.shape, WIDE)
        for at, size in chunks(row_count, 256):
            part = slice(at, at + size)
            grad_rows, gain_part = rms_back(
                x_ref[part, :].astype(WIDE), gain_ref[...], grad_total[part, :]
            )
            dgain = dgain + gain_part
            grad_x_ref[part, :] = grad_ref[part, :] + grad_rows
        dgain_ref[...] = dgain


def attention_backward(causal, x, source, grad, lengths, gain, weights, wave, kept):
    row_count, width = x.shape
    seq_count = lengths.shape[0]
    source_rows = row_count if causal else source.shape[0]
    length = row_count // seq_count
    groups = width // GROUP
    low = lambda rows: jax.ShapeDtypeStruct((rows, width), LOW)
    score = (2, length, length) if causal else (1, 8, PAIR)
    return pl.pallas_call(
        functools.partial(backward_kernel, causal, seq_count),
        grid=(groups,),
        in_specs=[
            pl.BlockSpec(memory_space=pltpu.SMEM),
            whole(x.shape),
            whole(source.shape),
            whole(grad.shape),
            whole(gain.shape),
            *weight_specs(width),
            whole(wave.shape),
            columns(row_count),
            columns(source_rows),
            columns(source_rows),
            columns(row_count),
            pl.BlockSpec((None, row_count, PAIR), lambda g: (g, 0, 0)),
            whole((row_count, width)),
        ],
        out_specs=[
            whole((row_count, width)),
            columns(source_rows),
            columns(source_rows),
            pl.BlockSpec((4, width, GROUP), lambda g: (0, 0, g)),
            whole((1, width)),
            whole(wave.shape),
        ],
        out_shape=[
            jax.ShapeDtypeStruct((row_count, width), WIDE),
            low(source_rows),
            low(source_rows),
            jax.ShapeDtypeStruct(weights.shape, LOW),
            jax.ShapeDtypeStruct((1, width), WIDE),
            jax.ShapeDtypeStruct(wave.shape, WIDE),
        ],
        scratch_shapes=[
            pltpu.VMEM((width, row_count), LOW),
            pltpu.VMEM((width, source_rows) if not causal else (16, PAIR), LOW),
            pltpu.VMEM((width, row_count), LOW),
            pltpu.VMEM((row_count, width), LOW),
            pltpu.VMEM((row_count, GROUP), LOW),
            pltpu.VMEM((row_count, GROUP), LOW),
            pltpu.VMEM(score, WIDE),
            pltpu.VMEM(score, WIDE),
            pltpu.VMEM((row_count, width), WIDE),
        ],
        cost_estimate=pl.CostEstimate(flops=int(45 * PEAK), bytes_accessed=40 << 20, transcendentals=0),
        compiler_params=pltpu.CompilerParams(vmem_limit_bytes=VMEM_BYTES),
        name="self_backward" if causal else "cross_backward",
    )(lengths, x, source, grad, gain, weights, weights, weights, weights, wave, *kept, kept[3])


def memory_kernel(gk_ref, gv_ref, wk_ref, wv_ref, out_ref):
    out_ref[...] = nt(gk_ref[...], wk_ref[...]) + nt(gv_ref[...], wv_ref[...])


def memory_gradient(grad_key, grad_value, weights):
    rows, width = grad_key.shape
    block = 256
    rowwise = pl.BlockSpec((block, width), lambda g: (g, 0))
    matrix = lambda at: pl.BlockSpec((None, width, width), lambda g: (at, 0, 0))
    return pl.pallas_call(
        memory_kernel,
        grid=(rows // block,),
        in_specs=[rowwise, rowwise, matrix(1), matrix(2)],
        out_specs=rowwise,
        out_shape=jax.ShapeDtypeStruct((rows, width), WIDE),
        cost_estimate=pl.CostEstimate(flops=int(7 * PEAK), bytes_accessed=10 << 20, transcendentals=0),
        compiler_params=pltpu.CompilerParams(vmem_limit_bytes=VMEM_BYTES),
        name="memory_gradient",
    )(grad_key, grad_value, weights, weights)


def flat_permute(value, target):
    reps, shards = lax.axis_size("rep"), lax.axis_size("fsdp")
    pairs = []
    for rep in range(reps):
        for shard in range(shards):
            to_rep, to_shard = target(rep, shard)
            pairs.append((rep * shards + shard, to_rep * shards + to_shard))
    return lax.ppermute(value, ("rep", "fsdp"), pairs)


def from_rep(value, way):
    return flat_permute(value, lambda rep, shard: (rep ^ way, shard))


def from_shard(value, way):
    return flat_permute(value, lambda rep, shard: (rep, shard ^ way))


def from_line(value, hops):
    shards = lax.axis_size("fsdp")
    return flat_permute(value, lambda rep, shard: (rep, (shard + 2 * hops) % shards))


def spread_quarter(piece):
    hops = lax.axis_size("fsdp") // 2
    line = jnp.stack([piece] + [from_line(piece, hop) for hop in range(1, hops)])
    near = [line] + [from_rep(line, way) for way in range(1, 4)]
    return near + [from_shard(part, 1) for part in near]


def assemble_kernel(place, hops, where_ref, *refs):
    parts, out_ref, sems = refs[:8], refs[8], refs[9]
    rep, line, core = where_ref[0], where_ref[1], where_ref[2]
    copies = []
    for other in range(2):
        for way in range(4):
            for hop in range(hops):
                shard = lax.rem(line - hop + hops, hops) * 2 + (core ^ other)
                copies.append(
                    pltpu.make_async_copy(
                        parts[4 * other + way].at[hop],
                        place(out_ref, rep ^ way, shard),
                        sems.at[len(copies)],
                    )
                )
    for copy in copies:
        copy.start()
    for copy in copies:
        copy.wait()


def assemble(parts, shape, place, name):
    hops = parts[0].shape[0]
    shard = lax.axis_index("fsdp")
    where = jnp.stack([lax.axis_index("rep"), shard // 2, shard % 2]).astype(jnp.int32)
    return pl.pallas_call(
        functools.partial(assemble_kernel, place, hops),
        in_specs=[pl.BlockSpec(memory_space=pltpu.SMEM)] + [pl.BlockSpec(memory_space=pl.ANY)] * 8,
        out_specs=pl.BlockSpec(memory_space=pl.ANY),
        out_shape=jax.ShapeDtypeStruct(shape, LOW),
        scratch_shapes=[pltpu.SemaphoreType.DMA((8 * hops,))],
        cost_estimate=pl.CostEstimate(flops=int(4 * PEAK), bytes_accessed=8 << 20, transcendentals=0),
        compiler_params=pltpu.CompilerParams(vmem_limit_bytes=VMEM_BYTES),
        name=name,
    )(where, *parts)


def rep_reduce(parts):
    rep = lax.axis_index("rep")
    pick = lambda at: lax.dynamic_index_in_dim(parts, at, 0, keepdims=False)
    total = pick(rep).astype(WIDE)
    for way in range(1, 4):
        total = total + from_rep(pick(rep ^ way), way).astype(WIDE)
    return total.astype(LOW)


def rep_collect(piece):
    rep = lax.axis_index("rep")
    near = jnp.stack([piece] + [from_rep(piece, way) for way in range(1, 4)])
    return jnp.stack([lax.dynamic_index_in_dim(near, at ^ rep, 0, keepdims=False) for at in range(4)])


def butterfly(vector, move, size):
    way = 1
    while way < size:
        vector = vector + move(vector, way)
        way *= 2
    return vector


def after(value, *earlier):
    return lax.optimization_barrier((value, *earlier))[0]


def factored_update(gradient, weight, row_state, col_state, reduce):
    count, rows, cols = weight.shape
    squares = gradient * gradient + TINY_TERM
    row_moment = DECAY_RATE * row_state + (1.0 - DECAY_RATE) * jnp.mean(squares, axis=2)
    local = jnp.concatenate(
        [
            jnp.sum(squares, axis=1).reshape(-1),
            jnp.sum(row_moment, axis=1),
            jnp.sum(weight * weight, axis=(1, 2)),
        ]
    )
    total = reduce(local)
    whole_rows = rows * lax.axis_size("fsdp")
    col_sum = total[: count * cols].reshape(count, cols)
    row_mean = total[count * cols : count * cols + count] / whole_rows
    square = total[count * cols + count :] / (whole_rows * cols)
    col_moment = DECAY_RATE * col_state + (1.0 - DECAY_RATE) * col_sum / whole_rows
    direction = gradient * lax.rsqrt(
        row_moment[:, :, None] * col_moment[:, None, :] / row_mean[:, None, None]
    )
    step = STEP_RATE * jnp.sqrt(square + 1e-06)
    return weight - step[:, None, None] * direction, row_moment, col_moment


def plain_update(gradient, weight, moment, square):
    moment = DECAY_RATE * moment + (1.0 - DECAY_RATE) * (gradient * gradient + TINY_TERM)
    step = STEP_RATE * jnp.sqrt(square + 1e-06)
    return weight - step * gradient * lax.rsqrt(moment), moment


def per_device(
    dec_in,
    memory,
    out_grad,
    dec_len,
    enc_len,
    buckets,
    self_weight,
    cross_weight,
    ffn_in,
    ffn_out,
    gains,
    table,
    self_rows,
    self_cols,
    cross_rows,
    cross_cols,
    in_rows,
    in_cols,
    out_rows,
    out_cols,
    gain_moment,
    table_moment,
):
    seq_count, seq_length, model_width = dec_in.shape
    mem_length = memory.shape[1]
    row_count = seq_count * seq_length
    hidden_width = ffn_in.shape[2]
    reps, shards = lax.axis_size("rep"), lax.axis_size("fsdp")
    rep, shard = lax.axis_index("rep"), lax.axis_index("fsdp")
    quarters = reps == 4 and shards == 8
    part_rows = hidden_width // shards
    w_self = lax.all_gather(self_weight.astype(LOW), "fsdp", axis=1, tiled=True)
    gain_full = lax.all_gather(gains.astype(LOW), "fsdp", axis=1, tiled=True).astype(WIDE)
    w_in = lax.all_gather(ffn_in.astype(LOW), "fsdp", axis=1, tiled=True)
    if quarters:
        cross_quarter = lax.dynamic_index_in_dim(cross_weight, rep, 0, keepdims=False).astype(LOW)
        out_quarter = lax.dynamic_index_in_dim(
            ffn_out.reshape(4, part_rows // 4, model_width), rep, 0, keepdims=False
        ).astype(LOW)
        cross_pieces = spread_quarter(cross_quarter)
        out_pieces = spread_quarter(out_quarter)
        cross_rows_each, out_rows_each = cross_weight.shape[1], part_rows // 4
        w_cross = assemble(
            cross_pieces,
            (4, model_width, model_width),
            lambda ref, quarter, at: ref.at[quarter, pl.ds(at * cross_rows_each, cross_rows_each)],
            "assemble_cross",
        )
        w_out = assemble(
            out_pieces,
            (hidden_width, model_width),
            lambda ref, quarter, at: ref.at[pl.ds((at * 4 + quarter) * out_rows_each, out_rows_each)],
            "assemble_out",
        )
    else:
        w_cross = lax.all_gather(cross_weight.astype(LOW), "fsdp", axis=1, tiled=True)
        w_out = lax.all_gather(ffn_out.astype(LOW), "fsdp", axis=0, tiled=True)

    bucket_mask = (buckets[None, :] == jnp.arange(BUCKETS)[:, None]).astype(WIDE)
    by_distance = jnp.sum(table.T[:, :, None] * bucket_mask[None], axis=1)
    by_distance = jnp.pad(by_distance, ((0, 16 - H), (0, 0)))
    backwards = jnp.roll(by_distance[:, ::-1], 1, axis=1)
    no_bias = jnp.zeros((8, PAIR), WIDE)
    no_source = jnp.zeros((16, PAIR), LOW)

    dec_rows = dec_in.reshape(row_count, model_width)
    mem_rows = memory.reshape(seq_count * mem_length, model_width)
    grad_rows = out_grad.reshape(row_count, model_width)
    *kept_one, after_self = attention_forward(
        True, dec_rows, no_source, dec_len, gain_full[0:1], w_self, backwards
    )
    *kept_two, after_cross = attention_forward(
        False, after_self, mem_rows, enc_len, gain_full[1:2], w_cross, no_bias
    )
    layer_out, grad_cross, grad_in, grad_out, gain_three = feed_forward_both(
        after_cross, grad_rows, dec_len, gain_full[2:3], w_in, w_out
    )
    grad_self, grad_k_two, grad_v_two, grad_cross_weights, gain_two, _ = attention_backward(
        False, after_self, mem_rows, grad_cross, enc_len, gain_full[1:2], w_cross, no_bias, kept_two
    )
    input_grad, _, _, grad_self_weights, gain_one, dist_grad = attention_backward(
        True, dec_rows, no_source, grad_self, dec_len, gain_full[0:1], w_self, by_distance, kept_one
    )
    memory_grad = memory_gradient(after(grad_k_two, gain_one), grad_v_two, w_cross)
    layer_out = layer_out.reshape(dec_in.shape)
    input_grad = input_grad.reshape(dec_in.shape)
    memory_grad = memory_grad.reshape(memory.shape)
    table_part = jnp.sum(bucket_mask[:, None, :] * dist_grad[None, :H, :], axis=2)

    scatter = lambda value, at: lax.psum_scatter(value, "fsdp", scatter_dimension=at, tiled=True)
    small = jnp.concatenate(
        [gain_one.reshape(-1), gain_two.reshape(-1), gain_three.reshape(-1), table_part.reshape(-1)]
    )
    if quarters:
        cut = lambda value: value.reshape(4, -1, value.shape[-1])
        own_in = scatter(grad_in, 1)
        own_in = rep_collect(rep_reduce(cut(own_in))).reshape(own_in.shape)
        own_out = scatter(rep_reduce(grad_out).reshape(-1, model_width), 0)
        own_out = rep_collect(own_out).reshape(ffn_out.shape)
        own_cross = rep_collect(scatter(rep_reduce(grad_cross_weights), 0))
        own_self = scatter(grad_self_weights, 1)
        own_self = rep_collect(rep_reduce(own_self))
        over_shards = lambda vector: butterfly(vector, from_shard, shards)
        small = butterfly(butterfly(small, from_shard, shards), from_rep, reps)
    else:
        over_reps = lambda value: lax.psum(value, "rep")
        own_in = over_reps(scatter(grad_in, 1))
        own_out = over_reps(
            scatter(grad_out.transpose(1, 0, 2, 3).reshape(hidden_width, model_width), 0)
        )
        own_cross = over_reps(scatter(grad_cross_weights, 1))
        own_self = over_reps(scatter(grad_self_weights, 1))
        over_shards = lambda vector: lax.psum(vector, "fsdp")
        small = lax.psum(small, ("rep", "fsdp"))

    grad_factor = 1.0 / math.sqrt(row_count * reps * shards)
    self_grad, cross_grad, ffn_in_grad, feedforward_output_gradient = [
        member.astype(WIDE) * grad_factor for member in (own_self, own_cross, own_in, own_out)
    ]
    small = small * grad_factor
    gains_grad = lax.dynamic_slice_in_dim(
        small[: 3 * model_width].reshape(3, model_width), shard * gains.shape[1], gains.shape[1], axis=1
    )
    table_grad = small[3 * model_width :].reshape(BUCKETS, H)
    new_ffn_in, new_in_rows, new_in_cols = factored_update(
        ffn_in_grad, ffn_in, in_rows, in_cols, over_shards
    )
    new_ffn_out, new_out_rows, new_out_cols = [
        member[0]
        for member in factored_update(
            feedforward_output_gradient[None], ffn_out[None], out_rows[None], out_cols[None], over_shards
        )
    ]
    new_cross, new_cross_rows, new_cross_cols = factored_update(
        cross_grad, cross_weight, cross_rows, cross_cols, over_shards
    )
    new_self, new_self_rows, new_self_cols = factored_update(
        self_grad, self_weight, self_rows, self_cols, over_shards
    )
    gain_square = over_shards(jnp.sum(gains * gains, axis=1)) / model_width
    new_gains, new_gain_moment = plain_update(gains_grad, gains, gain_moment, gain_square[:, None])
    new_table, new_table_moment = plain_update(
        table_grad, table, table_moment, jnp.mean(table * table)
    )
    return (
        layer_out,
        input_grad,
        memory_grad,
        self_grad,
        cross_grad,
        ffn_in_grad,
        feedforward_output_gradient,
        gains_grad,
        table_grad,
        new_self,
        new_cross,
        new_ffn_in,
        new_ffn_out,
        new_gains,
        new_table,
        new_self_rows,
        new_self_cols,
        new_cross_rows,
        new_cross_cols,
        new_in_rows,
        new_in_cols,
        new_out_rows,
        new_out_cols,
        new_gain_moment,
        new_table_moment,
    )


def solution(mesh):
    placed = (
        P(("rep", "fsdp"), None, None),
        P(("rep", "fsdp"), None, None),
        P(("rep", "fsdp"), None, None),
        P(("rep", "fsdp")),
        P(("rep", "fsdp")),
        P(),
        P(None, "fsdp", None),
        P(None, "fsdp", None),
        P(None, "fsdp", None),
        P("fsdp", None),
        P(None, "fsdp"),
        P(),
        P(None, "fsdp"),
        P(),
        P(None, "fsdp"),
        P(),
        P(None, "fsdp"),
        P(),
        P("fsdp"),
        P(),
        P(None, "fsdp"),
        P(),
    )
    return jax.shard_map(
        per_device,
        mesh=mesh,
        in_specs=placed,
        out_specs=(
            P(("rep", "fsdp"), None, None),
            P(("rep", "fsdp"), None, None),
            P(("rep", "fsdp"), None, None),
            P(None, "fsdp", None),
            P(None, "fsdp", None),
            P(None, "fsdp", None),
            P("fsdp", None),
            P(None, "fsdp"),
            P(),
            P(None, "fsdp", None),
            P(None, "fsdp", None),
            P(None, "fsdp", None),
            P("fsdp", None),
            P(None, "fsdp"),
            P(),
            P(None, "fsdp"),
            P(),
            P(None, "fsdp"),
            P(),
            P(None, "fsdp"),
            P(),
            P("fsdp"),
            P(),
            P(None, "fsdp"),
            P(),
        ),
        check_vma=False,
    )
```

```python
import functools
import math

import jax
import jax.numpy as jnp
from jax import lax
from jax.experimental import pallas as pl
from jax.experimental.pallas import tpu as pltpu
from jax.sharding import PartitionSpec as P

H = 12
DH = 64
BUCKETS = 32
DECAY_RATE = 0.8
STEP_RATE = 0.2
TINY_TERM = 1e-30
PAIR = 2 * DH
GROUP = 4 * DH
HIDDEN = -1e30
VMEM_BYTES = 60 * 1024 * 1024
PEAK = 1.15e9
LOW = jnp.bfloat16
WIDE = jnp.float32


def nn(left, right):
    return lax.dot_general(left, right, (((1,), (0,)), ((), ())), preferred_element_type=WIDE)


def nt(left, right):
    return lax.dot_general(left, right, (((1,), (1,)), ((), ())), preferred_element_type=WIDE)


def tn(left, right):
    return lax.dot_general(left, right, (((0,), (0,)), ((), ())), preferred_element_type=WIDE)


def rms_rate(rows):
    return lax.rsqrt(jnp.mean(rows * rows, axis=-1, keepdims=True) + 1e-06)


def three_parts(column):
    high = column.astype(LOW)
    rest = column - high.astype(WIDE)
    middle = rest.astype(LOW)
    low = (rest - middle.astype(WIDE)).astype(LOW)
    return high, middle, low


def chunks(total, size):
    return [(at, min(size, total - at)) for at in range(0, total, size)]


def lanes(rows):
    return lax.broadcasted_iota(jnp.int32, (rows, PAIR), 1)


def own_lanes(rows, side):
    lane = lanes(rows)
    return (lane >= DH * side) & (lane < DH * (side + 1))


def key_extras(rows, side, length):
    lane = lanes(rows) - DH * (1 - side)
    dead = lax.broadcasted_iota(jnp.int32, (rows, PAIR), 0) >= length
    mask = jnp.where(dead, HIDDEN, 0.0)
    return jnp.where(
        (lane >= 0) & (lane < 3), 1.0, jnp.where(lane == 3, mask, 0.0)
    ).astype(LOW)


def row_extras(rows, side, column, last):
    lane = lanes(rows) - DH * (1 - side)
    high, middle, low = three_parts(column)
    wide = lambda part: jnp.broadcast_to(part.astype(WIDE), (rows, PAIR))
    return jnp.where(
        lane == 0,
        wide(high),
        jnp.where(
            lane == 1, wide(middle), jnp.where(lane == 2, wide(low), jnp.where(lane == 3, last, 0.0))
        ),
    ).astype(LOW)


def forward_body(causal, seq_count, length_ref, wave_ref, bias_ref, q_ref, k_ref, v_ref, mix_ref, total_ref, group):
    rows = q_ref.shape[0] // seq_count
    keys = k_ref.shape[0] // seq_count
    block = 256
    for pair in range(2):
        at = pair * PAIR
        for side in range(2):
            head = 2 * pair + side
            if causal:
                wave = wave_ref[pl.ds(group * 4 + head, 1), :]
                spread = pltpu.roll(
                    jnp.broadcast_to(wave, (rows, keys)), 0, 1, stride=1, stride_axis=0
                )
                row = lax.broadcasted_iota(jnp.int32, (rows, keys), 0)
                column = lax.broadcasted_iota(jnp.int32, (rows, keys), 1)
                bias_ref[side] = jnp.where(column <= row, spread, HIDDEN)
        for seq in range(seq_count):
            outs = []
            for side in range(2):
                own_q = own_lanes(rows, side)
                own_k = own_lanes(keys, side)
                query = jnp.where(
                    own_q,
                    q_ref[seq * rows : (seq + 1) * rows, at : at + PAIR],
                    (lanes(rows) == DH * (1 - side) + 3).astype(LOW),
                )
                key = jnp.where(
                    own_k,
                    k_ref[seq * keys : (seq + 1) * keys, at : at + PAIR],
                    key_extras(keys, side, length_ref[seq]),
                )
                value = jnp.where(
                    own_k,
                    v_ref[seq * keys : (seq + 1) * keys, at : at + PAIR],
                    jnp.ones((), LOW),
                )
                parts = []
                for start in range(0, rows, block):
                    span = start + block if causal else keys
                    scores = nt(query[start : start + block], key[:span])
                    if causal:
                        scores = scores + bias_ref[side, start : start + block, :span]
                    top = jnp.max(scores, axis=1, keepdims=True)
                    weight = jnp.exp(scores - top)
                    out = nn(weight.astype(LOW), value[:span])
                    total = out[:, DH * (1 - side) : DH * (1 - side) + 1]
                    parts.append(out * (1.0 / total))
                    spot = pl.ds(seq * rows + start, block)
                    lane = lanes(block)
                    seen = total_ref[spot, :] if (pair or side) else jnp.zeros((block, PAIR), WIDE)
                    total_ref[spot, :] = jnp.where(
                        lane == 2 * pair + side, top + jnp.log(total), seen
                    )
                outs.append(jnp.concatenate(parts, axis=0))
            mix_ref[seq * rows : (seq + 1) * rows, at : at + PAIR] = jnp.where(
                own_lanes(rows, 0), outs[0], outs[1]
            ).astype(LOW)


def forward_kernel(
    causal, seq_count, length_ref, x_ref, source_ref, gain_ref, wq_ref, wk_ref, wv_ref, wo_ref, wave_ref,
    q_ref, k_ref, v_ref, mix_ref, total_ref, after_ref, normed, bias,
):
    group = pl.program_id(0)

    @pl.when(group == 0)
    def _():
        for at, size in chunks(x_ref.shape[0], 256):
            rows = x_ref[at : at + size, :].astype(WIDE)
            normed[at : at + size, :] = (rows * rms_rate(rows) * gain_ref[...]).astype(LOW)
            after_ref[at : at + size, :] = rows

    source = normed if causal else source_ref
    q_ref[...] = nn(normed[...], wq_ref[...]).astype(LOW)
    k_ref[...] = nn(source[...], wk_ref[...]).astype(LOW)
    v_ref[...] = nn(source[...], wv_ref[...]).astype(LOW)
    forward_body(causal, seq_count, length_ref, wave_ref, bias, q_ref, k_ref, v_ref, mix_ref, total_ref, group)
    after_ref[...] += nn(mix_ref[...], wo_ref[...])


def weight_specs(width):
    across = lambda at: pl.BlockSpec((None, width, GROUP), lambda g, at=at: (at, 0, g))
    return [across(0), across(1), across(2), pl.BlockSpec((None, GROUP, width), lambda g: (3, g, 0))]


def whole(shape):
    return pl.BlockSpec(shape, lambda g: (0,) * len(shape))


def columns(rows):
    return pl.BlockSpec((rows, GROUP), lambda g: (0, g))


def attention_forward(causal, x, source, lengths, gain, weights, wave):
    row_count, width = x.shape
    seq_count = lengths.shape[0]
    source_rows = row_count if causal else source.shape[0]
    length = row_count // seq_count
    groups = width // GROUP
    low = lambda rows: jax.ShapeDtypeStruct((rows, width), LOW)
    args = [lengths, x, source, gain, weights, weights, weights, weights, wave]
    return pl.pallas_call(
        functools.partial(forward_kernel, causal, seq_count),
        grid=(groups,),
        in_specs=[
            pl.BlockSpec(memory_space=pltpu.SMEM),
            whole(x.shape),
            whole(source.shape),
            whole(gain.shape),
            *weight_specs(width),
            whole(wave.shape),
        ],
        out_specs=[
            columns(row_count),
            columns(source_rows),
            columns(source_rows),
            columns(row_count),
            pl.BlockSpec((None, row_count, PAIR), lambda g: (g, 0, 0)),
            whole((row_count, width)),
        ],
        out_shape=[
            low(row_count),
            low(source_rows),
            low(source_rows),
            low(row_count),
            jax.ShapeDtypeStruct((groups, row_count, PAIR), WIDE),
            jax.ShapeDtypeStruct((row_count, width), WIDE),
        ],
        scratch_shapes=[
            pltpu.VMEM((row_count, width), LOW),
            pltpu.VMEM((2, length, length) if causal else (1, 8, PAIR), WIDE),
        ],
        cost_estimate=pl.CostEstimate(flops=int(27 * PEAK), bytes_accessed=20 << 20, transcendentals=0),
        compiler_params=pltpu.CompilerParams(vmem_limit_bytes=VMEM_BYTES),
        name="self_forward" if causal else "cross_forward",
    )(*args)


def gelu_parts(gate):
    root = 0.7978845608028654
    square = gate * gate
    inner = jnp.tanh(root * gate * (1.0 + 0.044715 * square))
    half = 0.5 * (1.0 + inner)
    value = gate * half
    slope = half + 0.5 * gate * (1.0 - inner * inner) * (root * (1.0 + 3 * 0.044715 * square))
    return value, slope


def rms_back(rows, gain, grad):
    rate = rms_rate(rows)
    scaled = rows * rate
    low = grad * gain
    grad_rows = rate * (low - scaled * jnp.mean(scaled * low, axis=-1, keepdims=True))
    return grad_rows, jnp.sum(grad * scaled, axis=0, keepdims=True)


def feed_kernel(
    seq_count, length_ref, after_ref, out_grad_ref, gain_ref, wg_ref, wu_ref, wd_ref,
    layer_ref, grad_cross_ref, dwi_ref, dwd_ref, dgain_ref,
    normed, normed_t, down, out_total, grad_total,
):
    step = pl.program_id(0)
    row_count = after_ref.shape[0]
    length = row_count // seq_count

    def live(at, size):
        position = lax.broadcasted_iota(jnp.int32, (size, 1), 0) + (at % length)
        return (position < length_ref[at // length]).astype(WIDE)

    @pl.when(step == 0)
    def _():
        for at, size in chunks(row_count, 256):
            rows = after_ref[at : at + size, :]
            low = (rows * rms_rate(rows) * gain_ref[...]).astype(LOW)
            normed[at : at + size, :] = low
            normed_t[:, at : at + size] = low.T
            down[at : at + size, :] = (
                out_grad_ref[at : at + size, :].astype(WIDE) * live(at, size)
            ).astype(LOW)
            out_total[at : at + size, :] = rows
            grad_total[at : at + size, :] = jnp.zeros((size, rows.shape[1]), WIDE)

    gate = nn(normed[...], wg_ref[...])
    up = nn(normed[...], wu_ref[...])
    value, slope = gelu_parts(gate)
    hidden = (value * up).astype(LOW)
    out_total[...] += nn(hidden, wd_ref[...])
    grad_hidden = nt(down[...], wd_ref[...])
    dwd_ref[...] = tn(hidden, down[...]).astype(LOW).reshape(dwd_ref.shape)
    grad_gate = (grad_hidden * up * slope).astype(LOW)
    grad_up = (grad_hidden * value).astype(LOW)
    dwi_ref[0] = nn(normed_t[...], grad_gate).astype(LOW)
    dwi_ref[1] = nn(normed_t[...], grad_up).astype(LOW)
    grad_total[...] += nt(grad_gate, wg_ref[...]) + nt(grad_up, wu_ref[...])

    @pl.when(step == pl.num_programs(0) - 1)
    def _():
        dgain = jnp.zeros(dgain_ref.shape, WIDE)
        for at, size in chunks(row_count, 256):
            part = slice(at, at + size)
            layer_ref[part, :] = (out_total[part, :] * live(at, size)).astype(LOW)
            grad_rows, gain_part = rms_back(after_ref[part, :], gain_ref[...], grad_total[part, :])
            dgain = dgain + gain_part
            grad_cross_ref[part, :] = (
                out_grad_ref[part, :].astype(WIDE) * live(at, size) + grad_rows
            )
        dgain_ref[...] = dgain


def feed_forward_both(after, out_grad, lengths, gain, w_in, w_out, block=256):
    row_count, width = after.shape
    hidden = w_out.shape[0]
    seq_count = lengths.shape[0]
    wide = pl.BlockSpec((None, width, block), lambda g: (0, 0, g))
    wide_up = pl.BlockSpec((None, width, block), lambda g: (1, 0, g))
    tall = pl.BlockSpec((block, width), lambda g: (g, 0))
    both = pl.BlockSpec((2, width, block), lambda g: (0, 0, g))
    quarter = block // 4
    cut = pl.BlockSpec((4, None, quarter, width), lambda g: (0, g, 0, 0))
    return pl.pallas_call(
        functools.partial(feed_kernel, seq_count),
        grid=(hidden // block,),
        in_specs=[
            pl.BlockSpec(memory_space=pltpu.SMEM),
            whole(after.shape),
            whole(out_grad.shape),
            whole(gain.shape),
            wide,
            wide_up,
            tall,
        ],
        out_specs=[whole(after.shape), whole(after.shape), both, cut, whole((1, width))],
        out_shape=[
            jax.ShapeDtypeStruct((row_count, width), LOW),
            jax.ShapeDtypeStruct((row_count, width), WIDE),
            jax.ShapeDtypeStruct((2, width, hidden), LOW),
            jax.ShapeDtypeStruct((4, hidden // block, quarter, width), LOW),
            jax.ShapeDtypeStruct((1, width), WIDE),
        ],
        scratch_shapes=[
            pltpu.VMEM((row_count, width), LOW),
            pltpu.VMEM((width, row_count), LOW),
            pltpu.VMEM((row_count, width), LOW),
            pltpu.VMEM((row_count, width), WIDE),
            pltpu.VMEM((row_count, width), WIDE),
        ],
        cost_estimate=pl.CostEstimate(flops=int(46 * PEAK), bytes_accessed=40 << 20, transcendentals=0),
        compiler_params=pltpu.CompilerParams(vmem_limit_bytes=VMEM_BYTES),
        name="feed_forward_both",
    )(lengths, after, out_grad, gain, w_in, w_in, w_out)


def backward_kernel(
    causal, seq_count, length_ref, x_ref, source_ref, grad_ref, gain_ref, wq_ref, wk_ref, wv_ref, wo_ref, wave_ref,
    q_ref, k_ref, v_ref, mix_ref, total_ref, mix_all_ref,
    grad_x_ref, gk_out_ref, gv_out_ref, dw_ref, dgain_ref, dist_ref,
    normed_t, source_t, mix_t, branch, grad_mix, gq, bias, score_sum, grad_total,
):
    group = pl.program_id(0)
    row_count = x_ref.shape[0]
    rows = q_ref.shape[0] // seq_count
    keys = k_ref.shape[0] // seq_count
    block = 256

    @pl.when(group == 0)
    def _():
        for at, size in chunks(row_count, 256):
            value = x_ref[at : at + size, :].astype(WIDE)
            low = (value * rms_rate(value) * gain_ref[...]).astype(LOW)
            normed_t[:, at : at + size] = low.T
            mix_t[:, at : at + size] = mix_all_ref[at : at + size, :].T
            branch[at : at + size, :] = grad_ref[at : at + size, :].astype(LOW)
            grad_total[at : at + size, :] = jnp.zeros((size, value.shape[1]), WIDE)
        if not causal:
            for at, size in chunks(source_ref.shape[0], 256):
                source_t[:, at : at + size] = source_ref[at : at + size, :].T

    grad_mix[...] = nt(branch[...], wo_ref[...]).astype(LOW)
    across = pl.ds(pl.multiple_of(group * GROUP, GROUP), GROUP)
    dw_ref[3] = nn(mix_t[...], branch[:, across]).astype(LOW)

    for pair in range(2):
        at = pair * PAIR
        if causal:
            for side in range(2):
                head = 2 * pair + side
                wave = wave_ref[pl.ds(group * 4 + head, 1), :]
                spread = pltpu.roll(
                    jnp.broadcast_to(wave, (keys, rows)), 0, 1, stride=1, stride_axis=0
                )
                row = lax.broadcasted_iota(jnp.int32, (keys, rows), 0)
                column = lax.broadcasted_iota(jnp.int32, (keys, rows), 1)
                bias[side] = jnp.where(column >= row, spread, HIDDEN)
        for seq in range(seq_count):
            span_q = slice(seq * rows, (seq + 1) * rows)
            span_k = slice(seq * keys, (seq + 1) * keys)
            sides = []
            for side in range(2):
                head = 2 * pair + side
                own_q = own_lanes(rows, side)
                own_k = own_lanes(keys, side)
                total = jnp.sum(
                    jnp.where(lanes(rows) == head, total_ref[span_q, :], 0.0), axis=1, keepdims=True
                )
                grad_low = grad_mix[span_q, at : at + PAIR]
                product = grad_low.astype(WIDE) * mix_ref[span_q, at : at + PAIR].astype(WIDE)
                delta = jnp.sum(jnp.where(own_q, product, 0.0), axis=1, keepdims=True)
                query = jnp.where(
                    own_q, q_ref[span_q, at : at + PAIR], row_extras(rows, side, -total, 1.0)
                )
                grad_out = jnp.where(own_q, grad_low, row_extras(rows, side, -delta, 0.0))
                key = jnp.where(
                    own_k,
                    k_ref[span_k, at : at + PAIR],
                    key_extras(keys, side, length_ref[seq]),
                )
                value = jnp.where(own_k, v_ref[span_k, at : at + PAIR], jnp.ones((), LOW))
                grad_query = []
                grad_key = None
                grad_value = None
                for start in range(0, rows, block):
                    span = start + block if causal else keys
                    scores = nt(key[:span], query[start : start + block])
                    if causal:
                        scores = scores + bias[side, :span, start : start + block]
                    weight = jnp.exp(scores)
                    low = weight.astype(LOW)
                    grad_weight = nt(value[:span], grad_out[start : start + block])
                    grad_score = (weight * grad_weight).astype(LOW)
                    if causal:
                        if seq == 0:
                            score_sum[side, :span, start : start + block] = grad_score.astype(WIDE)
                        else:
                            score_sum[side, :span, start : start + block] += grad_score.astype(WIDE)
                    key_part = nn(grad_score, query[start : start + block])
                    value_part = nn(low, grad_out[start : start + block])
                    grad_query.append(tn(grad_score, key[:span]))
                    if causal and start == 0 and rows > block:
                        rest = jnp.zeros((keys - span, PAIR), WIDE)
                        key_part = jnp.concatenate([key_part, rest], axis=0)
                        value_part = jnp.concatenate([value_part, rest], axis=0)
                    grad_key = key_part if grad_key is None else grad_key + key_part
                    grad_value = value_part if grad_value is None else grad_value + value_part
                sides.append((jnp.concatenate(grad_query, axis=0), grad_key, grad_value))
            pick_q = own_lanes(rows, 0)
            pick_k = own_lanes(keys, 0)
            gq[span_q, at : at + PAIR] = jnp.where(pick_q, sides[0][0], sides[1][0]).astype(LOW)
            gk_out_ref[span_k, at : at + PAIR] = jnp.where(pick_k, sides[0][1], sides[1][1]).astype(LOW)
            gv_out_ref[span_k, at : at + PAIR] = jnp.where(pick_k, sides[0][2], sides[1][2]).astype(LOW)
        if causal:
            for side in range(2):
                head = 2 * pair + side
                row = lax.broadcasted_iota(jnp.int32, (keys, rows), 0)
                column = lax.broadcasted_iota(jnp.int32, (keys, rows), 1)
                held = jnp.where(column >= row, score_sum[side], 0.0)
                while held.shape[0] > 1:
                    half = held.shape[0] // 2
                    held = held[:half] + pltpu.roll(held[half:], rows - half, 1)
                dist_ref[pl.ds(group * 4 + head, 1), :] = held

    if causal:
        source_t = normed_t
    dw_ref[0] = nn(normed_t[...], gq[...]).astype(LOW)
    dw_ref[1] = nn(source_t[...], gk_out_ref[...]).astype(LOW)
    dw_ref[2] = nn(source_t[...], gv_out_ref[...]).astype(LOW)
    update = nt(gq[...], wq_ref[...])
    if causal:
        update = update + nt(gk_out_ref[...], wk_ref[...]) + nt(gv_out_ref[...], wv_ref[...])
    grad_total[...] += update

    @pl.when(group == pl.num_programs(0) - 1)
    def _():
        dgain = jnp.zeros(dgain_ref.shape, WIDE)
        for at, size in chunks(row_count, 256):
            part = slice(at, at + size)
            grad_rows, gain_part = rms_back(
                x_ref[part, :].astype(WIDE), gain_ref[...], grad_total[part, :]
            )
            dgain = dgain + gain_part
            grad_x_ref[part, :] = grad_ref[part, :] + grad_rows
        dgain_ref[...] = dgain


def attention_backward(causal, x, source, grad, lengths, gain, weights, wave, kept):
    row_count, width = x.shape
    seq_count = lengths.shape[0]
    source_rows = row_count if causal else source.shape[0]
    length = row_count // seq_count
    groups = width // GROUP
    low = lambda rows: jax.ShapeDtypeStruct((rows, width), LOW)
    score = (2, length, length) if causal else (1, 8, PAIR)
    return pl.pallas_call(
        functools.partial(backward_kernel, causal, seq_count),
        grid=(groups,),
        in_specs=[
            pl.BlockSpec(memory_space=pltpu.SMEM),
            whole(x.shape),
            whole(source.shape),
            whole(grad.shape),
            whole(gain.shape),
            *weight_specs(width),
            whole(wave.shape),
            columns(row_count),
            columns(source_rows),
            columns(source_rows),
            columns(row_count),
            pl.BlockSpec((None, row_count, PAIR), lambda g: (g, 0, 0)),
            whole((row_count, width)),
        ],
        out_specs=[
            whole((row_count, width)),
            columns(source_rows),
            columns(source_rows),
            pl.BlockSpec((4, width, GROUP), lambda g: (0, 0, g)),
            whole((1, width)),
            whole(wave.shape),
        ],
        out_shape=[
            jax.ShapeDtypeStruct((row_count, width), WIDE),
            low(source_rows),
            low(source_rows),
            jax.ShapeDtypeStruct(weights.shape, LOW),
            jax.ShapeDtypeStruct((1, width), WIDE),
            jax.ShapeDtypeStruct(wave.shape, WIDE),
        ],
        scratch_shapes=[
            pltpu.VMEM((width, row_count), LOW),
            pltpu.VMEM((width, source_rows) if not causal else (16, PAIR), LOW),
            pltpu.VMEM((width, row_count), LOW),
            pltpu.VMEM((row_count, width), LOW),
            pltpu.VMEM((row_count, GROUP), LOW),
            pltpu.VMEM((row_count, GROUP), LOW),
            pltpu.VMEM(score, WIDE),
            pltpu.VMEM(score, WIDE),
            pltpu.VMEM((row_count, width), WIDE),
        ],
        cost_estimate=pl.CostEstimate(flops=int(45 * PEAK), bytes_accessed=40 << 20, transcendentals=0),
        compiler_params=pltpu.CompilerParams(vmem_limit_bytes=VMEM_BYTES),
        name="self_backward" if causal else "cross_backward",
    )(lengths, x, source, grad, gain, weights, weights, weights, weights, wave, *kept, kept[3])


def memory_kernel(gk_ref, gv_ref, wk_ref, wv_ref, out_ref):
    out_ref[...] = nt(gk_ref[...], wk_ref[...]) + nt(gv_ref[...], wv_ref[...])


def memory_gradient(grad_key, grad_value, weights):
    rows, width = grad_key.shape
    block = 256
    rowwise = pl.BlockSpec((block, width), lambda g: (g, 0))
    matrix = lambda at: pl.BlockSpec((None, width, width), lambda g: (at, 0, 0))
    return pl.pallas_call(
        memory_kernel,
        grid=(rows // block,),
        in_specs=[rowwise, rowwise, matrix(1), matrix(2)],
        out_specs=rowwise,
        out_shape=jax.ShapeDtypeStruct((rows, width), WIDE),
        cost_estimate=pl.CostEstimate(flops=int(7 * PEAK), bytes_accessed=10 << 20, transcendentals=0),
        compiler_params=pltpu.CompilerParams(vmem_limit_bytes=VMEM_BYTES),
        name="memory_gradient",
    )(grad_key, grad_value, weights, weights)


def flat_permute(value, target):
    reps, shards = lax.axis_size("rep"), lax.axis_size("fsdp")
    pairs = []
    for rep in range(reps):
        for shard in range(shards):
            to_rep, to_shard = target(rep, shard)
            pairs.append((rep * shards + shard, to_rep * shards + to_shard))
    return lax.ppermute(value, ("rep", "fsdp"), pairs)


def from_rep(value, way):
    return flat_permute(value, lambda rep, shard: (rep ^ way, shard))


def from_shard(value, way):
    return flat_permute(value, lambda rep, shard: (rep, shard ^ way))


def from_line(value, hops):
    shards = lax.axis_size("fsdp")
    return flat_permute(value, lambda rep, shard: (rep, (shard + 2 * hops) % shards))


def along_line(piece):
    hops = lax.axis_size("fsdp") // 2
    return jnp.stack([piece] + [from_line(piece, hop) for hop in range(1, hops)])


def across_reps(line):
    return [line] + [from_rep(line, way) for way in range(1, 4)]


def with_partner(parts):
    return parts + [from_shard(part, 1) for part in parts]


def scatter_line(quarter):
    shards = quarter.shape[0]
    hops = shards // 2
    shard = lax.axis_index("fsdp")
    line, core = shard // 2, shard % 2
    halves = quarter.reshape(hops, 2, *quarter.shape[1:])
    pick = lambda at: lax.dynamic_index_in_dim(halves, at, 1, keepdims=False)
    chip = (pick(core).astype(WIDE) + from_shard(pick(core ^ 1), 1).astype(WIDE)).astype(LOW)
    at_hop = lambda hop: lax.dynamic_index_in_dim(chip, (line + hop) % hops, 0, keepdims=False)
    total = at_hop(0).astype(WIDE)
    for hop in range(1, hops):
        total = total + from_line(at_hop(hop), hop).astype(WIDE)
    return total.astype(LOW)


def assemble_kernel(place, hops, where_ref, *refs):
    parts, out_ref, sems = refs[:8], refs[8], refs[9]
    rep, line, core = where_ref[0], where_ref[1], where_ref[2]
    copies = []
    for other in range(2):
        for way in range(4):
            for hop in range(hops):
                shard = lax.rem(line - hop + hops, hops) * 2 + (core ^ other)
                copies.append(
                    pltpu.make_async_copy(
                        parts[4 * other + way].at[hop],
                        place(out_ref, rep ^ way, shard),
                        sems.at[len(copies)],
                    )
                )
    for copy in copies:
        copy.start()
    for copy in copies:
        copy.wait()


def assemble(parts, shape, place, name):
    hops = parts[0].shape[0]
    shard = lax.axis_index("fsdp")
    where = jnp.stack([lax.axis_index("rep"), shard // 2, shard % 2]).astype(jnp.int32)
    return pl.pallas_call(
        functools.partial(assemble_kernel, place, hops),
        in_specs=[pl.BlockSpec(memory_space=pltpu.SMEM)] + [pl.BlockSpec(memory_space=pl.ANY)] * 8,
        out_specs=pl.BlockSpec(memory_space=pltpu.VMEM),
        out_shape=jax.ShapeDtypeStruct(shape, LOW),
        scratch_shapes=[pltpu.SemaphoreType.DMA((8 * hops,))],
        cost_estimate=pl.CostEstimate(flops=int(4 * PEAK), bytes_accessed=8 << 20, transcendentals=0),
        compiler_params=pltpu.CompilerParams(vmem_limit_bytes=VMEM_BYTES),
        name=name,
    )(where, *parts)


def rep_parts(parts):
    rep = lax.axis_index("rep")
    pick = lambda at: lax.dynamic_index_in_dim(parts, at, 0, keepdims=False)
    return [pick(rep)] + [from_rep(pick(rep ^ way), way) for way in range(1, 4)]


def add_up(parts):
    return sum(part.astype(WIDE) for part in parts).astype(LOW)


def rep_collect(piece):
    rep = lax.axis_index("rep")
    near = jnp.stack([piece] + [from_rep(piece, way) for way in range(1, 4)])
    return jnp.stack([lax.dynamic_index_in_dim(near, at ^ rep, 0, keepdims=False) for at in range(4)])


def butterfly(vector, move, size):
    way = 1
    while way < size:
        vector = vector + move(vector, way)
        way *= 2
    return vector


def after(value, *earlier):
    return lax.optimization_barrier((value, *earlier))[0]


def factored_update(gradient, weight, row_state, col_state, reduce):
    count, rows, cols = weight.shape
    squares = gradient * gradient + TINY_TERM
    row_moment = DECAY_RATE * row_state + (1.0 - DECAY_RATE) * jnp.mean(squares, axis=2)
    local = jnp.concatenate(
        [
            jnp.sum(squares, axis=1).reshape(-1),
            jnp.sum(row_moment, axis=1),
            jnp.sum(weight * weight, axis=(1, 2)),
        ]
    )
    total = reduce(local)
    whole_rows = rows * lax.axis_size("fsdp")
    col_sum = total[: count * cols].reshape(count, cols)
    row_mean = total[count * cols : count * cols + count] / whole_rows
    square = total[count * cols + count :] / (whole_rows * cols)
    col_moment = DECAY_RATE * col_state + (1.0 - DECAY_RATE) * col_sum / whole_rows
    direction = gradient * lax.rsqrt(
        row_moment[:, :, None] * col_moment[:, None, :] / row_mean[:, None, None]
    )
    step = STEP_RATE * jnp.sqrt(square + 1e-06)
    return weight - step[:, None, None] * direction, row_moment, col_moment


def plain_update(gradient, weight, moment, square):
    moment = DECAY_RATE * moment + (1.0 - DECAY_RATE) * (gradient * gradient + TINY_TERM)
    step = STEP_RATE * jnp.sqrt(square + 1e-06)
    return weight - step * gradient * lax.rsqrt(moment), moment


def per_device(
    dec_in,
    memory,
    out_grad,
    dec_len,
    enc_len,
    buckets,
    self_weight,
    cross_weight,
    ffn_in,
    ffn_out,
    gains,
    table,
    self_rows,
    self_cols,
    cross_rows,
    cross_cols,
    in_rows,
    in_cols,
    out_rows,
    out_cols,
    gain_moment,
    table_moment,
):
    seq_count, seq_length, model_width = dec_in.shape
    mem_length = memory.shape[1]
    row_count = seq_count * seq_length
    hidden_width = ffn_in.shape[2]
    reps, shards = lax.axis_size("rep"), lax.axis_size("fsdp")
    rep, shard = lax.axis_index("rep"), lax.axis_index("fsdp")
    quarters = reps == 4 and shards == 8
    part_rows = hidden_width // shards
    w_self = lax.all_gather(self_weight.astype(LOW), "fsdp", axis=1, tiled=True)
    gain_full = lax.all_gather(gains.astype(LOW), "fsdp", axis=1, tiled=True).astype(WIDE)
    w_in = lax.all_gather(ffn_in.astype(LOW), "fsdp", axis=1, tiled=True)

    bucket_mask = (buckets[None, :] == jnp.arange(BUCKETS)[:, None]).astype(WIDE)
    by_distance = jnp.sum(table.T[:, :, None] * bucket_mask[None], axis=1)
    by_distance = jnp.pad(by_distance, ((0, 16 - H), (0, 0)))
    backwards = jnp.roll(by_distance[:, ::-1], 1, axis=1)
    no_bias = jnp.zeros((8, PAIR), WIDE)
    no_source = jnp.zeros((16, PAIR), LOW)

    dec_rows = dec_in.reshape(row_count, model_width)
    mem_rows = memory.reshape(seq_count * mem_length, model_width)
    grad_rows = out_grad.reshape(row_count, model_width)
    *kept_one, after_self = attention_forward(
        True, dec_rows, no_source, dec_len, gain_full[0:1], w_self, backwards
    )
    if quarters:
        cross_quarter = lax.dynamic_index_in_dim(cross_weight, rep, 0, keepdims=False).astype(LOW)
        out_quarter = lax.dynamic_index_in_dim(
            ffn_out.reshape(4, part_rows // 4, model_width), rep, 0, keepdims=False
        ).astype(LOW)
        cross_rows_each, out_rows_each = cross_weight.shape[1], part_rows // 4
        cross_pieces = with_partner(across_reps(along_line(cross_quarter)))
        w_cross = assemble(
            list(lax.optimization_barrier((*cross_pieces, after_self))[:-1]),
            (4, model_width, model_width),
            lambda ref, quarter, at: ref.at[quarter, pl.ds(at * cross_rows_each, cross_rows_each)],
            "assemble_cross",
        )
        out_line = along_line(after(out_quarter, w_self))
        out_near = across_reps(after(out_line, after_self))
    else:
        w_cross = lax.all_gather(cross_weight.astype(LOW), "fsdp", axis=1, tiled=True)
        w_out = lax.all_gather(ffn_out.astype(LOW), "fsdp", axis=0, tiled=True)
    *kept_two, after_cross = attention_forward(
        False, after_self, mem_rows, enc_len, gain_full[1:2], w_cross, no_bias
    )
    if quarters:
        out_near = list(lax.optimization_barrier((*out_near, after_cross))[:-1])
        w_out = assemble(
            with_partner(out_near),
            (hidden_width, model_width),
            lambda ref, quarter, at: ref.at[pl.ds((at * 4 + quarter) * out_rows_each, out_rows_each)],
            "assemble_out",
        )
    layer_out, grad_cross, grad_in, grad_out, gain_three = feed_forward_both(
        after_cross, grad_rows, dec_len, gain_full[2:3], w_in, w_out
    )
    scatter = lambda value, at: lax.psum_scatter(value, "fsdp", scatter_dimension=at, tiled=True)
    if quarters:
        own_gate = scatter(grad_in[0], 0)
        out_sum = rep_parts(grad_out)
    grad_self, grad_k_two, grad_v_two, grad_cross_weights, gain_two, _ = attention_backward(
        False, after_self, mem_rows, grad_cross, enc_len, gain_full[1:2], w_cross, no_bias, kept_two
    )
    if quarters:
        grad_self, own_gate, *out_sum = lax.optimization_barrier((grad_self, own_gate, *out_sum))
        own_up = scatter(grad_in[1], 0)
        cross_sum = rep_parts(grad_cross_weights)
    input_grad, _, _, grad_self_weights, gain_one, dist_grad = attention_backward(
        True, dec_rows, no_source, grad_self, dec_len, gain_full[0:1], w_self, by_distance, kept_one
    )
    if quarters:
        gain_one, own_gate, own_up, *sums = lax.optimization_barrier(
            (gain_one, own_gate, own_up, *out_sum, *cross_sum)
        )
        out_sum, cross_sum = sums[:4], sums[4:]
    memory_grad = memory_gradient(after(grad_k_two, gain_one), grad_v_two, w_cross)
    layer_out = layer_out.reshape(dec_in.shape)
    input_grad = input_grad.reshape(dec_in.shape)
    memory_grad = memory_grad.reshape(memory.shape)
    table_part = jnp.sum(bucket_mask[:, None, :] * dist_grad[None, :H, :], axis=2)

    small = jnp.concatenate(
        [gain_one.reshape(-1), gain_two.reshape(-1), gain_three.reshape(-1), table_part.reshape(-1)]
    )
    if quarters:
        own_self = scatter(grad_self_weights, 1)
        quarter = jnp.concatenate(
            [
                add_up(cross_sum).reshape(shards, -1, model_width),
                add_up(out_sum).reshape(shards, -1, model_width),
            ],
            axis=1,
        )
        both = rep_collect(scatter_line(quarter))
        own_cross, own_out = both[:, : cross_weight.shape[1]], both[:, cross_weight.shape[1] :]
        own_out = own_out.reshape(ffn_out.shape)
        own_in = jnp.stack([own_gate, own_up])
        own_in = rep_collect(add_up(rep_parts(own_in.reshape(4, -1, hidden_width)))).reshape(ffn_in.shape)
        own_self = rep_collect(add_up(rep_parts(own_self)))
        over_shards = lambda vector: butterfly(vector, from_shard, shards)
        small = butterfly(butterfly(small, from_shard, shards), from_rep, reps)
    else:
        over_reps = lambda value: lax.psum(value, "rep")
        own_in = over_reps(scatter(grad_in, 1))
        own_out = over_reps(
            scatter(grad_out.transpose(1, 0, 2, 3).reshape(hidden_width, model_width), 0)
        )
        own_cross = over_reps(scatter(grad_cross_weights, 1))
        own_self = over_reps(scatter(grad_self_weights, 1))
        over_shards = lambda vector: lax.psum(vector, "fsdp")
        small = lax.psum(small, ("rep", "fsdp"))

    grad_factor = 1.0 / math.sqrt(row_count * reps * shards)
    self_grad, cross_grad, ffn_in_grad, feedforward_output_gradient = [
        member.astype(WIDE) * grad_factor for member in (own_self, own_cross, own_in, own_out)
    ]
    small = small * grad_factor
    gains_grad = lax.dynamic_slice_in_dim(
        small[: 3 * model_width].reshape(3, model_width), shard * gains.shape[1], gains.shape[1], axis=1
    )
    table_grad = small[3 * model_width :].reshape(BUCKETS, H)
    new_ffn_in, new_in_rows, new_in_cols = factored_update(
        ffn_in_grad, ffn_in, in_rows, in_cols, over_shards
    )
    new_ffn_out, new_out_rows, new_out_cols = [
        member[0]
        for member in factored_update(
            feedforward_output_gradient[None], ffn_out[None], out_rows[None], out_cols[None], over_shards
        )
    ]
    new_cross, new_cross_rows, new_cross_cols = factored_update(
        cross_grad, cross_weight, cross_rows, cross_cols, over_shards
    )
    new_self, new_self_rows, new_self_cols = factored_update(
        self_grad, self_weight, self_rows, self_cols, over_shards
    )
    gain_square = over_shards(jnp.sum(gains * gains, axis=1)) / model_width
    new_gains, new_gain_moment = plain_update(gains_grad, gains, gain_moment, gain_square[:, None])
    new_table, new_table_moment = plain_update(
        table_grad, table, table_moment, jnp.mean(table * table)
    )
    return (
        layer_out,
        input_grad,
        memory_grad,
        self_grad,
        cross_grad,
        ffn_in_grad,
        feedforward_output_gradient,
        gains_grad,
        table_grad,
        new_self,
        new_cross,
        new_ffn_in,
        new_ffn_out,
        new_gains,
        new_table,
        new_self_rows,
        new_self_cols,
        new_cross_rows,
        new_cross_cols,
        new_in_rows,
        new_in_cols,
        new_out_rows,
        new_out_cols,
        new_gain_moment,
        new_table_moment,
    )


def solution(mesh):
    placed = (
        P(("rep", "fsdp"), None, None),
        P(("rep", "fsdp"), None, None),
        P(("rep", "fsdp"), None, None),
        P(("rep", "fsdp")),
        P(("rep", "fsdp")),
        P(),
        P(None, "fsdp", None),
        P(None, "fsdp", None),
        P(None, "fsdp", None),
        P("fsdp", None),
        P(None, "fsdp"),
        P(),
        P(None, "fsdp"),
        P(),
        P(None, "fsdp"),
        P(),
        P(None, "fsdp"),
        P(),
        P("fsdp"),
        P(),
        P(None, "fsdp"),
        P(),
    )
    return jax.shard_map(
        per_device,
        mesh=mesh,
        in_specs=placed,
        out_specs=(
            P(("rep", "fsdp"), None, None),
            P(("rep", "fsdp"), None, None),
            P(("rep", "fsdp"), None, None),
            P(None, "fsdp", None),
            P(None, "fsdp", None),
            P(None, "fsdp", None),
            P("fsdp", None),
            P(None, "fsdp"),
            P(),
            P(None, "fsdp", None),
            P(None, "fsdp", None),
            P(None, "fsdp", None),
            P("fsdp", None),
            P(None, "fsdp"),
            P(),
            P(None, "fsdp"),
            P(),
            P(None, "fsdp"),
            P(),
            P(None, "fsdp"),
            P(),
            P("fsdp"),
            P(),
            P(None, "fsdp"),
            P(),
        ),
        check_vma=False,
    )
```

```python
import functools
import math

import jax
import jax.numpy as jnp
from jax import lax
from jax.experimental import pallas as pl
from jax.experimental.pallas import tpu as pltpu
from jax.sharding import PartitionSpec as P

H = 12
DH = 64
BUCKETS = 32
DECAY_RATE = 0.8
STEP_RATE = 0.2
TINY_TERM = 1e-30
PAIR = 2 * DH
GROUP = 4 * DH
HIDDEN = -1e30
VMEM_BYTES = 60 * 1024 * 1024
PEAK = 1.15e9
LOW = jnp.bfloat16
WIDE = jnp.float32


def nn(left, right):
    return lax.dot_general(left, right, (((1,), (0,)), ((), ())), preferred_element_type=WIDE)


def nt(left, right):
    return lax.dot_general(left, right, (((1,), (1,)), ((), ())), preferred_element_type=WIDE)


def tn(left, right):
    return lax.dot_general(left, right, (((0,), (0,)), ((), ())), preferred_element_type=WIDE)


def rms_rate(rows):
    return lax.rsqrt(jnp.mean(rows * rows, axis=-1, keepdims=True) + 1e-06)


def three_parts(column):
    high = column.astype(LOW)
    rest = column - high.astype(WIDE)
    middle = rest.astype(LOW)
    low = (rest - middle.astype(WIDE)).astype(LOW)
    return high, middle, low


def chunks(total, size):
    return [(at, min(size, total - at)) for at in range(0, total, size)]


def lanes(rows):
    return lax.broadcasted_iota(jnp.int32, (rows, PAIR), 1)


def own_lanes(rows, side):
    lane = lanes(rows)
    return (lane >= DH * side) & (lane < DH * (side + 1))


def key_extras(rows, side, length):
    lane = lanes(rows) - DH * (1 - side)
    dead = lax.broadcasted_iota(jnp.int32, (rows, PAIR), 0) >= length
    mask = jnp.where(dead, HIDDEN, 0.0)
    return jnp.where(
        (lane >= 0) & (lane < 3), 1.0, jnp.where(lane == 3, mask, 0.0)
    ).astype(LOW)


def row_extras(rows, side, column, last):
    lane = lanes(rows) - DH * (1 - side)
    high, middle, low = three_parts(column)
    wide = lambda part: jnp.broadcast_to(part.astype(WIDE), (rows, PAIR))
    return jnp.where(
        lane == 0,
        wide(high),
        jnp.where(
            lane == 1, wide(middle), jnp.where(lane == 2, wide(low), jnp.where(lane == 3, last, 0.0))
        ),
    ).astype(LOW)


def forward_body(causal, seq_count, length_ref, wave_ref, bias_ref, q_ref, k_ref, v_ref, mix_ref, total_ref, group):
    rows = q_ref.shape[0] // seq_count
    keys = k_ref.shape[0] // seq_count
    block = 256
    for pair in range(2):
        at = pair * PAIR
        for side in range(2):
            head = 2 * pair + side
            if causal:
                wave = wave_ref[pl.ds(group * 4 + head, 1), :]
                spread = pltpu.roll(
                    jnp.broadcast_to(wave, (rows, keys)), 0, 1, stride=1, stride_axis=0
                )
                row = lax.broadcasted_iota(jnp.int32, (rows, keys), 0)
                column = lax.broadcasted_iota(jnp.int32, (rows, keys), 1)
                bias_ref[side] = jnp.where(column <= row, spread, HIDDEN)
        for seq in range(seq_count):
            outs = []
            for side in range(2):
                own_q = own_lanes(rows, side)
                own_k = own_lanes(keys, side)
                query = jnp.where(
                    own_q,
                    q_ref[seq * rows : (seq + 1) * rows, at : at + PAIR],
                    (lanes(rows) == DH * (1 - side) + 3).astype(LOW),
                )
                key = jnp.where(
                    own_k,
                    k_ref[seq * keys : (seq + 1) * keys, at : at + PAIR],
                    key_extras(keys, side, length_ref[seq]),
                )
                value = jnp.where(
                    own_k,
                    v_ref[seq * keys : (seq + 1) * keys, at : at + PAIR],
                    jnp.ones((), LOW),
                )
                parts = []
                for start in range(0, rows, block):
                    span = start + block if causal else keys
                    scores = nt(query[start : start + block], key[:span])
                    if causal:
                        scores = scores + bias_ref[side, start : start + block, :span]
                    top = jnp.max(scores, axis=1, keepdims=True)
                    weight = jnp.exp(scores - top)
                    out = nn(weight.astype(LOW), value[:span])
                    total = out[:, DH * (1 - side) : DH * (1 - side) + 1]
                    parts.append(out * (1.0 / total))
                    spot = pl.ds(seq * rows + start, block)
                    lane = lanes(block)
                    seen = total_ref[spot, :] if (pair or side) else jnp.zeros((block, PAIR), WIDE)
                    total_ref[spot, :] = jnp.where(
                        lane == 2 * pair + side, top + jnp.log(total), seen
                    )
                outs.append(jnp.concatenate(parts, axis=0))
            mix_ref[seq * rows : (seq + 1) * rows, at : at + PAIR] = jnp.where(
                own_lanes(rows, 0), outs[0], outs[1]
            ).astype(LOW)


def forward_kernel(
    causal, seq_count, length_ref, x_ref, source_ref, gain_ref, wq_ref, wk_ref, wv_ref, wo_ref, wave_ref,
    q_ref, k_ref, v_ref, mix_ref, total_ref, after_ref, normed, bias,
):
    group = pl.program_id(0)

    @pl.when(group == 0)
    def _():
        for at, size in chunks(x_ref.shape[0], 256):
            rows = x_ref[at : at + size, :].astype(WIDE)
            normed[at : at + size, :] = (rows * rms_rate(rows) * gain_ref[...]).astype(LOW)
            after_ref[at : at + size, :] = rows

    source = normed if causal else source_ref
    q_ref[...] = nn(normed[...], wq_ref[...]).astype(LOW)
    k_ref[...] = nn(source[...], wk_ref[...]).astype(LOW)
    v_ref[...] = nn(source[...], wv_ref[...]).astype(LOW)
    forward_body(causal, seq_count, length_ref, wave_ref, bias, q_ref, k_ref, v_ref, mix_ref, total_ref, group)
    after_ref[...] += nn(mix_ref[...], wo_ref[...])


def weight_specs(width):
    across = lambda at: pl.BlockSpec((None, width, GROUP), lambda g, at=at: (at, 0, g))
    return [across(0), across(1), across(2), pl.BlockSpec((None, GROUP, width), lambda g: (3, g, 0))]


def whole(shape):
    return pl.BlockSpec(shape, lambda g: (0,) * len(shape))


def columns(rows):
    return pl.BlockSpec((rows, GROUP), lambda g: (0, g))


def attention_forward(causal, x, source, lengths, gain, weights, wave):
    row_count, width = x.shape
    seq_count = lengths.shape[0]
    source_rows = row_count if causal else source.shape[0]
    length = row_count // seq_count
    groups = width // GROUP
    low = lambda rows: jax.ShapeDtypeStruct((rows, width), LOW)
    args = [lengths, x, source, gain, weights, weights, weights, weights, wave]
    return pl.pallas_call(
        functools.partial(forward_kernel, causal, seq_count),
        grid=(groups,),
        in_specs=[
            pl.BlockSpec(memory_space=pltpu.SMEM),
            whole(x.shape),
            whole(source.shape),
            whole(gain.shape),
            *weight_specs(width),
            whole(wave.shape),
        ],
        out_specs=[
            columns(row_count),
            columns(source_rows),
            columns(source_rows),
            columns(row_count),
            pl.BlockSpec((None, row_count, PAIR), lambda g: (g, 0, 0)),
            whole((row_count, width)),
        ],
        out_shape=[
            low(row_count),
            low(source_rows),
            low(source_rows),
            low(row_count),
            jax.ShapeDtypeStruct((groups, row_count, PAIR), WIDE),
            jax.ShapeDtypeStruct((row_count, width), WIDE),
        ],
        scratch_shapes=[
            pltpu.VMEM((row_count, width), LOW),
            pltpu.VMEM((2, length, length) if causal else (1, 8, PAIR), WIDE),
        ],
        cost_estimate=pl.CostEstimate(flops=int(27 * PEAK), bytes_accessed=20 << 20, transcendentals=0),
        compiler_params=pltpu.CompilerParams(vmem_limit_bytes=VMEM_BYTES),
        name="self_forward" if causal else "cross_forward",
    )(*args)


def gelu_parts(gate):
    root = 0.7978845608028654
    square = gate * gate
    inner = jnp.tanh(root * gate * (1.0 + 0.044715 * square))
    half = 0.5 * (1.0 + inner)
    value = gate * half
    slope = half + 0.5 * gate * (1.0 - inner * inner) * (root * (1.0 + 3 * 0.044715 * square))
    return value, slope


def rms_back(rows, gain, grad):
    rate = rms_rate(rows)
    scaled = rows * rate
    low = grad * gain
    grad_rows = rate * (low - scaled * jnp.mean(scaled * low, axis=-1, keepdims=True))
    return grad_rows, jnp.sum(grad * scaled, axis=0, keepdims=True)


def feed_kernel(
    seq_count, length_ref, after_ref, out_grad_ref, gain_ref, wg_ref, wu_ref, wd_ref,
    layer_ref, grad_cross_ref, dwi_ref, dwd_ref, dgain_ref,
    normed, normed_t, down, out_total, grad_total,
):
    step = pl.program_id(0)
    row_count = after_ref.shape[0]
    length = row_count // seq_count

    def live(at, size):
        position = lax.broadcasted_iota(jnp.int32, (size, 1), 0) + (at % length)
        return (position < length_ref[at // length]).astype(WIDE)

    @pl.when(step == 0)
    def _():
        for at, size in chunks(row_count, 256):
            rows = after_ref[at : at + size, :]
            low = (rows * rms_rate(rows) * gain_ref[...]).astype(LOW)
            normed[at : at + size, :] = low
            normed_t[:, at : at + size] = low.T
            down[at : at + size, :] = (
                out_grad_ref[at : at + size, :].astype(WIDE) * live(at, size)
            ).astype(LOW)
            out_total[at : at + size, :] = rows
            grad_total[at : at + size, :] = jnp.zeros((size, rows.shape[1]), WIDE)

    gate = nn(normed[...], wg_ref[...])
    up = nn(normed[...], wu_ref[...])
    value, slope = gelu_parts(gate)
    hidden = (value * up).astype(LOW)
    out_total[...] += nn(hidden, wd_ref[...])
    grad_hidden = nt(down[...], wd_ref[...])
    dwd_ref[...] = tn(hidden, down[...]).astype(LOW).reshape(dwd_ref.shape)
    grad_gate = (grad_hidden * up * slope).astype(LOW)
    grad_up = (grad_hidden * value).astype(LOW)
    dwi_ref[0] = nn(normed_t[...], grad_gate).astype(LOW)
    dwi_ref[1] = nn(normed_t[...], grad_up).astype(LOW)
    grad_total[...] += nt(grad_gate, wg_ref[...]) + nt(grad_up, wu_ref[...])

    @pl.when(step == pl.num_programs(0) - 1)
    def _():
        dgain = jnp.zeros(dgain_ref.shape, WIDE)
        for at, size in chunks(row_count, 256):
            part = slice(at, at + size)
            layer_ref[part, :] = (out_total[part, :] * live(at, size)).astype(LOW)
            grad_rows, gain_part = rms_back(after_ref[part, :], gain_ref[...], grad_total[part, :])
            dgain = dgain + gain_part
            grad_cross_ref[part, :] = (
                out_grad_ref[part, :].astype(WIDE) * live(at, size) + grad_rows
            )
        dgain_ref[...] = dgain


def feed_forward_both(after, out_grad, lengths, gain, w_in, w_out, block=256):
    row_count, width = after.shape
    hidden = w_out.shape[0]
    seq_count = lengths.shape[0]
    wide = pl.BlockSpec((None, width, block), lambda g: (0, 0, g))
    wide_up = pl.BlockSpec((None, width, block), lambda g: (1, 0, g))
    tall = pl.BlockSpec((block, width), lambda g: (g, 0))
    both = pl.BlockSpec((2, width, block), lambda g: (0, 0, g))
    quarter = block // 4
    cut = pl.BlockSpec((4, None, quarter, width), lambda g: (0, g, 0, 0))
    return pl.pallas_call(
        functools.partial(feed_kernel, seq_count),
        grid=(hidden // block,),
        in_specs=[
            pl.BlockSpec(memory_space=pltpu.SMEM),
            whole(after.shape),
            whole(out_grad.shape),
            whole(gain.shape),
            wide,
            wide_up,
            tall,
        ],
        out_specs=[whole(after.shape), whole(after.shape), both, cut, whole((1, width))],
        out_shape=[
            jax.ShapeDtypeStruct((row_count, width), LOW),
            jax.ShapeDtypeStruct((row_count, width), WIDE),
            jax.ShapeDtypeStruct((2, width, hidden), LOW),
            jax.ShapeDtypeStruct((4, hidden // block, quarter, width), LOW),
            jax.ShapeDtypeStruct((1, width), WIDE),
        ],
        scratch_shapes=[
            pltpu.VMEM((row_count, width), LOW),
            pltpu.VMEM((width, row_count), LOW),
            pltpu.VMEM((row_count, width), LOW),
            pltpu.VMEM((row_count, width), WIDE),
            pltpu.VMEM((row_count, width), WIDE),
        ],
        cost_estimate=pl.CostEstimate(flops=int(46 * PEAK), bytes_accessed=40 << 20, transcendentals=0),
        compiler_params=pltpu.CompilerParams(vmem_limit_bytes=VMEM_BYTES),
        name="feed_forward_both",
    )(lengths, after, out_grad, gain, w_in, w_in, w_out)


def backward_kernel(
    causal, seq_count, length_ref, x_ref, source_ref, grad_ref, gain_ref, wq_ref, wo_ref, wave_ref,
    q_ref, k_ref, v_ref, mix_ref, total_ref, mix_all_ref, *refs,
):
    if causal:
        gq, gk_out_ref, gv_out_ref, dw_ref, dist_ref = refs[:5]
        normed_t, branch, grad_mix, bias, score_sum = refs[5:]
        source_t = normed_t
    else:
        grad_x_ref, gk_out_ref, gv_out_ref, dw_ref, dgain_ref, next_ref = refs[:6]
        normed_t, branch, grad_mix, gq, source_t, mix_t, grad_total = refs[6:]
    group = pl.program_id(0)
    row_count = x_ref.shape[0]
    rows = q_ref.shape[0] // seq_count
    keys = k_ref.shape[0] // seq_count
    block = 256

    @pl.when(group == 0)
    def _():
        for at, size in chunks(row_count, 256):
            value = x_ref[at : at + size, :].astype(WIDE)
            low = (value * rms_rate(value) * gain_ref[...]).astype(LOW)
            normed_t[:, at : at + size] = low.T
            branch[at : at + size, :] = grad_ref[at : at + size, :].astype(LOW)
            if not causal:
                mix_t[:, at : at + size] = mix_all_ref[0, at : at + size, :].T
                grad_total[at : at + size, :] = jnp.zeros((size, value.shape[1]), WIDE)
        if not causal:
            for at, size in chunks(source_ref.shape[0], 256):
                source_t[:, at : at + size] = source_ref[at : at + size, :].T

    grad_mix[...] = nt(branch[...], wo_ref[...]).astype(LOW)
    if not causal:
        across = pl.ds(pl.multiple_of(group * GROUP, GROUP), GROUP)
        dw_ref[3] = nn(mix_t[...], branch[:, across]).astype(LOW)

    for pair in range(2):
        at = pair * PAIR
        if causal:
            for side in range(2):
                head = 2 * pair + side
                wave = wave_ref[pl.ds(group * 4 + head, 1), :]
                spread = pltpu.roll(
                    jnp.broadcast_to(wave, (keys, rows)), 0, 1, stride=1, stride_axis=0
                )
                row = lax.broadcasted_iota(jnp.int32, (keys, rows), 0)
                column = lax.broadcasted_iota(jnp.int32, (keys, rows), 1)
                bias[side] = jnp.where(column >= row, spread, HIDDEN)
        for seq in range(seq_count):
            span_q = slice(seq * rows, (seq + 1) * rows)
            span_k = slice(seq * keys, (seq + 1) * keys)
            sides = []
            for side in range(2):
                head = 2 * pair + side
                own_q = own_lanes(rows, side)
                own_k = own_lanes(keys, side)
                total = jnp.sum(
                    jnp.where(lanes(rows) == head, total_ref[span_q, :], 0.0), axis=1, keepdims=True
                )
                grad_low = grad_mix[span_q, at : at + PAIR]
                product = grad_low.astype(WIDE) * mix_ref[span_q, at : at + PAIR].astype(WIDE)
                delta = jnp.sum(jnp.where(own_q, product, 0.0), axis=1, keepdims=True)
                query = jnp.where(
                    own_q, q_ref[span_q, at : at + PAIR], row_extras(rows, side, -total, 1.0)
                )
                grad_out = jnp.where(own_q, grad_low, row_extras(rows, side, -delta, 0.0))
                key = jnp.where(
                    own_k,
                    k_ref[span_k, at : at + PAIR],
                    key_extras(keys, side, length_ref[seq]),
                )
                value = jnp.where(own_k, v_ref[span_k, at : at + PAIR], jnp.ones((), LOW))
                grad_query = []
                grad_key = None
                grad_value = None
                for start in range(0, rows, block):
                    span = start + block if causal else keys
                    scores = nt(key[:span], query[start : start + block])
                    if causal:
                        scores = scores + bias[side, :span, start : start + block]
                    weight = jnp.exp(scores)
                    low = weight.astype(LOW)
                    grad_weight = nt(value[:span], grad_out[start : start + block])
                    grad_score = (weight * grad_weight).astype(LOW)
                    if causal:
                        if seq == 0:
                            score_sum[side, :span, start : start + block] = grad_score.astype(WIDE)
                        else:
                            score_sum[side, :span, start : start + block] += grad_score.astype(WIDE)
                    key_part = nn(grad_score, query[start : start + block])
                    value_part = nn(low, grad_out[start : start + block])
                    grad_query.append(tn(grad_score, key[:span]))
                    if causal and start == 0 and rows > block:
                        rest = jnp.zeros((keys - span, PAIR), WIDE)
                        key_part = jnp.concatenate([key_part, rest], axis=0)
                        value_part = jnp.concatenate([value_part, rest], axis=0)
                    grad_key = key_part if grad_key is None else grad_key + key_part
                    grad_value = value_part if grad_value is None else grad_value + value_part
                sides.append((jnp.concatenate(grad_query, axis=0), grad_key, grad_value))
            pick_q = own_lanes(rows, 0)
            pick_k = own_lanes(keys, 0)
            gq[span_q, at : at + PAIR] = jnp.where(pick_q, sides[0][0], sides[1][0]).astype(LOW)
            gk_out_ref[span_k, at : at + PAIR] = jnp.where(pick_k, sides[0][1], sides[1][1]).astype(LOW)
            gv_out_ref[span_k, at : at + PAIR] = jnp.where(pick_k, sides[0][2], sides[1][2]).astype(LOW)
        if causal:
            for side in range(2):
                head = 2 * pair + side
                row = lax.broadcasted_iota(jnp.int32, (keys, rows), 0)
                column = lax.broadcasted_iota(jnp.int32, (keys, rows), 1)
                held = jnp.where(column >= row, score_sum[side], 0.0)
                while held.shape[0] > 1:
                    half = held.shape[0] // 2
                    held = held[:half] + pltpu.roll(held[half:], rows - half, 1)
                dist_ref[pl.ds(group * 4 + head, 1), :] = held

    dw_ref[0] = nn(normed_t[...], gq[...]).astype(LOW)
    dw_ref[1] = nn(source_t[...], gk_out_ref[...]).astype(LOW)
    dw_ref[2] = nn(source_t[...], gv_out_ref[...]).astype(LOW)
    if causal:
        return
    grad_total[...] += nt(gq[...], wq_ref[...])

    @pl.when(group == pl.num_programs(0) - 1)
    def _():
        dgain = jnp.zeros(dgain_ref.shape, WIDE)
        for at, size in chunks(row_count, 256):
            part = slice(at, at + size)
            grad_rows, gain_part = rms_back(
                x_ref[part, :].astype(WIDE), gain_ref[...], grad_total[part, :]
            )
            dgain = dgain + gain_part
            grad_rows = grad_ref[part, :] + grad_rows
            grad_x_ref[part, :] = grad_rows
            branch[part, :] = grad_rows.astype(LOW)
            mix_t[:, part] = mix_all_ref[1, part, :].T
        dgain_ref[...] = dgain
        next_ref[...] = nn(mix_t[...], branch[...]).astype(LOW)


def attention_backward(causal, x, source, grad, lengths, gain, weights, wave, kept, mixes):
    row_count, width = x.shape
    seq_count = lengths.shape[0]
    source_rows = row_count if causal else source.shape[0]
    length = row_count // seq_count
    groups = width // GROUP
    low = lambda rows: jax.ShapeDtypeStruct((rows, width), LOW)
    matrices = 3 if causal else 4
    gradients = pl.BlockSpec((matrices, width, GROUP), lambda g: (0, 0, g))
    gradient_shape = jax.ShapeDtypeStruct((matrices, width, width), LOW)
    if causal:
        out_specs = [
            columns(row_count), columns(source_rows), columns(source_rows), gradients, whole(wave.shape),
        ]
        out_shape = [
            low(row_count), low(source_rows), low(source_rows), gradient_shape,
            jax.ShapeDtypeStruct(wave.shape, WIDE),
        ]
        scratch = [pltpu.VMEM((2, length, length), WIDE)] * 2
    else:
        out_specs = [
            whole((row_count, width)), columns(source_rows), columns(source_rows), gradients,
            whole((1, width)), whole((width, width)),
        ]
        out_shape = [
            jax.ShapeDtypeStruct((row_count, width), WIDE), low(source_rows), low(source_rows), gradient_shape,
            jax.ShapeDtypeStruct((1, width), WIDE), jax.ShapeDtypeStruct((width, width), LOW),
        ]
        scratch = [
            pltpu.VMEM((row_count, GROUP), LOW),
            pltpu.VMEM((width, source_rows), LOW),
            pltpu.VMEM((width, row_count), LOW),
            pltpu.VMEM((row_count, width), WIDE),
        ]
    return pl.pallas_call(
        functools.partial(backward_kernel, causal, seq_count),
        grid=(groups,),
        in_specs=[
            pl.BlockSpec(memory_space=pltpu.SMEM),
            whole(x.shape),
            whole(source.shape),
            whole(grad.shape),
            whole(gain.shape),
            weight_specs(width)[0],
            weight_specs(width)[3],
            whole(wave.shape),
            columns(row_count),
            columns(source_rows),
            columns(source_rows),
            columns(row_count),
            pl.BlockSpec((None, row_count, PAIR), lambda g: (g, 0, 0)),
            whole(mixes.shape),
        ],
        out_specs=out_specs,
        out_shape=out_shape,
        scratch_shapes=[
            pltpu.VMEM((width, row_count), LOW),
            pltpu.VMEM((row_count, width), LOW),
            pltpu.VMEM((row_count, GROUP), LOW),
            *scratch,
        ],
        cost_estimate=pl.CostEstimate(flops=int(45 * PEAK), bytes_accessed=40 << 20, transcendentals=0),
        compiler_params=pltpu.CompilerParams(vmem_limit_bytes=VMEM_BYTES),
        name="self_backward" if causal else "cross_backward",
    )(lengths, x, source, grad, gain, weights, weights, wave, *kept, mixes)


def input_kernel(gq_ref, gk_ref, gv_ref, wq_ref, wk_ref, wv_ref, x_ref, grad_ref, gain_ref, out_ref, dgain_ref):
    total = nt(gq_ref[...], wq_ref[...]) + nt(gk_ref[...], wk_ref[...]) + nt(gv_ref[...], wv_ref[...])
    grad_rows, dgain = rms_back(x_ref[...].astype(WIDE), gain_ref[...], total)
    out_ref[...] = grad_ref[...] + grad_rows

    @pl.when(pl.program_id(0) == 0)
    def _():
        dgain_ref[...] = jnp.zeros_like(dgain_ref)

    dgain_ref[...] += dgain


def input_gradient(grads, weights, x, grad, gain):
    rows, width = x.shape
    block = 256
    rowwise = pl.BlockSpec((block, width), lambda g: (g, 0))
    matrix = lambda at: pl.BlockSpec((None, width, width), lambda g: (at, 0, 0))
    return pl.pallas_call(
        input_kernel,
        grid=(rows // block,),
        in_specs=[rowwise, rowwise, rowwise, matrix(0), matrix(1), matrix(2), rowwise, rowwise, whole((1, width))],
        out_specs=[rowwise, whole((1, width))],
        out_shape=[jax.ShapeDtypeStruct((rows, width), WIDE), jax.ShapeDtypeStruct((1, width), WIDE)],
        cost_estimate=pl.CostEstimate(flops=int(8 * PEAK), bytes_accessed=12 << 20, transcendentals=0),
        compiler_params=pltpu.CompilerParams(vmem_limit_bytes=VMEM_BYTES),
        name="input_gradient",
    )(*grads, weights, weights, weights, x, grad, gain)


def memory_kernel(gk_ref, gv_ref, wk_ref, wv_ref, out_ref):
    out_ref[...] = nt(gk_ref[...], wk_ref[...]) + nt(gv_ref[...], wv_ref[...])


def memory_gradient(grad_key, grad_value, weights):
    rows, width = grad_key.shape
    block = 256
    rowwise = pl.BlockSpec((block, width), lambda g: (g, 0))
    matrix = lambda at: pl.BlockSpec((None, width, width), lambda g: (at, 0, 0))
    return pl.pallas_call(
        memory_kernel,
        grid=(rows // block,),
        in_specs=[rowwise, rowwise, matrix(1), matrix(2)],
        out_specs=rowwise,
        out_shape=jax.ShapeDtypeStruct((rows, width), WIDE),
        cost_estimate=pl.CostEstimate(flops=int(7 * PEAK), bytes_accessed=10 << 20, transcendentals=0),
        compiler_params=pltpu.CompilerParams(vmem_limit_bytes=VMEM_BYTES),
        name="memory_gradient",
    )(grad_key, grad_value, weights, weights)


def flat_permute(value, target):
    reps, shards = lax.axis_size("rep"), lax.axis_size("fsdp")
    pairs = []
    for rep in range(reps):
        for shard in range(shards):
            to_rep, to_shard = target(rep, shard)
            pairs.append((rep * shards + shard, to_rep * shards + to_shard))
    return lax.ppermute(value, ("rep", "fsdp"), pairs)


def from_rep(value, way):
    return flat_permute(value, lambda rep, shard: (rep ^ way, shard))


def from_shard(value, way):
    return flat_permute(value, lambda rep, shard: (rep, shard ^ way))


def from_line(value, hops):
    shards = lax.axis_size("fsdp")
    return flat_permute(value, lambda rep, shard: (rep, (shard + 2 * hops) % shards))


def along_line(piece):
    hops = lax.axis_size("fsdp") // 2
    return jnp.stack([piece] + [from_line(piece, hop) for hop in range(1, hops)])


def across_reps(line):
    return [line] + [from_rep(line, way) for way in range(1, 4)]


def with_partner(parts):
    return parts + [from_shard(part, 1) for part in parts]


def scatter_line(quarter):
    shards = quarter.shape[0]
    hops = shards // 2
    shard = lax.axis_index("fsdp")
    line, core = shard // 2, shard % 2
    halves = quarter.reshape(hops, 2, *quarter.shape[1:])
    pick = lambda at: lax.dynamic_index_in_dim(halves, at, 1, keepdims=False)
    chip = (pick(core).astype(WIDE) + from_shard(pick(core ^ 1), 1).astype(WIDE)).astype(LOW)
    at_hop = lambda hop: lax.dynamic_index_in_dim(chip, (line + hop) % hops, 0, keepdims=False)
    total = at_hop(0).astype(WIDE)
    for hop in range(1, hops):
        total = total + from_line(at_hop(hop), hop).astype(WIDE)
    return total.astype(LOW)


def assemble_kernel(place, hops, where_ref, *refs):
    parts, out_ref, sems = refs[:8], refs[8], refs[9]
    rep, line, core = where_ref[0], where_ref[1], where_ref[2]
    copies = []
    for other in range(2):
        for way in range(4):
            for hop in range(hops):
                shard = lax.rem(line - hop + hops, hops) * 2 + (core ^ other)
                copies.append(
                    pltpu.make_async_copy(
                        parts[4 * other + way].at[hop],
                        place(out_ref, rep ^ way, shard),
                        sems.at[len(copies)],
                    )
                )
    for copy in copies:
        copy.start()
    for copy in copies:
        copy.wait()


def assemble(parts, shape, place, name):
    hops = parts[0].shape[0]
    shard = lax.axis_index("fsdp")
    where = jnp.stack([lax.axis_index("rep"), shard // 2, shard % 2]).astype(jnp.int32)
    return pl.pallas_call(
        functools.partial(assemble_kernel, place, hops),
        in_specs=[pl.BlockSpec(memory_space=pltpu.SMEM)] + [pl.BlockSpec(memory_space=pl.ANY)] * 8,
        out_specs=pl.BlockSpec(memory_space=pltpu.VMEM),
        out_shape=jax.ShapeDtypeStruct(shape, LOW),
        scratch_shapes=[pltpu.SemaphoreType.DMA((8 * hops,))],
        cost_estimate=pl.CostEstimate(flops=int(4 * PEAK), bytes_accessed=8 << 20, transcendentals=0),
        compiler_params=pltpu.CompilerParams(vmem_limit_bytes=VMEM_BYTES),
        name=name,
    )(where, *parts)


def rep_parts(parts):
    rep = lax.axis_index("rep")
    pick = lambda at: lax.dynamic_index_in_dim(parts, at, 0, keepdims=False)
    return [pick(rep)] + [from_rep(pick(rep ^ way), way) for way in range(1, 4)]


def add_up(parts):
    return sum(part.astype(WIDE) for part in parts).astype(LOW)


def rep_collect(piece):
    rep = lax.axis_index("rep")
    near = jnp.stack([piece] + [from_rep(piece, way) for way in range(1, 4)])
    return jnp.stack([lax.dynamic_index_in_dim(near, at ^ rep, 0, keepdims=False) for at in range(4)])


def butterfly(vector, move, size):
    way = 1
    while way < size:
        vector = vector + move(vector, way)
        way *= 2
    return vector


def after(value, *earlier):
    return lax.optimization_barrier((value, *earlier))[0]


def factored_update(gradient, weight, row_state, col_state, reduce):
    count, rows, cols = weight.shape
    squares = gradient * gradient + TINY_TERM
    row_moment = DECAY_RATE * row_state + (1.0 - DECAY_RATE) * jnp.mean(squares, axis=2)
    local = jnp.concatenate(
        [
            jnp.sum(squares, axis=1).reshape(-1),
            jnp.sum(row_moment, axis=1),
            jnp.sum(weight * weight, axis=(1, 2)),
        ]
    )
    total = reduce(local)
    whole_rows = rows * lax.axis_size("fsdp")
    col_sum = total[: count * cols].reshape(count, cols)
    row_mean = total[count * cols : count * cols + count] / whole_rows
    square = total[count * cols + count :] / (whole_rows * cols)
    col_moment = DECAY_RATE * col_state + (1.0 - DECAY_RATE) * col_sum / whole_rows
    direction = gradient * lax.rsqrt(
        row_moment[:, :, None] * col_moment[:, None, :] / row_mean[:, None, None]
    )
    step = STEP_RATE * jnp.sqrt(square + 1e-06)
    return weight - step[:, None, None] * direction, row_moment, col_moment


def plain_update(gradient, weight, moment, square):
    moment = DECAY_RATE * moment + (1.0 - DECAY_RATE) * (gradient * gradient + TINY_TERM)
    step = STEP_RATE * jnp.sqrt(square + 1e-06)
    return weight - step * gradient * lax.rsqrt(moment), moment


def per_device(
    dec_in,
    memory,
    out_grad,
    dec_len,
    enc_len,
    buckets,
    self_weight,
    cross_weight,
    ffn_in,
    ffn_out,
    gains,
    table,
    self_rows,
    self_cols,
    cross_rows,
    cross_cols,
    in_rows,
    in_cols,
    out_rows,
    out_cols,
    gain_moment,
    table_moment,
):
    seq_count, seq_length, model_width = dec_in.shape
    mem_length = memory.shape[1]
    row_count = seq_count * seq_length
    hidden_width = ffn_in.shape[2]
    reps, shards = lax.axis_size("rep"), lax.axis_size("fsdp")
    rep, shard = lax.axis_index("rep"), lax.axis_index("fsdp")
    quarters = reps == 4 and shards == 8
    part_rows = hidden_width // shards
    w_self = lax.all_gather(self_weight.astype(LOW), "fsdp", axis=1, tiled=True)
    gain_full = lax.all_gather(gains.astype(LOW), "fsdp", axis=1, tiled=True).astype(WIDE)
    w_in = lax.all_gather(ffn_in.astype(LOW), "fsdp", axis=1, tiled=True)

    bucket_mask = (buckets[None, :] == jnp.arange(BUCKETS)[:, None]).astype(WIDE)
    by_distance = jnp.sum(table.T[:, :, None] * bucket_mask[None], axis=1)
    by_distance = jnp.pad(by_distance, ((0, 16 - H), (0, 0)))
    backwards = jnp.roll(by_distance[:, ::-1], 1, axis=1)
    no_bias = jnp.zeros((8, PAIR), WIDE)
    no_source = jnp.zeros((16, PAIR), LOW)

    dec_rows = dec_in.reshape(row_count, model_width)
    mem_rows = memory.reshape(seq_count * mem_length, model_width)
    grad_rows = out_grad.reshape(row_count, model_width)
    *kept_one, after_self = attention_forward(
        True, dec_rows, no_source, dec_len, gain_full[0:1], w_self, backwards
    )
    if quarters:
        cross_quarter = lax.dynamic_index_in_dim(cross_weight, rep, 0, keepdims=False).astype(LOW)
        out_quarter = lax.dynamic_index_in_dim(
            ffn_out.reshape(4, part_rows // 4, model_width), rep, 0, keepdims=False
        ).astype(LOW)
        cross_rows_each, out_rows_each = cross_weight.shape[1], part_rows // 4
        cross_pieces = with_partner(across_reps(along_line(cross_quarter)))
        w_cross = assemble(
            list(lax.optimization_barrier((*cross_pieces, after_self))[:-1]),
            (4, model_width, model_width),
            lambda ref, quarter, at: ref.at[quarter, pl.ds(at * cross_rows_each, cross_rows_each)],
            "assemble_cross",
        )
        out_line = along_line(after(out_quarter, w_self))
        out_near = across_reps(after(out_line, after_self))
    else:
        w_cross = lax.all_gather(cross_weight.astype(LOW), "fsdp", axis=1, tiled=True)
        w_out = lax.all_gather(ffn_out.astype(LOW), "fsdp", axis=0, tiled=True)
    *kept_two, after_cross = attention_forward(
        False, after_self, mem_rows, enc_len, gain_full[1:2], w_cross, no_bias
    )
    if quarters:
        out_near = list(lax.optimization_barrier((*out_near, after_cross))[:-1])
        w_out = assemble(
            with_partner(out_near),
            (hidden_width, model_width),
            lambda ref, quarter, at: ref.at[pl.ds((at * 4 + quarter) * out_rows_each, out_rows_each)],
            "assemble_out",
        )
    layer_out, grad_cross, grad_in, grad_out, gain_three = feed_forward_both(
        after_cross, grad_rows, dec_len, gain_full[2:3], w_in, w_out
    )
    scatter = lambda value, at: lax.psum_scatter(value, "fsdp", scatter_dimension=at, tiled=True)
    if quarters:
        own_gate = scatter(grad_in[0], 0)
        out_sum = rep_parts(grad_out)
    grad_self, grad_k_two, grad_v_two, grad_cross_weights, gain_two, grad_wo = attention_backward(
        False, after_self, mem_rows, grad_cross, enc_len, gain_full[1:2], w_cross, no_bias, kept_two,
        jnp.stack([kept_two[3], kept_one[3]]),
    )
    if quarters:
        grad_self, own_gate, *out_sum = lax.optimization_barrier((grad_self, own_gate, *out_sum))
        own_up = scatter(grad_in[1], 0)
        cut_wo = grad_wo.reshape(shards, 4, -1, model_width)
        rep_pick = lambda at: jnp.concatenate(
            [
                lax.dynamic_index_in_dim(grad_cross_weights, at, 0, False).reshape(shards, -1, model_width),
                lax.dynamic_index_in_dim(cut_wo, at, 1, False),
            ],
            axis=1,
        )
        grad_self, *cross_parts = lax.optimization_barrier(
            (grad_self, *[rep_pick(rep ^ way) for way in range(4)])
        )
        cross_sum = cross_parts[:1] + [from_rep(cross_parts[way], way) for way in range(1, 4)]
    *grads_one, grad_self_weights, dist_grad = attention_backward(
        True, dec_rows, no_source, grad_self, dec_len, gain_full[0:1], w_self, by_distance, kept_one, no_source
    )
    if quarters:
        grad_self_weights, *near = lax.optimization_barrier((grad_self_weights, *cross_sum[:3]))
        cross_sum = near + cross_sum[3:]
        own_self = scatter(grad_self_weights, 1)
        grads_one = list(lax.optimization_barrier((*grads_one, grad_self_weights))[:-1])
    input_grad, gain_one = input_gradient(grads_one, w_self, dec_rows, grad_self, gain_full[0:1])
    memory_grad = memory_gradient(after(grad_k_two, gain_one), grad_v_two, w_cross)
    if quarters:
        memory_grad, own_up, *sums = lax.optimization_barrier((memory_grad, own_up, *out_sum, *cross_sum))
        out_sum, cross_sum = sums[:4], sums[4:]
    layer_out = layer_out.reshape(dec_in.shape)
    input_grad = input_grad.reshape(dec_in.shape)
    memory_grad = memory_grad.reshape(memory.shape)
    table_part = jnp.sum(bucket_mask[:, None, :] * dist_grad[None, :H, :], axis=2)

    small = jnp.concatenate(
        [gain_one.reshape(-1), gain_two.reshape(-1), gain_three.reshape(-1), table_part.reshape(-1)]
    )
    if quarters:
        in_parts = rep_parts(jnp.stack([own_gate, own_up]).reshape(4, -1, hidden_width))
        quarter = scatter_line(
            jnp.concatenate(
                [add_up(cross_sum), add_up(out_sum).reshape(shards, -1, model_width)], axis=1
            )
        )
        own_in = rep_collect(add_up(in_parts)).reshape(ffn_in.shape)
        both = rep_collect(quarter)
        cross_end = cross_weight.shape[1]
        wo_end = cross_end + cross_weight.shape[1] // 4
        own_cross, own_out = both[:, :cross_end], both[:, wo_end:].reshape(ffn_out.shape)
        own_self = rep_collect(add_up(rep_parts(own_self.reshape(4, -1, model_width))))
        own_self = jnp.concatenate(
            [
                own_self.reshape(3, *self_weight.shape[1:]),
                both[:, cross_end:wo_end].reshape(1, *self_weight.shape[1:]),
            ]
        )
        over_shards = lambda vector: butterfly(vector, from_shard, shards)
        small = butterfly(butterfly(small, from_shard, shards), from_rep, reps)
    else:
        over_reps = lambda value: lax.psum(value, "rep")
        own_in = over_reps(scatter(grad_in, 1))
        own_out = over_reps(
            scatter(grad_out.transpose(1, 0, 2, 3).reshape(hidden_width, model_width), 0)
        )
        own_cross = over_reps(scatter(grad_cross_weights, 1))
        own_self = over_reps(scatter(jnp.concatenate([grad_self_weights, grad_wo[None]]), 1))
        over_shards = lambda vector: lax.psum(vector, "fsdp")
        small = lax.psum(small, ("rep", "fsdp"))

    grad_factor = 1.0 / math.sqrt(row_count * reps * shards)
    self_grad, cross_grad, ffn_in_grad, feedforward_output_gradient = [
        member.astype(WIDE) * grad_factor for member in (own_self, own_cross, own_in, own_out)
    ]
    small = small * grad_factor
    gains_grad = lax.dynamic_slice_in_dim(
        small[: 3 * model_width].reshape(3, model_width), shard * gains.shape[1], gains.shape[1], axis=1
    )
    table_grad = small[3 * model_width :].reshape(BUCKETS, H)
    new_ffn_in, new_in_rows, new_in_cols = factored_update(
        ffn_in_grad, ffn_in, in_rows, in_cols, over_shards
    )
    new_ffn_out, new_out_rows, new_out_cols = [
        member[0]
        for member in factored_update(
            feedforward_output_gradient[None], ffn_out[None], out_rows[None], out_cols[None], over_shards
        )
    ]
    new_cross, new_cross_rows, new_cross_cols = factored_update(
        cross_grad, cross_weight, cross_rows, cross_cols, over_shards
    )
    new_self, new_self_rows, new_self_cols = factored_update(
        self_grad, self_weight, self_rows, self_cols, over_shards
    )
    gain_square = over_shards(jnp.sum(gains * gains, axis=1)) / model_width
    new_gains, new_gain_moment = plain_update(gains_grad, gains, gain_moment, gain_square[:, None])
    new_table, new_table_moment = plain_update(
        table_grad, table, table_moment, jnp.mean(table * table)
    )
    return (
        layer_out,
        input_grad,
        memory_grad,
        self_grad,
        cross_grad,
        ffn_in_grad,
        feedforward_output_gradient,
        gains_grad,
        table_grad,
        new_self,
        new_cross,
        new_ffn_in,
        new_ffn_out,
        new_gains,
        new_table,
        new_self_rows,
        new_self_cols,
        new_cross_rows,
        new_cross_cols,
        new_in_rows,
        new_in_cols,
        new_out_rows,
        new_out_cols,
        new_gain_moment,
        new_table_moment,
    )


def solution(mesh):
    placed = (
        P(("rep", "fsdp"), None, None),
        P(("rep", "fsdp"), None, None),
        P(("rep", "fsdp"), None, None),
        P(("rep", "fsdp")),
        P(("rep", "fsdp")),
        P(),
        P(None, "fsdp", None),
        P(None, "fsdp", None),
        P(None, "fsdp", None),
        P("fsdp", None),
        P(None, "fsdp"),
        P(),
        P(None, "fsdp"),
        P(),
        P(None, "fsdp"),
        P(),
        P(None, "fsdp"),
        P(),
        P("fsdp"),
        P(),
        P(None, "fsdp"),
        P(),
    )
    return jax.shard_map(
        per_device,
        mesh=mesh,
        in_specs=placed,
        out_specs=(
            P(("rep", "fsdp"), None, None),
            P(("rep", "fsdp"), None, None),
            P(("rep", "fsdp"), None, None),
            P(None, "fsdp", None),
            P(None, "fsdp", None),
            P(None, "fsdp", None),
            P("fsdp", None),
            P(None, "fsdp"),
            P(),
            P(None, "fsdp", None),
            P(None, "fsdp", None),
            P(None, "fsdp", None),
            P("fsdp", None),
            P(None, "fsdp"),
            P(),
            P(None, "fsdp"),
            P(),
            P(None, "fsdp"),
            P(),
            P(None, "fsdp"),
            P(),
            P("fsdp"),
            P(),
            P(None, "fsdp"),
            P(),
        ),
        check_vma=False,
    )
```

```python
import functools
import math

import jax
import jax.numpy as jnp
from jax import lax
from jax.experimental import pallas as pl
from jax.experimental.pallas import tpu as pltpu
from jax.sharding import PartitionSpec as P

H = 12
DH = 64
BUCKETS = 32
DECAY_RATE = 0.8
STEP_RATE = 0.2
TINY_TERM = 1e-30
PAIR = 2 * DH
GROUP = 4 * DH
HIDDEN = -1e30
VMEM_BYTES = 60 * 1024 * 1024
PEAK = 1.15e9
LINE = 4
LINE_CORES = 2
LOW = jnp.bfloat16
WIDE = jnp.float32


def nn(left, right):
    return lax.dot_general(left, right, (((1,), (0,)), ((), ())), preferred_element_type=WIDE)


def nt(left, right):
    return lax.dot_general(left, right, (((1,), (1,)), ((), ())), preferred_element_type=WIDE)


def tn(left, right):
    return lax.dot_general(left, right, (((0,), (0,)), ((), ())), preferred_element_type=WIDE)


def rms_rate(rows):
    return lax.rsqrt(jnp.mean(rows * rows, axis=-1, keepdims=True) + 1e-06)


def three_parts(column):
    high = column.astype(LOW)
    rest = column - high.astype(WIDE)
    middle = rest.astype(LOW)
    low = (rest - middle.astype(WIDE)).astype(LOW)
    return high, middle, low


def chunks(total, size):
    return [(at, min(size, total - at)) for at in range(0, total, size)]


def lanes(rows):
    return lax.broadcasted_iota(jnp.int32, (rows, PAIR), 1)


def own_lanes(rows, side):
    lane = lanes(rows)
    return (lane >= DH * side) & (lane < DH * (side + 1))


def key_extras(rows, side, length):
    lane = lanes(rows) - DH * (1 - side)
    dead = lax.broadcasted_iota(jnp.int32, (rows, PAIR), 0) >= length
    mask = jnp.where(dead, HIDDEN, 0.0)
    return jnp.where(
        (lane >= 0) & (lane < 3), 1.0, jnp.where(lane == 3, mask, 0.0)
    ).astype(LOW)


def row_extras(rows, side, column, last):
    lane = lanes(rows) - DH * (1 - side)
    high, middle, low = three_parts(column)
    wide = lambda part: jnp.broadcast_to(part.astype(WIDE), (rows, PAIR))
    return jnp.where(
        lane == 0,
        wide(high),
        jnp.where(
            lane == 1, wide(middle), jnp.where(lane == 2, wide(low), jnp.where(lane == 3, last, 0.0))
        ),
    ).astype(LOW)


def forward_body(causal, seq_count, length_ref, wave_ref, bias_ref, q_ref, k_ref, v_ref, mix_ref, total_ref, group):
    rows = q_ref.shape[0] // seq_count
    keys = k_ref.shape[0] // seq_count
    block = 256
    for pair in range(2):
        at = pair * PAIR
        for side in range(2):
            head = 2 * pair + side
            if causal:
                wave = wave_ref[pl.ds(group * 4 + head, 1), :]
                spread = pltpu.roll(
                    jnp.broadcast_to(wave, (rows, keys)), 0, 1, stride=1, stride_axis=0
                )
                row = lax.broadcasted_iota(jnp.int32, (rows, keys), 0)
                column = lax.broadcasted_iota(jnp.int32, (rows, keys), 1)
                bias_ref[side] = jnp.where(column <= row, spread, HIDDEN)
        for seq in range(seq_count):
            outs = []
            for side in range(2):
                own_q = own_lanes(rows, side)
                own_k = own_lanes(keys, side)
                query = jnp.where(
                    own_q,
                    q_ref[seq * rows : (seq + 1) * rows, at : at + PAIR],
                    (lanes(rows) == DH * (1 - side) + 3).astype(LOW),
                )
                key = jnp.where(
                    own_k,
                    k_ref[seq * keys : (seq + 1) * keys, at : at + PAIR],
                    key_extras(keys, side, length_ref[seq]),
                )
                value = jnp.where(
                    own_k,
                    v_ref[seq * keys : (seq + 1) * keys, at : at + PAIR],
                    jnp.ones((), LOW),
                )
                parts = []
                for start in range(0, rows, block):
                    span = start + block if causal else keys
                    scores = nt(query[start : start + block], key[:span])
                    if causal:
                        scores = scores + bias_ref[side, start : start + block, :span]
                    top = jnp.max(scores, axis=1, keepdims=True)
                    weight = jnp.exp(scores - top)
                    out = nn(weight.astype(LOW), value[:span])
                    total = out[:, DH * (1 - side) : DH * (1 - side) + 1]
                    parts.append(out * (1.0 / total))
                    spot = pl.ds(seq * rows + start, block)
                    lane = lanes(block)
                    seen = total_ref[spot, :] if (pair or side) else jnp.zeros((block, PAIR), WIDE)
                    total_ref[spot, :] = jnp.where(
                        lane == 2 * pair + side, top + jnp.log(total), seen
                    )
                outs.append(jnp.concatenate(parts, axis=0))
            mix_ref[seq * rows : (seq + 1) * rows, at : at + PAIR] = jnp.where(
                own_lanes(rows, 0), outs[0], outs[1]
            ).astype(LOW)


def forward_kernel(
    causal, seq_count, length_ref, x_ref, source_ref, gain_ref, wq_ref, wk_ref, wv_ref, wo_ref, wave_ref,
    q_ref, k_ref, v_ref, mix_ref, total_ref, after_ref, normed, bias,
):
    group = pl.program_id(0)

    @pl.when(group == 0)
    def _():
        for at, size in chunks(x_ref.shape[0], 256):
            rows = x_ref[at : at + size, :].astype(WIDE)
            normed[at : at + size, :] = (rows * rms_rate(rows) * gain_ref[...]).astype(LOW)
            after_ref[at : at + size, :] = rows

    source = normed if causal else source_ref
    q_ref[...] = nn(normed[...], wq_ref[...]).astype(LOW)
    k_ref[...] = nn(source[...], wk_ref[...]).astype(LOW)
    v_ref[...] = nn(source[...], wv_ref[...]).astype(LOW)
    forward_body(causal, seq_count, length_ref, wave_ref, bias, q_ref, k_ref, v_ref, mix_ref, total_ref, group)
    after_ref[...] += nn(mix_ref[...], wo_ref[...])


def weight_specs(width):
    across = lambda at: pl.BlockSpec((None, width, GROUP), lambda g, at=at: (at, 0, g))
    return [across(0), across(1), across(2), pl.BlockSpec((None, GROUP, width), lambda g: (3, g, 0))]


def whole(shape):
    return pl.BlockSpec(shape, lambda g: (0,) * len(shape))


def columns(rows):
    return pl.BlockSpec((rows, GROUP), lambda g: (0, g))


def attention_forward(causal, x, source, lengths, gain, weights, wave):
    row_count, width = x.shape
    seq_count = lengths.shape[0]
    source_rows = row_count if causal else source.shape[0]
    length = row_count // seq_count
    groups = width // GROUP
    low = lambda rows: jax.ShapeDtypeStruct((rows, width), LOW)
    args = [lengths, x, source, gain, weights, weights, weights, weights, wave]
    return pl.pallas_call(
        functools.partial(forward_kernel, causal, seq_count),
        grid=(groups,),
        in_specs=[
            pl.BlockSpec(memory_space=pltpu.SMEM),
            whole(x.shape),
            whole(source.shape),
            whole(gain.shape),
            *weight_specs(width),
            whole(wave.shape),
        ],
        out_specs=[
            columns(row_count),
            columns(source_rows),
            columns(source_rows),
            columns(row_count),
            pl.BlockSpec((None, row_count, PAIR), lambda g: (g, 0, 0)),
            whole((row_count, width)),
        ],
        out_shape=[
            low(row_count),
            low(source_rows),
            low(source_rows),
            low(row_count),
            jax.ShapeDtypeStruct((groups, row_count, PAIR), WIDE),
            jax.ShapeDtypeStruct((row_count, width), WIDE),
        ],
        scratch_shapes=[
            pltpu.VMEM((row_count, width), LOW),
            pltpu.VMEM((2, length, length) if causal else (1, 8, PAIR), WIDE),
        ],
        cost_estimate=pl.CostEstimate(flops=int(27 * PEAK), bytes_accessed=20 << 20, transcendentals=0),
        compiler_params=pltpu.CompilerParams(vmem_limit_bytes=VMEM_BYTES),
        name="self_forward" if causal else "cross_forward",
    )(*args)


def gelu_parts(gate):
    root = 0.7978845608028654
    square = gate * gate
    inner = jnp.tanh(root * gate * (1.0 + 0.044715 * square))
    half = 0.5 * (1.0 + inner)
    value = gate * half
    slope = half + 0.5 * gate * (1.0 - inner * inner) * (root * (1.0 + 3 * 0.044715 * square))
    return value, slope


def rms_back(rows, gain, grad):
    rate = rms_rate(rows)
    scaled = rows * rate
    low = grad * gain
    grad_rows = rate * (low - scaled * jnp.mean(scaled * low, axis=-1, keepdims=True))
    return grad_rows, jnp.sum(grad * scaled, axis=0, keepdims=True)


def shard_slot(where_ref, shard):
    return (shard % LINE_CORES) ^ where_ref[2], lax.rem(shard // LINE_CORES - where_ref[1] + LINE, LINE)


def feed_kernel(
    seq_count, length_ref, where_ref, after_ref, out_grad_ref, gain_ref, wg_ref, wu_ref, wd_ref,
    layer_ref, grad_cross_ref, dwg_ref, dwu_ref, *refs,
):
    near_refs = refs[:4]
    dgain_ref, normed, normed_t, down, out_total, grad_total, cut = refs[4:]
    step = pl.program_id(0)
    row_count = after_ref.shape[0]
    length = row_count // seq_count

    def live(at, size):
        position = lax.broadcasted_iota(jnp.int32, (size, 1), 0) + (at % length)
        return (position < length_ref[at // length]).astype(WIDE)

    @pl.when(step == 0)
    def _():
        for at, size in chunks(row_count, 256):
            rows = after_ref[at : at + size, :]
            low = (rows * rms_rate(rows) * gain_ref[...]).astype(LOW)
            normed[at : at + size, :] = low
            normed_t[:, at : at + size] = low.T
            down[at : at + size, :] = (
                out_grad_ref[at : at + size, :].astype(WIDE) * live(at, size)
            ).astype(LOW)
            out_total[at : at + size, :] = rows
            grad_total[at : at + size, :] = jnp.zeros((size, rows.shape[1]), WIDE)

    gate = nn(normed[...], wg_ref[...])
    up = nn(normed[...], wu_ref[...])
    value, slope = gelu_parts(gate)
    hidden = (value * up).astype(LOW)
    out_total[...] += nn(hidden, wd_ref[...])
    grad_hidden = nt(down[...], wd_ref[...])
    cut[...] = tn(hidden, down[...]).astype(LOW).reshape(cut.shape)
    core, hop = shard_slot(where_ref, step)
    for way in range(4):
        near_refs[way][core, hop] = cut[where_ref[0] ^ way]
    grad_gate = (grad_hidden * up * slope).astype(LOW)
    grad_up = (grad_hidden * value).astype(LOW)
    dwg_ref[...] = nn(normed_t[...], grad_gate).astype(LOW)
    dwu_ref[...] = nn(normed_t[...], grad_up).astype(LOW)
    grad_total[...] += nt(grad_gate, wg_ref[...]) + nt(grad_up, wu_ref[...])

    @pl.when(step == pl.num_programs(0) - 1)
    def _():
        dgain = jnp.zeros(dgain_ref.shape, WIDE)
        for at, size in chunks(row_count, 256):
            part = slice(at, at + size)
            layer_ref[part, :] = (out_total[part, :] * live(at, size)).astype(LOW)
            grad_rows, gain_part = rms_back(after_ref[part, :], gain_ref[...], grad_total[part, :])
            dgain = dgain + gain_part
            grad_cross_ref[part, :] = (
                out_grad_ref[part, :].astype(WIDE) * live(at, size) + grad_rows
            )
        dgain_ref[...] = dgain


def feed_forward_both(after, out_grad, lengths, where, gain, w_in, w_out):
    row_count, width = after.shape
    hidden = w_out.shape[0]
    block = hidden // (LINE * LINE_CORES)
    seq_count = lengths.shape[0]
    wide = pl.BlockSpec((None, width, block), lambda g: (0, 0, g))
    wide_up = pl.BlockSpec((None, width, block), lambda g: (1, 0, g))
    tall = pl.BlockSpec((block, width), lambda g: (g, 0))
    flat = pl.BlockSpec((width, block), lambda g: (0, g))
    near = (LINE_CORES, LINE, block // 4, width)
    return pl.pallas_call(
        functools.partial(feed_kernel, seq_count),
        grid=(hidden // block,),
        in_specs=[
            pl.BlockSpec(memory_space=pltpu.SMEM),
            pl.BlockSpec(memory_space=pltpu.SMEM),
            whole(after.shape),
            whole(out_grad.shape),
            whole(gain.shape),
            wide,
            wide_up,
            tall,
        ],
        out_specs=[whole(after.shape), whole(after.shape), flat, flat, *[whole(near)] * 4, whole((1, width))],
        out_shape=[
            jax.ShapeDtypeStruct((row_count, width), LOW),
            jax.ShapeDtypeStruct((row_count, width), WIDE),
            jax.ShapeDtypeStruct((width, hidden), LOW),
            jax.ShapeDtypeStruct((width, hidden), LOW),
            *[jax.ShapeDtypeStruct(near, LOW)] * 4,
            jax.ShapeDtypeStruct((1, width), WIDE),
        ],
        scratch_shapes=[
            pltpu.VMEM((row_count, width), LOW),
            pltpu.VMEM((width, row_count), LOW),
            pltpu.VMEM((row_count, width), LOW),
            pltpu.VMEM((row_count, width), WIDE),
            pltpu.VMEM((row_count, width), WIDE),
            pltpu.VMEM((4, block // 4, width), LOW),
        ],
        cost_estimate=pl.CostEstimate(flops=int(46 * PEAK), bytes_accessed=40 << 20, transcendentals=0),
        compiler_params=pltpu.CompilerParams(vmem_limit_bytes=VMEM_BYTES),
        name="feed_forward_both",
    )(lengths, where, after, out_grad, gain, w_in, w_in, w_out)


def backward_kernel(
    causal, seq_count, length_ref, where_ref, x_ref, source_ref, grad_ref, gain_ref, wq_ref, wo_ref, wave_ref,
    q_ref, k_ref, v_ref, mix_ref, total_ref, mix_all_ref, mix_past_ref, *refs,
):
    if causal:
        gq, gk_out_ref, gv_out_ref, dw_ref, dist_ref = refs[:5]
        normed_t, branch, grad_mix, bias, score_sum = refs[5:]
        source_t = normed_t
    else:
        grad_x_ref, gk_out_ref, gv_out_ref, dgain_ref = refs[:4]
        near_refs, far_ref = refs[4:8], refs[8]
        normed_t, branch, grad_mix, gq, source_t, mix_t, grad_total, dw_ref, past = refs[9:]
    group = pl.program_id(0)
    row_count = x_ref.shape[0]
    rows = q_ref.shape[0] // seq_count
    keys = k_ref.shape[0] // seq_count
    block = 256

    @pl.when(group == 0)
    def _():
        for at, size in chunks(row_count, 256):
            value = x_ref[at : at + size, :].astype(WIDE)
            low = (value * rms_rate(value) * gain_ref[...]).astype(LOW)
            normed_t[:, at : at + size] = low.T
            branch[at : at + size, :] = grad_ref[at : at + size, :].astype(LOW)
            if not causal:
                mix_t[:, at : at + size] = mix_all_ref[at : at + size, :].T
                grad_total[at : at + size, :] = jnp.zeros((size, value.shape[1]), WIDE)
        if not causal:
            for at, size in chunks(source_ref.shape[0], 256):
                source_t[:, at : at + size] = source_ref[at : at + size, :].T

    grad_mix[...] = nt(branch[...], wo_ref[...]).astype(LOW)
    if not causal:
        across = pl.ds(pl.multiple_of(group * GROUP, GROUP), GROUP)
        put = lambda at, value: dw_ref.__setitem__(at, value.astype(LOW).reshape(dw_ref.shape[1:]))
        put(3, nn(mix_t[...], branch[:, across]))

    for pair in range(2):
        at = pair * PAIR
        if causal:
            for side in range(2):
                head = 2 * pair + side
                wave = wave_ref[pl.ds(group * 4 + head, 1), :]
                spread = pltpu.roll(
                    jnp.broadcast_to(wave, (keys, rows)), 0, 1, stride=1, stride_axis=0
                )
                row = lax.broadcasted_iota(jnp.int32, (keys, rows), 0)
                column = lax.broadcasted_iota(jnp.int32, (keys, rows), 1)
                bias[side] = jnp.where(column >= row, spread, HIDDEN)
        for seq in range(seq_count):
            span_q = slice(seq * rows, (seq + 1) * rows)
            span_k = slice(seq * keys, (seq + 1) * keys)
            sides = []
            for side in range(2):
                head = 2 * pair + side
                own_q = own_lanes(rows, side)
                own_k = own_lanes(keys, side)
                total = jnp.sum(
                    jnp.where(lanes(rows) == head, total_ref[span_q, :], 0.0), axis=1, keepdims=True
                )
                grad_low = grad_mix[span_q, at : at + PAIR]
                product = grad_low.astype(WIDE) * mix_ref[span_q, at : at + PAIR].astype(WIDE)
                delta = jnp.sum(jnp.where(own_q, product, 0.0), axis=1, keepdims=True)
                query = jnp.where(
                    own_q, q_ref[span_q, at : at + PAIR], row_extras(rows, side, -total, 1.0)
                )
                grad_out = jnp.where(own_q, grad_low, row_extras(rows, side, -delta, 0.0))
                key = jnp.where(
                    own_k,
                    k_ref[span_k, at : at + PAIR],
                    key_extras(keys, side, length_ref[seq]),
                )
                value = jnp.where(own_k, v_ref[span_k, at : at + PAIR], jnp.ones((), LOW))
                grad_query = []
                grad_key = None
                grad_value = None
                for start in range(0, rows, block):
                    span = start + block if causal else keys
                    scores = nt(key[:span], query[start : start + block])
                    if causal:
                        scores = scores + bias[side, :span, start : start + block]
                    weight = jnp.exp(scores)
                    low = weight.astype(LOW)
                    grad_weight = nt(value[:span], grad_out[start : start + block])
                    grad_score = (weight * grad_weight).astype(LOW)
                    if causal:
                        if seq == 0:
                            score_sum[side, :span, start : start + block] = grad_score.astype(WIDE)
                        else:
                            score_sum[side, :span, start : start + block] += grad_score.astype(WIDE)
                    key_part = nn(grad_score, query[start : start + block])
                    value_part = nn(low, grad_out[start : start + block])
                    grad_query.append(tn(grad_score, key[:span]))
                    if causal and start == 0 and rows > block:
                        rest = jnp.zeros((keys - span, PAIR), WIDE)
                        key_part = jnp.concatenate([key_part, rest], axis=0)
                        value_part = jnp.concatenate([value_part, rest], axis=0)
                    grad_key = key_part if grad_key is None else grad_key + key_part
                    grad_value = value_part if grad_value is None else grad_value + value_part
                sides.append((jnp.concatenate(grad_query, axis=0), grad_key, grad_value))
            pick_q = own_lanes(rows, 0)
            pick_k = own_lanes(keys, 0)
            gq[span_q, at : at + PAIR] = jnp.where(pick_q, sides[0][0], sides[1][0]).astype(LOW)
            gk_out_ref[span_k, at : at + PAIR] = jnp.where(pick_k, sides[0][1], sides[1][1]).astype(LOW)
            gv_out_ref[span_k, at : at + PAIR] = jnp.where(pick_k, sides[0][2], sides[1][2]).astype(LOW)
        if causal:
            for side in range(2):
                head = 2 * pair + side
                row = lax.broadcasted_iota(jnp.int32, (keys, rows), 0)
                column = lax.broadcasted_iota(jnp.int32, (keys, rows), 1)
                held = jnp.where(column >= row, score_sum[side], 0.0)
                while held.shape[0] > 1:
                    half = held.shape[0] // 2
                    held = held[:half] + pltpu.roll(held[half:], rows - half, 1)
                dist_ref[pl.ds(group * 4 + head, 1), :] = held

    if causal:
        dw_ref[0] = nn(normed_t[...], gq[...]).astype(LOW)
        dw_ref[1] = nn(source_t[...], gk_out_ref[...]).astype(LOW)
        dw_ref[2] = nn(source_t[...], gv_out_ref[...]).astype(LOW)
        return
    put(0, nn(normed_t[...], gq[...]))
    put(1, nn(source_t[...], gk_out_ref[...]))
    put(2, nn(source_t[...], gv_out_ref[...]))
    grad_total[...] += nt(gq[...], wq_ref[...])
    rep, line, core = where_ref[0], where_ref[1], where_ref[2]
    held = dw_ref.shape[2]
    slots = []
    for way in range(4):
        for hop in range(LINE):
            at = lax.rem(line + hop, LINE) * LINE_CORES
            slots.append((near_refs[way].at[hop], rep ^ way, at + core))
            slots.append((far_ref.at[way, hop], rep ^ way, at + (core ^ 1)))
    for slot, quarter, shard in slots:
        slot[0:held, across] = dw_ref[quarter, shard]

    @pl.when(group == pl.num_programs(0) - 1)
    def _():
        dgain = jnp.zeros(dgain_ref.shape, WIDE)
        for at, size in chunks(row_count, 256):
            part = slice(at, at + size)
            grad_rows, gain_part = rms_back(
                x_ref[part, :].astype(WIDE), gain_ref[...], grad_total[part, :]
            )
            dgain = dgain + gain_part
            grad_rows = grad_ref[part, :] + grad_rows
            grad_x_ref[part, :] = grad_rows
            branch[part, :] = grad_rows.astype(LOW)
            mix_t[:, part] = mix_past_ref[part, :].T
        dgain_ref[...] = dgain
        thirds = nn(mix_t[...], branch[...]).astype(LOW)
        past[:, 0:3] = thirds.reshape(past.shape[0], 3, *past.shape[2:])
        past[:, 3] = jnp.zeros_like(past[:, 3])
        for slot, quarter, shard in slots:
            slot[held:, :] = past[shard, quarter]


def attention_backward(causal, x, source, grad, lengths, where, gain, weights, wave, kept, mix, past):
    row_count, width = x.shape
    seq_count = lengths.shape[0]
    source_rows = row_count if causal else source.shape[0]
    length = row_count // seq_count
    groups = width // GROUP
    low = lambda rows: jax.ShapeDtypeStruct((rows, width), LOW)
    if causal:
        out_specs = [
            columns(row_count), columns(source_rows), columns(source_rows),
            pl.BlockSpec((3, width, GROUP), lambda g: (0, 0, g)), whole(wave.shape),
        ]
        out_shape = [
            low(row_count), low(source_rows), low(source_rows),
            jax.ShapeDtypeStruct((3, width, width), LOW), jax.ShapeDtypeStruct(wave.shape, WIDE),
        ]
        scratch = [pltpu.VMEM((2, length, length), WIDE)] * 2
    else:
        shards = LINE * LINE_CORES
        each, third = width // shards, width // shards // 3
        near = (LINE, each + third, width)
        out_specs = [
            whole((row_count, width)), columns(source_rows), columns(source_rows), whole((1, width)),
            *[whole(near)] * 4, whole((4, *near)),
        ]
        out_shape = [
            jax.ShapeDtypeStruct((row_count, width), WIDE), low(source_rows), low(source_rows),
            jax.ShapeDtypeStruct((1, width), WIDE), *[jax.ShapeDtypeStruct(near, LOW)] * 4,
            jax.ShapeDtypeStruct((4, *near), LOW),
        ]
        scratch = [
            pltpu.VMEM((row_count, GROUP), LOW),
            pltpu.VMEM((width, source_rows), LOW),
            pltpu.VMEM((width, row_count), LOW),
            pltpu.VMEM((row_count, width), WIDE),
            pltpu.VMEM((4, shards, each, GROUP), LOW),
            pltpu.VMEM((shards, 4, third, width), LOW),
        ]
    return pl.pallas_call(
        functools.partial(backward_kernel, causal, seq_count),
        grid=(groups,),
        in_specs=[
            pl.BlockSpec(memory_space=pltpu.SMEM),
            pl.BlockSpec(memory_space=pltpu.SMEM),
            whole(x.shape),
            whole(source.shape),
            whole(grad.shape),
            whole(gain.shape),
            weight_specs(width)[0],
            weight_specs(width)[3],
            whole(wave.shape),
            columns(row_count),
            columns(source_rows),
            columns(source_rows),
            columns(row_count),
            pl.BlockSpec((None, row_count, PAIR), lambda g: (g, 0, 0)),
            whole(mix.shape),
            whole(past.shape),
        ],
        out_specs=out_specs,
        out_shape=out_shape,
        scratch_shapes=[
            pltpu.VMEM((width, row_count), LOW),
            pltpu.VMEM((row_count, width), LOW),
            pltpu.VMEM((row_count, GROUP), LOW),
            *scratch,
        ],
        cost_estimate=pl.CostEstimate(flops=int(45 * PEAK), bytes_accessed=40 << 20, transcendentals=0),
        compiler_params=pltpu.CompilerParams(vmem_limit_bytes=VMEM_BYTES),
        name="self_backward" if causal else "cross_backward",
    )(lengths, where, x, source, grad, gain, weights, weights, wave, *kept, mix, past)


def input_kernel(gq_ref, gk_ref, gv_ref, wq_ref, wk_ref, wv_ref, x_ref, grad_ref, gain_ref, out_ref, dgain_ref):
    total = nt(gq_ref[...], wq_ref[...]) + nt(gk_ref[...], wk_ref[...]) + nt(gv_ref[...], wv_ref[...])
    grad_rows, dgain = rms_back(x_ref[...].astype(WIDE), gain_ref[...], total)
    out_ref[...] = grad_ref[...] + grad_rows

    @pl.when(pl.program_id(0) == 0)
    def _():
        dgain_ref[...] = jnp.zeros_like(dgain_ref)

    dgain_ref[...] += dgain


def input_gradient(grads, weights, x, grad, gain):
    rows, width = x.shape
    block = 256
    rowwise = pl.BlockSpec((block, width), lambda g: (g, 0))
    matrix = lambda at: pl.BlockSpec((None, width, width), lambda g: (at, 0, 0))
    return pl.pallas_call(
        input_kernel,
        grid=(rows // block,),
        in_specs=[rowwise, rowwise, rowwise, matrix(0), matrix(1), matrix(2), rowwise, rowwise, whole((1, width))],
        out_specs=[rowwise, whole((1, width))],
        out_shape=[jax.ShapeDtypeStruct((rows, width), WIDE), jax.ShapeDtypeStruct((1, width), WIDE)],
        cost_estimate=pl.CostEstimate(flops=int(8 * PEAK), bytes_accessed=12 << 20, transcendentals=0),
        compiler_params=pltpu.CompilerParams(vmem_limit_bytes=VMEM_BYTES),
        name="input_gradient",
    )(*grads, weights, weights, weights, x, grad, gain)


def memory_kernel(gk_ref, gv_ref, wk_ref, wv_ref, out_ref):
    out_ref[...] = nt(gk_ref[...], wk_ref[...]) + nt(gv_ref[...], wv_ref[...])


def memory_gradient(grad_key, grad_value, weights):
    rows, width = grad_key.shape
    block = 256
    rowwise = pl.BlockSpec((block, width), lambda g: (g, 0))
    matrix = lambda at: pl.BlockSpec((None, width, width), lambda g: (at, 0, 0))
    return pl.pallas_call(
        memory_kernel,
        grid=(rows // block,),
        in_specs=[rowwise, rowwise, matrix(1), matrix(2)],
        out_specs=rowwise,
        out_shape=jax.ShapeDtypeStruct((rows, width), WIDE),
        cost_estimate=pl.CostEstimate(flops=int(7 * PEAK), bytes_accessed=10 << 20, transcendentals=0),
        compiler_params=pltpu.CompilerParams(vmem_limit_bytes=VMEM_BYTES),
        name="memory_gradient",
    )(grad_key, grad_value, weights, weights)


def flat_permute(value, target):
    reps, shards = lax.axis_size("rep"), lax.axis_size("fsdp")
    pairs = []
    for rep in range(reps):
        for shard in range(shards):
            to_rep, to_shard = target(rep, shard)
            pairs.append((rep * shards + shard, to_rep * shards + to_shard))
    return lax.ppermute(value, ("rep", "fsdp"), pairs)


def from_rep(value, way):
    return flat_permute(value, lambda rep, shard: (rep ^ way, shard))


def from_shard(value, way):
    return flat_permute(value, lambda rep, shard: (rep, shard ^ way))


def from_line(value, hops):
    shards = lax.axis_size("fsdp")
    return flat_permute(value, lambda rep, shard: (rep, (shard + 2 * hops) % shards))


def along_line(piece):
    hops = lax.axis_size("fsdp") // 2
    return jnp.stack([piece] + [from_line(piece, hop) for hop in range(1, hops)])


def across_reps(line):
    return [line] + [from_rep(line, way) for way in range(1, 4)]


def with_partner(parts):
    return parts + [from_shard(part, 1) for part in parts]


def add_line(parts):
    return [parts[0]] + [from_line(parts[hop], hop) for hop in range(1, LINE)]


def assemble_kernel(place, hops, where_ref, *refs):
    parts, out_ref, sems = refs[:8], refs[8], refs[9]
    rep, line, core = where_ref[0], where_ref[1], where_ref[2]
    copies = []
    for other in range(2):
        for way in range(4):
            for hop in range(hops):
                shard = lax.rem(line - hop + hops, hops) * 2 + (core ^ other)
                copies.append(
                    pltpu.make_async_copy(
                        parts[4 * other + way].at[hop],
                        place(out_ref, rep ^ way, shard),
                        sems.at[len(copies)],
                    )
                )
    for copy in copies:
        copy.start()
    for copy in copies:
        copy.wait()


def assemble(parts, where, shape, place, name):
    hops = parts[0].shape[0]
    return pl.pallas_call(
        functools.partial(assemble_kernel, place, hops),
        in_specs=[pl.BlockSpec(memory_space=pltpu.SMEM)] + [pl.BlockSpec(memory_space=pl.ANY)] * 8,
        out_specs=pl.BlockSpec(memory_space=pltpu.VMEM),
        out_shape=jax.ShapeDtypeStruct(shape, LOW),
        scratch_shapes=[pltpu.SemaphoreType.DMA((8 * hops,))],
        cost_estimate=pl.CostEstimate(flops=int(4 * PEAK), bytes_accessed=8 << 20, transcendentals=0),
        compiler_params=pltpu.CompilerParams(vmem_limit_bytes=VMEM_BYTES),
        name=name,
    )(where, *parts)


def rep_parts(parts):
    rep = lax.axis_index("rep")
    pick = lambda at: lax.dynamic_index_in_dim(parts, at, 0, keepdims=False)
    return [pick(rep)] + [from_rep(pick(rep ^ way), way) for way in range(1, 4)]


def add_up(parts):
    return sum(part.astype(WIDE) for part in parts).astype(LOW)


def rep_near(piece):
    return [piece] + [from_rep(piece, way) for way in range(1, 4)]


def rep_order(near):
    rep = lax.axis_index("rep")
    near = jnp.stack(near)
    return jnp.stack([lax.dynamic_index_in_dim(near, at ^ rep, 0, keepdims=False) for at in range(4)])


def hold(*values):
    return lax.optimization_barrier(values)


def butterfly(vector, move, size):
    way = 1
    while way < size:
        vector = vector + move(vector, way)
        way *= 2
    return vector


def after(value, *earlier):
    return lax.optimization_barrier((value, *earlier))[0]


def factored_sums(gradient, weight, row_state):
    squares = gradient * gradient + TINY_TERM
    row_moment = DECAY_RATE * row_state + (1.0 - DECAY_RATE) * jnp.mean(squares, axis=2)
    local = jnp.concatenate(
        [
            jnp.sum(squares, axis=1).reshape(-1),
            jnp.sum(row_moment, axis=1),
            jnp.sum(weight * weight, axis=(1, 2)),
        ]
    )
    return row_moment, local


def factored_update(gradient, weight, row_moment, col_state, total):
    count, rows, cols = weight.shape
    whole_rows = rows * lax.axis_size("fsdp")
    col_sum = total[: count * cols].reshape(count, cols)
    row_mean = total[count * cols : count * cols + count] / whole_rows
    square = total[count * cols + count :] / (whole_rows * cols)
    col_moment = DECAY_RATE * col_state + (1.0 - DECAY_RATE) * col_sum / whole_rows
    direction = gradient * lax.rsqrt(
        row_moment[:, :, None] * col_moment[:, None, :] / row_mean[:, None, None]
    )
    step = STEP_RATE * jnp.sqrt(square + 1e-06)
    return weight - step[:, None, None] * direction, col_moment


def plain_update(gradient, weight, moment, square):
    moment = DECAY_RATE * moment + (1.0 - DECAY_RATE) * (gradient * gradient + TINY_TERM)
    step = STEP_RATE * jnp.sqrt(square + 1e-06)
    return weight - step * gradient * lax.rsqrt(moment), moment


def per_device(
    dec_in,
    memory,
    out_grad,
    dec_len,
    enc_len,
    buckets,
    self_weight,
    cross_weight,
    ffn_in,
    ffn_out,
    gains,
    table,
    self_rows,
    self_cols,
    cross_rows,
    cross_cols,
    in_rows,
    in_cols,
    out_rows,
    out_cols,
    gain_moment,
    table_moment,
):
    seq_count, seq_length, model_width = dec_in.shape
    mem_length = memory.shape[1]
    row_count = seq_count * seq_length
    hidden_width = ffn_in.shape[2]
    reps, shards = lax.axis_size("rep"), lax.axis_size("fsdp")
    rep, shard = lax.axis_index("rep"), lax.axis_index("fsdp")
    quarters = reps == 4 and shards == 8
    part_rows = hidden_width // shards
    where = jnp.stack([rep, shard // 2, shard % 2]).astype(jnp.int32) * int(quarters)
    w_self = lax.all_gather(self_weight.astype(LOW), "fsdp", axis=1, tiled=True)
    gain_full = lax.all_gather(gains.astype(LOW), "fsdp", axis=1, tiled=True).astype(WIDE)
    w_in = lax.all_gather(ffn_in.astype(LOW), "fsdp", axis=1, tiled=True)

    bucket_mask = (buckets[None, :] == jnp.arange(BUCKETS)[:, None]).astype(WIDE)
    by_distance = jnp.sum(table.T[:, :, None] * bucket_mask[None], axis=1)
    by_distance = jnp.pad(by_distance, ((0, 16 - H), (0, 0)))
    backwards = jnp.roll(by_distance[:, ::-1], 1, axis=1)
    no_bias = jnp.zeros((8, PAIR), WIDE)
    no_source = jnp.zeros((16, PAIR), LOW)

    dec_rows = dec_in.reshape(row_count, model_width)
    mem_rows = memory.reshape(seq_count * mem_length, model_width)
    grad_rows = out_grad.reshape(row_count, model_width)
    *kept_one, after_self = attention_forward(
        True, dec_rows, no_source, dec_len, gain_full[0:1], w_self, backwards
    )
    if quarters:
        cross_quarter = lax.dynamic_index_in_dim(cross_weight, rep, 0, keepdims=False).astype(LOW)
        out_quarter = lax.dynamic_index_in_dim(
            ffn_out.reshape(4, part_rows // 4, model_width), rep, 0, keepdims=False
        ).astype(LOW)
        cross_rows_each, out_rows_each = cross_weight.shape[1], part_rows // 4
        cross_pieces = with_partner(across_reps(along_line(cross_quarter)))
        w_cross = assemble(
            hold(*cross_pieces, after_self)[:-1],
            where,
            (4, model_width, model_width),
            lambda ref, quarter, at: ref.at[quarter, pl.ds(at * cross_rows_each, cross_rows_each)],
            "assemble_cross",
        )
        out_line = along_line(after(out_quarter, w_self))
        out_near = across_reps(after(out_line, after_self))
    else:
        w_cross = lax.all_gather(cross_weight.astype(LOW), "fsdp", axis=1, tiled=True)
        w_out = lax.all_gather(ffn_out.astype(LOW), "fsdp", axis=0, tiled=True)
    *kept_two, after_cross = attention_forward(
        False, after_self, mem_rows, enc_len, gain_full[1:2], w_cross, no_bias
    )
    if quarters:
        out_near = list(hold(*out_near, after_cross)[:-1])
        w_out = assemble(
            with_partner(out_near),
            where,
            (hidden_width, model_width),
            lambda ref, quarter, at: ref.at[pl.ds((at * 4 + quarter) * out_rows_each, out_rows_each)],
            "assemble_out",
        )
    layer_out, grad_cross, grad_gate, grad_up, *out_near, gain_three = feed_forward_both(
        after_cross, grad_rows, dec_len, where, gain_full[2:3], w_in, w_out
    )
    scatter = lambda value, at: lax.psum_scatter(value, "fsdp", scatter_dimension=at, tiled=True)
    if quarters:
        own_gate = scatter(grad_gate, 0)
        out_near = out_near[:1] + [from_rep(out_near[way], way) for way in range(1, 4)]
    grad_self, grad_k_two, grad_v_two, gain_two, *cross_near, cross_far = attention_backward(
        False, after_self, mem_rows, grad_cross, enc_len, where, gain_full[1:2], w_cross, no_bias, kept_two,
        kept_two[3], kept_one[3],
    )
    if quarters:
        cross_far, grad_k_two, *out_near = hold(cross_far, grad_k_two, *out_near)
        pair = from_shard(cross_far, 1)
        memory_grad = memory_gradient(grad_k_two, grad_v_two, w_cross)
        memory_grad, pair, own_gate = hold(memory_grad, pair, own_gate)
        own_up = scatter(grad_up, 0)
        cross_chip = [add_up([cross_near[way], pair[way]]) for way in range(4)]
        grad_self, *cross_chip = hold(grad_self, *cross_chip)
        cross_near = cross_chip[:1] + [from_rep(cross_chip[way], way) for way in range(1, 4)]
    else:
        memory_grad = memory_gradient(grad_k_two, grad_v_two, w_cross)
    *grads_one, grad_self_weights, dist_grad = attention_backward(
        True, dec_rows, no_source, grad_self, dec_len, where, gain_full[0:1], w_self, by_distance, kept_one,
        no_source, no_source,
    )
    if quarters:
        own_self = scatter(grad_self_weights, 1)
        dist_grad, own_up, *rest = hold(dist_grad, own_up, *grads_one, *cross_near)
        grads_one, cross_near = rest[:3], rest[3:]
        in_parts = rep_parts(jnp.stack([own_gate, own_up]).reshape(4, -1, hidden_width))
        out_sum = add_up(out_near)
        out_pair = from_shard(out_sum[1], 1)
        input_grad, gain_one = input_gradient(grads_one, w_self, dec_rows, grad_self, gain_full[0:1])
        input_grad, out_pair = hold(input_grad, out_pair)
        line = jnp.concatenate([add_up(cross_near), add_up([out_sum[0], out_pair])], axis=1)
        line_parts = add_line(line)
    else:
        input_grad, gain_one = input_gradient(grads_one, w_self, dec_rows, grad_self, gain_full[0:1])
    layer_out = layer_out.reshape(dec_in.shape)
    input_grad = input_grad.reshape(dec_in.shape)
    memory_grad = memory_grad.reshape(memory.shape)
    table_part = jnp.sum(bucket_mask[:, None, :] * dist_grad[None, :H, :], axis=2)
    small = jnp.concatenate(
        [gain_one.reshape(-1), gain_two.reshape(-1), gain_three.reshape(-1), table_part.reshape(-1)]
    )
    each = model_width // (LINE * LINE_CORES)
    if quarters:
        small = butterfly(butterfly(small, from_shard, shards), from_rep, reps)
        in_near = rep_near(add_up(in_parts))
        both_near = rep_near(add_up(line_parts))
        self_parts = rep_parts(own_self.reshape(4, -1, model_width))
        rest = hold(small, *in_near, *both_near, *self_parts)
        small, in_near, both_near, self_parts = rest[0], rest[1:5], rest[5:9], rest[9:]
        own_in = rep_order(in_near).reshape(ffn_in.shape)
        both = rep_order(both_near)
        own_cross = both[:, :each]
        own_out = both[:, each + each // 3 :].reshape(ffn_out.shape)
        own_self = jnp.concatenate(
            [
                rep_order(rep_near(add_up(self_parts))).reshape(3, *self_weight.shape[1:]),
                both[:3, each : each + each // 3].reshape(1, *self_weight.shape[1:]),
            ]
        )
        over_shards = lambda vector: butterfly(vector, from_shard, shards)
    else:
        over_reps = lambda value: lax.psum(value, "rep")
        own_in = over_reps(scatter(jnp.stack([grad_gate, grad_up]), 1))
        grad_out = jnp.stack(out_near)
        grad_out = grad_out.transpose(2, 1, 0, 3, 4).reshape(hidden_width, model_width)
        own_out = over_reps(scatter(grad_out, 0))
        packed = jnp.stack([jnp.stack(cross_near), cross_far]).transpose(1, 2, 0, 3, 4)
        cross_parts = packed[..., :each, :].reshape(4, model_width, model_width)
        past = packed[:3, ..., each:, :].transpose(1, 2, 0, 3, 4).reshape(1, model_width, model_width)
        own_cross = over_reps(scatter(cross_parts, 1))
        own_self = over_reps(scatter(jnp.concatenate([grad_self_weights, past]), 1))
        over_shards = lambda vector: lax.psum(vector, "fsdp")
        small = lax.psum(small, ("rep", "fsdp"))

    grad_factor = 1.0 / math.sqrt(row_count * reps * shards)
    self_grad, cross_grad, ffn_in_grad, feedforward_output_gradient = [
        member.astype(WIDE) * grad_factor for member in (own_self, own_cross, own_in, own_out)
    ]
    small = small * grad_factor
    gains_grad = lax.dynamic_slice_in_dim(
        small[: 3 * model_width].reshape(3, model_width), shard * gains.shape[1], gains.shape[1], axis=1
    )
    table_grad = small[3 * model_width :].reshape(BUCKETS, H)
    groups = (
        (ffn_in_grad, ffn_in, in_rows, in_cols),
        (feedforward_output_gradient[None], ffn_out[None], out_rows[None], out_cols[None]),
        (cross_grad, cross_weight, cross_rows, cross_cols),
        (self_grad, self_weight, self_rows, self_cols),
    )
    sums = [factored_sums(gradient, weight, row_state) for gradient, weight, row_state, _ in groups]
    vectors = [member[1] for member in sums] + [jnp.sum(gains * gains, axis=1)]
    total = over_shards(jnp.concatenate(vectors))
    totals = []
    for vector in vectors:
        totals.append(total[: vector.shape[0]])
        total = total[vector.shape[0] :]
    updated = [
        factored_update(gradient, weight, sums[at][0], col_state, totals[at])
        for at, (gradient, weight, _, col_state) in enumerate(groups)
    ]
    new_ffn_in, new_ffn_out, new_cross, new_self = [member[0] for member in updated]
    new_in_cols, new_out_cols, new_cross_cols, new_self_cols = [member[1] for member in updated]
    new_in_rows, new_out_rows, new_cross_rows, new_self_rows = [member[0] for member in sums]
    new_ffn_out, new_out_rows, new_out_cols = new_ffn_out[0], new_out_rows[0], new_out_cols[0]
    gain_square = totals[4] / model_width
    new_gains, new_gain_moment = plain_update(gains_grad, gains, gain_moment, gain_square[:, None])
    new_table, new_table_moment = plain_update(
        table_grad, table, table_moment, jnp.mean(table * table)
    )
    return (
        layer_out,
        input_grad,
        memory_grad,
        self_grad,
        cross_grad,
        ffn_in_grad,
        feedforward_output_gradient,
        gains_grad,
        table_grad,
        new_self,
        new_cross,
        new_ffn_in,
        new_ffn_out,
        new_gains,
        new_table,
        new_self_rows,
        new_self_cols,
        new_cross_rows,
        new_cross_cols,
        new_in_rows,
        new_in_cols,
        new_out_rows,
        new_out_cols,
        new_gain_moment,
        new_table_moment,
    )


def solution(mesh):
    placed = (
        P(("rep", "fsdp"), None, None),
        P(("rep", "fsdp"), None, None),
        P(("rep", "fsdp"), None, None),
        P(("rep", "fsdp")),
        P(("rep", "fsdp")),
        P(),
        P(None, "fsdp", None),
        P(None, "fsdp", None),
        P(None, "fsdp", None),
        P("fsdp", None),
        P(None, "fsdp"),
        P(),
        P(None, "fsdp"),
        P(),
        P(None, "fsdp"),
        P(),
        P(None, "fsdp"),
        P(),
        P("fsdp"),
        P(),
        P(None, "fsdp"),
        P(),
    )
    return jax.shard_map(
        per_device,
        mesh=mesh,
        in_specs=placed,
        out_specs=(
            P(("rep", "fsdp"), None, None),
            P(("rep", "fsdp"), None, None),
            P(("rep", "fsdp"), None, None),
            P(None, "fsdp", None),
            P(None, "fsdp", None),
            P(None, "fsdp", None),
            P("fsdp", None),
            P(None, "fsdp"),
            P(),
            P(None, "fsdp", None),
            P(None, "fsdp", None),
            P(None, "fsdp", None),
            P("fsdp", None),
            P(None, "fsdp"),
            P(),
            P(None, "fsdp"),
            P(),
            P(None, "fsdp"),
            P(),
            P(None, "fsdp"),
            P(),
            P("fsdp"),
            P(),
            P(None, "fsdp"),
            P(),
        ),
        check_vma=False,
    )
```

```python
import functools
import math

import jax
import jax.numpy as jnp
from jax import lax
from jax.experimental import pallas as pl
from jax.experimental.pallas import tpu as pltpu
from jax.sharding import PartitionSpec as P

H = 12
DH = 64
BUCKETS = 32
DECAY_RATE = 0.8
STEP_RATE = 0.2
TINY_TERM = 1e-30
PAIR = 2 * DH
GROUP = 4 * DH
HIDDEN = -1e30
VMEM_BYTES = 60 * 1024 * 1024
PEAK = 1.15e9
LINE = 4
LINE_CORES = 2
LOW = jnp.bfloat16
WIDE = jnp.float32


def nn(left, right):
    return lax.dot_general(left, right, (((1,), (0,)), ((), ())), preferred_element_type=WIDE)


def nt(left, right):
    return lax.dot_general(left, right, (((1,), (1,)), ((), ())), preferred_element_type=WIDE)


def tn(left, right):
    return lax.dot_general(left, right, (((0,), (0,)), ((), ())), preferred_element_type=WIDE)


def rms_rate(rows):
    return lax.rsqrt(jnp.mean(rows * rows, axis=-1, keepdims=True) + 1e-06)


def three_parts(column):
    high = column.astype(LOW)
    rest = column - high.astype(WIDE)
    middle = rest.astype(LOW)
    low = (rest - middle.astype(WIDE)).astype(LOW)
    return high, middle, low


def chunks(total, size):
    return [(at, min(size, total - at)) for at in range(0, total, size)]


def lanes(rows):
    return lax.broadcasted_iota(jnp.int32, (rows, PAIR), 1)


def own_lanes(rows, side):
    lane = lanes(rows)
    return (lane >= DH * side) & (lane < DH * (side + 1))


def key_extras(rows, side, length):
    lane = lanes(rows) - DH * (1 - side)
    dead = lax.broadcasted_iota(jnp.int32, (rows, PAIR), 0) >= length
    mask = jnp.where(dead, HIDDEN, 0.0)
    return jnp.where(
        (lane >= 0) & (lane < 3), 1.0, jnp.where(lane == 3, mask, 0.0)
    ).astype(LOW)


def row_extras(rows, side, column, last):
    lane = lanes(rows) - DH * (1 - side)
    high, middle, low = three_parts(column)
    wide = lambda part: jnp.broadcast_to(part.astype(WIDE), (rows, PAIR))
    return jnp.where(
        lane == 0,
        wide(high),
        jnp.where(
            lane == 1, wide(middle), jnp.where(lane == 2, wide(low), jnp.where(lane == 3, last, 0.0))
        ),
    ).astype(LOW)


def forward_body(causal, seq_count, length_ref, wave_ref, bias_ref, q_ref, k_ref, v_ref, mix_ref, total_ref, group):
    rows = q_ref.shape[0] // seq_count
    keys = k_ref.shape[0] // seq_count
    block = 256
    for pair in range(2):
        at = pair * PAIR
        for side in range(2):
            head = 2 * pair + side
            if causal:
                wave = wave_ref[pl.ds(group * 4 + head, 1), :]
                spread = pltpu.roll(
                    jnp.broadcast_to(wave, (rows, keys)), 0, 1, stride=1, stride_axis=0
                )
                row = lax.broadcasted_iota(jnp.int32, (rows, keys), 0)
                column = lax.broadcasted_iota(jnp.int32, (rows, keys), 1)
                bias_ref[side] = jnp.where(column <= row, spread, HIDDEN)
        for seq in range(seq_count):
            outs = []
            for side in range(2):
                own_q = own_lanes(rows, side)
                own_k = own_lanes(keys, side)
                query = jnp.where(
                    own_q,
                    q_ref[seq * rows : (seq + 1) * rows, at : at + PAIR],
                    (lanes(rows) == DH * (1 - side) + 3).astype(LOW),
                )
                key = jnp.where(
                    own_k,
                    k_ref[seq * keys : (seq + 1) * keys, at : at + PAIR],
                    key_extras(keys, side, length_ref[seq]),
                )
                value = jnp.where(
                    own_k,
                    v_ref[seq * keys : (seq + 1) * keys, at : at + PAIR],
                    jnp.ones((), LOW),
                )
                parts = []
                for start in range(0, rows, block):
                    span = start + block if causal else keys
                    scores = nt(query[start : start + block], key[:span])
                    if causal:
                        scores = scores + bias_ref[side, start : start + block, :span]
                    top = jnp.max(scores, axis=1, keepdims=True)
                    weight = jnp.exp(scores - top)
                    out = nn(weight.astype(LOW), value[:span])
                    total = out[:, DH * (1 - side) : DH * (1 - side) + 1]
                    parts.append(out * (1.0 / total))
                    spot = pl.ds(seq * rows + start, block)
                    lane = lanes(block)
                    seen = total_ref[spot, :] if (pair or side) else jnp.zeros((block, PAIR), WIDE)
                    total_ref[spot, :] = jnp.where(
                        lane == 2 * pair + side, top + jnp.log(total), seen
                    )
                outs.append(jnp.concatenate(parts, axis=0))
            mix_ref[seq * rows : (seq + 1) * rows, at : at + PAIR] = jnp.where(
                own_lanes(rows, 0), outs[0], outs[1]
            ).astype(LOW)


def forward_kernel(
    causal, seq_count, length_ref, x_ref, source_ref, gain_ref, wq_ref, wk_ref, wv_ref, wo_ref, wave_ref,
    q_ref, k_ref, v_ref, mix_ref, total_ref, after_ref, normed, bias,
):
    group = pl.program_id(0)

    @pl.when(group == 0)
    def _():
        for at, size in chunks(x_ref.shape[0], 256):
            rows = x_ref[at : at + size, :].astype(WIDE)
            normed[at : at + size, :] = (rows * rms_rate(rows) * gain_ref[...]).astype(LOW)
            after_ref[at : at + size, :] = rows

    source = normed if causal else source_ref
    q_ref[...] = nn(normed[...], wq_ref[...]).astype(LOW)
    k_ref[...] = nn(source[...], wk_ref[...]).astype(LOW)
    v_ref[...] = nn(source[...], wv_ref[...]).astype(LOW)
    forward_body(causal, seq_count, length_ref, wave_ref, bias, q_ref, k_ref, v_ref, mix_ref, total_ref, group)
    after_ref[...] += nn(mix_ref[...], wo_ref[...])


def weight_specs(width):
    across = lambda at: pl.BlockSpec((None, width, GROUP), lambda g, at=at: (at, 0, g))
    return [across(0), across(1), across(2), pl.BlockSpec((None, GROUP, width), lambda g: (3, g, 0))]


def whole(shape):
    return pl.BlockSpec(shape, lambda g: (0,) * len(shape))


def columns(rows):
    return pl.BlockSpec((rows, GROUP), lambda g: (0, g))


def attention_forward(causal, x, source, lengths, gain, weights, wave):
    row_count, width = x.shape
    seq_count = lengths.shape[0]
    source_rows = row_count if causal else source.shape[0]
    length = row_count // seq_count
    groups = width // GROUP
    low = lambda rows: jax.ShapeDtypeStruct((rows, width), LOW)
    args = [lengths, x, source, gain, weights, weights, weights, weights, wave]
    return pl.pallas_call(
        functools.partial(forward_kernel, causal, seq_count),
        grid=(groups,),
        in_specs=[
            pl.BlockSpec(memory_space=pltpu.SMEM),
            whole(x.shape),
            whole(source.shape),
            whole(gain.shape),
            *weight_specs(width),
            whole(wave.shape),
        ],
        out_specs=[
            columns(row_count),
            columns(source_rows),
            columns(source_rows),
            columns(row_count),
            pl.BlockSpec((None, row_count, PAIR), lambda g: (g, 0, 0)),
            whole((row_count, width)),
        ],
        out_shape=[
            low(row_count),
            low(source_rows),
            low(source_rows),
            low(row_count),
            jax.ShapeDtypeStruct((groups, row_count, PAIR), WIDE),
            jax.ShapeDtypeStruct((row_count, width), WIDE),
        ],
        scratch_shapes=[
            pltpu.VMEM((row_count, width), LOW),
            pltpu.VMEM((2, length, length) if causal else (1, 8, PAIR), WIDE),
        ],
        cost_estimate=pl.CostEstimate(flops=int(27 * PEAK), bytes_accessed=20 << 20, transcendentals=0),
        compiler_params=pltpu.CompilerParams(vmem_limit_bytes=VMEM_BYTES),
        name="self_forward" if causal else "cross_forward",
    )(*args)


def gelu_parts(gate):
    root = 0.7978845608028654
    square = gate * gate
    inner = jnp.tanh(root * gate * (1.0 + 0.044715 * square))
    half = 0.5 * (1.0 + inner)
    value = gate * half
    slope = half + 0.5 * gate * (1.0 - inner * inner) * (root * (1.0 + 3 * 0.044715 * square))
    return value, slope


def rms_back(rows, gain, grad):
    rate = rms_rate(rows)
    scaled = rows * rate
    low = grad * gain
    grad_rows = rate * (low - scaled * jnp.mean(scaled * low, axis=-1, keepdims=True))
    return grad_rows, jnp.sum(grad * scaled, axis=0, keepdims=True)


def shard_slot(where_ref, shard):
    return (shard % LINE_CORES) ^ where_ref[2], lax.rem(shard // LINE_CORES - where_ref[1] + LINE, LINE)


def feed_kernel(
    seq_count, length_ref, where_ref, after_ref, out_grad_ref, gain_ref, wg_ref, wu_ref, wd_ref,
    layer_ref, grad_cross_ref, dwg_ref, dwu_ref, *refs,
):
    near_refs = refs[:4]
    dgain_ref, normed, normed_t, down, out_total, grad_total, cut = refs[4:]
    step = pl.program_id(0)
    row_count = after_ref.shape[0]
    length = row_count // seq_count

    def live(at, size):
        position = lax.broadcasted_iota(jnp.int32, (size, 1), 0) + (at % length)
        return (position < length_ref[at // length]).astype(WIDE)

    @pl.when(step == 0)
    def _():
        for at, size in chunks(row_count, 256):
            rows = after_ref[at : at + size, :]
            low = (rows * rms_rate(rows) * gain_ref[...]).astype(LOW)
            normed[at : at + size, :] = low
            normed_t[:, at : at + size] = low.T
            down[at : at + size, :] = (
                out_grad_ref[at : at + size, :].astype(WIDE) * live(at, size)
            ).astype(LOW)
            out_total[at : at + size, :] = rows
            grad_total[at : at + size, :] = jnp.zeros((size, rows.shape[1]), WIDE)

    gate = nn(normed[...], wg_ref[...])
    up = nn(normed[...], wu_ref[...])
    value, slope = gelu_parts(gate)
    hidden = (value * up).astype(LOW)
    out_total[...] += nn(hidden, wd_ref[...])
    grad_hidden = nt(down[...], wd_ref[...])
    cut[...] = tn(hidden, down[...]).astype(LOW).reshape(cut.shape)
    core, hop = shard_slot(where_ref, step)
    for way in range(4):
        near_refs[way][core, hop] = cut[where_ref[0] ^ way]
    grad_gate = (grad_hidden * up * slope).astype(LOW)
    grad_up = (grad_hidden * value).astype(LOW)
    dwg_ref[...] = nn(normed_t[...], grad_gate).astype(LOW)
    dwu_ref[...] = nn(normed_t[...], grad_up).astype(LOW)
    grad_total[...] += nt(grad_gate, wg_ref[...]) + nt(grad_up, wu_ref[...])

    @pl.when(step == pl.num_programs(0) - 1)
    def _():
        dgain = jnp.zeros(dgain_ref.shape, WIDE)
        for at, size in chunks(row_count, 256):
            part = slice(at, at + size)
            layer_ref[part, :] = (out_total[part, :] * live(at, size)).astype(LOW)
            grad_rows, gain_part = rms_back(after_ref[part, :], gain_ref[...], grad_total[part, :])
            dgain = dgain + gain_part
            grad_cross_ref[part, :] = (
                out_grad_ref[part, :].astype(WIDE) * live(at, size) + grad_rows
            )
        dgain_ref[...] = dgain


def feed_forward_both(after, out_grad, lengths, where, gain, w_in, w_out):
    row_count, width = after.shape
    hidden = w_out.shape[0]
    block = hidden // (LINE * LINE_CORES)
    seq_count = lengths.shape[0]
    wide = pl.BlockSpec((None, width, block), lambda g: (0, 0, g))
    wide_up = pl.BlockSpec((None, width, block), lambda g: (1, 0, g))
    tall = pl.BlockSpec((block, width), lambda g: (g, 0))
    flat = pl.BlockSpec((width, block), lambda g: (0, g))
    near = (LINE_CORES, LINE, block // 4, width)
    return pl.pallas_call(
        functools.partial(feed_kernel, seq_count),
        grid=(hidden // block,),
        in_specs=[
            pl.BlockSpec(memory_space=pltpu.SMEM),
            pl.BlockSpec(memory_space=pltpu.SMEM),
            whole(after.shape),
            whole(out_grad.shape),
            whole(gain.shape),
            wide,
            wide_up,
            tall,
        ],
        out_specs=[whole(after.shape), whole(after.shape), flat, flat, *[whole(near)] * 4, whole((1, width))],
        out_shape=[
            jax.ShapeDtypeStruct((row_count, width), LOW),
            jax.ShapeDtypeStruct((row_count, width), WIDE),
            jax.ShapeDtypeStruct((width, hidden), LOW),
            jax.ShapeDtypeStruct((width, hidden), LOW),
            *[jax.ShapeDtypeStruct(near, LOW)] * 4,
            jax.ShapeDtypeStruct((1, width), WIDE),
        ],
        scratch_shapes=[
            pltpu.VMEM((row_count, width), LOW),
            pltpu.VMEM((width, row_count), LOW),
            pltpu.VMEM((row_count, width), LOW),
            pltpu.VMEM((row_count, width), WIDE),
            pltpu.VMEM((row_count, width), WIDE),
            pltpu.VMEM((4, block // 4, width), LOW),
        ],
        cost_estimate=pl.CostEstimate(flops=int(46 * PEAK), bytes_accessed=40 << 20, transcendentals=0),
        compiler_params=pltpu.CompilerParams(vmem_limit_bytes=VMEM_BYTES),
        name="feed_forward_both",
    )(lengths, where, after, out_grad, gain, w_in, w_in, w_out)


def backward_kernel(
    causal, seq_count, length_ref, where_ref, x_ref, source_ref, grad_ref, gain_ref, wq_ref, wo_ref, wave_ref,
    q_ref, k_ref, v_ref, mix_ref, total_ref, mix_all_ref, mix_past_ref, *refs,
):
    if causal:
        gq, gk_out_ref, gv_out_ref, dw_ref, dist_ref = refs[:5]
        normed_t, branch, grad_mix, bias, score_sum = refs[5:]
        source_t = normed_t
    else:
        grad_x_ref, gk_out_ref, gv_out_ref, dgain_ref = refs[:4]
        near_refs, far_ref = refs[4:8], refs[8]
        normed_t, branch, grad_mix, gq, source_t, mix_t, grad_total, dw_ref, past = refs[9:]
    group = pl.program_id(0)
    row_count = x_ref.shape[0]
    rows = q_ref.shape[0] // seq_count
    keys = k_ref.shape[0] // seq_count
    block = 256

    @pl.when(group == 0)
    def _():
        for at, size in chunks(row_count, 256):
            value = x_ref[at : at + size, :].astype(WIDE)
            low = (value * rms_rate(value) * gain_ref[...]).astype(LOW)
            normed_t[:, at : at + size] = low.T
            branch[at : at + size, :] = grad_ref[at : at + size, :].astype(LOW)
            if not causal:
                mix_t[:, at : at + size] = mix_all_ref[at : at + size, :].T
                grad_total[at : at + size, :] = jnp.zeros((size, value.shape[1]), WIDE)
        if not causal:
            for at, size in chunks(source_ref.shape[0], 256):
                source_t[:, at : at + size] = source_ref[at : at + size, :].T

    grad_mix[...] = nt(branch[...], wo_ref[...]).astype(LOW)
    if not causal:
        across = pl.ds(pl.multiple_of(group * GROUP, GROUP), GROUP)
        put = lambda at, value: dw_ref.__setitem__(at, value.astype(LOW).reshape(dw_ref.shape[1:]))
        put(3, nn(mix_t[...], branch[:, across]))

    for pair in range(2):
        at = pair * PAIR
        if causal:
            for side in range(2):
                head = 2 * pair + side
                wave = wave_ref[pl.ds(group * 4 + head, 1), :]
                spread = pltpu.roll(
                    jnp.broadcast_to(wave, (keys, rows)), 0, 1, stride=1, stride_axis=0
                )
                row = lax.broadcasted_iota(jnp.int32, (keys, rows), 0)
                column = lax.broadcasted_iota(jnp.int32, (keys, rows), 1)
                bias[side] = jnp.where(column >= row, spread, HIDDEN)
        for seq in range(seq_count):
            span_q = slice(seq * rows, (seq + 1) * rows)
            span_k = slice(seq * keys, (seq + 1) * keys)
            sides = []
            for side in range(2):
                head = 2 * pair + side
                own_q = own_lanes(rows, side)
                own_k = own_lanes(keys, side)
                total = jnp.sum(
                    jnp.where(lanes(rows) == head, total_ref[span_q, :], 0.0), axis=1, keepdims=True
                )
                grad_low = grad_mix[span_q, at : at + PAIR]
                product = grad_low.astype(WIDE) * mix_ref[span_q, at : at + PAIR].astype(WIDE)
                delta = jnp.sum(jnp.where(own_q, product, 0.0), axis=1, keepdims=True)
                query = jnp.where(
                    own_q, q_ref[span_q, at : at + PAIR], row_extras(rows, side, -total, 1.0)
                )
                grad_out = jnp.where(own_q, grad_low, row_extras(rows, side, -delta, 0.0))
                key = jnp.where(
                    own_k,
                    k_ref[span_k, at : at + PAIR],
                    key_extras(keys, side, length_ref[seq]),
                )
                value = jnp.where(own_k, v_ref[span_k, at : at + PAIR], jnp.ones((), LOW))
                grad_query = []
                grad_key = None
                grad_value = None
                for start in range(0, rows, block):
                    span = start + block if causal else keys
                    scores = nt(key[:span], query[start : start + block])
                    if causal:
                        scores = scores + bias[side, :span, start : start + block]
                    weight = jnp.exp(scores)
                    low = weight.astype(LOW)
                    grad_weight = nt(value[:span], grad_out[start : start + block])
                    grad_score = (weight * grad_weight).astype(LOW)
                    if causal:
                        if seq == 0:
                            score_sum[side, :span, start : start + block] = grad_score.astype(WIDE)
                        else:
                            score_sum[side, :span, start : start + block] += grad_score.astype(WIDE)
                    key_part = nn(grad_score, query[start : start + block])
                    value_part = nn(low, grad_out[start : start + block])
                    grad_query.append(tn(grad_score, key[:span]))
                    if causal and start == 0 and rows > block:
                        rest = jnp.zeros((keys - span, PAIR), WIDE)
                        key_part = jnp.concatenate([key_part, rest], axis=0)
                        value_part = jnp.concatenate([value_part, rest], axis=0)
                    grad_key = key_part if grad_key is None else grad_key + key_part
                    grad_value = value_part if grad_value is None else grad_value + value_part
                sides.append((jnp.concatenate(grad_query, axis=0), grad_key, grad_value))
            pick_q = own_lanes(rows, 0)
            pick_k = own_lanes(keys, 0)
            gq[span_q, at : at + PAIR] = jnp.where(pick_q, sides[0][0], sides[1][0]).astype(LOW)
            gk_out_ref[span_k, at : at + PAIR] = jnp.where(pick_k, sides[0][1], sides[1][1]).astype(LOW)
            gv_out_ref[span_k, at : at + PAIR] = jnp.where(pick_k, sides[0][2], sides[1][2]).astype(LOW)
        if causal:
            for side in range(2):
                head = 2 * pair + side
                row = lax.broadcasted_iota(jnp.int32, (keys, rows), 0)
                column = lax.broadcasted_iota(jnp.int32, (keys, rows), 1)
                held = jnp.where(column >= row, score_sum[side], 0.0)
                while held.shape[0] > 1:
                    half = held.shape[0] // 2
                    held = held[:half] + pltpu.roll(held[half:], rows - half, 1)
                dist_ref[pl.ds(group * 4 + head, 1), :] = held

    if causal:
        dw_ref[0] = nn(normed_t[...], gq[...]).astype(LOW)
        dw_ref[1] = nn(source_t[...], gk_out_ref[...]).astype(LOW)
        dw_ref[2] = nn(source_t[...], gv_out_ref[...]).astype(LOW)
        return
    put(0, nn(normed_t[...], gq[...]))
    put(1, nn(source_t[...], gk_out_ref[...]))
    put(2, nn(source_t[...], gv_out_ref[...]))
    grad_total[...] += nt(gq[...], wq_ref[...])
    rep, line, core = where_ref[0], where_ref[1], where_ref[2]
    held = dw_ref.shape[2]
    slots = []
    for way in range(4):
        for hop in range(LINE):
            at = lax.rem(line + hop, LINE) * LINE_CORES
            slots.append((near_refs[way].at[hop], rep ^ way, at + core))
            slots.append((far_ref.at[way, hop], rep ^ way, at + (core ^ 1)))
    for slot, quarter, shard in slots:
        slot[0:held, across] = dw_ref[quarter, shard]

    @pl.when(group == pl.num_programs(0) - 1)
    def _():
        dgain = jnp.zeros(dgain_ref.shape, WIDE)
        for at, size in chunks(row_count, 256):
            part = slice(at, at + size)
            grad_rows, gain_part = rms_back(
                x_ref[part, :].astype(WIDE), gain_ref[...], grad_total[part, :]
            )
            dgain = dgain + gain_part
            grad_rows = grad_ref[part, :] + grad_rows
            grad_x_ref[part, :] = grad_rows
            branch[part, :] = grad_rows.astype(LOW)
            mix_t[:, part] = mix_past_ref[part, :].T
        dgain_ref[...] = dgain
        thirds = nn(mix_t[...], branch[...]).astype(LOW)
        past[:, 0:3] = thirds.reshape(past.shape[0], 3, *past.shape[2:])
        past[:, 3] = jnp.zeros_like(past[:, 3])
        for slot, quarter, shard in slots:
            slot[held:, :] = past[shard, quarter]


def attention_backward(causal, x, source, grad, lengths, where, gain, weights, wave, kept, mix, past):
    row_count, width = x.shape
    seq_count = lengths.shape[0]
    source_rows = row_count if causal else source.shape[0]
    length = row_count // seq_count
    groups = width // GROUP
    low = lambda rows: jax.ShapeDtypeStruct((rows, width), LOW)
    if causal:
        out_specs = [
            columns(row_count), columns(source_rows), columns(source_rows),
            pl.BlockSpec((3, width, GROUP), lambda g: (0, 0, g)), whole(wave.shape),
        ]
        out_shape = [
            low(row_count), low(source_rows), low(source_rows),
            jax.ShapeDtypeStruct((3, width, width), LOW), jax.ShapeDtypeStruct(wave.shape, WIDE),
        ]
        scratch = [pltpu.VMEM((2, length, length), WIDE)] * 2
    else:
        shards = LINE * LINE_CORES
        each, third = width // shards, width // shards // 3
        near = (LINE, each + third, width)
        out_specs = [
            whole((row_count, width)), columns(source_rows), columns(source_rows), whole((1, width)),
            *[whole(near)] * 4, whole((4, *near)),
        ]
        out_shape = [
            jax.ShapeDtypeStruct((row_count, width), WIDE), low(source_rows), low(source_rows),
            jax.ShapeDtypeStruct((1, width), WIDE), *[jax.ShapeDtypeStruct(near, LOW)] * 4,
            jax.ShapeDtypeStruct((4, *near), LOW),
        ]
        scratch = [
            pltpu.VMEM((row_count, GROUP), LOW),
            pltpu.VMEM((width, source_rows), LOW),
            pltpu.VMEM((width, row_count), LOW),
            pltpu.VMEM((row_count, width), WIDE),
            pltpu.VMEM((4, shards, each, GROUP), LOW),
            pltpu.VMEM((shards, 4, third, width), LOW),
        ]
    return pl.pallas_call(
        functools.partial(backward_kernel, causal, seq_count),
        grid=(groups,),
        in_specs=[
            pl.BlockSpec(memory_space=pltpu.SMEM),
            pl.BlockSpec(memory_space=pltpu.SMEM),
            whole(x.shape),
            whole(source.shape),
            whole(grad.shape),
            whole(gain.shape),
            weight_specs(width)[0],
            weight_specs(width)[3],
            whole(wave.shape),
            columns(row_count),
            columns(source_rows),
            columns(source_rows),
            columns(row_count),
            pl.BlockSpec((None, row_count, PAIR), lambda g: (g, 0, 0)),
            whole(mix.shape),
            whole(past.shape),
        ],
        out_specs=out_specs,
        out_shape=out_shape,
        scratch_shapes=[
            pltpu.VMEM((width, row_count), LOW),
            pltpu.VMEM((row_count, width), LOW),
            pltpu.VMEM((row_count, GROUP), LOW),
            *scratch,
        ],
        cost_estimate=pl.CostEstimate(flops=int(45 * PEAK), bytes_accessed=40 << 20, transcendentals=0),
        compiler_params=pltpu.CompilerParams(vmem_limit_bytes=VMEM_BYTES),
        name="self_backward" if causal else "cross_backward",
    )(lengths, where, x, source, grad, gain, weights, weights, wave, *kept, mix, past)


def input_kernel(gq_ref, gk_ref, gv_ref, wq_ref, wk_ref, wv_ref, x_ref, grad_ref, gain_ref, out_ref, dgain_ref):
    total = nt(gq_ref[...], wq_ref[...]) + nt(gk_ref[...], wk_ref[...]) + nt(gv_ref[...], wv_ref[...])
    grad_rows, dgain = rms_back(x_ref[...].astype(WIDE), gain_ref[...], total)
    out_ref[...] = grad_ref[...] + grad_rows

    @pl.when(pl.program_id(0) == 0)
    def _():
        dgain_ref[...] = jnp.zeros_like(dgain_ref)

    dgain_ref[...] += dgain


def input_gradient(grads, weights, x, grad, gain):
    rows, width = x.shape
    block = 256
    rowwise = pl.BlockSpec((block, width), lambda g: (g, 0))
    matrix = lambda at: pl.BlockSpec((None, width, width), lambda g: (at, 0, 0))
    return pl.pallas_call(
        input_kernel,
        grid=(rows // block,),
        in_specs=[rowwise, rowwise, rowwise, matrix(0), matrix(1), matrix(2), rowwise, rowwise, whole((1, width))],
        out_specs=[rowwise, whole((1, width))],
        out_shape=[jax.ShapeDtypeStruct((rows, width), WIDE), jax.ShapeDtypeStruct((1, width), WIDE)],
        cost_estimate=pl.CostEstimate(flops=int(8 * PEAK), bytes_accessed=12 << 20, transcendentals=0),
        compiler_params=pltpu.CompilerParams(vmem_limit_bytes=VMEM_BYTES),
        name="input_gradient",
    )(*grads, weights, weights, weights, x, grad, gain)


def memory_kernel(gk_ref, gv_ref, wk_ref, wv_ref, out_ref):
    out_ref[...] = nt(gk_ref[...], wk_ref[...]) + nt(gv_ref[...], wv_ref[...])


def memory_gradient(grad_key, grad_value, weights):
    rows, width = grad_key.shape
    block = 256
    rowwise = pl.BlockSpec((block, width), lambda g: (g, 0))
    matrix = lambda at: pl.BlockSpec((None, width, width), lambda g: (at, 0, 0))
    return pl.pallas_call(
        memory_kernel,
        grid=(rows // block,),
        in_specs=[rowwise, rowwise, matrix(1), matrix(2)],
        out_specs=rowwise,
        out_shape=jax.ShapeDtypeStruct((rows, width), WIDE),
        cost_estimate=pl.CostEstimate(flops=int(7 * PEAK), bytes_accessed=10 << 20, transcendentals=0),
        compiler_params=pltpu.CompilerParams(vmem_limit_bytes=VMEM_BYTES),
        name="memory_gradient",
    )(grad_key, grad_value, weights, weights)


def flat_permute(value, target):
    reps, shards = lax.axis_size("rep"), lax.axis_size("fsdp")
    pairs = []
    for rep in range(reps):
        for shard in range(shards):
            to_rep, to_shard = target(rep, shard)
            pairs.append((rep * shards + shard, to_rep * shards + to_shard))
    return lax.ppermute(value, ("rep", "fsdp"), pairs)


def from_rep(value, way):
    return flat_permute(value, lambda rep, shard: (rep ^ way, shard))


def from_shard(value, way):
    return flat_permute(value, lambda rep, shard: (rep, shard ^ way))


def from_line(value, hops):
    shards = lax.axis_size("fsdp")
    return flat_permute(value, lambda rep, shard: (rep, (shard + 2 * hops) % shards))


def along_line(piece):
    hops = lax.axis_size("fsdp") // 2
    return jnp.stack([piece] + [from_line(piece, hop) for hop in range(1, hops)])


def across_reps(line):
    return [line] + [from_rep(line, way) for way in range(1, 4)]


def with_partner(parts):
    return parts + [from_shard(part, 1) for part in parts]


def add_line(parts):
    return [parts[0]] + [from_line(parts[hop], hop) for hop in range(1, LINE)]


def assemble_kernel(place, hops, where_ref, *refs):
    parts, out_ref, sems = refs[:8], refs[8], refs[9]
    rep, line, core = where_ref[0], where_ref[1], where_ref[2]
    copies = []
    for other in range(2):
        for way in range(4):
            for hop in range(hops):
                shard = lax.rem(line - hop + hops, hops) * 2 + (core ^ other)
                copies.append(
                    pltpu.make_async_copy(
                        parts[4 * other + way].at[hop],
                        place(out_ref, rep ^ way, shard),
                        sems.at[len(copies)],
                    )
                )
    for copy in copies:
        copy.start()
    for copy in copies:
        copy.wait()


def assemble(parts, where, shape, place, name):
    hops = parts[0].shape[0]
    return pl.pallas_call(
        functools.partial(assemble_kernel, place, hops),
        in_specs=[pl.BlockSpec(memory_space=pltpu.SMEM)] + [pl.BlockSpec(memory_space=pl.ANY)] * 8,
        out_specs=pl.BlockSpec(memory_space=pltpu.VMEM),
        out_shape=jax.ShapeDtypeStruct(shape, LOW),
        scratch_shapes=[pltpu.SemaphoreType.DMA((8 * hops,))],
        cost_estimate=pl.CostEstimate(flops=int(4 * PEAK), bytes_accessed=8 << 20, transcendentals=0),
        compiler_params=pltpu.CompilerParams(vmem_limit_bytes=VMEM_BYTES),
        name=name,
    )(where, *parts)


def rep_parts(parts):
    rep = lax.axis_index("rep")
    pick = lambda at: lax.dynamic_index_in_dim(parts, at, 0, keepdims=False)
    return [pick(rep)] + [from_rep(pick(rep ^ way), way) for way in range(1, 4)]


def add_up(parts):
    return sum(part.astype(WIDE) for part in parts).astype(LOW)


def rep_near(piece):
    return [piece] + [from_rep(piece, way) for way in range(1, 4)]


def rep_order(near):
    rep = lax.axis_index("rep")
    near = jnp.stack(near)
    return jnp.stack([lax.dynamic_index_in_dim(near, at ^ rep, 0, keepdims=False) for at in range(4)])


def hold(*values):
    return lax.optimization_barrier(values)


def butterfly(vector, move, size):
    way = 1
    while way < size:
        vector = vector + move(vector, way)
        way *= 2
    return vector


def after(value, *earlier):
    return lax.optimization_barrier((value, *earlier))[0]


def factored_sums(gradient, weight, row_state):
    squares = gradient * gradient + TINY_TERM
    row_moment = DECAY_RATE * row_state + (1.0 - DECAY_RATE) * jnp.mean(squares, axis=2)
    local = jnp.concatenate(
        [
            jnp.sum(squares, axis=1).reshape(-1),
            jnp.sum(row_moment, axis=1),
            jnp.sum(weight * weight, axis=(1, 2)),
        ]
    )
    return row_moment, local


def factored_update(gradient, weight, row_moment, col_state, total):
    count, rows, cols = weight.shape
    whole_rows = rows * lax.axis_size("fsdp")
    col_sum = total[: count * cols].reshape(count, cols)
    row_mean = total[count * cols : count * cols + count] / whole_rows
    square = total[count * cols + count :] / (whole_rows * cols)
    col_moment = DECAY_RATE * col_state + (1.0 - DECAY_RATE) * col_sum / whole_rows
    direction = gradient * lax.rsqrt(
        row_moment[:, :, None] * col_moment[:, None, :] / row_mean[:, None, None]
    )
    step = STEP_RATE * jnp.sqrt(square + 1e-06)
    return weight - step[:, None, None] * direction, col_moment


def plain_update(gradient, weight, moment, square):
    moment = DECAY_RATE * moment + (1.0 - DECAY_RATE) * (gradient * gradient + TINY_TERM)
    step = STEP_RATE * jnp.sqrt(square + 1e-06)
    return weight - step * gradient * lax.rsqrt(moment), moment


def per_device(
    dec_in,
    memory,
    out_grad,
    dec_len,
    enc_len,
    buckets,
    self_weight,
    cross_weight,
    ffn_in,
    ffn_out,
    gains,
    table,
    self_rows,
    self_cols,
    cross_rows,
    cross_cols,
    in_rows,
    in_cols,
    out_rows,
    out_cols,
    gain_moment,
    table_moment,
):
    seq_count, seq_length, model_width = dec_in.shape
    mem_length = memory.shape[1]
    row_count = seq_count * seq_length
    hidden_width = ffn_in.shape[2]
    reps, shards = lax.axis_size("rep"), lax.axis_size("fsdp")
    rep, shard = lax.axis_index("rep"), lax.axis_index("fsdp")
    quarters = reps == 4 and shards == 8
    part_rows = hidden_width // shards
    where = jnp.stack([rep, shard // 2, shard % 2]).astype(jnp.int32) * int(quarters)
    w_self = lax.all_gather(self_weight.astype(LOW), "fsdp", axis=1, tiled=True)
    gain_full = lax.all_gather(gains.astype(LOW), "fsdp", axis=1, tiled=True).astype(WIDE)
    w_in = lax.all_gather(ffn_in.astype(LOW), "fsdp", axis=1, tiled=True)

    bucket_mask = (buckets[None, :] == jnp.arange(BUCKETS)[:, None]).astype(WIDE)
    by_distance = jnp.sum(table.T[:, :, None] * bucket_mask[None], axis=1)
    by_distance = jnp.pad(by_distance, ((0, 16 - H), (0, 0)))
    backwards = jnp.roll(by_distance[:, ::-1], 1, axis=1)
    no_bias = jnp.zeros((8, PAIR), WIDE)
    no_source = jnp.zeros((16, PAIR), LOW)

    dec_rows = dec_in.reshape(row_count, model_width)
    mem_rows = memory.reshape(seq_count * mem_length, model_width)
    grad_rows = out_grad.reshape(row_count, model_width)
    *kept_one, after_self = attention_forward(
        True, dec_rows, no_source, dec_len, gain_full[0:1], w_self, backwards
    )
    if quarters:
        cross_quarter = lax.dynamic_index_in_dim(cross_weight, rep, 0, keepdims=False).astype(LOW)
        out_quarter = lax.dynamic_index_in_dim(
            ffn_out.reshape(4, part_rows // 4, model_width), rep, 0, keepdims=False
        ).astype(LOW)
        cross_rows_each, out_rows_each = cross_weight.shape[1], part_rows // 4
        cross_pieces = with_partner(across_reps(along_line(cross_quarter)))
        w_cross = assemble(
            hold(*cross_pieces, after_self)[:-1],
            where,
            (4, model_width, model_width),
            lambda ref, quarter, at: ref.at[quarter, pl.ds(at * cross_rows_each, cross_rows_each)],
            "assemble_cross",
        )
        out_line = along_line(after(out_quarter, w_self))
        out_near = across_reps(after(out_line, after_self))
    else:
        w_cross = lax.all_gather(cross_weight.astype(LOW), "fsdp", axis=1, tiled=True)
        w_out = lax.all_gather(ffn_out.astype(LOW), "fsdp", axis=0, tiled=True)
    *kept_two, after_cross = attention_forward(
        False, after_self, mem_rows, enc_len, gain_full[1:2], w_cross, no_bias
    )
    if quarters:
        out_near = list(hold(*out_near, after_cross)[:-1])
        w_out = assemble(
            with_partner(out_near),
            where,
            (hidden_width, model_width),
            lambda ref, quarter, at: ref.at[pl.ds((at * 4 + quarter) * out_rows_each, out_rows_each)],
            "assemble_out",
        )
    layer_out, grad_cross, grad_gate, grad_up, *out_near, gain_three = feed_forward_both(
        after_cross, grad_rows, dec_len, where, gain_full[2:3], w_in, w_out
    )
    scatter = lambda value, at: lax.psum_scatter(value, "fsdp", scatter_dimension=at, tiled=True)
    if quarters:
        own_gate = scatter(grad_gate, 0)
        out_near = out_near[:1] + [from_rep(out_near[way], way) for way in range(1, 4)]
    grad_self, grad_k_two, grad_v_two, gain_two, *cross_near, cross_far = attention_backward(
        False, after_self, mem_rows, grad_cross, enc_len, where, gain_full[1:2], w_cross, no_bias, kept_two,
        kept_two[3], kept_one[3],
    )
    if quarters:
        cross_far, grad_k_two, *out_near = hold(cross_far, grad_k_two, *out_near)
        pair = from_shard(cross_far, 1)
        memory_grad = memory_gradient(grad_k_two, grad_v_two, w_cross)
        memory_grad, pair, own_gate = hold(memory_grad, pair, own_gate)
        own_up = scatter(grad_up, 0)
        cross_chip = [add_up([cross_near[way], pair[way]]) for way in range(4)]
        grad_self, *cross_chip = hold(grad_self, *cross_chip)
        cross_near = cross_chip[:1] + [from_rep(cross_chip[way], way) for way in range(1, 4)]
    else:
        memory_grad = memory_gradient(grad_k_two, grad_v_two, w_cross)
    *grads_one, grad_self_weights, dist_grad = attention_backward(
        True, dec_rows, no_source, grad_self, dec_len, where, gain_full[0:1], w_self, by_distance, kept_one,
        no_source, no_source,
    )
    if quarters:
        dist_grad, own_up, grad_self_weights, *rest = hold(
            dist_grad, own_up, grad_self_weights, *grads_one, *cross_near, *out_near
        )
        grads_one, cross_near, out_near = rest[:3], rest[3:7], rest[7:]
        own_self = scatter(grad_self_weights, 1)
        out_sum = add_up(out_near)
        out_pair = from_shard(out_sum[1], 1)
        in_parts = rep_parts(jnp.stack([own_gate, own_up]).reshape(4, -1, hidden_width))
        line = jnp.concatenate([add_up(cross_near), add_up([out_sum[0], out_pair])], axis=1)
        line_parts = add_line(line)
        input_grad, gain_one = input_gradient(grads_one, w_self, dec_rows, grad_self, gain_full[0:1])
    else:
        input_grad, gain_one = input_gradient(grads_one, w_self, dec_rows, grad_self, gain_full[0:1])
    layer_out = layer_out.reshape(dec_in.shape)
    input_grad = input_grad.reshape(dec_in.shape)
    memory_grad = memory_grad.reshape(memory.shape)
    table_part = jnp.sum(bucket_mask[:, None, :] * dist_grad[None, :H, :], axis=2)
    small = jnp.concatenate(
        [gain_one.reshape(-1), gain_two.reshape(-1), gain_three.reshape(-1), table_part.reshape(-1)]
    )
    each = model_width // (LINE * LINE_CORES)
    if quarters:
        small = butterfly(small, from_rep, reps)
        in_near = rep_near(add_up(in_parts))
        both_near = rep_near(add_up(line_parts))
        self_parts = rep_parts(own_self.reshape(4, -1, model_width))
        rest = hold(small, *in_near, *both_near, *self_parts)
        small, in_near, both_near, self_parts = rest[0], rest[1:5], rest[5:9], rest[9:]
        own_in = rep_order(in_near).reshape(ffn_in.shape)
        both = rep_order(both_near)
        own_cross = both[:, :each]
        own_out = both[:, each + each // 3 :].reshape(ffn_out.shape)
        own_self = jnp.concatenate(
            [
                rep_order(rep_near(add_up(self_parts))).reshape(3, *self_weight.shape[1:]),
                both[:3, each : each + each // 3].reshape(1, *self_weight.shape[1:]),
            ]
        )
        over_shards = lambda vector: butterfly(vector, from_shard, shards)
    else:
        over_reps = lambda value: lax.psum(value, "rep")
        own_in = over_reps(scatter(jnp.stack([grad_gate, grad_up]), 1))
        grad_out = jnp.stack(out_near)
        grad_out = grad_out.transpose(2, 1, 0, 3, 4).reshape(hidden_width, model_width)
        own_out = over_reps(scatter(grad_out, 0))
        packed = jnp.stack([jnp.stack(cross_near), cross_far]).transpose(1, 2, 0, 3, 4)
        cross_parts = packed[..., :each, :].reshape(4, model_width, model_width)
        past = packed[:3, ..., each:, :].transpose(1, 2, 0, 3, 4).reshape(1, model_width, model_width)
        own_cross = over_reps(scatter(cross_parts, 1))
        own_self = over_reps(scatter(jnp.concatenate([grad_self_weights, past]), 1))
        over_shards = lambda vector: lax.psum(vector, "fsdp")
        small = lax.psum(small, "rep")

    grad_factor = 1.0 / math.sqrt(row_count * reps * shards)
    self_grad, cross_grad, ffn_in_grad, feedforward_output_gradient = [
        member.astype(WIDE) * grad_factor for member in (own_self, own_cross, own_in, own_out)
    ]
    groups = (
        (ffn_in_grad, ffn_in, in_rows, in_cols),
        (feedforward_output_gradient[None], ffn_out[None], out_rows[None], out_cols[None]),
        (cross_grad, cross_weight, cross_rows, cross_cols),
        (self_grad, self_weight, self_rows, self_cols),
    )
    sums = [factored_sums(gradient, weight, row_state) for gradient, weight, row_state, _ in groups]
    vectors = [member[1] for member in sums] + [jnp.sum(gains * gains, axis=1), small]
    total = over_shards(jnp.concatenate(vectors))
    totals = []
    for vector in vectors:
        totals.append(total[: vector.shape[0]])
        total = total[vector.shape[0] :]
    updated = [
        factored_update(gradient, weight, sums[at][0], col_state, totals[at])
        for at, (gradient, weight, _, col_state) in enumerate(groups)
    ]
    new_ffn_in, new_ffn_out, new_cross, new_self = [member[0] for member in updated]
    new_in_cols, new_out_cols, new_cross_cols, new_self_cols = [member[1] for member in updated]
    new_in_rows, new_out_rows, new_cross_rows, new_self_rows = [member[0] for member in sums]
    new_ffn_out, new_out_rows, new_out_cols = new_ffn_out[0], new_out_rows[0], new_out_cols[0]
    gain_square = totals[4] / model_width
    small = totals[5] * grad_factor
    gains_grad = lax.dynamic_slice_in_dim(
        small[: 3 * model_width].reshape(3, model_width), shard * gains.shape[1], gains.shape[1], axis=1
    )
    table_grad = small[3 * model_width :].reshape(BUCKETS, H)
    new_gains, new_gain_moment = plain_update(gains_grad, gains, gain_moment, gain_square[:, None])
    new_table, new_table_moment = plain_update(
        table_grad, table, table_moment, jnp.mean(table * table)
    )
    return (
        layer_out,
        input_grad,
        memory_grad,
        self_grad,
        cross_grad,
        ffn_in_grad,
        feedforward_output_gradient,
        gains_grad,
        table_grad,
        new_self,
        new_cross,
        new_ffn_in,
        new_ffn_out,
        new_gains,
        new_table,
        new_self_rows,
        new_self_cols,
        new_cross_rows,
        new_cross_cols,
        new_in_rows,
        new_in_cols,
        new_out_rows,
        new_out_cols,
        new_gain_moment,
        new_table_moment,
    )


def solution(mesh):
    placed = (
        P(("rep", "fsdp"), None, None),
        P(("rep", "fsdp"), None, None),
        P(("rep", "fsdp"), None, None),
        P(("rep", "fsdp")),
        P(("rep", "fsdp")),
        P(),
        P(None, "fsdp", None),
        P(None, "fsdp", None),
        P(None, "fsdp", None),
        P("fsdp", None),
        P(None, "fsdp"),
        P(),
        P(None, "fsdp"),
        P(),
        P(None, "fsdp"),
        P(),
        P(None, "fsdp"),
        P(),
        P("fsdp"),
        P(),
        P(None, "fsdp"),
        P(),
    )
    return jax.shard_map(
        per_device,
        mesh=mesh,
        in_specs=placed,
        out_specs=(
            P(("rep", "fsdp"), None, None),
            P(("rep", "fsdp"), None, None),
            P(("rep", "fsdp"), None, None),
            P(None, "fsdp", None),
            P(None, "fsdp", None),
            P(None, "fsdp", None),
            P("fsdp", None),
            P(None, "fsdp"),
            P(),
            P(None, "fsdp", None),
            P(None, "fsdp", None),
            P(None, "fsdp", None),
            P("fsdp", None),
            P(None, "fsdp"),
            P(),
            P(None, "fsdp"),
            P(),
            P(None, "fsdp"),
            P(),
            P(None, "fsdp"),
            P(),
            P("fsdp"),
            P(),
            P(None, "fsdp"),
            P(),
        ),
        check_vma=False,
    )
```

```python
import functools
import math

import jax
import jax.numpy as jnp
from jax import lax
from jax.experimental import pallas as pl
from jax.experimental.pallas import tpu as pltpu
from jax.sharding import PartitionSpec as P

H = 12
DH = 64
BUCKETS = 32
DECAY_RATE = 0.8
STEP_RATE = 0.2
TINY_TERM = 1e-30
PAIR = 2 * DH
GROUP = 4 * DH
HIDDEN = -1e30
MEGABYTE = 1024 * 1024
PEAK = 1.15e9
LINE = 4
LINE_CORES = 2
LOW = jnp.bfloat16
WIDE = jnp.float32


def nn(left, right):
    return lax.dot_general(left, right, (((1,), (0,)), ((), ())), preferred_element_type=WIDE)


def nt(left, right):
    return lax.dot_general(left, right, (((1,), (1,)), ((), ())), preferred_element_type=WIDE)


def tn(left, right):
    return lax.dot_general(left, right, (((0,), (0,)), ((), ())), preferred_element_type=WIDE)


def rms_rate(rows):
    return lax.rsqrt(jnp.mean(rows * rows, axis=-1, keepdims=True) + 1e-06)


def three_parts(column):
    high = column.astype(LOW)
    rest = column - high.astype(WIDE)
    middle = rest.astype(LOW)
    low = (rest - middle.astype(WIDE)).astype(LOW)
    return high, middle, low


def chunks(total, size):
    return [(at, min(size, total - at)) for at in range(0, total, size)]


def lanes(rows):
    return lax.broadcasted_iota(jnp.int32, (rows, PAIR), 1)


def own_lanes(rows, side):
    lane = lanes(rows)
    return (lane >= DH * side) & (lane < DH * (side + 1))


def key_extras(rows, side, length):
    lane = lanes(rows) - DH * (1 - side)
    dead = lax.broadcasted_iota(jnp.int32, (rows, PAIR), 0) >= length
    mask = jnp.where(dead, HIDDEN, 0.0)
    return jnp.where(
        (lane >= 0) & (lane < 3), 1.0, jnp.where(lane == 3, mask, 0.0)
    ).astype(LOW)


def row_extras(rows, side, column, last):
    lane = lanes(rows) - DH * (1 - side)
    high, middle, low = three_parts(column)
    wide = lambda part: jnp.broadcast_to(part.astype(WIDE), (rows, PAIR))
    return jnp.where(
        lane == 0,
        wide(high),
        jnp.where(
            lane == 1, wide(middle), jnp.where(lane == 2, wide(low), jnp.where(lane == 3, last, 0.0))
        ),
    ).astype(LOW)


def forward_body(causal, seq_count, length_ref, wave_ref, bias_ref, q_ref, k_ref, v_ref, mix_ref, total_ref, group):
    rows = q_ref.shape[0] // seq_count
    keys = k_ref.shape[0] // seq_count
    block = rows
    for pair in range(2):
        at = pair * PAIR
        for side in range(2):
            head = 2 * pair + side
            if causal:
                wave = wave_ref[pl.ds(group * 4 + head, 1), :]
                spread = pltpu.roll(
                    jnp.broadcast_to(wave, (rows, keys)), 0, 1, stride=1, stride_axis=0
                )
                row = lax.broadcasted_iota(jnp.int32, (rows, keys), 0)
                column = lax.broadcasted_iota(jnp.int32, (rows, keys), 1)
                bias_ref[side] = jnp.where(column <= row, spread, HIDDEN)
        for seq in range(seq_count):
            outs = []
            for side in range(2):
                own_q = own_lanes(rows, side)
                own_k = own_lanes(keys, side)
                query = jnp.where(
                    own_q,
                    q_ref[seq * rows : (seq + 1) * rows, at : at + PAIR],
                    (lanes(rows) == DH * (1 - side) + 3).astype(LOW),
                )
                key = jnp.where(
                    own_k,
                    k_ref[seq * keys : (seq + 1) * keys, at : at + PAIR],
                    key_extras(keys, side, length_ref[seq]),
                )
                value = jnp.where(
                    own_k,
                    v_ref[seq * keys : (seq + 1) * keys, at : at + PAIR],
                    jnp.ones((), LOW),
                )
                parts = []
                for start in range(0, rows, block):
                    span = start + block if causal else keys
                    scores = nt(query[start : start + block], key[:span])
                    if causal:
                        scores = scores + bias_ref[side, start : start + block, :span]
                    top = jnp.max(scores, axis=1, keepdims=True)
                    weight = jnp.exp(scores - top)
                    out = nn(weight.astype(LOW), value[:span])
                    total = out[:, DH * (1 - side) : DH * (1 - side) + 1]
                    parts.append(out * (1.0 / total))
                    spot = pl.ds(seq * rows + start, block)
                    lane = lanes(block)
                    seen = total_ref[spot, :] if (pair or side) else jnp.zeros((block, PAIR), WIDE)
                    total_ref[spot, :] = jnp.where(
                        lane == 2 * pair + side, top + jnp.log(total), seen
                    )
                outs.append(jnp.concatenate(parts, axis=0))
            mix_ref[seq * rows : (seq + 1) * rows, at : at + PAIR] = jnp.where(
                own_lanes(rows, 0), outs[0], outs[1]
            ).astype(LOW)


def forward_kernel(
    causal, seq_count, length_ref, x_ref, source_ref, gain_ref, wq_ref, wk_ref, wv_ref, wo_ref, wave_ref,
    q_ref, k_ref, v_ref, mix_ref, total_ref, after_ref, normed, bias,
):
    group = pl.program_id(0)

    @pl.when(group == 0)
    def _():
        for at, size in chunks(x_ref.shape[0], 256):
            rows = x_ref[at : at + size, :].astype(WIDE)
            normed[at : at + size, :] = (rows * rms_rate(rows) * gain_ref[...]).astype(LOW)
            after_ref[at : at + size, :] = rows

    source = normed if causal else source_ref
    q_ref[...] = nn(normed[...], wq_ref[...]).astype(LOW)
    k_ref[...] = nn(source[...], wk_ref[...]).astype(LOW)
    v_ref[...] = nn(source[...], wv_ref[...]).astype(LOW)
    forward_body(causal, seq_count, length_ref, wave_ref, bias, q_ref, k_ref, v_ref, mix_ref, total_ref, group)
    after_ref[...] += nn(mix_ref[...], wo_ref[...])


def weight_specs(width):
    across = lambda at: pl.BlockSpec((None, width, GROUP), lambda g, at=at: (at, 0, g))
    return [across(0), across(1), across(2), pl.BlockSpec((None, GROUP, width), lambda g: (3, g, 0))]


def whole(shape):
    return pl.BlockSpec(shape, lambda g: (0,) * len(shape), pipeline_mode=pl.Buffered(1))


def columns(rows):
    return pl.BlockSpec((rows, GROUP), lambda g: (0, g))


def attention_forward(causal, x, source, lengths, gain, weights, wave):
    row_count, width = x.shape
    seq_count = lengths.shape[0]
    source_rows = row_count if causal else source.shape[0]
    length = row_count // seq_count
    groups = width // GROUP
    low = lambda rows: jax.ShapeDtypeStruct((rows, width), LOW)
    args = [lengths, x, source, gain, weights, weights, weights, weights, wave]
    return pl.pallas_call(
        functools.partial(forward_kernel, causal, seq_count),
        grid=(groups,),
        in_specs=[
            pl.BlockSpec(memory_space=pltpu.SMEM),
            whole(x.shape),
            whole(source.shape),
            whole(gain.shape),
            *weight_specs(width),
            whole(wave.shape),
        ],
        out_specs=[
            columns(row_count),
            columns(source_rows),
            columns(source_rows),
            columns(row_count),
            pl.BlockSpec((None, row_count, PAIR), lambda g: (g, 0, 0)),
            whole((row_count, width)),
        ],
        out_shape=[
            low(row_count),
            low(source_rows),
            low(source_rows),
            low(row_count),
            jax.ShapeDtypeStruct((groups, row_count, PAIR), WIDE),
            jax.ShapeDtypeStruct((row_count, width), WIDE),
        ],
        scratch_shapes=[
            pltpu.VMEM((row_count, width), LOW),
            pltpu.VMEM((2, length, length) if causal else (1, 8, PAIR), WIDE),
        ],
        cost_estimate=pl.CostEstimate(flops=int(27 * PEAK), bytes_accessed=20 << 20, transcendentals=0),
        compiler_params=pltpu.CompilerParams(vmem_limit_bytes=36 * MEGABYTE),
        name="self_forward" if causal else "cross_forward",
    )(*args)


def gelu_parts(gate):
    root = 0.7978845608028654
    square = gate * gate
    inner = jnp.tanh(root * gate * (1.0 + 0.044715 * square))
    half = 0.5 * (1.0 + inner)
    value = gate * half
    slope = half + 0.5 * gate * (1.0 - inner * inner) * (root * (1.0 + 3 * 0.044715 * square))
    return value, slope


def rms_back(rows, gain, grad):
    rate = rms_rate(rows)
    scaled = rows * rate
    low = grad * gain
    grad_rows = rate * (low - scaled * jnp.mean(scaled * low, axis=-1, keepdims=True))
    return grad_rows, jnp.sum(grad * scaled, axis=0, keepdims=True)


def shard_slot(where_ref, shard):
    return (shard % LINE_CORES) ^ where_ref[2], lax.rem(shard // LINE_CORES - where_ref[1] + LINE, LINE)


def feed_kernel(
    seq_count, length_ref, where_ref, after_ref, out_grad_ref, gain_ref, wg_ref, wu_ref, wd_ref,
    layer_ref, grad_cross_ref, dwg_ref, dwu_ref, *refs,
):
    near_refs = refs[:4]
    dgain_ref, normed, normed_t, down, out_total, grad_total, cut = refs[4:]
    step = pl.program_id(0)
    row_count = after_ref.shape[0]
    length = row_count // seq_count

    def live(at, size):
        position = lax.broadcasted_iota(jnp.int32, (size, 1), 0) + (at % length)
        return (position < length_ref[at // length]).astype(WIDE)

    @pl.when(step == 0)
    def _():
        for at, size in chunks(row_count, 256):
            rows = after_ref[at : at + size, :]
            low = (rows * rms_rate(rows) * gain_ref[...]).astype(LOW)
            normed[at : at + size, :] = low
            normed_t[:, at : at + size] = low.T
            down[at : at + size, :] = (
                out_grad_ref[at : at + size, :].astype(WIDE) * live(at, size)
            ).astype(LOW)
            out_total[at : at + size, :] = rows
            grad_total[at : at + size, :] = jnp.zeros((size, rows.shape[1]), WIDE)

    gate = nn(normed[...], wg_ref[...])
    up = nn(normed[...], wu_ref[...])
    value, slope = gelu_parts(gate)
    hidden = (value * up).astype(LOW)
    out_total[...] += nn(hidden, wd_ref[...])
    grad_hidden = nt(down[...], wd_ref[...])
    cut[...] = tn(hidden, down[...]).astype(LOW).reshape(cut.shape)
    core, hop = shard_slot(where_ref, step)
    for way in range(4):
        near_refs[way][core, hop] = cut[where_ref[0] ^ way]
    grad_gate = (grad_hidden * up * slope).astype(LOW)
    grad_up = (grad_hidden * value).astype(LOW)
    dwg_ref[...] = nn(normed_t[...], grad_gate).astype(LOW)
    dwu_ref[...] = nn(normed_t[...], grad_up).astype(LOW)
    grad_total[...] += nt(grad_gate, wg_ref[...]) + nt(grad_up, wu_ref[...])

    @pl.when(step == pl.num_programs(0) - 1)
    def _():
        dgain = jnp.zeros(dgain_ref.shape, WIDE)
        for at, size in chunks(row_count, 256):
            part = slice(at, at + size)
            layer_ref[part, :] = (out_total[part, :] * live(at, size)).astype(LOW)
            grad_rows, gain_part = rms_back(after_ref[part, :], gain_ref[...], grad_total[part, :])
            dgain = dgain + gain_part
            grad_cross_ref[part, :] = (
                out_grad_ref[part, :].astype(WIDE) * live(at, size) + grad_rows
            )
        dgain_ref[...] = dgain


def feed_forward_both(after, out_grad, lengths, where, gain, w_in, w_out):
    row_count, width = after.shape
    hidden = w_out.shape[0]
    block = hidden // (LINE * LINE_CORES)
    seq_count = lengths.shape[0]
    wide = pl.BlockSpec((None, width, block), lambda g: (0, 0, g))
    wide_up = pl.BlockSpec((None, width, block), lambda g: (1, 0, g))
    tall = pl.BlockSpec((block, width), lambda g: (g, 0))
    flat = pl.BlockSpec((width, block), lambda g: (0, g))
    near = (LINE_CORES, LINE, block // 4, width)
    return pl.pallas_call(
        functools.partial(feed_kernel, seq_count),
        grid=(hidden // block,),
        in_specs=[
            pl.BlockSpec(memory_space=pltpu.SMEM),
            pl.BlockSpec(memory_space=pltpu.SMEM),
            whole(after.shape),
            whole(out_grad.shape),
            whole(gain.shape),
            wide,
            wide_up,
            tall,
        ],
        out_specs=[whole(after.shape), whole(after.shape), flat, flat, *[whole(near)] * 4, whole((1, width))],
        out_shape=[
            jax.ShapeDtypeStruct((row_count, width), LOW),
            jax.ShapeDtypeStruct((row_count, width), WIDE),
            jax.ShapeDtypeStruct((width, hidden), LOW),
            jax.ShapeDtypeStruct((width, hidden), LOW),
            *[jax.ShapeDtypeStruct(near, LOW)] * 4,
            jax.ShapeDtypeStruct((1, width), WIDE),
        ],
        scratch_shapes=[
            pltpu.VMEM((row_count, width), LOW),
            pltpu.VMEM((width, row_count), LOW),
            pltpu.VMEM((row_count, width), LOW),
            pltpu.VMEM((row_count, width), WIDE),
            pltpu.VMEM((row_count, width), WIDE),
            pltpu.VMEM((4, block // 4, width), LOW),
        ],
        cost_estimate=pl.CostEstimate(flops=int(46 * PEAK), bytes_accessed=40 << 20, transcendentals=0),
        compiler_params=pltpu.CompilerParams(vmem_limit_bytes=40 * MEGABYTE),
        name="feed_forward_both",
    )(lengths, where, after, out_grad, gain, w_in, w_in, w_out)


def backward_kernel(
    causal, seq_count, length_ref, where_ref, x_ref, source_ref, grad_ref, gain_ref, wq_ref, wo_ref, wave_ref,
    q_ref, k_ref, v_ref, mix_ref, total_ref, mix_all_ref, mix_past_ref, *refs,
):
    if causal:
        gq, gk_out_ref, gv_out_ref, dw_ref, dist_ref = refs[:5]
        normed_t, branch, grad_mix, bias, score_sum = refs[5:]
        source_t = normed_t
    else:
        grad_x_ref, gk_out_ref, gv_out_ref, dgain_ref = refs[:4]
        near_refs, far_ref = refs[4:8], refs[8]
        normed_t, branch, grad_mix, gq, source_t, mix_t, grad_total, dw_ref, past = refs[9:]
    group = pl.program_id(0)
    row_count = x_ref.shape[0]
    rows = q_ref.shape[0] // seq_count
    keys = k_ref.shape[0] // seq_count
    block = rows

    @pl.when(group == 0)
    def _():
        for at, size in chunks(row_count, 256):
            value = x_ref[at : at + size, :].astype(WIDE)
            low = (value * rms_rate(value) * gain_ref[...]).astype(LOW)
            normed_t[:, at : at + size] = low.T
            branch[at : at + size, :] = grad_ref[at : at + size, :].astype(LOW)
            if not causal:
                mix_t[:, at : at + size] = mix_all_ref[at : at + size, :].T
                grad_total[at : at + size, :] = jnp.zeros((size, value.shape[1]), WIDE)
        if not causal:
            for at, size in chunks(source_ref.shape[0], 256):
                source_t[:, at : at + size] = source_ref[at : at + size, :].T

    grad_mix[...] = nt(branch[...], wo_ref[...]).astype(LOW)
    if not causal:
        across = pl.ds(pl.multiple_of(group * GROUP, GROUP), GROUP)
        put = lambda at, value: dw_ref.__setitem__(at, value.astype(LOW).reshape(dw_ref.shape[1:]))
        put(3, nn(mix_t[...], branch[:, across]))

    for pair in range(2):
        at = pair * PAIR
        if causal:
            for side in range(2):
                head = 2 * pair + side
                wave = wave_ref[pl.ds(group * 4 + head, 1), :]
                spread = pltpu.roll(
                    jnp.broadcast_to(wave, (keys, rows)), 0, 1, stride=1, stride_axis=0
                )
                row = lax.broadcasted_iota(jnp.int32, (keys, rows), 0)
                column = lax.broadcasted_iota(jnp.int32, (keys, rows), 1)
                bias[side] = jnp.where(column >= row, spread, HIDDEN)
        for seq in range(seq_count):
            span_q = slice(seq * rows, (seq + 1) * rows)
            span_k = slice(seq * keys, (seq + 1) * keys)
            sides = []
            for side in range(2):
                head = 2 * pair + side
                own_q = own_lanes(rows, side)
                own_k = own_lanes(keys, side)
                total = jnp.sum(
                    jnp.where(lanes(rows) == head, total_ref[span_q, :], 0.0), axis=1, keepdims=True
                )
                grad_low = grad_mix[span_q, at : at + PAIR]
                product = grad_low.astype(WIDE) * mix_ref[span_q, at : at + PAIR].astype(WIDE)
                delta = jnp.sum(jnp.where(own_q, product, 0.0), axis=1, keepdims=True)
                query = jnp.where(
                    own_q, q_ref[span_q, at : at + PAIR], row_extras(rows, side, -total, 1.0)
                )
                grad_out = jnp.where(own_q, grad_low, row_extras(rows, side, -delta, 0.0))
                key = jnp.where(
                    own_k,
                    k_ref[span_k, at : at + PAIR],
                    key_extras(keys, side, length_ref[seq]),
                )
                value = jnp.where(own_k, v_ref[span_k, at : at + PAIR], jnp.ones((), LOW))
                grad_query = []
                grad_key = None
                grad_value = None
                for start in range(0, rows, block):
                    span = start + block if causal else keys
                    scores = nt(key[:span], query[start : start + block])
                    if causal:
                        scores = scores + bias[side, :span, start : start + block]
                    weight = jnp.exp(scores)
                    low = weight.astype(LOW)
                    grad_weight = nt(value[:span], grad_out[start : start + block])
                    grad_score = (weight * grad_weight).astype(LOW)
                    if causal:
                        if seq == 0:
                            score_sum[side, :span, start : start + block] = grad_score.astype(WIDE)
                        else:
                            score_sum[side, :span, start : start + block] += grad_score.astype(WIDE)
                    key_part = nn(grad_score, query[start : start + block])
                    value_part = nn(low, grad_out[start : start + block])
                    grad_query.append(tn(grad_score, key[:span]))
                    if causal and start == 0 and rows > block:
                        rest = jnp.zeros((keys - span, PAIR), WIDE)
                        key_part = jnp.concatenate([key_part, rest], axis=0)
                        value_part = jnp.concatenate([value_part, rest], axis=0)
                    grad_key = key_part if grad_key is None else grad_key + key_part
                    grad_value = value_part if grad_value is None else grad_value + value_part
                sides.append((jnp.concatenate(grad_query, axis=0), grad_key, grad_value))
            pick_q = own_lanes(rows, 0)
            pick_k = own_lanes(keys, 0)
            gq[span_q, at : at + PAIR] = jnp.where(pick_q, sides[0][0], sides[1][0]).astype(LOW)
            gk_out_ref[span_k, at : at + PAIR] = jnp.where(pick_k, sides[0][1], sides[1][1]).astype(LOW)
            gv_out_ref[span_k, at : at + PAIR] = jnp.where(pick_k, sides[0][2], sides[1][2]).astype(LOW)
        if causal:
            for side in range(2):
                head = 2 * pair + side
                row = lax.broadcasted_iota(jnp.int32, (keys, rows), 0)
                column = lax.broadcasted_iota(jnp.int32, (keys, rows), 1)
                held = jnp.where(column >= row, score_sum[side], 0.0)
                while held.shape[0] > 1:
                    half = held.shape[0] // 2
                    held = held[:half] + pltpu.roll(held[half:], rows - half, 1)
                dist_ref[pl.ds(group * 4 + head, 1), :] = held

    if causal:
        dw_ref[0] = nn(normed_t[...], gq[...]).astype(LOW)
        dw_ref[1] = nn(source_t[...], gk_out_ref[...]).astype(LOW)
        dw_ref[2] = nn(source_t[...], gv_out_ref[...]).astype(LOW)
        return
    put(0, nn(normed_t[...], gq[...]))
    put(1, nn(source_t[...], gk_out_ref[...]))
    put(2, nn(source_t[...], gv_out_ref[...]))
    grad_total[...] += nt(gq[...], wq_ref[...])
    rep, line, core = where_ref[0], where_ref[1], where_ref[2]
    held = dw_ref.shape[2]
    slots = []
    for way in range(4):
        for hop in range(LINE):
            at = lax.rem(line + hop, LINE) * LINE_CORES
            slots.append((near_refs[way].at[hop], rep ^ way, at + core))
            slots.append((far_ref.at[way, hop], rep ^ way, at + (core ^ 1)))
    for slot, quarter, shard in slots:
        slot[0:held, across] = dw_ref[quarter, shard]

    @pl.when(group == pl.num_programs(0) - 1)
    def _():
        dgain = jnp.zeros(dgain_ref.shape, WIDE)
        for at, size in chunks(row_count, 256):
            part = slice(at, at + size)
            grad_rows, gain_part = rms_back(
                x_ref[part, :].astype(WIDE), gain_ref[...], grad_total[part, :]
            )
            dgain = dgain + gain_part
            grad_rows = grad_ref[part, :] + grad_rows
            grad_x_ref[part, :] = grad_rows
            branch[part, :] = grad_rows.astype(LOW)
            mix_t[:, part] = mix_past_ref[part, :].T
        dgain_ref[...] = dgain
        thirds = nn(mix_t[...], branch[...]).astype(LOW)
        past[:, 0:3] = thirds.reshape(past.shape[0], 3, *past.shape[2:])
        past[:, 3] = jnp.zeros_like(past[:, 3])
        for slot, quarter, shard in slots:
            slot[held:, :] = past[shard, quarter]


def attention_backward(causal, x, source, grad, lengths, where, gain, weights, wave, kept, mix, past):
    row_count, width = x.shape
    seq_count = lengths.shape[0]
    source_rows = row_count if causal else source.shape[0]
    length = row_count // seq_count
    groups = width // GROUP
    low = lambda rows: jax.ShapeDtypeStruct((rows, width), LOW)
    if causal:
        out_specs = [
            columns(row_count), columns(source_rows), columns(source_rows),
            pl.BlockSpec((3, width, GROUP), lambda g: (0, 0, g)), whole(wave.shape),
        ]
        out_shape = [
            low(row_count), low(source_rows), low(source_rows),
            jax.ShapeDtypeStruct((3, width, width), LOW), jax.ShapeDtypeStruct(wave.shape, WIDE),
        ]
        scratch = [pltpu.VMEM((2, length, length), WIDE)] * 2
    else:
        shards = LINE * LINE_CORES
        each, third = width // shards, width // shards // 3
        near = (LINE, each + third, width)
        out_specs = [
            whole((row_count, width)), columns(source_rows), columns(source_rows), whole((1, width)),
            *[whole(near)] * 4, whole((4, *near)),
        ]
        out_shape = [
            jax.ShapeDtypeStruct((row_count, width), WIDE), low(source_rows), low(source_rows),
            jax.ShapeDtypeStruct((1, width), WIDE), *[jax.ShapeDtypeStruct(near, LOW)] * 4,
            jax.ShapeDtypeStruct((4, *near), LOW),
        ]
        scratch = [
            pltpu.VMEM((row_count, GROUP), LOW),
            pltpu.VMEM((width, source_rows), LOW),
            pltpu.VMEM((width, row_count), LOW),
            pltpu.VMEM((row_count, width), WIDE),
            pltpu.VMEM((4, shards, each, GROUP), LOW),
            pltpu.VMEM((shards, 4, third, width), LOW),
        ]
    return pl.pallas_call(
        functools.partial(backward_kernel, causal, seq_count),
        grid=(groups,),
        in_specs=[
            pl.BlockSpec(memory_space=pltpu.SMEM),
            pl.BlockSpec(memory_space=pltpu.SMEM),
            whole(x.shape),
            whole(source.shape),
            whole(grad.shape),
            whole(gain.shape),
            weight_specs(width)[0],
            weight_specs(width)[3],
            whole(wave.shape),
            columns(row_count),
            columns(source_rows),
            columns(source_rows),
            columns(row_count),
            pl.BlockSpec((None, row_count, PAIR), lambda g: (g, 0, 0)),
            whole(mix.shape),
            whole(past.shape),
        ],
        out_specs=out_specs,
        out_shape=out_shape,
        scratch_shapes=[
            pltpu.VMEM((width, row_count), LOW),
            pltpu.VMEM((row_count, width), LOW),
            pltpu.VMEM((row_count, GROUP), LOW),
            *scratch,
        ],
        cost_estimate=pl.CostEstimate(flops=int(45 * PEAK), bytes_accessed=40 << 20, transcendentals=0),
        compiler_params=pltpu.CompilerParams(vmem_limit_bytes=(36 if causal else 46) * MEGABYTE),
        name="self_backward" if causal else "cross_backward",
    )(lengths, where, x, source, grad, gain, weights, weights, wave, *kept, mix, past)


def input_kernel(gq_ref, gk_ref, gv_ref, wq_ref, wk_ref, wv_ref, x_ref, grad_ref, gain_ref, out_ref, dgain_ref):
    total = nt(gq_ref[...], wq_ref[...]) + nt(gk_ref[...], wk_ref[...]) + nt(gv_ref[...], wv_ref[...])
    grad_rows, dgain = rms_back(x_ref[...].astype(WIDE), gain_ref[...], total)
    out_ref[...] = grad_ref[...] + grad_rows

    @pl.when(pl.program_id(0) == 0)
    def _():
        dgain_ref[...] = jnp.zeros_like(dgain_ref)

    dgain_ref[...] += dgain


def input_gradient(grads, weights, x, grad, gain):
    rows, width = x.shape
    block = 256
    rowwise = pl.BlockSpec((block, width), lambda g: (g, 0))
    matrix = lambda at: pl.BlockSpec((None, width, width), lambda g: (at, 0, 0))
    return pl.pallas_call(
        input_kernel,
        grid=(rows // block,),
        in_specs=[rowwise, rowwise, rowwise, matrix(0), matrix(1), matrix(2), rowwise, rowwise, whole((1, width))],
        out_specs=[rowwise, whole((1, width))],
        out_shape=[jax.ShapeDtypeStruct((rows, width), WIDE), jax.ShapeDtypeStruct((1, width), WIDE)],
        cost_estimate=pl.CostEstimate(flops=int(8 * PEAK), bytes_accessed=12 << 20, transcendentals=0),
        compiler_params=pltpu.CompilerParams(vmem_limit_bytes=24 * MEGABYTE),
        name="input_gradient",
    )(*grads, weights, weights, weights, x, grad, gain)


def memory_kernel(gk_ref, gv_ref, wk_ref, wv_ref, out_ref):
    out_ref[...] = nt(gk_ref[...], wk_ref[...]) + nt(gv_ref[...], wv_ref[...])


def memory_gradient(grad_key, grad_value, weights):
    rows, width = grad_key.shape
    block = 256
    rowwise = pl.BlockSpec((block, width), lambda g: (g, 0))
    matrix = lambda at: pl.BlockSpec((None, width, width), lambda g: (at, 0, 0))
    return pl.pallas_call(
        memory_kernel,
        grid=(rows // block,),
        in_specs=[rowwise, rowwise, matrix(1), matrix(2)],
        out_specs=rowwise,
        out_shape=jax.ShapeDtypeStruct((rows, width), WIDE),
        cost_estimate=pl.CostEstimate(flops=int(7 * PEAK), bytes_accessed=10 << 20, transcendentals=0),
        compiler_params=pltpu.CompilerParams(vmem_limit_bytes=24 * MEGABYTE),
        name="memory_gradient",
    )(grad_key, grad_value, weights, weights)


def flat_permute(value, target):
    reps, shards = lax.axis_size("rep"), lax.axis_size("fsdp")
    pairs = []
    for rep in range(reps):
        for shard in range(shards):
            to_rep, to_shard = target(rep, shard)
            pairs.append((rep * shards + shard, to_rep * shards + to_shard))
    return lax.ppermute(value, ("rep", "fsdp"), pairs)


def from_rep(value, way):
    return flat_permute(value, lambda rep, shard: (rep ^ way, shard))


def from_shard(value, way):
    return flat_permute(value, lambda rep, shard: (rep, shard ^ way))


def from_line(value, hops):
    shards = lax.axis_size("fsdp")
    return flat_permute(value, lambda rep, shard: (rep, (shard + 2 * hops) % shards))


def along_line(piece):
    hops = lax.axis_size("fsdp") // 2
    return jnp.stack([piece] + [from_line(piece, hop) for hop in range(1, hops)])


def across_reps(line):
    return [line] + [from_rep(line, way) for way in range(1, 4)]


def with_partner(parts):
    return parts + [from_shard(part, 1) for part in parts]


def add_line(parts):
    return [parts[0]] + [from_line(parts[hop], hop) for hop in range(1, LINE)]


def assemble_kernel(place, hops, where_ref, *refs):
    parts, out_ref, sems = refs[:8], refs[8], refs[9]
    rep, line, core = where_ref[0], where_ref[1], where_ref[2]
    copies = []
    for other in range(2):
        for way in range(4):
            for hop in range(hops):
                shard = lax.rem(line - hop + hops, hops) * 2 + (core ^ other)
                copies.append(
                    pltpu.make_async_copy(
                        parts[4 * other + way].at[hop],
                        place(out_ref, rep ^ way, shard),
                        sems.at[len(copies)],
                    )
                )
    for copy in copies:
        copy.start()
    for copy in copies:
        copy.wait()


def assemble(parts, where, shape, place, name):
    hops = parts[0].shape[0]
    return pl.pallas_call(
        functools.partial(assemble_kernel, place, hops),
        in_specs=[pl.BlockSpec(memory_space=pltpu.SMEM)] + [pl.BlockSpec(memory_space=pl.ANY)] * 8,
        out_specs=pl.BlockSpec(memory_space=pltpu.VMEM),
        out_shape=jax.ShapeDtypeStruct(shape, LOW),
        scratch_shapes=[pltpu.SemaphoreType.DMA((8 * hops,))],
        cost_estimate=pl.CostEstimate(flops=int(4 * PEAK), bytes_accessed=8 << 20, transcendentals=0),
        compiler_params=pltpu.CompilerParams(vmem_limit_bytes=24 * MEGABYTE),
        name=name,
    )(where, *parts)


def rep_parts(parts):
    rep = lax.axis_index("rep")
    pick = lambda at: lax.dynamic_index_in_dim(parts, at, 0, keepdims=False)
    return [pick(rep)] + [from_rep(pick(rep ^ way), way) for way in range(1, 4)]


def add_up(parts):
    return sum(part.astype(WIDE) for part in parts).astype(LOW)


def rep_near(piece):
    return [piece] + [from_rep(piece, way) for way in range(1, 4)]


def rep_order(near):
    rep = lax.axis_index("rep")
    near = jnp.stack(near)
    return jnp.stack([lax.dynamic_index_in_dim(near, at ^ rep, 0, keepdims=False) for at in range(4)])


def hold(*values):
    return lax.optimization_barrier(values)


def butterfly(vector, move, size):
    way = 1
    while way < size:
        vector = vector + move(vector, way)
        way *= 2
    return vector


def after(value, *earlier):
    return lax.optimization_barrier((value, *earlier))[0]


def factored_sums(gradient, weight, row_state):
    squares = gradient * gradient + TINY_TERM
    row_moment = DECAY_RATE * row_state + (1.0 - DECAY_RATE) * jnp.mean(squares, axis=2)
    local = jnp.concatenate(
        [
            jnp.sum(squares, axis=1).reshape(-1),
            jnp.sum(row_moment, axis=1),
            jnp.sum(weight * weight, axis=(1, 2)),
        ]
    )
    return row_moment, local


def factored_update(gradient, weight, row_moment, col_state, total):
    count, rows, cols = weight.shape
    whole_rows = rows * lax.axis_size("fsdp")
    col_sum = total[: count * cols].reshape(count, cols)
    row_mean = total[count * cols : count * cols + count] / whole_rows
    square = total[count * cols + count :] / (whole_rows * cols)
    col_moment = DECAY_RATE * col_state + (1.0 - DECAY_RATE) * col_sum / whole_rows
    direction = gradient * lax.rsqrt(
        row_moment[:, :, None] * col_moment[:, None, :] / row_mean[:, None, None]
    )
    step = STEP_RATE * jnp.sqrt(square + 1e-06)
    return weight - step[:, None, None] * direction, col_moment


def plain_update(gradient, weight, moment, square):
    moment = DECAY_RATE * moment + (1.0 - DECAY_RATE) * (gradient * gradient + TINY_TERM)
    step = STEP_RATE * jnp.sqrt(square + 1e-06)
    return weight - step * gradient * lax.rsqrt(moment), moment


def per_device(
    dec_in,
    memory,
    out_grad,
    dec_len,
    enc_len,
    buckets,
    self_weight,
    cross_weight,
    ffn_in,
    ffn_out,
    gains,
    table,
    self_rows,
    self_cols,
    cross_rows,
    cross_cols,
    in_rows,
    in_cols,
    out_rows,
    out_cols,
    gain_moment,
    table_moment,
):
    seq_count, seq_length, model_width = dec_in.shape
    mem_length = memory.shape[1]
    row_count = seq_count * seq_length
    hidden_width = ffn_in.shape[2]
    reps, shards = lax.axis_size("rep"), lax.axis_size("fsdp")
    rep, shard = lax.axis_index("rep"), lax.axis_index("fsdp")
    quarters = reps == 4 and shards == 8
    part_rows = hidden_width // shards
    where = jnp.stack([rep, shard // 2, shard % 2]).astype(jnp.int32) * int(quarters)
    w_self = lax.all_gather(self_weight.astype(LOW), "fsdp", axis=1, tiled=True)
    gain_full = lax.all_gather(gains.astype(LOW), "fsdp", axis=1, tiled=True).astype(WIDE)
    w_in = lax.all_gather(ffn_in.astype(LOW), "fsdp", axis=1, tiled=True)

    bucket_mask = (buckets[None, :] == jnp.arange(BUCKETS)[:, None]).astype(WIDE)
    by_distance = jnp.sum(table.T[:, :, None] * bucket_mask[None], axis=1)
    by_distance = jnp.pad(by_distance, ((0, 16 - H), (0, 0)))
    backwards = jnp.roll(by_distance[:, ::-1], 1, axis=1)
    no_bias = jnp.zeros((8, PAIR), WIDE)
    no_source = jnp.zeros((16, PAIR), LOW)

    dec_rows = dec_in.reshape(row_count, model_width)
    mem_rows = memory.reshape(seq_count * mem_length, model_width)
    grad_rows = out_grad.reshape(row_count, model_width)
    *kept_one, after_self = attention_forward(
        True, dec_rows, no_source, dec_len, gain_full[0:1], w_self, backwards
    )
    if quarters:
        cross_quarter = lax.dynamic_index_in_dim(cross_weight, rep, 0, keepdims=False).astype(LOW)
        out_quarter = lax.dynamic_index_in_dim(
            ffn_out.reshape(4, part_rows // 4, model_width), rep, 0, keepdims=False
        ).astype(LOW)
        cross_rows_each, out_rows_each = cross_weight.shape[1], part_rows // 4
        cross_pieces = with_partner(across_reps(along_line(cross_quarter)))
        w_cross = assemble(
            hold(*cross_pieces, after_self)[:-1],
            where,
            (4, model_width, model_width),
            lambda ref, quarter, at: ref.at[quarter, pl.ds(at * cross_rows_each, cross_rows_each)],
            "assemble_cross",
        )
        out_line = along_line(after(out_quarter, w_self))
        out_near = across_reps(after(out_line, after_self))
    else:
        w_cross = lax.all_gather(cross_weight.astype(LOW), "fsdp", axis=1, tiled=True)
        w_out = lax.all_gather(ffn_out.astype(LOW), "fsdp", axis=0, tiled=True)
    *kept_two, after_cross = attention_forward(
        False, after_self, mem_rows, enc_len, gain_full[1:2], w_cross, no_bias
    )
    if quarters:
        out_near = list(hold(*out_near, after_cross)[:-1])
        w_out = assemble(
            with_partner(out_near),
            where,
            (hidden_width, model_width),
            lambda ref, quarter, at: ref.at[pl.ds((at * 4 + quarter) * out_rows_each, out_rows_each)],
            "assemble_out",
        )
    layer_out, grad_cross, grad_gate, grad_up, *out_near, gain_three = feed_forward_both(
        after_cross, grad_rows, dec_len, where, gain_full[2:3], w_in, w_out
    )
    scatter = lambda value, at: lax.psum_scatter(value, "fsdp", scatter_dimension=at, tiled=True)
    if quarters:
        own_gate = scatter(grad_gate, 0)
        out_near = out_near[:1] + [from_rep(out_near[way], way) for way in range(1, 4)]
    grad_self, grad_k_two, grad_v_two, gain_two, *cross_near, cross_far = attention_backward(
        False, after_self, mem_rows, grad_cross, enc_len, where, gain_full[1:2], w_cross, no_bias, kept_two,
        kept_two[3], kept_one[3],
    )
    if quarters:
        cross_far, grad_k_two, *out_near = hold(cross_far, grad_k_two, *out_near)
        pair = from_shard(cross_far, 1)
        memory_grad = memory_gradient(grad_k_two, grad_v_two, w_cross)
        memory_grad, pair, own_gate = hold(memory_grad, pair, own_gate)
        own_up = scatter(grad_up, 0)
        cross_chip = [add_up([cross_near[way], pair[way]]) for way in range(4)]
        grad_self, *cross_chip = hold(grad_self, *cross_chip)
        cross_near = cross_chip[:1] + [from_rep(cross_chip[way], way) for way in range(1, 4)]
    else:
        memory_grad = memory_gradient(grad_k_two, grad_v_two, w_cross)
    *grads_one, grad_self_weights, dist_grad = attention_backward(
        True, dec_rows, no_source, grad_self, dec_len, where, gain_full[0:1], w_self, by_distance, kept_one,
        no_source, no_source,
    )
    if quarters:
        dist_grad, own_up, grad_self_weights, *rest = hold(
            dist_grad, own_up, grad_self_weights, *grads_one, *cross_near, *out_near
        )
        grads_one, cross_near, out_near = rest[:3], rest[3:7], rest[7:]
        own_self = scatter(grad_self_weights, 1)
        out_sum = add_up(out_near)
        out_pair = from_shard(out_sum[1], 1)
        in_parts = rep_parts(jnp.stack([own_gate, own_up]).reshape(4, -1, hidden_width))
        line = jnp.concatenate([add_up(cross_near), add_up([out_sum[0], out_pair])], axis=1)
        line_parts = add_line(line)
        input_grad, gain_one = input_gradient(grads_one, w_self, dec_rows, grad_self, gain_full[0:1])
    else:
        input_grad, gain_one = input_gradient(grads_one, w_self, dec_rows, grad_self, gain_full[0:1])
    layer_out = layer_out.reshape(dec_in.shape)
    input_grad = input_grad.reshape(dec_in.shape)
    memory_grad = memory_grad.reshape(memory.shape)
    table_part = jnp.sum(bucket_mask[:, None, :] * dist_grad[None, :H, :], axis=2)
    small = jnp.concatenate(
        [gain_one.reshape(-1), gain_two.reshape(-1), gain_three.reshape(-1), table_part.reshape(-1)]
    )
    each = model_width // (LINE * LINE_CORES)
    if quarters:
        small = butterfly(small, from_rep, reps)
        in_near = rep_near(add_up(in_parts))
        both_near = rep_near(add_up(line_parts))
        self_parts = rep_parts(own_self.reshape(4, -1, model_width))
        rest = hold(small, *in_near, *both_near, *self_parts)
        small, in_near, both_near, self_parts = rest[0], rest[1:5], rest[5:9], rest[9:]
        own_in = rep_order(in_near).reshape(ffn_in.shape)
        both = rep_order(both_near)
        own_cross = both[:, :each]
        own_out = both[:, each + each // 3 :].reshape(ffn_out.shape)
        own_self = jnp.concatenate(
            [
                rep_order(rep_near(add_up(self_parts))).reshape(3, *self_weight.shape[1:]),
                both[:3, each : each + each // 3].reshape(1, *self_weight.shape[1:]),
            ]
        )
        over_shards = lambda vector: butterfly(vector, from_shard, shards)
    else:
        over_reps = lambda value: lax.psum(value, "rep")
        own_in = over_reps(scatter(jnp.stack([grad_gate, grad_up]), 1))
        grad_out = jnp.stack(out_near)
        grad_out = grad_out.transpose(2, 1, 0, 3, 4).reshape(hidden_width, model_width)
        own_out = over_reps(scatter(grad_out, 0))
        packed = jnp.stack([jnp.stack(cross_near), cross_far]).transpose(1, 2, 0, 3, 4)
        cross_parts = packed[..., :each, :].reshape(4, model_width, model_width)
        past = packed[:3, ..., each:, :].transpose(1, 2, 0, 3, 4).reshape(1, model_width, model_width)
        own_cross = over_reps(scatter(cross_parts, 1))
        own_self = over_reps(scatter(jnp.concatenate([grad_self_weights, past]), 1))
        over_shards = lambda vector: lax.psum(vector, "fsdp")
        small = lax.psum(small, "rep")

    grad_factor = 1.0 / math.sqrt(row_count * reps * shards)
    self_grad, cross_grad, ffn_in_grad, feedforward_output_gradient = [
        member.astype(WIDE) * grad_factor for member in (own_self, own_cross, own_in, own_out)
    ]
    groups = (
        (ffn_in_grad, ffn_in, in_rows, in_cols),
        (feedforward_output_gradient[None], ffn_out[None], out_rows[None], out_cols[None]),
        (cross_grad, cross_weight, cross_rows, cross_cols),
        (self_grad, self_weight, self_rows, self_cols),
    )
    sums = [factored_sums(gradient, weight, row_state) for gradient, weight, row_state, _ in groups]
    vectors = [member[1] for member in sums] + [jnp.sum(gains * gains, axis=1), small]
    total = over_shards(jnp.concatenate(vectors))
    totals = []
    for vector in vectors:
        totals.append(total[: vector.shape[0]])
        total = total[vector.shape[0] :]
    updated = [
        factored_update(gradient, weight, sums[at][0], col_state, totals[at])
        for at, (gradient, weight, _, col_state) in enumerate(groups)
    ]
    new_ffn_in, new_ffn_out, new_cross, new_self = [member[0] for member in updated]
    new_in_cols, new_out_cols, new_cross_cols, new_self_cols = [member[1] for member in updated]
    new_in_rows, new_out_rows, new_cross_rows, new_self_rows = [member[0] for member in sums]
    new_ffn_out, new_out_rows, new_out_cols = new_ffn_out[0], new_out_rows[0], new_out_cols[0]
    gain_square = totals[4] / model_width
    small = totals[5] * grad_factor
    gains_grad = lax.dynamic_slice_in_dim(
        small[: 3 * model_width].reshape(3, model_width), shard * gains.shape[1], gains.shape[1], axis=1
    )
    table_grad = small[3 * model_width :].reshape(BUCKETS, H)
    new_gains, new_gain_moment = plain_update(gains_grad, gains, gain_moment, gain_square[:, None])
    new_table, new_table_moment = plain_update(
        table_grad, table, table_moment, jnp.mean(table * table)
    )
    return (
        layer_out,
        input_grad,
        memory_grad,
        self_grad,
        cross_grad,
        ffn_in_grad,
        feedforward_output_gradient,
        gains_grad,
        table_grad,
        new_self,
        new_cross,
        new_ffn_in,
        new_ffn_out,
        new_gains,
        new_table,
        new_self_rows,
        new_self_cols,
        new_cross_rows,
        new_cross_cols,
        new_in_rows,
        new_in_cols,
        new_out_rows,
        new_out_cols,
        new_gain_moment,
        new_table_moment,
    )


def solution(mesh):
    placed = (
        P(("rep", "fsdp"), None, None),
        P(("rep", "fsdp"), None, None),
        P(("rep", "fsdp"), None, None),
        P(("rep", "fsdp")),
        P(("rep", "fsdp")),
        P(),
        P(None, "fsdp", None),
        P(None, "fsdp", None),
        P(None, "fsdp", None),
        P("fsdp", None),
        P(None, "fsdp"),
        P(),
        P(None, "fsdp"),
        P(),
        P(None, "fsdp"),
        P(),
        P(None, "fsdp"),
        P(),
        P("fsdp"),
        P(),
        P(None, "fsdp"),
        P(),
    )
    return jax.shard_map(
        per_device,
        mesh=mesh,
        in_specs=placed,
        out_specs=(
            P(("rep", "fsdp"), None, None),
            P(("rep", "fsdp"), None, None),
            P(("rep", "fsdp"), None, None),
            P(None, "fsdp", None),
            P(None, "fsdp", None),
            P(None, "fsdp", None),
            P("fsdp", None),
            P(None, "fsdp"),
            P(),
            P(None, "fsdp", None),
            P(None, "fsdp", None),
            P(None, "fsdp", None),
            P("fsdp", None),
            P(None, "fsdp"),
            P(),
            P(None, "fsdp"),
            P(),
            P(None, "fsdp"),
            P(),
            P(None, "fsdp"),
            P(),
            P("fsdp"),
            P(),
            P(None, "fsdp"),
            P(),
        ),
        check_vma=False,
    )
```

```python
import functools
import math

import jax
import jax.numpy as jnp
from jax import lax
from jax.experimental import pallas as pl
from jax.experimental.pallas import tpu as pltpu
from jax.sharding import PartitionSpec as P

H = 12
DH = 64
BUCKETS = 32
DECAY_RATE = 0.8
STEP_RATE = 0.2
TINY_TERM = 1e-30
PAIR = 2 * DH
GROUP = 4 * DH
HIDDEN = -1e30
MEGABYTE = 1024 * 1024
PEAK = 1.15e9
LINE = 4
LINE_CORES = 2
LOW = jnp.bfloat16
WIDE = jnp.float32


def nn(left, right):
    return lax.dot_general(left, right, (((1,), (0,)), ((), ())), preferred_element_type=WIDE)


def nt(left, right):
    return lax.dot_general(left, right, (((1,), (1,)), ((), ())), preferred_element_type=WIDE)


def tn(left, right):
    return lax.dot_general(left, right, (((0,), (0,)), ((), ())), preferred_element_type=WIDE)


def rms_rate(rows):
    return lax.rsqrt(jnp.mean(rows * rows, axis=-1, keepdims=True) + 1e-06)


def three_parts(column):
    high = column.astype(LOW)
    rest = column - high.astype(WIDE)
    middle = rest.astype(LOW)
    low = (rest - middle.astype(WIDE)).astype(LOW)
    return high, middle, low


def chunks(total, size):
    return [(at, min(size, total - at)) for at in range(0, total, size)]


def lanes(rows):
    return lax.broadcasted_iota(jnp.int32, (rows, PAIR), 1)


def own_lanes(rows, side):
    lane = lanes(rows)
    return (lane >= DH * side) & (lane < DH * (side + 1))


def key_extras(rows, side, length):
    lane = lanes(rows) - DH * (1 - side)
    dead = lax.broadcasted_iota(jnp.int32, (rows, PAIR), 0) >= length
    mask = jnp.where(dead, HIDDEN, 0.0)
    return jnp.where(
        (lane >= 0) & (lane < 3), 1.0, jnp.where(lane == 3, mask, 0.0)
    ).astype(LOW)


def row_extras(rows, side, column, last):
    lane = lanes(rows) - DH * (1 - side)
    high, middle, low = three_parts(column)
    wide = lambda part: jnp.broadcast_to(part.astype(WIDE), (rows, PAIR))
    return jnp.where(
        lane == 0,
        wide(high),
        jnp.where(
            lane == 1, wide(middle), jnp.where(lane == 2, wide(low), jnp.where(lane == 3, last, 0.0))
        ),
    ).astype(LOW)


def forward_body(causal, seq_count, length_ref, wave_ref, bias_ref, q_ref, k_ref, v_ref, mix_ref, total_ref, group):
    rows = q_ref.shape[0] // seq_count
    keys = k_ref.shape[0] // seq_count
    block = rows
    for pair in range(2):
        at = pair * PAIR
        for side in range(2):
            head = 2 * pair + side
            if causal:
                wave = wave_ref[pl.ds(group * 4 + head, 1), :]
                spread = pltpu.roll(
                    jnp.broadcast_to(wave, (rows, keys)), 0, 1, stride=1, stride_axis=0
                )
                row = lax.broadcasted_iota(jnp.int32, (rows, keys), 0)
                column = lax.broadcasted_iota(jnp.int32, (rows, keys), 1)
                bias_ref[side] = jnp.where(column <= row, spread, HIDDEN)
        for seq in range(seq_count):
            outs = []
            for side in range(2):
                own_q = own_lanes(rows, side)
                own_k = own_lanes(keys, side)
                query = jnp.where(
                    own_q,
                    q_ref[seq * rows : (seq + 1) * rows, at : at + PAIR],
                    (lanes(rows) == DH * (1 - side) + 3).astype(LOW),
                )
                key = jnp.where(
                    own_k,
                    k_ref[seq * keys : (seq + 1) * keys, at : at + PAIR],
                    key_extras(keys, side, length_ref[seq]),
                )
                value = jnp.where(
                    own_k,
                    v_ref[seq * keys : (seq + 1) * keys, at : at + PAIR],
                    jnp.ones((), LOW),
                )
                parts = []
                for start in range(0, rows, block):
                    span = start + block if causal else keys
                    scores = nt(query[start : start + block], key[:span])
                    if causal:
                        scores = scores + bias_ref[side, start : start + block, :span]
                    top = jnp.max(scores, axis=1, keepdims=True)
                    weight = jnp.exp(scores - top)
                    out = nn(weight.astype(LOW), value[:span])
                    total = out[:, DH * (1 - side) : DH * (1 - side) + 1]
                    parts.append(out * (1.0 / total))
                    spot = pl.ds(seq * rows + start, block)
                    lane = lanes(block)
                    seen = total_ref[spot, :] if (pair or side) else jnp.zeros((block, PAIR), WIDE)
                    total_ref[spot, :] = jnp.where(
                        lane == 2 * pair + side, top + jnp.log(total), seen
                    )
                outs.append(jnp.concatenate(parts, axis=0))
            mix_ref[seq * rows : (seq + 1) * rows, at : at + PAIR] = jnp.where(
                own_lanes(rows, 0), outs[0], outs[1]
            ).astype(LOW)


def forward_kernel(
    causal, seq_count, length_ref, x_ref, source_ref, gain_ref, wq_ref, wk_ref, wv_ref, wo_ref, wave_ref,
    q_ref, k_ref, v_ref, mix_ref, total_ref, after_ref, normed, bias,
):
    group = pl.program_id(0)

    @pl.when(group == 0)
    def _():
        for at, size in chunks(x_ref.shape[0], 256):
            rows = x_ref[at : at + size, :].astype(WIDE)
            normed[at : at + size, :] = (rows * rms_rate(rows) * gain_ref[...]).astype(LOW)
            after_ref[at : at + size, :] = rows

    source = normed if causal else source_ref
    q_ref[...] = nn(normed[...], wq_ref[...]).astype(LOW)
    k_ref[...] = nn(source[...], wk_ref[...]).astype(LOW)
    v_ref[...] = nn(source[...], wv_ref[...]).astype(LOW)
    forward_body(causal, seq_count, length_ref, wave_ref, bias, q_ref, k_ref, v_ref, mix_ref, total_ref, group)
    after_ref[...] += nn(mix_ref[...], wo_ref[...])


def weight_specs(width):
    across = lambda at: pl.BlockSpec((None, width, GROUP), lambda g, at=at: (at, 0, g))
    return [across(0), across(1), across(2), pl.BlockSpec((None, GROUP, width), lambda g: (3, g, 0))]


def whole(shape):
    return pl.BlockSpec(shape, lambda g: (0,) * len(shape), pipeline_mode=pl.Buffered(1))


def columns(rows):
    return pl.BlockSpec((rows, GROUP), lambda g: (0, g))


def attention_forward(causal, x, source, lengths, gain, weights, wave):
    row_count, width = x.shape
    seq_count = lengths.shape[0]
    source_rows = row_count if causal else source.shape[0]
    length = row_count // seq_count
    groups = width // GROUP
    low = lambda rows: jax.ShapeDtypeStruct((rows, width), LOW)
    args = [lengths, x, source, gain, weights, weights, weights, weights, wave]
    return pl.pallas_call(
        functools.partial(forward_kernel, causal, seq_count),
        grid=(groups,),
        in_specs=[
            pl.BlockSpec(memory_space=pltpu.SMEM),
            whole(x.shape),
            whole(source.shape),
            whole(gain.shape),
            *weight_specs(width),
            whole(wave.shape),
        ],
        out_specs=[
            columns(row_count),
            columns(source_rows),
            columns(source_rows),
            columns(row_count),
            pl.BlockSpec((None, row_count, PAIR), lambda g: (g, 0, 0)),
            whole((row_count, width)),
        ],
        out_shape=[
            low(row_count),
            low(source_rows),
            low(source_rows),
            low(row_count),
            jax.ShapeDtypeStruct((groups, row_count, PAIR), WIDE),
            jax.ShapeDtypeStruct((row_count, width), WIDE),
        ],
        scratch_shapes=[
            pltpu.VMEM((row_count, width), LOW),
            pltpu.VMEM((2, length, length) if causal else (1, 8, PAIR), WIDE),
        ],
        cost_estimate=pl.CostEstimate(flops=int(27 * PEAK), bytes_accessed=20 << 20, transcendentals=0),
        compiler_params=pltpu.CompilerParams(vmem_limit_bytes=60 * MEGABYTE),
        name="self_forward" if causal else "cross_forward",
    )(*args)


def gelu_parts(gate):
    root = 0.7978845608028654
    square = gate * gate
    inner = jnp.tanh(root * gate * (1.0 + 0.044715 * square))
    half = 0.5 * (1.0 + inner)
    value = gate * half
    slope = half + 0.5 * gate * (1.0 - inner * inner) * (root * (1.0 + 3 * 0.044715 * square))
    return value, slope


def rms_back(rows, gain, grad):
    rate = rms_rate(rows)
    scaled = rows * rate
    low = grad * gain
    grad_rows = rate * (low - scaled * jnp.mean(scaled * low, axis=-1, keepdims=True))
    return grad_rows, jnp.sum(grad * scaled, axis=0, keepdims=True)


def shard_slot(where_ref, shard):
    return (shard % LINE_CORES) ^ where_ref[2], lax.rem(shard // LINE_CORES - where_ref[1] + LINE, LINE)


def feed_kernel(
    seq_count, length_ref, where_ref, after_ref, out_grad_ref, gain_ref, wg_ref, wu_ref, wd_ref,
    layer_ref, grad_cross_ref, dwg_ref, dwu_ref, *refs,
):
    near_refs = refs[:4]
    dgain_ref, normed, normed_t, down, out_total, grad_total, cut = refs[4:]
    step = pl.program_id(0)
    row_count = after_ref.shape[0]
    length = row_count // seq_count

    def live(at, size):
        position = lax.broadcasted_iota(jnp.int32, (size, 1), 0) + (at % length)
        return (position < length_ref[at // length]).astype(WIDE)

    @pl.when(step == 0)
    def _():
        for at, size in chunks(row_count, 256):
            rows = after_ref[at : at + size, :]
            low = (rows * rms_rate(rows) * gain_ref[...]).astype(LOW)
            normed[at : at + size, :] = low
            normed_t[:, at : at + size] = low.T
            down[at : at + size, :] = (
                out_grad_ref[at : at + size, :].astype(WIDE) * live(at, size)
            ).astype(LOW)
            out_total[at : at + size, :] = rows
            grad_total[at : at + size, :] = jnp.zeros((size, rows.shape[1]), WIDE)

    gate = nn(normed[...], wg_ref[...])
    up = nn(normed[...], wu_ref[...])
    value, slope = gelu_parts(gate)
    hidden = (value * up).astype(LOW)
    out_total[...] += nn(hidden, wd_ref[...])
    grad_hidden = nt(down[...], wd_ref[...])
    cut[...] = tn(hidden, down[...]).astype(LOW).reshape(cut.shape)
    core, hop = shard_slot(where_ref, step)
    for way in range(4):
        near_refs[way][core, hop] = cut[where_ref[0] ^ way]
    grad_gate = (grad_hidden * up * slope).astype(LOW)
    grad_up = (grad_hidden * value).astype(LOW)
    dwg_ref[...] = nn(normed_t[...], grad_gate).astype(LOW)
    dwu_ref[...] = nn(normed_t[...], grad_up).astype(LOW)
    grad_total[...] += nt(grad_gate, wg_ref[...]) + nt(grad_up, wu_ref[...])

    @pl.when(step == pl.num_programs(0) - 1)
    def _():
        dgain = jnp.zeros(dgain_ref.shape, WIDE)
        for at, size in chunks(row_count, 256):
            part = slice(at, at + size)
            layer_ref[part, :] = (out_total[part, :] * live(at, size)).astype(LOW)
            grad_rows, gain_part = rms_back(after_ref[part, :], gain_ref[...], grad_total[part, :])
            dgain = dgain + gain_part
            grad_cross_ref[part, :] = (
                out_grad_ref[part, :].astype(WIDE) * live(at, size) + grad_rows
            )
        dgain_ref[...] = dgain


def feed_forward_both(after, out_grad, lengths, where, gain, w_in, w_out):
    row_count, width = after.shape
    hidden = w_out.shape[0]
    block = hidden // (LINE * LINE_CORES)
    seq_count = lengths.shape[0]
    wide = pl.BlockSpec((None, width, block), lambda g: (0, 0, g))
    wide_up = pl.BlockSpec((None, width, block), lambda g: (1, 0, g))
    tall = pl.BlockSpec((block, width), lambda g: (g, 0))
    flat = pl.BlockSpec((width, block), lambda g: (0, g))
    near = (LINE_CORES, LINE, block // 4, width)
    return pl.pallas_call(
        functools.partial(feed_kernel, seq_count),
        grid=(hidden // block,),
        in_specs=[
            pl.BlockSpec(memory_space=pltpu.SMEM),
            pl.BlockSpec(memory_space=pltpu.SMEM),
            whole(after.shape),
            whole(out_grad.shape),
            whole(gain.shape),
            wide,
            wide_up,
            tall,
        ],
        out_specs=[whole(after.shape), whole(after.shape), flat, flat, *[whole(near)] * 4, whole((1, width))],
        out_shape=[
            jax.ShapeDtypeStruct((row_count, width), LOW),
            jax.ShapeDtypeStruct((row_count, width), WIDE),
            jax.ShapeDtypeStruct((width, hidden), LOW),
            jax.ShapeDtypeStruct((width, hidden), LOW),
            *[jax.ShapeDtypeStruct(near, LOW)] * 4,
            jax.ShapeDtypeStruct((1, width), WIDE),
        ],
        scratch_shapes=[
            pltpu.VMEM((row_count, width), LOW),
            pltpu.VMEM((width, row_count), LOW),
            pltpu.VMEM((row_count, width), LOW),
            pltpu.VMEM((row_count, width), WIDE),
            pltpu.VMEM((row_count, width), WIDE),
            pltpu.VMEM((4, block // 4, width), LOW),
        ],
        cost_estimate=pl.CostEstimate(flops=int(46 * PEAK), bytes_accessed=40 << 20, transcendentals=0),
        compiler_params=pltpu.CompilerParams(vmem_limit_bytes=60 * MEGABYTE),
        name="feed_forward_both",
    )(lengths, where, after, out_grad, gain, w_in, w_in, w_out)


def backward_kernel(
    causal, seq_count, length_ref, where_ref, x_ref, source_ref, grad_ref, gain_ref, wq_ref, wo_ref, wave_ref,
    q_ref, k_ref, v_ref, mix_ref, total_ref, mix_all_ref, mix_past_ref, *refs,
):
    if causal:
        gq, gk_out_ref, gv_out_ref, dw_ref, dist_ref = refs[:5]
        normed_t, branch, grad_mix, bias, score_sum = refs[5:]
        source_t = normed_t
    else:
        grad_x_ref, gk_out_ref, gv_out_ref, dgain_ref = refs[:4]
        near_refs, far_ref = refs[4:8], refs[8]
        normed_t, branch, grad_mix, gq, source_t, mix_t, grad_total, dw_ref, past = refs[9:]
    group = pl.program_id(0)
    row_count = x_ref.shape[0]
    rows = q_ref.shape[0] // seq_count
    keys = k_ref.shape[0] // seq_count
    block = rows

    @pl.when(group == 0)
    def _():
        for at, size in chunks(row_count, 256):
            value = x_ref[at : at + size, :].astype(WIDE)
            low = (value * rms_rate(value) * gain_ref[...]).astype(LOW)
            normed_t[:, at : at + size] = low.T
            branch[at : at + size, :] = grad_ref[at : at + size, :].astype(LOW)
            if not causal:
                mix_t[:, at : at + size] = mix_all_ref[at : at + size, :].T
                grad_total[at : at + size, :] = jnp.zeros((size, value.shape[1]), WIDE)
        if not causal:
            for at, size in chunks(source_ref.shape[0], 256):
                source_t[:, at : at + size] = source_ref[at : at + size, :].T

    grad_mix[...] = nt(branch[...], wo_ref[...]).astype(LOW)
    if not causal:
        across = pl.ds(pl.multiple_of(group * GROUP, GROUP), GROUP)
        put = lambda at, value: dw_ref.__setitem__(at, value.astype(LOW).reshape(dw_ref.shape[1:]))
        put(3, nn(mix_t[...], branch[:, across]))

    for pair in range(2):
        at = pair * PAIR
        if causal:
            for side in range(2):
                head = 2 * pair + side
                wave = wave_ref[pl.ds(group * 4 + head, 1), :]
                spread = pltpu.roll(
                    jnp.broadcast_to(wave, (keys, rows)), 0, 1, stride=1, stride_axis=0
                )
                row = lax.broadcasted_iota(jnp.int32, (keys, rows), 0)
                column = lax.broadcasted_iota(jnp.int32, (keys, rows), 1)
                bias[side] = jnp.where(column >= row, spread, HIDDEN)
        for seq in range(seq_count):
            span_q = slice(seq * rows, (seq + 1) * rows)
            span_k = slice(seq * keys, (seq + 1) * keys)
            sides = []
            for side in range(2):
                head = 2 * pair + side
                own_q = own_lanes(rows, side)
                own_k = own_lanes(keys, side)
                total = jnp.sum(
                    jnp.where(lanes(rows) == head, total_ref[span_q, :], 0.0), axis=1, keepdims=True
                )
                grad_low = grad_mix[span_q, at : at + PAIR]
                product = grad_low.astype(WIDE) * mix_ref[span_q, at : at + PAIR].astype(WIDE)
                delta = jnp.sum(jnp.where(own_q, product, 0.0), axis=1, keepdims=True)
                query = jnp.where(
                    own_q, q_ref[span_q, at : at + PAIR], row_extras(rows, side, -total, 1.0)
                )
                grad_out = jnp.where(own_q, grad_low, row_extras(rows, side, -delta, 0.0))
                key = jnp.where(
                    own_k,
                    k_ref[span_k, at : at + PAIR],
                    key_extras(keys, side, length_ref[seq]),
                )
                value = jnp.where(own_k, v_ref[span_k, at : at + PAIR], jnp.ones((), LOW))
                grad_query = []
                grad_key = None
                grad_value = None
                for start in range(0, rows, block):
                    span = start + block if causal else keys
                    scores = nt(key[:span], query[start : start + block])
                    if causal:
                        scores = scores + bias[side, :span, start : start + block]
                    weight = jnp.exp(scores)
                    low = weight.astype(LOW)
                    grad_weight = nt(value[:span], grad_out[start : start + block])
                    grad_score = (weight * grad_weight).astype(LOW)
                    if causal:
                        if seq == 0:
                            score_sum[side, :span, start : start + block] = grad_score.astype(WIDE)
                        else:
                            score_sum[side, :span, start : start + block] += grad_score.astype(WIDE)
                    key_part = nn(grad_score, query[start : start + block])
                    value_part = nn(low, grad_out[start : start + block])
                    grad_query.append(tn(grad_score, key[:span]))
                    if causal and start == 0 and rows > block:
                        rest = jnp.zeros((keys - span, PAIR), WIDE)
                        key_part = jnp.concatenate([key_part, rest], axis=0)
                        value_part = jnp.concatenate([value_part, rest], axis=0)
                    grad_key = key_part if grad_key is None else grad_key + key_part
                    grad_value = value_part if grad_value is None else grad_value + value_part
                sides.append((jnp.concatenate(grad_query, axis=0), grad_key, grad_value))
            pick_q = own_lanes(rows, 0)
            pick_k = own_lanes(keys, 0)
            gq[span_q, at : at + PAIR] = jnp.where(pick_q, sides[0][0], sides[1][0]).astype(LOW)
            gk_out_ref[span_k, at : at + PAIR] = jnp.where(pick_k, sides[0][1], sides[1][1]).astype(LOW)
            gv_out_ref[span_k, at : at + PAIR] = jnp.where(pick_k, sides[0][2], sides[1][2]).astype(LOW)
        if causal:
            for side in range(2):
                head = 2 * pair + side
                row = lax.broadcasted_iota(jnp.int32, (keys, rows), 0)
                column = lax.broadcasted_iota(jnp.int32, (keys, rows), 1)
                held = jnp.where(column >= row, score_sum[side], 0.0)
                while held.shape[0] > 1:
                    half = held.shape[0] // 2
                    held = held[:half] + pltpu.roll(held[half:], rows - half, 1)
                dist_ref[pl.ds(group * 4 + head, 1), :] = held

    if causal:
        dw_ref[0] = nn(normed_t[...], gq[...]).astype(LOW)
        dw_ref[1] = nn(source_t[...], gk_out_ref[...]).astype(LOW)
        dw_ref[2] = nn(source_t[...], gv_out_ref[...]).astype(LOW)
        return
    put(0, nn(normed_t[...], gq[...]))
    put(1, nn(source_t[...], gk_out_ref[...]))
    put(2, nn(source_t[...], gv_out_ref[...]))
    grad_total[...] += nt(gq[...], wq_ref[...])
    rep, line, core = where_ref[0], where_ref[1], where_ref[2]
    held = dw_ref.shape[2]
    slots = []
    for way in range(4):
        for hop in range(LINE):
            at = lax.rem(line + hop, LINE) * LINE_CORES
            slots.append((near_refs[way].at[hop], rep ^ way, at + core))
            slots.append((far_ref.at[way, hop], rep ^ way, at + (core ^ 1)))
    for slot, quarter, shard in slots:
        slot[0:held, across] = dw_ref[quarter, shard]

    @pl.when(group == pl.num_programs(0) - 1)
    def _():
        dgain = jnp.zeros(dgain_ref.shape, WIDE)
        for at, size in chunks(row_count, 256):
            part = slice(at, at + size)
            grad_rows, gain_part = rms_back(
                x_ref[part, :].astype(WIDE), gain_ref[...], grad_total[part, :]
            )
            dgain = dgain + gain_part
            grad_rows = grad_ref[part, :] + grad_rows
            grad_x_ref[part, :] = grad_rows
            branch[part, :] = grad_rows.astype(LOW)
            mix_t[:, part] = mix_past_ref[part, :].T
        dgain_ref[...] = dgain
        thirds = nn(mix_t[...], branch[...]).astype(LOW)
        past[:, 0:3] = thirds.reshape(past.shape[0], 3, *past.shape[2:])
        past[:, 3] = jnp.zeros_like(past[:, 3])
        for slot, quarter, shard in slots:
            slot[held:, :] = past[shard, quarter]


def attention_backward(causal, x, source, grad, lengths, where, gain, weights, wave, kept, mix, past):
    row_count, width = x.shape
    seq_count = lengths.shape[0]
    source_rows = row_count if causal else source.shape[0]
    length = row_count // seq_count
    groups = width // GROUP
    low = lambda rows: jax.ShapeDtypeStruct((rows, width), LOW)
    if causal:
        out_specs = [
            columns(row_count), columns(source_rows), columns(source_rows),
            pl.BlockSpec((3, width, GROUP), lambda g: (0, 0, g)), whole(wave.shape),
        ]
        out_shape = [
            low(row_count), low(source_rows), low(source_rows),
            jax.ShapeDtypeStruct((3, width, width), LOW), jax.ShapeDtypeStruct(wave.shape, WIDE),
        ]
        scratch = [pltpu.VMEM((2, length, length), WIDE)] * 2
    else:
        shards = LINE * LINE_CORES
        each, third = width // shards, width // shards // 3
        near = (LINE, each + third, width)
        out_specs = [
            whole((row_count, width)), columns(source_rows), columns(source_rows), whole((1, width)),
            *[whole(near)] * 4, whole((4, *near)),
        ]
        out_shape = [
            jax.ShapeDtypeStruct((row_count, width), WIDE), low(source_rows), low(source_rows),
            jax.ShapeDtypeStruct((1, width), WIDE), *[jax.ShapeDtypeStruct(near, LOW)] * 4,
            jax.ShapeDtypeStruct((4, *near), LOW),
        ]
        scratch = [
            pltpu.VMEM((row_count, GROUP), LOW),
            pltpu.VMEM((width, source_rows), LOW),
            pltpu.VMEM((width, row_count), LOW),
            pltpu.VMEM((row_count, width), WIDE),
            pltpu.VMEM((4, shards, each, GROUP), LOW),
            pltpu.VMEM((shards, 4, third, width), LOW),
        ]
    return pl.pallas_call(
        functools.partial(backward_kernel, causal, seq_count),
        grid=(groups,),
        in_specs=[
            pl.BlockSpec(memory_space=pltpu.SMEM),
            pl.BlockSpec(memory_space=pltpu.SMEM),
            whole(x.shape),
            whole(source.shape),
            whole(grad.shape),
            whole(gain.shape),
            weight_specs(width)[0],
            weight_specs(width)[3],
            whole(wave.shape),
            columns(row_count),
            columns(source_rows),
            columns(source_rows),
            columns(row_count),
            pl.BlockSpec((None, row_count, PAIR), lambda g: (g, 0, 0)),
            whole(mix.shape),
            whole(past.shape),
        ],
        out_specs=out_specs,
        out_shape=out_shape,
        scratch_shapes=[
            pltpu.VMEM((width, row_count), LOW),
            pltpu.VMEM((row_count, width), LOW),
            pltpu.VMEM((row_count, GROUP), LOW),
            *scratch,
        ],
        cost_estimate=pl.CostEstimate(flops=int(45 * PEAK), bytes_accessed=40 << 20, transcendentals=0),
        compiler_params=pltpu.CompilerParams(vmem_limit_bytes=60 * MEGABYTE),
        name="self_backward" if causal else "cross_backward",
    )(lengths, where, x, source, grad, gain, weights, weights, wave, *kept, mix, past)


def input_kernel(gq_ref, gk_ref, gv_ref, wq_ref, wk_ref, wv_ref, x_ref, grad_ref, gain_ref, out_ref, dgain_ref):
    total = nt(gq_ref[...], wq_ref[...]) + nt(gk_ref[...], wk_ref[...]) + nt(gv_ref[...], wv_ref[...])
    grad_rows, dgain = rms_back(x_ref[...].astype(WIDE), gain_ref[...], total)
    out_ref[...] = grad_ref[...] + grad_rows

    @pl.when(pl.program_id(0) == 0)
    def _():
        dgain_ref[...] = jnp.zeros_like(dgain_ref)

    dgain_ref[...] += dgain


def input_gradient(grads, weights, x, grad, gain):
    rows, width = x.shape
    block = 256
    rowwise = pl.BlockSpec((block, width), lambda g: (g, 0))
    matrix = lambda at: pl.BlockSpec((None, width, width), lambda g: (at, 0, 0))
    return pl.pallas_call(
        input_kernel,
        grid=(rows // block,),
        in_specs=[rowwise, rowwise, rowwise, matrix(0), matrix(1), matrix(2), rowwise, rowwise, whole((1, width))],
        out_specs=[rowwise, whole((1, width))],
        out_shape=[jax.ShapeDtypeStruct((rows, width), WIDE), jax.ShapeDtypeStruct((1, width), WIDE)],
        cost_estimate=pl.CostEstimate(flops=int(8 * PEAK), bytes_accessed=12 << 20, transcendentals=0),
        compiler_params=pltpu.CompilerParams(vmem_limit_bytes=60 * MEGABYTE),
        name="input_gradient",
    )(*grads, weights, weights, weights, x, grad, gain)


def memory_kernel(gk_ref, gv_ref, wk_ref, wv_ref, out_ref):
    out_ref[...] = nt(gk_ref[...], wk_ref[...]) + nt(gv_ref[...], wv_ref[...])


def memory_gradient(grad_key, grad_value, weights):
    rows, width = grad_key.shape
    block = 256
    rowwise = pl.BlockSpec((block, width), lambda g: (g, 0))
    matrix = lambda at: pl.BlockSpec((None, width, width), lambda g: (at, 0, 0))
    return pl.pallas_call(
        memory_kernel,
        grid=(rows // block,),
        in_specs=[rowwise, rowwise, matrix(1), matrix(2)],
        out_specs=rowwise,
        out_shape=jax.ShapeDtypeStruct((rows, width), WIDE),
        cost_estimate=pl.CostEstimate(flops=int(7 * PEAK), bytes_accessed=10 << 20, transcendentals=0),
        compiler_params=pltpu.CompilerParams(vmem_limit_bytes=60 * MEGABYTE),
        name="memory_gradient",
    )(grad_key, grad_value, weights, weights)


def flat_permute(value, target):
    reps, shards = lax.axis_size("rep"), lax.axis_size("fsdp")
    pairs = []
    for rep in range(reps):
        for shard in range(shards):
            to_rep, to_shard = target(rep, shard)
            pairs.append((rep * shards + shard, to_rep * shards + to_shard))
    return lax.ppermute(value, ("rep", "fsdp"), pairs)


def from_rep(value, way):
    return flat_permute(value, lambda rep, shard: (rep ^ way, shard))


def from_shard(value, way):
    return flat_permute(value, lambda rep, shard: (rep, shard ^ way))


def from_line(value, hops):
    shards = lax.axis_size("fsdp")
    return flat_permute(value, lambda rep, shard: (rep, (shard + 2 * hops) % shards))


def along_line(piece):
    hops = lax.axis_size("fsdp") // 2
    return jnp.stack([piece] + [from_line(piece, hop) for hop in range(1, hops)])


def across_reps(line):
    return [line] + [from_rep(line, way) for way in range(1, 4)]


def with_partner(parts):
    return parts + [from_shard(part, 1) for part in parts]


def add_line(parts):
    return [parts[0]] + [from_line(parts[hop], hop) for hop in range(1, LINE)]


def assemble_kernel(place, hops, where_ref, *refs):
    parts, out_ref, sems = refs[:8], refs[8], refs[9]
    rep, line, core = where_ref[0], where_ref[1], where_ref[2]
    copies = []
    for other in range(2):
        for way in range(4):
            for hop in range(hops):
                shard = lax.rem(line - hop + hops, hops) * 2 + (core ^ other)
                copies.append(
                    pltpu.make_async_copy(
                        parts[4 * other + way].at[hop],
                        place(out_ref, rep ^ way, shard),
                        sems.at[len(copies)],
                    )
                )
    for copy in copies:
        copy.start()
    for copy in copies:
        copy.wait()


def assemble(parts, where, shape, place, name):
    hops = parts[0].shape[0]
    return pl.pallas_call(
        functools.partial(assemble_kernel, place, hops),
        in_specs=[pl.BlockSpec(memory_space=pltpu.SMEM)] + [pl.BlockSpec(memory_space=pl.ANY)] * 8,
        out_specs=pl.BlockSpec(memory_space=pltpu.VMEM),
        out_shape=jax.ShapeDtypeStruct(shape, LOW),
        scratch_shapes=[pltpu.SemaphoreType.DMA((8 * hops,))],
        cost_estimate=pl.CostEstimate(flops=int(4 * PEAK), bytes_accessed=8 << 20, transcendentals=0),
        compiler_params=pltpu.CompilerParams(vmem_limit_bytes=60 * MEGABYTE),
        name=name,
    )(where, *parts)


def rep_parts(parts, axis):
    rep = lax.axis_index("rep")
    pick = lambda at: lax.dynamic_index_in_dim(parts, at, axis, keepdims=False)
    return [pick(rep)] + [from_rep(pick(rep ^ way), way) for way in range(1, 4)]


def add_up(parts):
    return sum(part.astype(WIDE) for part in parts).astype(LOW)


def rep_near(piece):
    return [piece] + [from_rep(piece, way) for way in range(1, 4)]


def rep_order(near):
    rep = lax.axis_index("rep")
    return [lax.select_n(rep, *[near[at ^ own] for own in range(4)]) for at in range(4)]


def hold(*values):
    return lax.optimization_barrier(values)


def butterfly(vector, move, size):
    way = 1
    while way < size:
        vector = vector + move(vector, way)
        way *= 2
    return vector


def after(value, *earlier):
    return lax.optimization_barrier((value, *earlier))[0]


def row_moments(gradient, row_state):
    squares = gradient * gradient + TINY_TERM
    return DECAY_RATE * row_state + (1.0 - DECAY_RATE) * jnp.mean(squares, axis=-1)


def factored_sums(gradient, row_state):
    squares = gradient * gradient + TINY_TERM
    return jnp.sum(squares, axis=1), jnp.sum(row_moments(gradient, row_state), axis=1)


def pack(values):
    return jnp.concatenate([value.reshape(-1) for value in values])


def unpack(vector, values):
    out = []
    for value in values:
        out.append(vector[: value.size].reshape(value.shape))
        vector = vector[value.size :]
    return out


def factored_update(gradient, weight, row_moment, col_state, col_sum, row_sum, square):
    count, rows, cols = weight.shape
    whole_rows = rows * lax.axis_size("fsdp")
    col_moment = DECAY_RATE * col_state + (1.0 - DECAY_RATE) * col_sum / whole_rows
    scale = lax.rsqrt(row_moment / (row_sum[:, None] / whole_rows))
    step = STEP_RATE * jnp.sqrt(square / (whole_rows * cols) + 1e-06)
    direction = gradient * scale[:, :, None] * lax.rsqrt(col_moment)[:, None, :]
    return weight - step[:, None, None] * direction, col_moment


def plain_update(gradient, weight, moment, square):
    moment = DECAY_RATE * moment + (1.0 - DECAY_RATE) * (gradient * gradient + TINY_TERM)
    step = STEP_RATE * jnp.sqrt(square + 1e-06)
    return weight - step * gradient * lax.rsqrt(moment), moment


def per_device(
    dec_in,
    memory,
    out_grad,
    dec_len,
    enc_len,
    buckets,
    self_weight,
    cross_weight,
    ffn_in,
    ffn_out,
    gains,
    table,
    self_rows,
    self_cols,
    cross_rows,
    cross_cols,
    in_rows,
    in_cols,
    out_rows,
    out_cols,
    gain_moment,
    table_moment,
):
    seq_count, seq_length, model_width = dec_in.shape
    mem_length = memory.shape[1]
    row_count = seq_count * seq_length
    hidden_width = ffn_in.shape[2]
    reps, shards = lax.axis_size("rep"), lax.axis_size("fsdp")
    rep, shard = lax.axis_index("rep"), lax.axis_index("fsdp")
    quarters = reps == 4 and shards == 8
    part_rows = hidden_width // shards
    where = jnp.stack([rep, shard // 2, shard % 2]).astype(jnp.int32) * int(quarters)
    w_self = lax.all_gather(self_weight.astype(LOW), "fsdp", axis=1, tiled=True)
    gain_full = lax.all_gather(gains.astype(LOW), "fsdp", axis=1, tiled=True).astype(WIDE)
    w_in = lax.all_gather(ffn_in.astype(LOW), "fsdp", axis=1, tiled=True)

    bucket_mask = (buckets[None, :] == jnp.arange(BUCKETS)[:, None]).astype(WIDE)
    by_distance = jnp.sum(table.T[:, :, None] * bucket_mask[None], axis=1)
    by_distance = jnp.pad(by_distance, ((0, 16 - H), (0, 0)))
    backwards = jnp.roll(by_distance[:, ::-1], 1, axis=1)
    no_bias = jnp.zeros((8, PAIR), WIDE)
    no_source = jnp.zeros((16, PAIR), LOW)

    dec_rows = dec_in.reshape(row_count, model_width)
    mem_rows = memory.reshape(seq_count * mem_length, model_width)
    grad_rows = out_grad.reshape(row_count, model_width)
    *kept_one, after_self = attention_forward(
        True, dec_rows, no_source, dec_len, gain_full[0:1], w_self, backwards
    )
    if quarters:
        cross_quarter = lax.dynamic_index_in_dim(cross_weight, rep, 0, keepdims=False).astype(LOW)
        out_quarter = lax.dynamic_index_in_dim(
            ffn_out.reshape(4, part_rows // 4, model_width), rep, 0, keepdims=False
        ).astype(LOW)
        cross_rows_each, out_rows_each = cross_weight.shape[1], part_rows // 4
        cross_pieces = with_partner(across_reps(along_line(cross_quarter)))
        w_cross = assemble(
            hold(*cross_pieces, after_self)[:-1],
            where,
            (4, model_width, model_width),
            lambda ref, quarter, at: ref.at[quarter, pl.ds(at * cross_rows_each, cross_rows_each)],
            "assemble_cross",
        )
        out_line = along_line(after(out_quarter, w_self))
        out_near = across_reps(after(out_line, after_self))
    else:
        w_cross = lax.all_gather(cross_weight.astype(LOW), "fsdp", axis=1, tiled=True)
        w_out = lax.all_gather(ffn_out.astype(LOW), "fsdp", axis=0, tiled=True)
    *kept_two, after_cross = attention_forward(
        False, after_self, mem_rows, enc_len, gain_full[1:2], w_cross, no_bias
    )
    if quarters:
        out_near = list(hold(*out_near, after_cross)[:-1])
        w_out = assemble(
            with_partner(out_near),
            where,
            (hidden_width, model_width),
            lambda ref, quarter, at: ref.at[pl.ds((at * 4 + quarter) * out_rows_each, out_rows_each)],
            "assemble_out",
        )
    layer_out, grad_cross, grad_gate, grad_up, *out_near, gain_three = feed_forward_both(
        after_cross, grad_rows, dec_len, where, gain_full[2:3], w_in, w_out
    )
    scatter = lambda value, at: lax.psum_scatter(value, "fsdp", scatter_dimension=at, tiled=True)
    if quarters:
        own_gate = scatter(grad_gate, 0)
        out_near = out_near[:1] + [from_rep(out_near[way], way) for way in range(1, 4)]
    grad_self, grad_k_two, grad_v_two, gain_two, *cross_near, cross_far = attention_backward(
        False, after_self, mem_rows, grad_cross, enc_len, where, gain_full[1:2], w_cross, no_bias, kept_two,
        kept_two[3], kept_one[3],
    )
    if quarters:
        cross_far, grad_k_two, *out_near = hold(cross_far, grad_k_two, *out_near)
        pair = from_shard(cross_far, 1)
        memory_grad = memory_gradient(grad_k_two, grad_v_two, w_cross)
        memory_grad, pair, own_gate = hold(memory_grad, pair, own_gate)
        own_up = scatter(grad_up, 0)
        cross_chip = [add_up([cross_near[way], pair[way]]) for way in range(4)]
        grad_self, *cross_chip = hold(grad_self, *cross_chip)
        cross_near = cross_chip[:1] + [from_rep(cross_chip[way], way) for way in range(1, 4)]
    else:
        memory_grad = memory_gradient(grad_k_two, grad_v_two, w_cross)
    *grads_one, grad_self_weights, dist_grad = attention_backward(
        True, dec_rows, no_source, grad_self, dec_len, where, gain_full[0:1], w_self, by_distance, kept_one,
        no_source, no_source,
    )
    if quarters:
        dist_grad, own_up, grad_self_weights, *rest = hold(
            dist_grad, own_up, grad_self_weights, *grads_one, *cross_near, *out_near
        )
        grads_one, cross_near, out_near = rest[:3], rest[3:7], rest[7:]
        own_self = scatter(grad_self_weights, 1)
        out_sum = add_up(out_near)
        out_pair = from_shard(out_sum[1], 1)
        in_parts = rep_parts(jnp.stack([own_gate, own_up]).reshape(2, 4, -1, hidden_width), 1)
        line = jnp.concatenate([add_up(cross_near), add_up([out_sum[0], out_pair])], axis=1)
        line_parts = add_line(line)
        input_grad, gain_one = input_gradient(grads_one, w_self, dec_rows, grad_self, gain_full[0:1])
    else:
        input_grad, gain_one = input_gradient(grads_one, w_self, dec_rows, grad_self, gain_full[0:1])
    layer_out = layer_out.reshape(dec_in.shape)
    input_grad = input_grad.reshape(dec_in.shape)
    memory_grad = memory_grad.reshape(memory.shape)
    table_part = jnp.sum(bucket_mask[:, None, :] * dist_grad[None, :H, :], axis=2)
    small = jnp.concatenate(
        [gain_one.reshape(-1), gain_two.reshape(-1), gain_three.reshape(-1), table_part.reshape(-1)]
    )
    grad_factor = 1.0 / math.sqrt(row_count * reps * shards)
    wide = lambda value: value.astype(WIDE) * grad_factor
    each = model_width // (LINE * LINE_CORES)
    small = small * grad_factor
    square = lambda value: jnp.sum(value * value, axis=(1, 2))
    squares = (
        square(ffn_in), square(ffn_out[None]), square(cross_weight), square(self_weight),
        jnp.sum(gains * gains, axis=1),
    )
    if quarters:
        quarter_of = lambda value, axis: lax.dynamic_index_in_dim(value, rep, axis, keepdims=False)
        third = each // 3
        in_piece, line_piece = add_up(in_parts), add_up(line_parts)
        in_near, line_near = rep_near(in_piece), rep_near(line_piece)
        cross_piece, past_piece, out_piece = (
            line_piece[:each], line_piece[each : each + third], line_piece[each + third :],
        )
        in_sums = factored_sums(
            wide(in_piece), quarter_of(in_rows.reshape(2, 4, -1), 1)
        )
        out_sums = factored_sums(wide(out_piece)[None], quarter_of(out_rows.reshape(4, -1), 0)[None])
        mine = jnp.arange(4) == rep
        cross_sums = factored_sums(wide(cross_piece)[None], quarter_of(cross_rows, 0)[None])
        cross_sums = [
            jnp.where(mine.reshape((4,) + (1,) * (member.ndim - 1)), member, 0.0) for member in cross_sums
        ]
        past_rows = lax.dynamic_slice_in_dim(self_rows[3], jnp.minimum(rep, 2) * third, third)
        past_sums = factored_sums(wide(past_piece)[None], past_rows[None])
        past_sums = [jnp.where(rep < 3, member, 0.0) for member in past_sums]
        early = [*in_sums, *out_sums, *cross_sums, *past_sums, *[member / reps for member in squares], small]
        over_all = lambda vector: butterfly(butterfly(vector, from_rep, reps), from_shard, shards)
        in_sums, out_sums, cross_sums, past_sums, rest = (
            lambda found: (found[0:2], found[2:4], found[4:6], found[6:8], found[8:])
        )(unpack(over_all(pack(early)), early))
        *squares, small = rest
        self_parts = rep_parts(own_self.reshape(3, 4, -1, model_width), 1)
        self_piece = add_up(self_parts)
        self_near = rep_near(self_piece)
        late = factored_sums(wide(self_piece), quarter_of(self_rows[:3].reshape(3, 4, -1), 1))
        late = unpack(over_all(pack(late)), late)
        self_sums = [jnp.concatenate(members) for members in zip(late, past_sums)]
        line_all = rep_order(line_near)
        own_in = jnp.stack(rep_order(in_near), axis=1).reshape(ffn_in.shape)
        own_cross = jnp.stack([member[:each] for member in line_all])
        own_out = jnp.concatenate([member[each + third :] for member in line_all])
        own_self = jnp.stack(rep_order(self_near), axis=1).reshape(3, *self_weight.shape[1:])
        own_past = jnp.concatenate([member[each : each + third] for member in line_all[:3]])
        own_self = jnp.concatenate([own_self, own_past[None]])
    else:
        over_reps = lambda value: lax.psum(value, "rep")
        own_in = over_reps(scatter(jnp.stack([grad_gate, grad_up]), 1))
        grad_out = jnp.stack(out_near)
        grad_out = grad_out.transpose(2, 1, 0, 3, 4).reshape(hidden_width, model_width)
        own_out = over_reps(scatter(grad_out, 0))
        packed = jnp.stack([jnp.stack(cross_near), cross_far]).transpose(1, 2, 0, 3, 4)
        cross_parts = packed[..., :each, :].reshape(4, model_width, model_width)
        past = packed[:3, ..., each:, :].transpose(1, 2, 0, 3, 4).reshape(1, model_width, model_width)
        own_cross = over_reps(scatter(cross_parts, 1))
        own_self = over_reps(scatter(jnp.concatenate([grad_self_weights, past]), 1))
    self_grad, cross_grad, ffn_in_grad, feedforward_output_gradient = [
        wide(member) for member in (own_self, own_cross, own_in, own_out)
    ]
    if not quarters:
        local = (
            *factored_sums(ffn_in_grad, in_rows),
            *factored_sums(feedforward_output_gradient[None], out_rows[None]),
            *factored_sums(cross_grad, cross_rows),
            *factored_sums(self_grad, self_rows),
            *squares,
        )
        found = unpack(lax.psum(pack(local), "fsdp"), local)
        in_sums, out_sums, cross_sums, self_sums, squares = (
            found[0:2], found[2:4], found[4:6], found[6:8], found[8:],
        )
        small = lax.psum(small, ("rep", "fsdp"))
    new_in_rows = row_moments(ffn_in_grad, in_rows)
    new_out_rows = row_moments(feedforward_output_gradient, out_rows)
    new_cross_rows = row_moments(cross_grad, cross_rows)
    new_self_rows = row_moments(self_grad, self_rows)
    new_ffn_in, new_in_cols = factored_update(
        ffn_in_grad, ffn_in, new_in_rows, in_cols, *in_sums, squares[0]
    )
    new_ffn_out, new_out_cols = [
        member[0]
        for member in factored_update(
            feedforward_output_gradient[None], ffn_out[None], new_out_rows[None], out_cols[None],
            *out_sums, squares[1],
        )
    ]
    new_cross, new_cross_cols = factored_update(
        cross_grad, cross_weight, new_cross_rows, cross_cols, *cross_sums, squares[2]
    )
    new_self, new_self_cols = factored_update(
        self_grad, self_weight, new_self_rows, self_cols, *self_sums, squares[3]
    )
    gains_grad = lax.dynamic_slice_in_dim(
        small[: 3 * model_width].reshape(3, model_width), shard * gains.shape[1], gains.shape[1], axis=1
    )
    table_grad = small[3 * model_width :].reshape(BUCKETS, H)
    new_gains, new_gain_moment = plain_update(
        gains_grad, gains, gain_moment, (squares[4] / model_width)[:, None]
    )
    new_table, new_table_moment = plain_update(
        table_grad, table, table_moment, jnp.mean(table * table)
    )
    return (
        layer_out,
        input_grad,
        memory_grad,
        self_grad,
        cross_grad,
        ffn_in_grad,
        feedforward_output_gradient,
        gains_grad,
        table_grad,
        new_self,
        new_cross,
        new_ffn_in,
        new_ffn_out,
        new_gains,
        new_table,
        new_self_rows,
        new_self_cols,
        new_cross_rows,
        new_cross_cols,
        new_in_rows,
        new_in_cols,
        new_out_rows,
        new_out_cols,
        new_gain_moment,
        new_table_moment,
    )


def solution(mesh):
    placed = (
        P(("rep", "fsdp"), None, None),
        P(("rep", "fsdp"), None, None),
        P(("rep", "fsdp"), None, None),
        P(("rep", "fsdp")),
        P(("rep", "fsdp")),
        P(),
        P(None, "fsdp", None),
        P(None, "fsdp", None),
        P(None, "fsdp", None),
        P("fsdp", None),
        P(None, "fsdp"),
        P(),
        P(None, "fsdp"),
        P(),
        P(None, "fsdp"),
        P(),
        P(None, "fsdp"),
        P(),
        P("fsdp"),
        P(),
        P(None, "fsdp"),
        P(),
    )
    return jax.shard_map(
        per_device,
        mesh=mesh,
        in_specs=placed,
        out_specs=(
            P(("rep", "fsdp"), None, None),
            P(("rep", "fsdp"), None, None),
            P(("rep", "fsdp"), None, None),
            P(None, "fsdp", None),
            P(None, "fsdp", None),
            P(None, "fsdp", None),
            P("fsdp", None),
            P(None, "fsdp"),
            P(),
            P(None, "fsdp", None),
            P(None, "fsdp", None),
            P(None, "fsdp", None),
            P("fsdp", None),
            P(None, "fsdp"),
            P(),
            P(None, "fsdp"),
            P(),
            P(None, "fsdp"),
            P(),
            P(None, "fsdp"),
            P(),
            P("fsdp"),
            P(),
            P(None, "fsdp"),
            P(),
        ),
        check_vma=False,
    )
```

```python
import functools
import math

import jax
import jax.numpy as jnp
from jax import lax
from jax.experimental import pallas as pl
from jax.experimental.pallas import tpu as pltpu
from jax.sharding import PartitionSpec as P

H = 12
DH = 64
BUCKETS = 32
DECAY_RATE = 0.8
STEP_RATE = 0.2
TINY_TERM = 1e-30
PAIR = 2 * DH
GROUP = 4 * DH
HIDDEN = -1e30
MEGABYTE = 1024 * 1024
PEAK = 1.15e9
LINE = 4
LINE_CORES = 2
LOW = jnp.bfloat16
WIDE = jnp.float32


def nn(left, right):
    return lax.dot_general(left, right, (((1,), (0,)), ((), ())), preferred_element_type=WIDE)


def nt(left, right):
    return lax.dot_general(left, right, (((1,), (1,)), ((), ())), preferred_element_type=WIDE)


def tn(left, right):
    return lax.dot_general(left, right, (((0,), (0,)), ((), ())), preferred_element_type=WIDE)


def rms_rate(rows):
    return lax.rsqrt(jnp.mean(rows * rows, axis=-1, keepdims=True) + 1e-06)


def three_parts(column):
    high = column.astype(LOW)
    rest = column - high.astype(WIDE)
    middle = rest.astype(LOW)
    low = (rest - middle.astype(WIDE)).astype(LOW)
    return high, middle, low


def chunks(total, size):
    return [(at, min(size, total - at)) for at in range(0, total, size)]


def lanes(rows):
    return lax.broadcasted_iota(jnp.int32, (rows, PAIR), 1)


def own_lanes(rows, side):
    lane = lanes(rows)
    return (lane >= DH * side) & (lane < DH * (side + 1))


def key_extras(rows, side, length):
    lane = lanes(rows) - DH * (1 - side)
    dead = lax.broadcasted_iota(jnp.int32, (rows, PAIR), 0) >= length
    mask = jnp.where(dead, HIDDEN, 0.0)
    return jnp.where(
        (lane >= 0) & (lane < 3), 1.0, jnp.where(lane == 3, mask, 0.0)
    ).astype(LOW)


def row_extras(rows, side, column, last):
    lane = lanes(rows) - DH * (1 - side)
    high, middle, low = three_parts(column)
    wide = lambda part: jnp.broadcast_to(part.astype(WIDE), (rows, PAIR))
    return jnp.where(
        lane == 0,
        wide(high),
        jnp.where(
            lane == 1, wide(middle), jnp.where(lane == 2, wide(low), jnp.where(lane == 3, last, 0.0))
        ),
    ).astype(LOW)


def forward_body(causal, seq_count, length_ref, wave_ref, bias_ref, q_ref, k_ref, v_ref, mix_ref, total_ref, group):
    rows = q_ref.shape[0] // seq_count
    keys = k_ref.shape[0] // seq_count
    block = rows
    for pair in range(2):
        at = pair * PAIR
        for side in range(2):
            head = 2 * pair + side
            if causal:
                wave = wave_ref[pl.ds(group * 4 + head, 1), :]
                spread = pltpu.roll(
                    jnp.broadcast_to(wave, (rows, keys)), 0, 1, stride=1, stride_axis=0
                )
                row = lax.broadcasted_iota(jnp.int32, (rows, keys), 0)
                column = lax.broadcasted_iota(jnp.int32, (rows, keys), 1)
                bias_ref[side] = jnp.where(column <= row, spread, HIDDEN)
        for seq in range(seq_count):
            outs = []
            for side in range(2):
                own_q = own_lanes(rows, side)
                own_k = own_lanes(keys, side)
                query = jnp.where(
                    own_q,
                    q_ref[seq * rows : (seq + 1) * rows, at : at + PAIR],
                    (lanes(rows) == DH * (1 - side) + 3).astype(LOW),
                )
                key = jnp.where(
                    own_k,
                    k_ref[seq * keys : (seq + 1) * keys, at : at + PAIR],
                    key_extras(keys, side, length_ref[seq]),
                )
                value = jnp.where(
                    own_k,
                    v_ref[seq * keys : (seq + 1) * keys, at : at + PAIR],
                    jnp.ones((), LOW),
                )
                parts = []
                for start in range(0, rows, block):
                    span = start + block if causal else keys
                    scores = nt(query[start : start + block], key[:span])
                    if causal:
                        scores = scores + bias_ref[side, start : start + block, :span]
                    top = jnp.max(scores, axis=1, keepdims=True)
                    weight = jnp.exp(scores - top)
                    out = nn(weight.astype(LOW), value[:span])
                    total = out[:, DH * (1 - side) : DH * (1 - side) + 1]
                    parts.append(out * (1.0 / total))
                    spot = pl.ds(seq * rows + start, block)
                    lane = lanes(block)
                    seen = total_ref[spot, :] if (pair or side) else jnp.zeros((block, PAIR), WIDE)
                    total_ref[spot, :] = jnp.where(
                        lane == 2 * pair + side, top + jnp.log(total), seen
                    )
                outs.append(jnp.concatenate(parts, axis=0))
            mix_ref[seq * rows : (seq + 1) * rows, at : at + PAIR] = jnp.where(
                own_lanes(rows, 0), outs[0], outs[1]
            ).astype(LOW)


def forward_kernel(
    causal, seq_count, length_ref, x_ref, source_ref, gain_ref, wq_ref, wk_ref, wv_ref, wo_ref, wave_ref,
    q_ref, k_ref, v_ref, mix_ref, total_ref, after_ref, normed, bias,
):
    group = pl.program_id(0)

    @pl.when(group == 0)
    def _():
        for at, size in chunks(x_ref.shape[0], 256):
            rows = x_ref[at : at + size, :].astype(WIDE)
            normed[at : at + size, :] = (rows * rms_rate(rows) * gain_ref[...]).astype(LOW)
            after_ref[at : at + size, :] = rows

    source = normed if causal else source_ref
    q_ref[...] = nn(normed[...], wq_ref[...]).astype(LOW)
    k_ref[...] = nn(source[...], wk_ref[...]).astype(LOW)
    v_ref[...] = nn(source[...], wv_ref[...]).astype(LOW)
    forward_body(causal, seq_count, length_ref, wave_ref, bias, q_ref, k_ref, v_ref, mix_ref, total_ref, group)
    after_ref[...] += nn(mix_ref[...], wo_ref[...])


def weight_specs(width):
    across = lambda at: pl.BlockSpec((None, width, GROUP), lambda g, at=at: (at, 0, g))
    return [across(0), across(1), across(2), pl.BlockSpec((None, GROUP, width), lambda g: (3, g, 0))]


def whole(shape):
    return pl.BlockSpec(shape, lambda g: (0,) * len(shape), pipeline_mode=pl.Buffered(1))


def columns(rows):
    return pl.BlockSpec((rows, GROUP), lambda g: (0, g))


def attention_forward(causal, x, source, lengths, gain, weights, wave):
    row_count, width = x.shape
    seq_count = lengths.shape[0]
    source_rows = row_count if causal else source.shape[0]
    length = row_count // seq_count
    groups = width // GROUP
    low = lambda rows: jax.ShapeDtypeStruct((rows, width), LOW)
    args = [lengths, x, source, gain, weights, weights, weights, weights, wave]
    return pl.pallas_call(
        functools.partial(forward_kernel, causal, seq_count),
        grid=(groups,),
        in_specs=[
            pl.BlockSpec(memory_space=pltpu.SMEM),
            whole(x.shape),
            whole(source.shape),
            whole(gain.shape),
            *weight_specs(width),
            whole(wave.shape),
        ],
        out_specs=[
            columns(row_count),
            columns(source_rows),
            columns(source_rows),
            columns(row_count),
            pl.BlockSpec((None, row_count, PAIR), lambda g: (g, 0, 0)),
            whole((row_count, width)),
        ],
        out_shape=[
            low(row_count),
            low(source_rows),
            low(source_rows),
            low(row_count),
            jax.ShapeDtypeStruct((groups, row_count, PAIR), WIDE),
            jax.ShapeDtypeStruct((row_count, width), WIDE),
        ],
        scratch_shapes=[
            pltpu.VMEM((row_count, width), LOW),
            pltpu.VMEM((2, length, length) if causal else (1, 8, PAIR), WIDE),
        ],
        cost_estimate=pl.CostEstimate(flops=int(27 * PEAK), bytes_accessed=20 << 20, transcendentals=0),
        compiler_params=pltpu.CompilerParams(vmem_limit_bytes=60 * MEGABYTE),
        name="self_forward" if causal else "cross_forward",
    )(*args)


def gelu_parts(gate):
    root = 0.7978845608028654
    square = gate * gate
    inner = jnp.tanh(root * gate * (1.0 + 0.044715 * square))
    half = 0.5 * (1.0 + inner)
    value = gate * half
    slope = half + 0.5 * gate * (1.0 - inner * inner) * (root * (1.0 + 3 * 0.044715 * square))
    return value, slope


def rms_back(rows, gain, grad):
    rate = rms_rate(rows)
    scaled = rows * rate
    low = grad * gain
    grad_rows = rate * (low - scaled * jnp.mean(scaled * low, axis=-1, keepdims=True))
    return grad_rows, jnp.sum(grad * scaled, axis=0, keepdims=True)


def shard_slot(where_ref, shard):
    return (shard % LINE_CORES) ^ where_ref[2], lax.rem(shard // LINE_CORES - where_ref[1] + LINE, LINE)


def feed_kernel(
    seq_count, length_ref, where_ref, after_ref, out_grad_ref, gain_ref, wg_ref, wu_ref, wd_ref,
    layer_ref, grad_cross_ref, dwg_ref, dwu_ref, *refs,
):
    near_refs = refs[:4]
    dgain_ref, normed, normed_t, down, out_total, grad_total, cut = refs[4:]
    step = pl.program_id(0)
    row_count = after_ref.shape[0]
    length = row_count // seq_count

    def live(at, size):
        position = lax.broadcasted_iota(jnp.int32, (size, 1), 0) + (at % length)
        return (position < length_ref[at // length]).astype(WIDE)

    @pl.when(step == 0)
    def _():
        for at, size in chunks(row_count, 256):
            rows = after_ref[at : at + size, :]
            low = (rows * rms_rate(rows) * gain_ref[...]).astype(LOW)
            normed[at : at + size, :] = low
            normed_t[:, at : at + size] = low.T
            down[at : at + size, :] = (
                out_grad_ref[at : at + size, :].astype(WIDE) * live(at, size)
            ).astype(LOW)
            out_total[at : at + size, :] = rows
            grad_total[at : at + size, :] = jnp.zeros((size, rows.shape[1]), WIDE)

    gate = nn(normed[...], wg_ref[...])
    up = nn(normed[...], wu_ref[...])
    value, slope = gelu_parts(gate)
    hidden = (value * up).astype(LOW)
    out_total[...] += nn(hidden, wd_ref[...])
    grad_hidden = nt(down[...], wd_ref[...])
    cut[...] = tn(hidden, down[...]).astype(LOW).reshape(cut.shape)
    core, hop = shard_slot(where_ref, step)
    for way in range(4):
        near_refs[way][core, hop] = cut[where_ref[0] ^ way]
    grad_gate = (grad_hidden * up * slope).astype(LOW)
    grad_up = (grad_hidden * value).astype(LOW)
    dwg_ref[...] = nn(normed_t[...], grad_gate).astype(LOW)
    dwu_ref[...] = nn(normed_t[...], grad_up).astype(LOW)
    grad_total[...] += nt(grad_gate, wg_ref[...]) + nt(grad_up, wu_ref[...])

    @pl.when(step == pl.num_programs(0) - 1)
    def _():
        dgain = jnp.zeros(dgain_ref.shape, WIDE)
        for at, size in chunks(row_count, 256):
            part = slice(at, at + size)
            layer_ref[part, :] = (out_total[part, :] * live(at, size)).astype(LOW)
            grad_rows, gain_part = rms_back(after_ref[part, :], gain_ref[...], grad_total[part, :])
            dgain = dgain + gain_part
            grad_cross_ref[part, :] = (
                out_grad_ref[part, :].astype(WIDE) * live(at, size) + grad_rows
            )
        dgain_ref[...] = dgain


def feed_forward_both(after, out_grad, lengths, where, gain, w_in, w_out):
    row_count, width = after.shape
    hidden = w_out.shape[0]
    block = hidden // (LINE * LINE_CORES)
    seq_count = lengths.shape[0]
    wide = pl.BlockSpec((None, width, block), lambda g: (0, 0, g))
    wide_up = pl.BlockSpec((None, width, block), lambda g: (1, 0, g))
    tall = pl.BlockSpec((block, width), lambda g: (g, 0))
    flat = pl.BlockSpec((width, block), lambda g: (0, g))
    near = (LINE_CORES, LINE, block // 4, width)
    return pl.pallas_call(
        functools.partial(feed_kernel, seq_count),
        grid=(hidden // block,),
        in_specs=[
            pl.BlockSpec(memory_space=pltpu.SMEM),
            pl.BlockSpec(memory_space=pltpu.SMEM),
            whole(after.shape),
            whole(out_grad.shape),
            whole(gain.shape),
            wide,
            wide_up,
            tall,
        ],
        out_specs=[whole(after.shape), whole(after.shape), flat, flat, *[whole(near)] * 4, whole((1, width))],
        out_shape=[
            jax.ShapeDtypeStruct((row_count, width), LOW),
            jax.ShapeDtypeStruct((row_count, width), WIDE),
            jax.ShapeDtypeStruct((width, hidden), LOW),
            jax.ShapeDtypeStruct((width, hidden), LOW),
            *[jax.ShapeDtypeStruct(near, LOW)] * 4,
            jax.ShapeDtypeStruct((1, width), WIDE),
        ],
        scratch_shapes=[
            pltpu.VMEM((row_count, width), LOW),
            pltpu.VMEM((width, row_count), LOW),
            pltpu.VMEM((row_count, width), LOW),
            pltpu.VMEM((row_count, width), WIDE),
            pltpu.VMEM((row_count, width), WIDE),
            pltpu.VMEM((4, block // 4, width), LOW),
        ],
        cost_estimate=pl.CostEstimate(flops=int(46 * PEAK), bytes_accessed=40 << 20, transcendentals=0),
        compiler_params=pltpu.CompilerParams(vmem_limit_bytes=60 * MEGABYTE),
        name="feed_forward_both",
    )(lengths, where, after, out_grad, gain, w_in, w_in, w_out)


def backward_kernel(
    causal, seq_count, length_ref, where_ref, x_ref, source_ref, grad_ref, gain_ref, wq_ref, wo_ref, wave_ref,
    q_ref, k_ref, v_ref, mix_ref, total_ref, mix_all_ref, mix_past_ref, *refs,
):
    if causal:
        gq, gk_out_ref, gv_out_ref, dw_ref, dist_ref = refs[:5]
        normed_t, branch, grad_mix, bias, score_sum = refs[5:]
        source_t = normed_t
    else:
        grad_x_ref, gk_out_ref, gv_out_ref, dgain_ref = refs[:4]
        near_refs, far_ref = refs[4:8], refs[8]
        normed_t, branch, grad_mix, gq, source_t, mix_t, grad_total, dw_ref, past = refs[9:]
    group = pl.program_id(0)
    row_count = x_ref.shape[0]
    rows = q_ref.shape[0] // seq_count
    keys = k_ref.shape[0] // seq_count
    block = rows

    @pl.when(group == 0)
    def _():
        for at, size in chunks(row_count, 256):
            value = x_ref[at : at + size, :].astype(WIDE)
            low = (value * rms_rate(value) * gain_ref[...]).astype(LOW)
            normed_t[:, at : at + size] = low.T
            branch[at : at + size, :] = grad_ref[at : at + size, :].astype(LOW)
            if not causal:
                mix_t[:, at : at + size] = mix_all_ref[at : at + size, :].T
                grad_total[at : at + size, :] = jnp.zeros((size, value.shape[1]), WIDE)
        if not causal:
            for at, size in chunks(source_ref.shape[0], 256):
                source_t[:, at : at + size] = source_ref[at : at + size, :].T

    grad_mix[...] = nt(branch[...], wo_ref[...]).astype(LOW)
    if not causal:
        across = pl.ds(pl.multiple_of(group * GROUP, GROUP), GROUP)
        put = lambda at, value: dw_ref.__setitem__(at, value.astype(LOW).reshape(dw_ref.shape[1:]))
        put(3, nn(mix_t[...], branch[:, across]))

    for pair in range(2):
        at = pair * PAIR
        if causal:
            for side in range(2):
                head = 2 * pair + side
                wave = wave_ref[pl.ds(group * 4 + head, 1), :]
                spread = pltpu.roll(
                    jnp.broadcast_to(wave, (keys, rows)), 0, 1, stride=1, stride_axis=0
                )
                row = lax.broadcasted_iota(jnp.int32, (keys, rows), 0)
                column = lax.broadcasted_iota(jnp.int32, (keys, rows), 1)
                bias[side] = jnp.where(column >= row, spread, HIDDEN)
        for seq in range(seq_count):
            span_q = slice(seq * rows, (seq + 1) * rows)
            span_k = slice(seq * keys, (seq + 1) * keys)
            sides = []
            for side in range(2):
                head = 2 * pair + side
                own_q = own_lanes(rows, side)
                own_k = own_lanes(keys, side)
                total = jnp.sum(
                    jnp.where(lanes(rows) == head, total_ref[span_q, :], 0.0), axis=1, keepdims=True
                )
                grad_low = grad_mix[span_q, at : at + PAIR]
                product = grad_low.astype(WIDE) * mix_ref[span_q, at : at + PAIR].astype(WIDE)
                delta = jnp.sum(jnp.where(own_q, product, 0.0), axis=1, keepdims=True)
                query = jnp.where(
                    own_q, q_ref[span_q, at : at + PAIR], row_extras(rows, side, -total, 1.0)
                )
                grad_out = jnp.where(own_q, grad_low, row_extras(rows, side, -delta, 0.0))
                key = jnp.where(
                    own_k,
                    k_ref[span_k, at : at + PAIR],
                    key_extras(keys, side, length_ref[seq]),
                )
                value = jnp.where(own_k, v_ref[span_k, at : at + PAIR], jnp.ones((), LOW))
                grad_query = []
                grad_key = None
                grad_value = None
                for start in range(0, rows, block):
                    span = start + block if causal else keys
                    scores = nt(key[:span], query[start : start + block])
                    if causal:
                        scores = scores + bias[side, :span, start : start + block]
                    weight = jnp.exp(scores)
                    low = weight.astype(LOW)
                    grad_weight = nt(value[:span], grad_out[start : start + block])
                    grad_score = (weight * grad_weight).astype(LOW)
                    if causal:
                        if seq == 0:
                            score_sum[side, :span, start : start + block] = grad_score.astype(WIDE)
                        else:
                            score_sum[side, :span, start : start + block] += grad_score.astype(WIDE)
                    key_part = nn(grad_score, query[start : start + block])
                    value_part = nn(low, grad_out[start : start + block])
                    grad_query.append(tn(grad_score, key[:span]))
                    if causal and start == 0 and rows > block:
                        rest = jnp.zeros((keys - span, PAIR), WIDE)
                        key_part = jnp.concatenate([key_part, rest], axis=0)
                        value_part = jnp.concatenate([value_part, rest], axis=0)
                    grad_key = key_part if grad_key is None else grad_key + key_part
                    grad_value = value_part if grad_value is None else grad_value + value_part
                sides.append((jnp.concatenate(grad_query, axis=0), grad_key, grad_value))
            pick_q = own_lanes(rows, 0)
            pick_k = own_lanes(keys, 0)
            gq[span_q, at : at + PAIR] = jnp.where(pick_q, sides[0][0], sides[1][0]).astype(LOW)
            gk_out_ref[span_k, at : at + PAIR] = jnp.where(pick_k, sides[0][1], sides[1][1]).astype(LOW)
            gv_out_ref[span_k, at : at + PAIR] = jnp.where(pick_k, sides[0][2], sides[1][2]).astype(LOW)
        if causal:
            for side in range(2):
                head = 2 * pair + side
                row = lax.broadcasted_iota(jnp.int32, (keys, rows), 0)
                column = lax.broadcasted_iota(jnp.int32, (keys, rows), 1)
                held = jnp.where(column >= row, score_sum[side], 0.0)
                while held.shape[0] > 1:
                    half = held.shape[0] // 2
                    held = held[:half] + pltpu.roll(held[half:], rows - half, 1)
                dist_ref[pl.ds(group * 4 + head, 1), :] = held

    if causal:
        dw_ref[0] = nn(normed_t[...], gq[...]).astype(LOW)
        dw_ref[1] = nn(source_t[...], gk_out_ref[...]).astype(LOW)
        dw_ref[2] = nn(source_t[...], gv_out_ref[...]).astype(LOW)
        return
    put(0, nn(normed_t[...], gq[...]))
    put(1, nn(source_t[...], gk_out_ref[...]))
    put(2, nn(source_t[...], gv_out_ref[...]))
    grad_total[...] += nt(gq[...], wq_ref[...])
    rep, line, core = where_ref[0], where_ref[1], where_ref[2]
    held = dw_ref.shape[2]
    slots = []
    for way in range(4):
        for hop in range(LINE):
            at = lax.rem(line + hop, LINE) * LINE_CORES
            slots.append((near_refs[way].at[hop], rep ^ way, at + core))
            slots.append((far_ref.at[way, hop], rep ^ way, at + (core ^ 1)))
    for slot, quarter, shard in slots:
        slot[0:held, across] = dw_ref[quarter, shard]

    @pl.when(group == pl.num_programs(0) - 1)
    def _():
        dgain = jnp.zeros(dgain_ref.shape, WIDE)
        for at, size in chunks(row_count, 256):
            part = slice(at, at + size)
            grad_rows, gain_part = rms_back(
                x_ref[part, :].astype(WIDE), gain_ref[...], grad_total[part, :]
            )
            dgain = dgain + gain_part
            grad_rows = grad_ref[part, :] + grad_rows
            grad_x_ref[part, :] = grad_rows
            branch[part, :] = grad_rows.astype(LOW)
            mix_t[:, part] = mix_past_ref[part, :].T
        dgain_ref[...] = dgain
        thirds = nn(mix_t[...], branch[...]).astype(LOW)
        past[:, 0:3] = thirds.reshape(past.shape[0], 3, *past.shape[2:])
        past[:, 3] = jnp.zeros_like(past[:, 3])
        for slot, quarter, shard in slots:
            slot[held:, :] = past[shard, quarter]


def attention_backward(causal, x, source, grad, lengths, where, gain, weights, wave, kept, mix, past):
    row_count, width = x.shape
    seq_count = lengths.shape[0]
    source_rows = row_count if causal else source.shape[0]
    length = row_count // seq_count
    groups = width // GROUP
    low = lambda rows: jax.ShapeDtypeStruct((rows, width), LOW)
    if causal:
        out_specs = [
            columns(row_count), columns(source_rows), columns(source_rows),
            pl.BlockSpec((3, width, GROUP), lambda g: (0, 0, g)), whole(wave.shape),
        ]
        out_shape = [
            low(row_count), low(source_rows), low(source_rows),
            jax.ShapeDtypeStruct((3, width, width), LOW), jax.ShapeDtypeStruct(wave.shape, WIDE),
        ]
        scratch = [pltpu.VMEM((2, length, length), WIDE)] * 2
    else:
        shards = LINE * LINE_CORES
        each, third = width // shards, width // shards // 3
        near = (LINE, each + third, width)
        out_specs = [
            whole((row_count, width)), columns(source_rows), columns(source_rows), whole((1, width)),
            *[whole(near)] * 4, whole((4, *near)),
        ]
        out_shape = [
            jax.ShapeDtypeStruct((row_count, width), WIDE), low(source_rows), low(source_rows),
            jax.ShapeDtypeStruct((1, width), WIDE), *[jax.ShapeDtypeStruct(near, LOW)] * 4,
            jax.ShapeDtypeStruct((4, *near), LOW),
        ]
        scratch = [
            pltpu.VMEM((row_count, GROUP), LOW),
            pltpu.VMEM((width, source_rows), LOW),
            pltpu.VMEM((width, row_count), LOW),
            pltpu.VMEM((row_count, width), WIDE),
            pltpu.VMEM((4, shards, each, GROUP), LOW),
            pltpu.VMEM((shards, 4, third, width), LOW),
        ]
    return pl.pallas_call(
        functools.partial(backward_kernel, causal, seq_count),
        grid=(groups,),
        in_specs=[
            pl.BlockSpec(memory_space=pltpu.SMEM),
            pl.BlockSpec(memory_space=pltpu.SMEM),
            whole(x.shape),
            whole(source.shape),
            whole(grad.shape),
            whole(gain.shape),
            weight_specs(width)[0],
            weight_specs(width)[3],
            whole(wave.shape),
            columns(row_count),
            columns(source_rows),
            columns(source_rows),
            columns(row_count),
            pl.BlockSpec((None, row_count, PAIR), lambda g: (g, 0, 0)),
            whole(mix.shape),
            whole(past.shape),
        ],
        out_specs=out_specs,
        out_shape=out_shape,
        scratch_shapes=[
            pltpu.VMEM((width, row_count), LOW),
            pltpu.VMEM((row_count, width), LOW),
            pltpu.VMEM((row_count, GROUP), LOW),
            *scratch,
        ],
        cost_estimate=pl.CostEstimate(flops=int(45 * PEAK), bytes_accessed=40 << 20, transcendentals=0),
        compiler_params=pltpu.CompilerParams(vmem_limit_bytes=60 * MEGABYTE),
        name="self_backward" if causal else "cross_backward",
    )(lengths, where, x, source, grad, gain, weights, weights, wave, *kept, mix, past)


def input_kernel(gq_ref, gk_ref, gv_ref, wq_ref, wk_ref, wv_ref, x_ref, grad_ref, gain_ref, out_ref, dgain_ref):
    total = nt(gq_ref[...], wq_ref[...]) + nt(gk_ref[...], wk_ref[...]) + nt(gv_ref[...], wv_ref[...])
    grad_rows, dgain = rms_back(x_ref[...].astype(WIDE), gain_ref[...], total)
    out_ref[...] = grad_ref[...] + grad_rows

    @pl.when(pl.program_id(0) == 0)
    def _():
        dgain_ref[...] = jnp.zeros_like(dgain_ref)

    dgain_ref[...] += dgain


def input_gradient(grads, weights, x, grad, gain):
    rows, width = x.shape
    block = 256
    rowwise = pl.BlockSpec((block, width), lambda g: (g, 0))
    matrix = lambda at: pl.BlockSpec((None, width, width), lambda g: (at, 0, 0))
    return pl.pallas_call(
        input_kernel,
        grid=(rows // block,),
        in_specs=[rowwise, rowwise, rowwise, matrix(0), matrix(1), matrix(2), rowwise, rowwise, whole((1, width))],
        out_specs=[rowwise, whole((1, width))],
        out_shape=[jax.ShapeDtypeStruct((rows, width), WIDE), jax.ShapeDtypeStruct((1, width), WIDE)],
        cost_estimate=pl.CostEstimate(flops=int(8 * PEAK), bytes_accessed=12 << 20, transcendentals=0),
        compiler_params=pltpu.CompilerParams(vmem_limit_bytes=60 * MEGABYTE),
        name="input_gradient",
    )(*grads, weights, weights, weights, x, grad, gain)


def memory_kernel(gk_ref, gv_ref, wk_ref, wv_ref, out_ref):
    out_ref[...] = nt(gk_ref[...], wk_ref[...]) + nt(gv_ref[...], wv_ref[...])


def memory_gradient(grad_key, grad_value, weights):
    rows, width = grad_key.shape
    block = 256
    rowwise = pl.BlockSpec((block, width), lambda g: (g, 0))
    matrix = lambda at: pl.BlockSpec((None, width, width), lambda g: (at, 0, 0))
    return pl.pallas_call(
        memory_kernel,
        grid=(rows // block,),
        in_specs=[rowwise, rowwise, matrix(1), matrix(2)],
        out_specs=rowwise,
        out_shape=jax.ShapeDtypeStruct((rows, width), WIDE),
        cost_estimate=pl.CostEstimate(flops=int(7 * PEAK), bytes_accessed=10 << 20, transcendentals=0),
        compiler_params=pltpu.CompilerParams(vmem_limit_bytes=60 * MEGABYTE),
        name="memory_gradient",
    )(grad_key, grad_value, weights, weights)


LANES = 128
IN_AT, OUT_AT, CROSS_AT, PAST_AT, SELF_AT, SMALL_AT = 0, 1, 2, 3, 4, 5


def vector_rows(width, hidden, small):
    one, big = width // LANES, hidden // LANES
    starts = [0]
    for size in (2 * big, one, 4 * one, one, 3 * one, small // LANES):
        starts.append(starts[-1] + size)
    return starts


def spill(ref, at, row):
    for part in range(row.shape[1] // LANES):
        ref[pl.ds(at + part, 1), :] = row[:, part * LANES : (part + 1) * LANES]


def fetch(ref, at, width):
    return jnp.concatenate([ref[at + part : at + part + 1, :] for part in range(width // LANES)], axis=1)


def column_sums(rows):
    return jnp.sum(rows * rows + TINY_TERM, axis=0, keepdims=True)


def in_kernel(factor, *refs):
    in_refs, in_ref, sums_ref = refs[:4], refs[4], refs[5]
    big = in_ref.shape[2] // LANES
    for matrix in range(2):
        piece = sum(ref[matrix].astype(WIDE) for ref in in_refs).astype(LOW)
        in_ref[matrix] = piece
        spill(sums_ref, matrix * big, column_sums(piece.astype(WIDE) * factor))


def gated_sums(factor, in_parts):
    shape = in_parts[0].shape
    return pl.pallas_call(
        functools.partial(in_kernel, factor),
        in_specs=[pl.BlockSpec(memory_space=pltpu.VMEM)] * 4,
        out_specs=[pl.BlockSpec(memory_space=pltpu.VMEM)] * 2,
        out_shape=[
            jax.ShapeDtypeStruct(shape, LOW),
            jax.ShapeDtypeStruct((2 * shape[2] // LANES, LANES), WIDE),
        ],
        cost_estimate=pl.CostEstimate(flops=int(2 * PEAK), bytes_accessed=2 << 20, transcendentals=0),
        compiler_params=pltpu.CompilerParams(vmem_limit_bytes=60 * MEGABYTE),
        name="gated_sums",
    )(*in_parts)


def early_kernel(factor, starts, where_ref, *refs):
    line_refs, sums_ref, constant_ref, line_ref, vector_ref = refs[0:4], *refs[4:]
    rep = where_ref[0]
    one = line_ref.shape[1] // LANES
    each = line_ref.shape[0] // 2
    third = each // 3
    line = sum(ref[...].astype(WIDE) for ref in line_refs).astype(LOW)
    line_ref[...] = line
    vector_ref[...] = jnp.zeros_like(vector_ref)
    vector_ref[starts[IN_AT] : starts[OUT_AT], :] = sums_ref[...]
    line = line.astype(WIDE) * factor
    spill(vector_ref, starts[OUT_AT], column_sums(line[each + third :]))
    spill(vector_ref, starts[CROSS_AT] + rep * one, column_sums(line[:each]))
    past = column_sums(line[each : each + third])
    spill(vector_ref, starts[PAST_AT], past * (rep < 3).astype(WIDE))
    vector_ref[starts[-1] : starts[-1] + 1, :] = constant_ref[...]


def early_sums(factor, starts, where, line_parts, sums, constants):
    rows = -(-(starts[-1] + 1) // 8) * 8
    return pl.pallas_call(
        functools.partial(early_kernel, factor, starts),
        in_specs=[pl.BlockSpec(memory_space=pltpu.SMEM)] + [pl.BlockSpec(memory_space=pltpu.VMEM)] * 6,
        out_specs=[pl.BlockSpec(memory_space=pltpu.VMEM)] * 2,
        out_shape=[
            jax.ShapeDtypeStruct(line_parts[0].shape, LOW),
            jax.ShapeDtypeStruct((rows, LANES), WIDE),
        ],
        cost_estimate=pl.CostEstimate(flops=int(2 * PEAK), bytes_accessed=2 << 20, transcendentals=0),
        compiler_params=pltpu.CompilerParams(vmem_limit_bytes=60 * MEGABYTE),
        name="early_sums",
    )(where, *line_parts, sums, constants)


def late_kernel(factor, starts, *refs):
    part_refs, small_ref, early_ref, piece_ref, vector_ref = refs[0:4], refs[4], refs[5], refs[6], refs[7]
    vector_ref[...] = early_ref[...]
    one = piece_ref.shape[2] // LANES
    for matrix in range(3):
        piece = sum(ref[matrix].astype(WIDE) for ref in part_refs).astype(LOW)
        piece_ref[matrix] = piece
        spill(vector_ref, starts[SELF_AT] + matrix * one, column_sums(piece.astype(WIDE) * factor))
    vector_ref[starts[SMALL_AT] : starts[SMALL_AT + 1], :] = small_ref[...]


def late_sums(factor, starts, self_parts, small, early):
    return pl.pallas_call(
        functools.partial(late_kernel, factor, starts),
        in_specs=[pl.BlockSpec(memory_space=pltpu.VMEM)] * 6,
        out_specs=[pl.BlockSpec(memory_space=pltpu.VMEM)] * 2,
        out_shape=[
            jax.ShapeDtypeStruct(self_parts[0].shape, LOW),
            jax.ShapeDtypeStruct(early.shape, WIDE),
        ],
        cost_estimate=pl.CostEstimate(flops=int(2 * PEAK), bytes_accessed=1 << 20, transcendentals=0),
        compiler_params=pltpu.CompilerParams(vmem_limit_bytes=60 * MEGABYTE),
        name="late_sums",
    )(*self_parts, small, early)


def to_column(row):
    size = row.shape[1]
    same = lax.broadcasted_iota(jnp.int32, (size, size), 0) == lax.broadcasted_iota(jnp.int32, (size, size), 1)
    return jnp.sum(jnp.where(same, jnp.broadcast_to(row, (size, size)), 0.0), axis=1, keepdims=True)


def to_row(column):
    size = column.shape[0]
    same = lax.broadcasted_iota(jnp.int32, (size, size), 0) == lax.broadcasted_iota(jnp.int32, (size, size), 1)
    return jnp.sum(jnp.where(same, jnp.broadcast_to(column, (size, size)), 0.0), axis=0, keepdims=True)


def update_kernel(factor, starts, shards, where_ref, total_ref, *refs):
    in_near, line_near, self_near = refs[0:4], refs[4:8], refs[8:12]
    (
        in_ref, out_ref, cross_ref, self_ref, in_rows_ref, out_rows_ref, cross_rows_ref, self_rows_ref,
        in_cols_ref, out_cols_ref, cross_cols_ref, self_cols_ref,
    ) = refs[12:24]
    (
        in_grad, out_grad, cross_grad, self_grad, new_in, new_out, new_cross, new_self,
        new_in_rows, new_out_rows, new_cross_rows, new_self_rows,
        new_in_cols, new_out_cols, new_cross_cols, new_self_cols,
        gains_grad, table_grad, new_gains, new_table, new_gain_moment, new_table_moment,
    ) = refs[28:50]
    gains_ref, table_ref, gain_moment_ref, table_moment_ref = refs[24:28]
    in_held, line_held, self_held = refs[50:]
    rep = where_ref[0]
    for way in range(4):
        in_held[rep ^ way] = in_near[way][...]
        line_held[rep ^ way] = line_near[way][...]
        self_held[rep ^ way] = self_near[way][...]
    width = cross_ref.shape[2]
    one, big = width // LANES, in_ref.shape[2] // LANES
    each = cross_ref.shape[1]
    third = each // 3
    scalars = total_ref[starts[-1] : starts[-1] + 1, :]

    def step(at, pieces, index, weight, grad, new, rows_ref, new_rows, cols_ref, new_cols, row_at, scalar):
        rows, cols = weight.shape[-2:]
        spans = []
        start = 0
        for piece in pieces:
            spans.append(slice(start, start + piece.shape[0]))
            start += piece.shape[0]
        whole_rows = rows * shards
        col_sum = fetch(total_ref, at, cols)
        state_sum = scalars[:, scalar : scalar + 1]
        square = scalars[:, 16 + scalar : 17 + scalar]
        col_moment = DECAY_RATE * cols_ref[row_at : row_at + 1, :] + (1.0 - DECAY_RATE) * col_sum / whole_rows
        new_cols[row_at : row_at + 1, :] = col_moment
        row_mean = (
            DECAY_RATE * state_sum
            + (1.0 - DECAY_RATE) / cols * jnp.sum(col_sum, axis=1, keepdims=True)
        ) / whole_rows
        blocks = [piece.astype(WIDE) * factor for piece in pieces]
        means = jnp.concatenate(
            [jnp.mean(block * block + TINY_TERM, axis=1, keepdims=True) for block in blocks], axis=0
        )
        row_moment = DECAY_RATE * to_column(rows_ref[row_at : row_at + 1, :]) + (1.0 - DECAY_RATE) * means
        new_rows[row_at : row_at + 1, :] = to_row(row_moment)
        size = STEP_RATE * jnp.sqrt(square / (whole_rows * cols) + 1e-06)
        scale = size * lax.rsqrt(row_moment / row_mean)
        across = lax.rsqrt(col_moment)
        for block, span in zip(blocks, spans):
            place = (span, slice(None)) if index is None else (index, span, slice(None))
            grad[place] = block
            new[place] = weight[place] - scale[span] * block * across

    def plain(grad, ref, moment_ref, square, out, new, new_moment, spot):
        moment = DECAY_RATE * moment_ref[spot] + (1.0 - DECAY_RATE) * (grad * grad + TINY_TERM)
        out[spot] = grad
        new_moment[spot] = moment
        new[spot] = ref[spot] - STEP_RATE * jnp.sqrt(square + 1e-06) * grad * lax.rsqrt(moment)

    part = gains_ref.shape[1]
    for norm in range(3):
        row = fetch(total_ref, starts[SMALL_AT] + norm * one, width)
        mine = where_ref[1] * LINE_CORES + where_ref[2]
        row = pltpu.roll(jnp.broadcast_to(row, (8, width)), lax.rem(width - mine * part, width), 1)
        plain(
            row[0:1, :part], gains_ref, gain_moment_ref, scalars[:, 27 + norm : 28 + norm] / width,
            gains_grad, new_gains, new_gain_moment, (slice(norm, norm + 1), slice(None)),
        )
    table = total_ref[starts[SMALL_AT] + 3 * one : starts[SMALL_AT + 1], 0 : table_ref.shape[1]]
    square = jnp.sum(jnp.sum(table_ref[...] * table_ref[...], axis=1, keepdims=True), axis=0, keepdims=True)
    plain(
        table, table_ref, table_moment_ref, square / (table_ref.shape[0] * table_ref.shape[1]),
        table_grad, new_table, new_table_moment, (slice(None), slice(None)),
    )
    quarters = range(4)
    for matrix in range(2):
        step(
            starts[IN_AT] + matrix * big, [in_held[at, matrix] for at in quarters], matrix,
            in_ref, in_grad, new_in, in_rows_ref, new_in_rows, in_cols_ref, new_in_cols, matrix, matrix,
        )
    step(
        starts[OUT_AT], [line_held[at, each + third :, :] for at in quarters], None,
        out_ref, out_grad, new_out, out_rows_ref, new_out_rows, out_cols_ref, new_out_cols, 0, 2,
    )
    for matrix in range(4):
        step(
            starts[CROSS_AT] + matrix * one, [line_held[matrix, 0:each, :]], matrix,
            cross_ref, cross_grad, new_cross, cross_rows_ref, new_cross_rows, cross_cols_ref, new_cross_cols,
            matrix, 3 + matrix,
        )
        if matrix < 3:
            at, pieces = starts[SELF_AT] + matrix * one, [self_held[at, matrix] for at in quarters]
        else:
            at, pieces = starts[PAST_AT], [line_held[at, each : each + third, :] for at in range(3)]
        step(
            at, pieces, matrix, self_ref, self_grad, new_self, self_rows_ref, new_self_rows,
            self_cols_ref, new_self_cols, matrix, 7 + matrix,
        )


def update_all(
    factor, starts, shards, where, total, in_near, line_near, self_near, weights, rows, cols, plain
):
    outs = (*weights, *weights, *rows, *cols, *plain[:2], *plain[:2], *plain[2:])
    out_shape = [jax.ShapeDtypeStruct(value.shape, WIDE) for value in outs]
    spec = pl.BlockSpec(memory_space=pltpu.VMEM)
    return pl.pallas_call(
        functools.partial(update_kernel, factor, starts, shards),
        in_specs=[pl.BlockSpec(memory_space=pltpu.SMEM)] + [spec] * 29,
        out_specs=[spec] * 22,
        out_shape=out_shape,
        scratch_shapes=[pltpu.VMEM((4, *near[0].shape), LOW) for near in (in_near, line_near, self_near)],
        cost_estimate=pl.CostEstimate(flops=int(8 * PEAK), bytes_accessed=16 << 20, transcendentals=0),
        compiler_params=pltpu.CompilerParams(vmem_limit_bytes=60 * MEGABYTE),
        name="update_all",
    )(where, total, *in_near, *line_near, *self_near, *weights, *rows, *cols, *plain)


def flat_permute(value, target):
    reps, shards = lax.axis_size("rep"), lax.axis_size("fsdp")
    pairs = []
    for rep in range(reps):
        for shard in range(shards):
            to_rep, to_shard = target(rep, shard)
            pairs.append((rep * shards + shard, to_rep * shards + to_shard))
    return lax.ppermute(value, ("rep", "fsdp"), pairs)


def from_rep(value, way):
    return flat_permute(value, lambda rep, shard: (rep ^ way, shard))


def from_shard(value, way):
    return flat_permute(value, lambda rep, shard: (rep, shard ^ way))


def from_line(value, hops):
    shards = lax.axis_size("fsdp")
    return flat_permute(value, lambda rep, shard: (rep, (shard + LINE_CORES * hops) % shards))


def along_line(piece):
    return jnp.stack([piece] + [from_line(piece, hop) for hop in range(1, LINE)])


def across_reps(line):
    return [line] + [from_rep(line, way) for way in range(1, 4)]


def with_partner(parts):
    return parts + [from_shard(part, 1) for part in parts]


def add_line(parts):
    return [parts[0]] + [from_line(parts[hop], hop) for hop in range(1, LINE)]


def assemble_kernel(place, hops, where_ref, *refs):
    parts, out_ref, sems = refs[:8], refs[8], refs[9]
    rep, line, core = where_ref[0], where_ref[1], where_ref[2]
    copies = []
    for other in range(2):
        for way in range(4):
            for hop in range(hops):
                shard = lax.rem(line - hop + hops, hops) * LINE_CORES + (core ^ other)
                copies.append(
                    pltpu.make_async_copy(
                        parts[4 * other + way].at[hop],
                        place(out_ref, rep ^ way, shard),
                        sems.at[len(copies)],
                    )
                )
    for copy in copies:
        copy.start()
    for copy in copies:
        copy.wait()


def assemble(parts, where, shape, place, name):
    hops = parts[0].shape[0]
    return pl.pallas_call(
        functools.partial(assemble_kernel, place, hops),
        in_specs=[pl.BlockSpec(memory_space=pltpu.SMEM)] + [pl.BlockSpec(memory_space=pl.ANY)] * 8,
        out_specs=pl.BlockSpec(memory_space=pltpu.VMEM),
        out_shape=jax.ShapeDtypeStruct(shape, LOW),
        scratch_shapes=[pltpu.SemaphoreType.DMA((8 * hops,))],
        cost_estimate=pl.CostEstimate(flops=int(4 * PEAK), bytes_accessed=8 << 20, transcendentals=0),
        compiler_params=pltpu.CompilerParams(vmem_limit_bytes=60 * MEGABYTE),
        name=name,
    )(where, *parts)


def rep_parts(parts, axis):
    rep = lax.axis_index("rep")
    pick = lambda at: lax.dynamic_index_in_dim(parts, at, axis, keepdims=False)
    return [pick(rep)] + [from_rep(pick(rep ^ way), way) for way in range(1, 4)]


def add_up(parts):
    return sum(part.astype(WIDE) for part in parts).astype(LOW)


def rep_near(piece):
    return [piece] + [from_rep(piece, way) for way in range(1, 4)]


def rep_order(near):
    rep = lax.axis_index("rep")
    return [lax.select_n(rep, *[near[at ^ own] for own in range(4)]) for at in range(4)]


def hold(*values):
    return lax.optimization_barrier(values)


def butterfly(vector, move, size):
    way = 1
    while way < size:
        vector = vector + move(vector, way)
        way *= 2
    return vector


def after(value, *earlier):
    return lax.optimization_barrier((value, *earlier))[0]


def row_moments(gradient, row_state):
    squares = gradient * gradient + TINY_TERM
    return DECAY_RATE * row_state + (1.0 - DECAY_RATE) * jnp.mean(squares, axis=-1)


def factored_sums(gradient, row_state):
    squares = gradient * gradient + TINY_TERM
    return jnp.sum(squares, axis=1), jnp.sum(row_moments(gradient, row_state), axis=1)


def pack(values):
    return jnp.concatenate([value.reshape(-1) for value in values])


def unpack(vector, values):
    out = []
    for value in values:
        out.append(vector[: value.size].reshape(value.shape))
        vector = vector[value.size :]
    return out


def factored_update(gradient, weight, row_moment, col_state, col_sum, row_sum, square):
    count, rows, cols = weight.shape
    whole_rows = rows * lax.axis_size("fsdp")
    col_moment = DECAY_RATE * col_state + (1.0 - DECAY_RATE) * col_sum / whole_rows
    scale = lax.rsqrt(row_moment / (row_sum[:, None] / whole_rows))
    step = STEP_RATE * jnp.sqrt(square / (whole_rows * cols) + 1e-06)
    direction = gradient * scale[:, :, None] * lax.rsqrt(col_moment)[:, None, :]
    return weight - step[:, None, None] * direction, col_moment


def plain_update(gradient, weight, moment, square):
    moment = DECAY_RATE * moment + (1.0 - DECAY_RATE) * (gradient * gradient + TINY_TERM)
    step = STEP_RATE * jnp.sqrt(square + 1e-06)
    return weight - step * gradient * lax.rsqrt(moment), moment


def per_device(
    dec_in,
    memory,
    out_grad,
    dec_len,
    enc_len,
    buckets,
    self_weight,
    cross_weight,
    ffn_in,
    ffn_out,
    gains,
    table,
    self_rows,
    self_cols,
    cross_rows,
    cross_cols,
    in_rows,
    in_cols,
    out_rows,
    out_cols,
    gain_moment,
    table_moment,
):
    seq_count, seq_length, model_width = dec_in.shape
    mem_length = memory.shape[1]
    row_count = seq_count * seq_length
    hidden_width = ffn_in.shape[2]
    reps, shards = lax.axis_size("rep"), lax.axis_size("fsdp")
    rep, shard = lax.axis_index("rep"), lax.axis_index("fsdp")
    quarters = reps == 4 and shards == 8
    part_rows = hidden_width // shards
    grad_factor = 1.0 / math.sqrt(row_count * reps * shards)
    where = jnp.stack([rep, shard // 2, shard % 2]).astype(jnp.int32) * int(quarters)
    w_self = lax.all_gather(self_weight.astype(LOW), "fsdp", axis=1, tiled=True)
    gain_full = lax.all_gather(gains.astype(LOW), "fsdp", axis=1, tiled=True).astype(WIDE)
    w_in = lax.all_gather(ffn_in.astype(LOW), "fsdp", axis=1, tiled=True)

    each = model_width // (LINE * LINE_CORES)
    if quarters:
        out_each = part_rows // 4
        cross_quarter = lax.dynamic_index_in_dim(cross_weight, rep, 0, keepdims=False).astype(LOW)
        out_quarter = lax.dynamic_index_in_dim(
            ffn_out.reshape(4, out_each, model_width), rep, 0, keepdims=False
        ).astype(LOW)
        cross_pieces = with_partner(across_reps(along_line(cross_quarter)))
    square = lambda value: jnp.sum(value * value, axis=(1, 2))
    squares = (
        square(ffn_in), square(ffn_out[None]), square(cross_weight), square(self_weight),
        jnp.sum(gains * gains, axis=1),
    )
    if quarters:
        state_sums = (
            jnp.sum(in_rows, axis=1), jnp.sum(out_rows)[None], jnp.sum(cross_rows, axis=1),
            jnp.sum(self_rows, axis=1),
        )
        blank = jnp.zeros((5,), WIDE)
        constants = pack([*state_sums, blank, *squares]) / reps
        constants = jnp.pad(constants, (0, LANES - constants.size)).reshape(1, LANES)
        gain_full, constants = hold(gain_full, constants)

    bucket_mask = (buckets[None, :] == jnp.arange(BUCKETS)[:, None]).astype(WIDE)
    by_distance = jnp.sum(table.T[:, :, None] * bucket_mask[None], axis=1)
    by_distance = jnp.pad(by_distance, ((0, 16 - H), (0, 0)))
    backwards = jnp.roll(by_distance[:, ::-1], 1, axis=1)
    no_bias = jnp.zeros((8, PAIR), WIDE)
    no_source = jnp.zeros((16, PAIR), LOW)

    dec_rows = dec_in.reshape(row_count, model_width)
    mem_rows = memory.reshape(seq_count * mem_length, model_width)
    grad_rows = out_grad.reshape(row_count, model_width)
    *kept_one, after_self = attention_forward(
        True, dec_rows, no_source, dec_len, gain_full[0:1], w_self, backwards
    )
    if quarters:
        w_cross = assemble(
            hold(*cross_pieces, after_self)[:-1],
            where,
            (4, model_width, model_width),
            lambda ref, quarter, at: ref.at[quarter, pl.ds(at * each, each)],
            "assemble_cross",
        )
        out_line = along_line(after(out_quarter, w_self))
        out_near = across_reps(after(out_line, after_self))
    else:
        w_cross = lax.all_gather(cross_weight.astype(LOW), "fsdp", axis=1, tiled=True)
        w_out = lax.all_gather(ffn_out.astype(LOW), "fsdp", axis=0, tiled=True)
    *kept_two, after_cross = attention_forward(
        False, after_self, mem_rows, enc_len, gain_full[1:2], w_cross, no_bias
    )
    if quarters:
        out_near = hold(*out_near, after_cross)[:-1]
        w_out = assemble(
            with_partner(list(out_near)),
            where,
            (hidden_width, model_width),
            lambda ref, quarter, at: ref.at[pl.ds((at * 4 + quarter) * out_each, out_each)],
            "assemble_out",
        )
    layer_out, grad_cross, grad_gate, grad_up, *out_near, gain_three = feed_forward_both(
        after_cross, grad_rows, dec_len, where, gain_full[2:3], w_in, w_out
    )
    scatter = lambda value, at: lax.psum_scatter(value, "fsdp", scatter_dimension=at, tiled=True)
    if quarters:
        own_gate = scatter(grad_gate, 0)
        out_near = out_near[:1] + [from_rep(out_near[way], way) for way in range(1, 4)]
    grad_self, grad_k_two, grad_v_two, gain_two, *cross_near, cross_far = attention_backward(
        False, after_self, mem_rows, grad_cross, enc_len, where, gain_full[1:2], w_cross, no_bias, kept_two,
        kept_two[3], kept_one[3],
    )
    if quarters:
        cross_far, grad_k_two, *out_near = hold(cross_far, grad_k_two, *out_near)
        pair = from_shard(cross_far, 1)
        memory_grad = memory_gradient(grad_k_two, grad_v_two, w_cross)
        memory_grad, pair, own_gate = hold(memory_grad, pair, own_gate)
        own_up = scatter(grad_up, 0)
        cross_chip = [add_up([cross_near[way], pair[way]]) for way in range(4)]
        grad_self, *cross_chip = hold(grad_self, *cross_chip)
        cross_near = cross_chip[:1] + [from_rep(cross_chip[way], way) for way in range(1, 4)]
    else:
        memory_grad = memory_gradient(grad_k_two, grad_v_two, w_cross)
    *grads_one, grad_self_weights, dist_grad = attention_backward(
        True, dec_rows, no_source, grad_self, dec_len, where, gain_full[0:1], w_self, by_distance, kept_one,
        no_source, no_source,
    )
    if quarters:
        dist_grad, own_up, grad_self_weights, *rest = hold(
            dist_grad, own_up, grad_self_weights, *grads_one, *cross_near, *out_near
        )
        grads_one, cross_near, out_near = rest[:3], rest[3:7], rest[7:]
        own_self = scatter(grad_self_weights, 1)
        out_sum = add_up(out_near)
        out_pair = from_shard(out_sum[1], 1)
        in_parts = rep_parts(jnp.stack([own_gate, own_up]).reshape(2, 4, -1, hidden_width), 1)
        line = jnp.concatenate([add_up(cross_near), add_up([out_sum[0], out_pair])], axis=1)
        in_piece, in_columns = gated_sums(grad_factor, in_parts)
        in_near = rep_near(in_piece)
        *line_parts, gate = hold(*add_line(line), grads_one[0])
        grads_one = [gate, *grads_one[1:]]
        input_grad, gain_one = input_gradient(grads_one, w_self, dec_rows, grad_self, gain_full[0:1])
    else:
        input_grad, gain_one = input_gradient(grads_one, w_self, dec_rows, grad_self, gain_full[0:1])
    layer_out = layer_out.reshape(dec_in.shape)
    input_grad = input_grad.reshape(dec_in.shape)
    memory_grad = memory_grad.reshape(memory.shape)
    table_part = jnp.sum(dist_grad[:H, None, :] * bucket_mask[None], axis=2)
    wide = lambda value: value.astype(WIDE) * grad_factor
    gain_parts = jnp.concatenate([gain_one, gain_two, gain_three]) * grad_factor
    table_part = table_part * grad_factor
    if quarters:
        starts = vector_rows(model_width, hidden_width, 3 * model_width + H * LANES)
        small = jnp.concatenate(
            [gain_parts.reshape(-1, LANES), jnp.pad(table_part, ((0, 0), (0, LANES - BUCKETS)))]
        )
        line_piece, early = early_sums(grad_factor, starts, where, line_parts, in_columns, constants)
        line_near = rep_near(line_piece)
        own_self, early, *near = hold(own_self, early, *in_near, *line_near[:3])
        in_near, line_near = near[:4], near[4:] + line_near[3:]
        self_parts = rep_parts(own_self.reshape(3, 4, -1, model_width), 1)
        self_piece, vector = late_sums(grad_factor, starts, self_parts, small, early)
        vector, *self_near = hold(butterfly(vector, from_rep, reps), *rep_near(self_piece))
        total = butterfly(vector, from_shard, shards)
        (
            ffn_in_grad, feedforward_output_gradient, cross_grad, self_grad,
            new_ffn_in, new_ffn_out, new_cross, new_self,
            new_in_rows, new_out_rows, new_cross_rows, new_self_rows,
            new_in_cols, new_out_cols, new_cross_cols, new_self_cols,
            gains_grad, table_grad, new_gains, new_table, new_gain_moment, new_table_moment,
        ) = update_all(
            grad_factor, starts, shards, where, total, in_near, line_near, self_near,
            (ffn_in, ffn_out, cross_weight, self_weight),
            (in_rows, out_rows[None], cross_rows, self_rows),
            (in_cols, out_cols[None], cross_cols, self_cols),
            (gains, table.T, gain_moment, table_moment.T),
        )
        table_grad, new_table, new_table_moment = table_grad.T, new_table.T, new_table_moment.T
        new_out_rows, new_out_cols = new_out_rows.reshape(-1), new_out_cols.reshape(-1)
    else:
        over_reps = lambda value: lax.psum(value, "rep")
        own_in = over_reps(scatter(jnp.stack([grad_gate, grad_up]), 1))
        grad_out = jnp.stack(out_near)
        grad_out = grad_out.transpose(2, 1, 0, 3, 4).reshape(hidden_width, model_width)
        own_out = over_reps(scatter(grad_out, 0))
        packed = jnp.stack([jnp.stack(cross_near), cross_far]).transpose(1, 2, 0, 3, 4)
        cross_parts = packed[..., :each, :].reshape(4, model_width, model_width)
        past = packed[:3, ..., each:, :].transpose(1, 2, 0, 3, 4).reshape(1, model_width, model_width)
        own_cross = over_reps(scatter(cross_parts, 1))
        own_self = over_reps(scatter(jnp.concatenate([grad_self_weights, past]), 1))
        self_grad, cross_grad, ffn_in_grad, feedforward_output_gradient = [
            wide(member) for member in (own_self, own_cross, own_in, own_out)
        ]
        local = (
            *factored_sums(ffn_in_grad, in_rows),
            *factored_sums(feedforward_output_gradient[None], out_rows[None]),
            *factored_sums(cross_grad, cross_rows),
            *factored_sums(self_grad, self_rows),
            *squares,
        )
        found = unpack(lax.psum(pack(local), "fsdp"), local)
        in_sums, out_sums, cross_sums, self_sums, squares = (
            found[0:2], found[2:4], found[4:6], found[6:8], found[8:],
        )
        gain_total, table_grad = lax.psum((gain_parts, table_part.T), ("rep", "fsdp"))
        gains_grad = lax.dynamic_slice_in_dim(gain_total, shard * gains.shape[1], gains.shape[1], axis=1)
        new_gains, new_gain_moment = plain_update(
            gains_grad, gains, gain_moment, (squares[4] / model_width)[:, None]
        )
        new_table, new_table_moment = plain_update(
            table_grad, table, table_moment, jnp.mean(table * table)
        )
        new_in_rows = row_moments(ffn_in_grad, in_rows)
        new_out_rows = row_moments(feedforward_output_gradient, out_rows)
        new_cross_rows = row_moments(cross_grad, cross_rows)
        new_self_rows = row_moments(self_grad, self_rows)
        new_ffn_in, new_in_cols = factored_update(
            ffn_in_grad, ffn_in, new_in_rows, in_cols, *in_sums, squares[0]
        )
        new_ffn_out, new_out_cols = [
            member[0]
            for member in factored_update(
                feedforward_output_gradient[None], ffn_out[None], new_out_rows[None], out_cols[None],
                *out_sums, squares[1],
            )
        ]
        new_cross, new_cross_cols = factored_update(
            cross_grad, cross_weight, new_cross_rows, cross_cols, *cross_sums, squares[2]
        )
        new_self, new_self_cols = factored_update(
            self_grad, self_weight, new_self_rows, self_cols, *self_sums, squares[3]
        )
    return (
        layer_out,
        input_grad,
        memory_grad,
        self_grad,
        cross_grad,
        ffn_in_grad,
        feedforward_output_gradient,
        gains_grad,
        table_grad,
        new_self,
        new_cross,
        new_ffn_in,
        new_ffn_out,
        new_gains,
        new_table,
        new_self_rows,
        new_self_cols,
        new_cross_rows,
        new_cross_cols,
        new_in_rows,
        new_in_cols,
        new_out_rows,
        new_out_cols,
        new_gain_moment,
        new_table_moment,
    )


def solution(mesh):
    placed = (
        P(("rep", "fsdp"), None, None),
        P(("rep", "fsdp"), None, None),
        P(("rep", "fsdp"), None, None),
        P(("rep", "fsdp")),
        P(("rep", "fsdp")),
        P(),
        P(None, "fsdp", None),
        P(None, "fsdp", None),
        P(None, "fsdp", None),
        P("fsdp", None),
        P(None, "fsdp"),
        P(),
        P(None, "fsdp"),
        P(),
        P(None, "fsdp"),
        P(),
        P(None, "fsdp"),
        P(),
        P("fsdp"),
        P(),
        P(None, "fsdp"),
        P(),
    )
    return jax.shard_map(
        per_device,
        mesh=mesh,
        in_specs=placed,
        out_specs=(
            P(("rep", "fsdp"), None, None),
            P(("rep", "fsdp"), None, None),
            P(("rep", "fsdp"), None, None),
            P(None, "fsdp", None),
            P(None, "fsdp", None),
            P(None, "fsdp", None),
            P("fsdp", None),
            P(None, "fsdp"),
            P(),
            P(None, "fsdp", None),
            P(None, "fsdp", None),
            P(None, "fsdp", None),
            P("fsdp", None),
            P(None, "fsdp"),
            P(),
            P(None, "fsdp"),
            P(),
            P(None, "fsdp"),
            P(),
            P(None, "fsdp"),
            P(),
            P("fsdp"),
            P(),
            P(None, "fsdp"),
            P(),
        ),
        check_vma=False,
    )
```

```python
import functools
import math

import jax
import jax.numpy as jnp
from jax import lax
from jax.experimental import pallas as pl
from jax.experimental.pallas import tpu as pltpu
from jax.sharding import PartitionSpec as P

H = 12
DH = 64
BUCKETS = 32
DECAY_RATE = 0.8
STEP_RATE = 0.2
TINY_TERM = 1e-30
PAIR = 2 * DH
GROUP = 4 * DH
HIDDEN = -1e30
MEGABYTE = 1024 * 1024
PEAK = 1.15e9
LINE = 4
LINE_CORES = 2
LOW = jnp.bfloat16
WIDE = jnp.float32


def nn(left, right):
    return lax.dot_general(left, right, (((1,), (0,)), ((), ())), preferred_element_type=WIDE)


def nt(left, right):
    return lax.dot_general(left, right, (((1,), (1,)), ((), ())), preferred_element_type=WIDE)


def tn(left, right):
    return lax.dot_general(left, right, (((0,), (0,)), ((), ())), preferred_element_type=WIDE)


def rms_rate(rows):
    return lax.rsqrt(jnp.mean(rows * rows, axis=-1, keepdims=True) + 1e-06)


def three_parts(column):
    high = column.astype(LOW)
    rest = column - high.astype(WIDE)
    middle = rest.astype(LOW)
    low = (rest - middle.astype(WIDE)).astype(LOW)
    return high, middle, low


def chunks(total, size):
    return [(at, min(size, total - at)) for at in range(0, total, size)]


def lanes(rows):
    return lax.broadcasted_iota(jnp.int32, (rows, PAIR), 1)


def own_lanes(rows, side):
    lane = lanes(rows)
    return (lane >= DH * side) & (lane < DH * (side + 1))


def key_extras(rows, side, length):
    lane = lanes(rows) - DH * (1 - side)
    dead = lax.broadcasted_iota(jnp.int32, (rows, PAIR), 0) >= length
    mask = jnp.where(dead, HIDDEN, 0.0)
    return jnp.where(
        (lane >= 0) & (lane < 3), 1.0, jnp.where(lane == 3, mask, 0.0)
    ).astype(LOW)


def row_extras(rows, side, column, last):
    lane = lanes(rows) - DH * (1 - side)
    high, middle, low = three_parts(column)
    wide = lambda part: jnp.broadcast_to(part.astype(WIDE), (rows, PAIR))
    return jnp.where(
        lane == 0,
        wide(high),
        jnp.where(
            lane == 1, wide(middle), jnp.where(lane == 2, wide(low), jnp.where(lane == 3, last, 0.0))
        ),
    ).astype(LOW)


def piece_copies(parts, where_ref, place, sems):
    rep, line, core = where_ref[0], where_ref[1], where_ref[2]
    copies = []
    for other in range(LINE_CORES):
        for way in range(4):
            for hop in range(LINE):
                shard = lax.rem(line - hop + LINE, LINE) * LINE_CORES + (core ^ other)
                source = parts[4 * other + way].at[hop]
                copies.append(pltpu.make_async_copy(source, place(rep ^ way, shard), sems.at[len(copies)]))
    return copies


def forward_body(causal, seq_count, length_ref, wave_ref, bias_ref, q_ref, k_ref, v_ref, mix_ref, total_ref, group):
    rows = q_ref.shape[0] // seq_count
    keys = k_ref.shape[0] // seq_count
    block = rows
    for pair in range(2):
        at = pair * PAIR
        for side in range(2):
            head = 2 * pair + side
            if causal:
                wave = wave_ref[pl.ds(group * 4 + head, 1), :]
                spread = pltpu.roll(
                    jnp.broadcast_to(wave, (rows, keys)), 0, 1, stride=1, stride_axis=0
                )
                row = lax.broadcasted_iota(jnp.int32, (rows, keys), 0)
                column = lax.broadcasted_iota(jnp.int32, (rows, keys), 1)
                bias_ref[side] = jnp.where(column <= row, spread, HIDDEN)
        for seq in range(seq_count):
            outs = []
            for side in range(2):
                own_q = own_lanes(rows, side)
                own_k = own_lanes(keys, side)
                query = jnp.where(
                    own_q,
                    q_ref[seq * rows : (seq + 1) * rows, at : at + PAIR],
                    (lanes(rows) == DH * (1 - side) + 3).astype(LOW),
                )
                key = jnp.where(
                    own_k,
                    k_ref[seq * keys : (seq + 1) * keys, at : at + PAIR],
                    key_extras(keys, side, length_ref[seq]),
                )
                value = jnp.where(
                    own_k,
                    v_ref[seq * keys : (seq + 1) * keys, at : at + PAIR],
                    jnp.ones((), LOW),
                )
                parts = []
                for start in range(0, rows, block):
                    span = start + block if causal else keys
                    scores = nt(query[start : start + block], key[:span])
                    if causal:
                        scores = scores + bias_ref[side, start : start + block, :span]
                    top = jnp.max(scores, axis=1, keepdims=True)
                    weight = jnp.exp(scores - top)
                    out = nn(weight.astype(LOW), value[:span])
                    total = out[:, DH * (1 - side) : DH * (1 - side) + 1]
                    parts.append(out * (1.0 / total))
                    spot = pl.ds(seq * rows + start, block)
                    lane = lanes(block)
                    seen = total_ref[spot, :] if (pair or side) else jnp.zeros((block, PAIR), WIDE)
                    total_ref[spot, :] = jnp.where(
                        lane == 2 * pair + side, top + jnp.log(total), seen
                    )
                outs.append(jnp.concatenate(parts, axis=0))
            mix_ref[seq * rows : (seq + 1) * rows, at : at + PAIR] = jnp.where(
                own_lanes(rows, 0), outs[0], outs[1]
            ).astype(LOW)


def forward_kernel(
    causal, seq_count, length_ref, x_ref, source_ref, gain_ref, wq_ref, wk_ref, wv_ref, wo_ref, wave_ref,
    q_ref, k_ref, v_ref, mix_ref, total_ref, after_ref, normed, bias,
):
    group = pl.program_id(0)

    @pl.when(group == 0)
    def _():
        for at, size in chunks(x_ref.shape[0], 256):
            rows = x_ref[at : at + size, :].astype(WIDE)
            normed[at : at + size, :] = (rows * rms_rate(rows) * gain_ref[...]).astype(LOW)
            after_ref[at : at + size, :] = rows

    source = normed if causal else source_ref
    q_ref[...] = nn(normed[...], wq_ref[...]).astype(LOW)
    k_ref[...] = nn(source[...], wk_ref[...]).astype(LOW)
    v_ref[...] = nn(source[...], wv_ref[...]).astype(LOW)
    forward_body(causal, seq_count, length_ref, wave_ref, bias, q_ref, k_ref, v_ref, mix_ref, total_ref, group)
    after_ref[...] += nn(mix_ref[...], wo_ref[...])


def weight_specs(width):
    across = lambda at: pl.BlockSpec((None, width, GROUP), lambda g, at=at: (at, 0, g))
    return [across(0), across(1), across(2), pl.BlockSpec((None, GROUP, width), lambda g: (3, g, 0))]


def whole(shape):
    return pl.BlockSpec(shape, lambda g: (0,) * len(shape), pipeline_mode=pl.Buffered(1))


def columns(rows):
    return pl.BlockSpec((rows, GROUP), lambda g: (0, g))


def attention_forward(causal, x, source, lengths, gain, weights, wave):
    row_count, width = x.shape
    seq_count = lengths.shape[0]
    source_rows = row_count if causal else source.shape[0]
    length = row_count // seq_count
    groups = width // GROUP
    low = lambda rows: jax.ShapeDtypeStruct((rows, width), LOW)
    args = [lengths, x, source, gain, weights, weights, weights, weights, wave]
    return pl.pallas_call(
        functools.partial(forward_kernel, causal, seq_count),
        grid=(groups,),
        in_specs=[
            pl.BlockSpec(memory_space=pltpu.SMEM),
            whole(x.shape),
            whole(source.shape),
            whole(gain.shape),
            *weight_specs(width),
            whole(wave.shape),
        ],
        out_specs=[
            columns(row_count),
            columns(source_rows),
            columns(source_rows),
            columns(row_count),
            pl.BlockSpec((None, row_count, PAIR), lambda g: (g, 0, 0)),
            whole((row_count, width)),
        ],
        out_shape=[
            low(row_count),
            low(source_rows),
            low(source_rows),
            low(row_count),
            jax.ShapeDtypeStruct((groups, row_count, PAIR), WIDE),
            jax.ShapeDtypeStruct((row_count, width), WIDE),
        ],
        scratch_shapes=[
            pltpu.VMEM((row_count, width), LOW),
            pltpu.VMEM((2, length, length) if causal else (1, 8, PAIR), WIDE),
        ],
        cost_estimate=pl.CostEstimate(flops=int(27 * PEAK), bytes_accessed=20 << 20, transcendentals=0),
        compiler_params=pltpu.CompilerParams(vmem_limit_bytes=60 * MEGABYTE),
        name="self_forward" if causal else "cross_forward",
    )(*args)


def gelu_parts(gate):
    root = 0.7978845608028654
    square = gate * gate
    inner = jnp.tanh(root * gate * (1.0 + 0.044715 * square))
    half = 0.5 * (1.0 + inner)
    value = gate * half
    slope = half + 0.5 * gate * (1.0 - inner * inner) * (root * (1.0 + 3 * 0.044715 * square))
    return value, slope


def rms_back(rows, gain, grad):
    rate = rms_rate(rows)
    scaled = rows * rate
    low = grad * gain
    grad_rows = rate * (low - scaled * jnp.mean(scaled * low, axis=-1, keepdims=True))
    return grad_rows, jnp.sum(grad * scaled, axis=0, keepdims=True)


def shard_slot(where_ref, shard):
    return (shard % LINE_CORES) ^ where_ref[2], lax.rem(shard // LINE_CORES - where_ref[1] + LINE, LINE)


def feed_kernel(
    seq_count, pieces, length_ref, where_ref, after_ref, out_grad_ref, gain_ref, wg_ref, wu_ref, *refs,
):
    wd_refs, (layer_ref, grad_cross_ref, dwg_ref, dwu_ref) = refs[:pieces], refs[pieces : pieces + 4]
    near_refs = refs[pieces + 4 : pieces + 8]
    dgain_ref, normed, normed_t, down, out_total, grad_total, cut, *held = refs[pieces + 8 :]
    step = pl.program_id(0)
    row_count = after_ref.shape[0]
    length = row_count // seq_count

    def live(at, size):
        position = lax.broadcasted_iota(jnp.int32, (size, 1), 0) + (at % length)
        return (position < length_ref[at // length]).astype(WIDE)

    @pl.when(step == 0)
    def _():
        if pieces > 1:
            place = lambda quarter, at: held[0].at[pl.ds((at * 4 + quarter) * cut.shape[2], cut.shape[2])]
            copies = piece_copies(wd_refs, where_ref, place, held[1])
            for copy in copies:
                copy.start()
        for at, size in chunks(row_count, 256):
            rows = after_ref[at : at + size, :]
            low = (rows * rms_rate(rows) * gain_ref[...]).astype(LOW)
            normed[at : at + size, :] = low
            normed_t[:, at : at + size] = low.T
            down[at : at + size, :] = (
                out_grad_ref[at : at + size, :].astype(WIDE) * live(at, size)
            ).astype(LOW)
            out_total[at : at + size, :] = rows
            grad_total[at : at + size, :] = jnp.zeros((size, rows.shape[1]), WIDE)
        if pieces > 1:
            for copy in copies:
                copy.wait()

    block = wg_ref.shape[1]
    if pieces > 1:
        wd_ref = held[0].at[pl.ds(pl.multiple_of(step * block, block), block)]
    else:
        wd_ref = wd_refs[0]
    gate = nn(normed[...], wg_ref[...])
    up = nn(normed[...], wu_ref[...])
    value, slope = gelu_parts(gate)
    hidden = (value * up).astype(LOW)
    out_total[...] += nn(hidden, wd_ref[...])
    grad_hidden = nt(down[...], wd_ref[...])
    cut[...] = tn(hidden, down[...]).astype(LOW).reshape(cut.shape)
    for part in range(cut.shape[0]):
        core, hop = shard_slot(where_ref, step * cut.shape[0] + part)
        for way in range(4):
            near_refs[way][core, hop] = cut[part, where_ref[0] ^ way]
    grad_gate = (grad_hidden * up * slope).astype(LOW)
    grad_up = (grad_hidden * value).astype(LOW)
    dwg_ref[...] = nn(normed_t[...], grad_gate).astype(LOW)
    dwu_ref[...] = nn(normed_t[...], grad_up).astype(LOW)
    grad_total[...] += nt(grad_gate, wg_ref[...]) + nt(grad_up, wu_ref[...])

    @pl.when(step == pl.num_programs(0) - 1)
    def _():
        dgain = jnp.zeros(dgain_ref.shape, WIDE)
        for at, size in chunks(row_count, 256):
            part = slice(at, at + size)
            layer_ref[part, :] = (out_total[part, :] * live(at, size)).astype(LOW)
            grad_rows, gain_part = rms_back(after_ref[part, :], gain_ref[...], grad_total[part, :])
            dgain = dgain + gain_part
            grad_cross_ref[part, :] = (
                out_grad_ref[part, :].astype(WIDE) * live(at, size) + grad_rows
            )
        dgain_ref[...] = dgain


def feed_forward_both(after, out_grad, lengths, where, gain, w_in, w_out):
    row_count, width = after.shape
    hidden = w_in.shape[2]
    each = hidden // (LINE * LINE_CORES)
    block = 2 * each
    seq_count = lengths.shape[0]
    wide = pl.BlockSpec((None, width, block), lambda g: (0, 0, g))
    wide_up = pl.BlockSpec((None, width, block), lambda g: (1, 0, g))
    tall = pl.BlockSpec((block, width), lambda g: (g, 0))
    flat = pl.BlockSpec((width, block), lambda g: (0, g))
    near = (LINE_CORES, LINE, each // 4, width)
    pieces = len(w_out)
    held = [pltpu.VMEM((hidden, width), LOW), pltpu.SemaphoreType.DMA((pieces * LINE,))] if pieces > 1 else []
    return pl.pallas_call(
        functools.partial(feed_kernel, seq_count, pieces),
        grid=(hidden // block,),
        in_specs=[
            pl.BlockSpec(memory_space=pltpu.SMEM),
            pl.BlockSpec(memory_space=pltpu.SMEM),
            whole(after.shape),
            whole(out_grad.shape),
            whole(gain.shape),
            wide,
            wide_up,
            *([pl.BlockSpec(memory_space=pl.ANY)] * pieces if pieces > 1 else [tall]),
        ],
        out_specs=[whole(after.shape), whole(after.shape), flat, flat, *[whole(near)] * 4, whole((1, width))],
        out_shape=[
            jax.ShapeDtypeStruct((row_count, width), LOW),
            jax.ShapeDtypeStruct((row_count, width), WIDE),
            jax.ShapeDtypeStruct((width, hidden), LOW),
            jax.ShapeDtypeStruct((width, hidden), LOW),
            *[jax.ShapeDtypeStruct(near, LOW)] * 4,
            jax.ShapeDtypeStruct((1, width), WIDE),
        ],
        scratch_shapes=[
            pltpu.VMEM((row_count, width), LOW),
            pltpu.VMEM((width, row_count), LOW),
            pltpu.VMEM((row_count, width), LOW),
            pltpu.VMEM((row_count, width), WIDE),
            pltpu.VMEM((row_count, width), WIDE),
            pltpu.VMEM((2, 4, each // 4, width), LOW),
            *held,
        ],
        cost_estimate=pl.CostEstimate(flops=int(46 * PEAK), bytes_accessed=40 << 20, transcendentals=0),
        compiler_params=pltpu.CompilerParams(vmem_limit_bytes=60 * MEGABYTE),
        name="feed_forward_both",
    )(lengths, where, after, out_grad, gain, w_in, w_in, *w_out)


def backward_kernel(
    causal, seq_count, length_ref, where_ref, x_ref, source_ref, grad_ref, gain_ref, wq_ref, wo_ref, wave_ref,
    q_ref, k_ref, v_ref, mix_ref, total_ref, mix_all_ref, mix_past_ref, *refs,
):
    if causal:
        gq, gk_out_ref, gv_out_ref, dw_ref, dist_ref = refs[:5]
        normed_t, branch, grad_mix, bias, score_sum = refs[5:]
        source_t = normed_t
    else:
        grad_x_ref, gk_out_ref, gv_out_ref, dgain_ref = refs[:4]
        near_refs, far_ref = refs[4:8], refs[8]
        normed_t, branch, grad_mix, gq, source_t, mix_t, grad_total, dw_ref, past = refs[9:]
    group = pl.program_id(0)
    row_count = x_ref.shape[0]
    rows = q_ref.shape[0] // seq_count
    keys = k_ref.shape[0] // seq_count
    block = rows

    @pl.when(group == 0)
    def _():
        for at, size in chunks(row_count, 256):
            value = x_ref[at : at + size, :].astype(WIDE)
            low = (value * rms_rate(value) * gain_ref[...]).astype(LOW)
            normed_t[:, at : at + size] = low.T
            branch[at : at + size, :] = grad_ref[at : at + size, :].astype(LOW)
            if not causal:
                mix_t[:, at : at + size] = mix_all_ref[at : at + size, :].T
                grad_total[at : at + size, :] = jnp.zeros((size, value.shape[1]), WIDE)
        if not causal:
            for at, size in chunks(source_ref.shape[0], 256):
                source_t[:, at : at + size] = source_ref[at : at + size, :].T

    grad_mix[...] = nt(branch[...], wo_ref[...]).astype(LOW)
    if not causal:
        across = pl.ds(pl.multiple_of(group * GROUP, GROUP), GROUP)
        put = lambda at, value: dw_ref.__setitem__(at, value.astype(LOW).reshape(dw_ref.shape[1:]))
        put(3, nn(mix_t[...], branch[:, across]))

    for pair in range(2):
        at = pair * PAIR
        if causal:
            for side in range(2):
                head = 2 * pair + side
                wave = wave_ref[pl.ds(group * 4 + head, 1), :]
                spread = pltpu.roll(
                    jnp.broadcast_to(wave, (keys, rows)), 0, 1, stride=1, stride_axis=0
                )
                row = lax.broadcasted_iota(jnp.int32, (keys, rows), 0)
                column = lax.broadcasted_iota(jnp.int32, (keys, rows), 1)
                bias[side] = jnp.where(column >= row, spread, HIDDEN)
        for seq in range(seq_count):
            span_q = slice(seq * rows, (seq + 1) * rows)
            span_k = slice(seq * keys, (seq + 1) * keys)
            sides = []
            for side in range(2):
                head = 2 * pair + side
                own_q = own_lanes(rows, side)
                own_k = own_lanes(keys, side)
                total = jnp.sum(
                    jnp.where(lanes(rows) == head, total_ref[span_q, :], 0.0), axis=1, keepdims=True
                )
                grad_low = grad_mix[span_q, at : at + PAIR]
                product = grad_low.astype(WIDE) * mix_ref[span_q, at : at + PAIR].astype(WIDE)
                delta = jnp.sum(jnp.where(own_q, product, 0.0), axis=1, keepdims=True)
                query = jnp.where(
                    own_q, q_ref[span_q, at : at + PAIR], row_extras(rows, side, -total, 1.0)
                )
                grad_out = jnp.where(own_q, grad_low, row_extras(rows, side, -delta, 0.0))
                key = jnp.where(
                    own_k,
                    k_ref[span_k, at : at + PAIR],
                    key_extras(keys, side, length_ref[seq]),
                )
                value = jnp.where(own_k, v_ref[span_k, at : at + PAIR], jnp.ones((), LOW))
                grad_query = []
                grad_key = None
                grad_value = None
                for start in range(0, rows, block):
                    span = start + block if causal else keys
                    scores = nt(key[:span], query[start : start + block])
                    if causal:
                        scores = scores + bias[side, :span, start : start + block]
                    weight = jnp.exp(scores)
                    low = weight.astype(LOW)
                    grad_weight = nt(value[:span], grad_out[start : start + block])
                    grad_score = (weight * grad_weight).astype(LOW)
                    if causal:
                        if seq == 0:
                            score_sum[side, :span, start : start + block] = grad_score.astype(WIDE)
                        else:
                            score_sum[side, :span, start : start + block] += grad_score.astype(WIDE)
                    key_part = nn(grad_score, query[start : start + block])
                    value_part = nn(low, grad_out[start : start + block])
                    grad_query.append(tn(grad_score, key[:span]))
                    if causal and start == 0 and rows > block:
                        rest = jnp.zeros((keys - span, PAIR), WIDE)
                        key_part = jnp.concatenate([key_part, rest], axis=0)
                        value_part = jnp.concatenate([value_part, rest], axis=0)
                    grad_key = key_part if grad_key is None else grad_key + key_part
                    grad_value = value_part if grad_value is None else grad_value + value_part
                sides.append((jnp.concatenate(grad_query, axis=0), grad_key, grad_value))
            pick_q = own_lanes(rows, 0)
            pick_k = own_lanes(keys, 0)
            gq[span_q, at : at + PAIR] = jnp.where(pick_q, sides[0][0], sides[1][0]).astype(LOW)
            gk_out_ref[span_k, at : at + PAIR] = jnp.where(pick_k, sides[0][1], sides[1][1]).astype(LOW)
            gv_out_ref[span_k, at : at + PAIR] = jnp.where(pick_k, sides[0][2], sides[1][2]).astype(LOW)
        if causal:
            for side in range(2):
                head = 2 * pair + side
                row = lax.broadcasted_iota(jnp.int32, (keys, rows), 0)
                column = lax.broadcasted_iota(jnp.int32, (keys, rows), 1)
                held = jnp.where(column >= row, score_sum[side], 0.0)
                while held.shape[0] > 1:
                    half = held.shape[0] // 2
                    held = held[:half] + pltpu.roll(held[half:], rows - half, 1)
                dist_ref[pl.ds(group * 4 + head, 1), :] = held

    if causal:
        dw_ref[0] = nn(normed_t[...], gq[...]).astype(LOW)
        dw_ref[1] = nn(source_t[...], gk_out_ref[...]).astype(LOW)
        dw_ref[2] = nn(source_t[...], gv_out_ref[...]).astype(LOW)
        return
    put(0, nn(normed_t[...], gq[...]))
    put(1, nn(source_t[...], gk_out_ref[...]))
    put(2, nn(source_t[...], gv_out_ref[...]))
    grad_total[...] += nt(gq[...], wq_ref[...])
    rep, line, core = where_ref[0], where_ref[1], where_ref[2]
    held = dw_ref.shape[2]
    slots = []
    for way in range(4):
        for hop in range(LINE):
            at = lax.rem(line + hop, LINE) * LINE_CORES
            slots.append((near_refs[way].at[hop], rep ^ way, at + core))
            slots.append((far_ref.at[way, hop], rep ^ way, at + (core ^ 1)))
    for slot, quarter, shard in slots:
        slot[0:held, across] = dw_ref[quarter, shard]

    @pl.when(group == pl.num_programs(0) - 1)
    def _():
        dgain = jnp.zeros(dgain_ref.shape, WIDE)
        for at, size in chunks(row_count, 256):
            part = slice(at, at + size)
            grad_rows, gain_part = rms_back(
                x_ref[part, :].astype(WIDE), gain_ref[...], grad_total[part, :]
            )
            dgain = dgain + gain_part
            grad_rows = grad_ref[part, :] + grad_rows
            grad_x_ref[part, :] = grad_rows
            branch[part, :] = grad_rows.astype(LOW)
            mix_t[:, part] = mix_past_ref[part, :].T
        dgain_ref[...] = dgain
        thirds = nn(mix_t[...], branch[...]).astype(LOW)
        past[:, 0:3] = thirds.reshape(past.shape[0], 3, *past.shape[2:])
        past[:, 3] = jnp.zeros_like(past[:, 3])
        for slot, quarter, shard in slots:
            slot[held:, :] = past[shard, quarter]


def attention_backward(causal, x, source, grad, lengths, where, gain, weights, wave, kept, mix, past):
    row_count, width = x.shape
    seq_count = lengths.shape[0]
    source_rows = row_count if causal else source.shape[0]
    length = row_count // seq_count
    groups = width // GROUP
    low = lambda rows: jax.ShapeDtypeStruct((rows, width), LOW)
    if causal:
        out_specs = [
            columns(row_count), columns(source_rows), columns(source_rows),
            pl.BlockSpec((3, width, GROUP), lambda g: (0, 0, g)), whole(wave.shape),
        ]
        out_shape = [
            low(row_count), low(source_rows), low(source_rows),
            jax.ShapeDtypeStruct((3, width, width), LOW), jax.ShapeDtypeStruct(wave.shape, WIDE),
        ]
        scratch = [pltpu.VMEM((2, length, length), WIDE)] * 2
    else:
        shards = LINE * LINE_CORES
        each, third = width // shards, width // shards // 3
        near = (LINE, each + third, width)
        out_specs = [
            whole((row_count, width)), columns(source_rows), columns(source_rows), whole((1, width)),
            *[whole(near)] * 4, whole((4, *near)),
        ]
        out_shape = [
            jax.ShapeDtypeStruct((row_count, width), WIDE), low(source_rows), low(source_rows),
            jax.ShapeDtypeStruct((1, width), WIDE), *[jax.ShapeDtypeStruct(near, LOW)] * 4,
            jax.ShapeDtypeStruct((4, *near), LOW),
        ]
        scratch = [
            pltpu.VMEM((row_count, GROUP), LOW),
            pltpu.VMEM((width, source_rows), LOW),
            pltpu.VMEM((width, row_count), LOW),
            pltpu.VMEM((row_count, width), WIDE),
            pltpu.VMEM((4, shards, each, GROUP), LOW),
            pltpu.VMEM((shards, 4, third, width), LOW),
        ]
    return pl.pallas_call(
        functools.partial(backward_kernel, causal, seq_count),
        grid=(groups,),
        in_specs=[
            pl.BlockSpec(memory_space=pltpu.SMEM),
            pl.BlockSpec(memory_space=pltpu.SMEM),
            whole(x.shape),
            whole(source.shape),
            whole(grad.shape),
            whole(gain.shape),
            weight_specs(width)[0],
            weight_specs(width)[3],
            whole(wave.shape),
            columns(row_count),
            columns(source_rows),
            columns(source_rows),
            columns(row_count),
            pl.BlockSpec((None, row_count, PAIR), lambda g: (g, 0, 0)),
            whole(mix.shape),
            whole(past.shape),
        ],
        out_specs=out_specs,
        out_shape=out_shape,
        scratch_shapes=[
            pltpu.VMEM((width, row_count), LOW),
            pltpu.VMEM((row_count, width), LOW),
            pltpu.VMEM((row_count, GROUP), LOW),
            *scratch,
        ],
        cost_estimate=pl.CostEstimate(flops=int(45 * PEAK), bytes_accessed=40 << 20, transcendentals=0),
        compiler_params=pltpu.CompilerParams(vmem_limit_bytes=60 * MEGABYTE),
        name="self_backward" if causal else "cross_backward",
    )(lengths, where, x, source, grad, gain, weights, weights, wave, *kept, mix, past)


def input_kernel(gq_ref, gk_ref, gv_ref, wq_ref, wk_ref, wv_ref, x_ref, grad_ref, gain_ref, out_ref, dgain_ref):
    total = nt(gq_ref[...], wq_ref[...]) + nt(gk_ref[...], wk_ref[...]) + nt(gv_ref[...], wv_ref[...])
    grad_rows, dgain = rms_back(x_ref[...].astype(WIDE), gain_ref[...], total)
    out_ref[...] = grad_ref[...] + grad_rows

    @pl.when(pl.program_id(0) == 0)
    def _():
        dgain_ref[...] = jnp.zeros_like(dgain_ref)

    dgain_ref[...] += dgain


def input_gradient(grads, weights, x, grad, gain):
    rows, width = x.shape
    block = 256
    rowwise = pl.BlockSpec((block, width), lambda g: (g, 0))
    matrix = lambda at: pl.BlockSpec((None, width, width), lambda g: (at, 0, 0))
    return pl.pallas_call(
        input_kernel,
        grid=(rows // block,),
        in_specs=[rowwise, rowwise, rowwise, matrix(0), matrix(1), matrix(2), rowwise, rowwise, whole((1, width))],
        out_specs=[rowwise, whole((1, width))],
        out_shape=[jax.ShapeDtypeStruct((rows, width), WIDE), jax.ShapeDtypeStruct((1, width), WIDE)],
        cost_estimate=pl.CostEstimate(flops=int(8 * PEAK), bytes_accessed=12 << 20, transcendentals=0),
        compiler_params=pltpu.CompilerParams(vmem_limit_bytes=60 * MEGABYTE),
        name="input_gradient",
    )(*grads, weights, weights, weights, x, grad, gain)


def memory_kernel(gk_ref, gv_ref, wk_ref, wv_ref, out_ref):
    out_ref[...] = nt(gk_ref[...], wk_ref[...]) + nt(gv_ref[...], wv_ref[...])


def memory_gradient(grad_key, grad_value, weights):
    rows, width = grad_key.shape
    block = 256
    rowwise = pl.BlockSpec((block, width), lambda g: (g, 0))
    matrix = lambda at: pl.BlockSpec((None, width, width), lambda g: (at, 0, 0))
    return pl.pallas_call(
        memory_kernel,
        grid=(rows // block,),
        in_specs=[rowwise, rowwise, matrix(1), matrix(2)],
        out_specs=rowwise,
        out_shape=jax.ShapeDtypeStruct((rows, width), WIDE),
        cost_estimate=pl.CostEstimate(flops=int(7 * PEAK), bytes_accessed=10 << 20, transcendentals=0),
        compiler_params=pltpu.CompilerParams(vmem_limit_bytes=60 * MEGABYTE),
        name="memory_gradient",
    )(grad_key, grad_value, weights, weights)


LANES = 128
IN_AT, OUT_AT, CROSS_AT, PAST_AT, SELF_AT, SMALL_AT = 0, 1, 2, 3, 4, 5


def vector_rows(width, hidden, small):
    one, big = width // LANES, hidden // LANES
    starts = [0]
    for size in (2 * big, one, 4 * one, one, 3 * one, small // LANES):
        starts.append(starts[-1] + size)
    return starts


def spill(ref, at, row):
    for part in range(row.shape[1] // LANES):
        ref[pl.ds(at + part, 1), :] = row[:, part * LANES : (part + 1) * LANES]


def fetch(ref, at, width):
    return jnp.concatenate([ref[at + part : at + part + 1, :] for part in range(width // LANES)], axis=1)


def column_sums(rows):
    return jnp.sum(rows * rows + TINY_TERM, axis=0, keepdims=True)


def in_kernel(factor, *refs):
    in_refs, in_ref, sums_ref = refs[:4], refs[4], refs[5]
    big = in_ref.shape[2] // LANES
    for matrix in range(2):
        piece = sum(ref[matrix].astype(WIDE) for ref in in_refs).astype(LOW)
        in_ref[matrix] = piece
        spill(sums_ref, matrix * big, column_sums(piece.astype(WIDE) * factor))


def gated_sums(factor, in_parts):
    shape = in_parts[0].shape
    return pl.pallas_call(
        functools.partial(in_kernel, factor),
        in_specs=[pl.BlockSpec(memory_space=pltpu.VMEM)] * 4,
        out_specs=[pl.BlockSpec(memory_space=pltpu.VMEM)] * 2,
        out_shape=[
            jax.ShapeDtypeStruct(shape, LOW),
            jax.ShapeDtypeStruct((2 * shape[2] // LANES, LANES), WIDE),
        ],
        cost_estimate=pl.CostEstimate(flops=int(2 * PEAK), bytes_accessed=2 << 20, transcendentals=0),
        compiler_params=pltpu.CompilerParams(vmem_limit_bytes=60 * MEGABYTE),
        name="gated_sums",
    )(*in_parts)


def early_kernel(factor, starts, where_ref, *refs):
    line_refs, sums_ref, constant_ref, line_ref, vector_ref = refs[0:4], *refs[4:]
    rep = where_ref[0]
    one = line_ref.shape[1] // LANES
    each = line_ref.shape[0] // 2
    third = each // 3
    line = sum(ref[...].astype(WIDE) for ref in line_refs).astype(LOW)
    line_ref[...] = line
    vector_ref[...] = jnp.zeros_like(vector_ref)
    vector_ref[starts[IN_AT] : starts[OUT_AT], :] = sums_ref[...]
    line = line.astype(WIDE) * factor
    spill(vector_ref, starts[OUT_AT], column_sums(line[each + third :]))
    spill(vector_ref, starts[CROSS_AT] + rep * one, column_sums(line[:each]))
    past = column_sums(line[each : each + third])
    spill(vector_ref, starts[PAST_AT], past * (rep < 3).astype(WIDE))
    vector_ref[starts[-1] : starts[-1] + 1, :] = constant_ref[...]


def early_sums(factor, starts, where, line_parts, sums, constants):
    rows = -(-(starts[-1] + 1) // 8) * 8
    return pl.pallas_call(
        functools.partial(early_kernel, factor, starts),
        in_specs=[pl.BlockSpec(memory_space=pltpu.SMEM)] + [pl.BlockSpec(memory_space=pltpu.VMEM)] * 6,
        out_specs=[pl.BlockSpec(memory_space=pltpu.VMEM)] * 2,
        out_shape=[
            jax.ShapeDtypeStruct(line_parts[0].shape, LOW),
            jax.ShapeDtypeStruct((rows, LANES), WIDE),
        ],
        cost_estimate=pl.CostEstimate(flops=int(2 * PEAK), bytes_accessed=2 << 20, transcendentals=0),
        compiler_params=pltpu.CompilerParams(vmem_limit_bytes=60 * MEGABYTE),
        name="early_sums",
    )(where, *line_parts, sums, constants)


def late_kernel(factor, starts, *refs):
    part_refs, small_ref, early_ref, piece_ref, vector_ref = refs[0:4], refs[4], refs[5], refs[6], refs[7]
    vector_ref[...] = early_ref[...]
    one = piece_ref.shape[2] // LANES
    for matrix in range(3):
        piece = sum(ref[matrix].astype(WIDE) for ref in part_refs).astype(LOW)
        piece_ref[matrix] = piece
        spill(vector_ref, starts[SELF_AT] + matrix * one, column_sums(piece.astype(WIDE) * factor))
    vector_ref[starts[SMALL_AT] : starts[SMALL_AT + 1], :] = small_ref[...]


def late_sums(factor, starts, self_parts, small, early):
    return pl.pallas_call(
        functools.partial(late_kernel, factor, starts),
        in_specs=[pl.BlockSpec(memory_space=pltpu.VMEM)] * 6,
        out_specs=[pl.BlockSpec(memory_space=pltpu.VMEM)] * 2,
        out_shape=[
            jax.ShapeDtypeStruct(self_parts[0].shape, LOW),
            jax.ShapeDtypeStruct(early.shape, WIDE),
        ],
        cost_estimate=pl.CostEstimate(flops=int(2 * PEAK), bytes_accessed=1 << 20, transcendentals=0),
        compiler_params=pltpu.CompilerParams(vmem_limit_bytes=60 * MEGABYTE),
        name="late_sums",
    )(*self_parts, small, early)


def to_column(row):
    size = row.shape[1]
    same = lax.broadcasted_iota(jnp.int32, (size, size), 0) == lax.broadcasted_iota(jnp.int32, (size, size), 1)
    return jnp.sum(jnp.where(same, jnp.broadcast_to(row, (size, size)), 0.0), axis=1, keepdims=True)


def to_row(column):
    size = column.shape[0]
    same = lax.broadcasted_iota(jnp.int32, (size, size), 0) == lax.broadcasted_iota(jnp.int32, (size, size), 1)
    return jnp.sum(jnp.where(same, jnp.broadcast_to(column, (size, size)), 0.0), axis=0, keepdims=True)


def update_kernel(factor, starts, shards, where_ref, total_ref, *refs):
    in_near, line_near, self_near = refs[0:4], refs[4:8], refs[8:12]
    (
        in_ref, out_ref, cross_ref, self_ref, in_rows_ref, out_rows_ref, cross_rows_ref, self_rows_ref,
        in_cols_ref, out_cols_ref, cross_cols_ref, self_cols_ref,
    ) = refs[12:24]
    (
        in_grad, out_grad, cross_grad, self_grad, new_in, new_out, new_cross, new_self,
        new_in_rows, new_out_rows, new_cross_rows, new_self_rows,
        new_in_cols, new_out_cols, new_cross_cols, new_self_cols,
        gains_grad, table_grad, new_gains, new_table, new_gain_moment, new_table_moment,
    ) = refs[28:50]
    gains_ref, table_ref, gain_moment_ref, table_moment_ref = refs[24:28]
    in_held, line_held, self_held = refs[50:]
    rep = where_ref[0]
    for way in range(4):
        in_held[rep ^ way] = in_near[way][...]
        line_held[rep ^ way] = line_near[way][...]
        self_held[rep ^ way] = self_near[way][...]
    width = cross_ref.shape[2]
    one, big = width // LANES, in_ref.shape[2] // LANES
    each = cross_ref.shape[1]
    third = each // 3
    scalars = total_ref[starts[-1] : starts[-1] + 1, :]

    def step(at, pieces, index, weight, grad, new, rows_ref, new_rows, cols_ref, new_cols, row_at, scalar):
        rows, cols = weight.shape[-2:]
        spans = []
        start = 0
        for piece in pieces:
            spans.append(slice(start, start + piece.shape[0]))
            start += piece.shape[0]
        whole_rows = rows * shards
        col_sum = fetch(total_ref, at, cols)
        state_sum = scalars[:, scalar : scalar + 1]
        square = scalars[:, 16 + scalar : 17 + scalar]
        col_moment = DECAY_RATE * cols_ref[row_at : row_at + 1, :] + (1.0 - DECAY_RATE) * col_sum / whole_rows
        new_cols[row_at : row_at + 1, :] = col_moment
        row_mean = (
            DECAY_RATE * state_sum
            + (1.0 - DECAY_RATE) / cols * jnp.sum(col_sum, axis=1, keepdims=True)
        ) / whole_rows
        blocks = [piece.astype(WIDE) * factor for piece in pieces]
        means = jnp.concatenate(
            [jnp.mean(block * block + TINY_TERM, axis=1, keepdims=True) for block in blocks], axis=0
        )
        row_moment = DECAY_RATE * to_column(rows_ref[row_at : row_at + 1, :]) + (1.0 - DECAY_RATE) * means
        new_rows[row_at : row_at + 1, :] = to_row(row_moment)
        size = STEP_RATE * jnp.sqrt(square / (whole_rows * cols) + 1e-06)
        scale = size * lax.rsqrt(row_moment / row_mean)
        across = lax.rsqrt(col_moment)
        for block, span in zip(blocks, spans):
            place = (span, slice(None)) if index is None else (index, span, slice(None))
            grad[place] = block
            new[place] = weight[place] - scale[span] * block * across

    def plain(grad, ref, moment_ref, square, out, new, new_moment, spot):
        moment = DECAY_RATE * moment_ref[spot] + (1.0 - DECAY_RATE) * (grad * grad + TINY_TERM)
        out[spot] = grad
        new_moment[spot] = moment
        new[spot] = ref[spot] - STEP_RATE * jnp.sqrt(square + 1e-06) * grad * lax.rsqrt(moment)

    part = gains_ref.shape[1]
    for norm in range(3):
        row = fetch(total_ref, starts[SMALL_AT] + norm * one, width)
        mine = where_ref[1] * LINE_CORES + where_ref[2]
        row = pltpu.roll(jnp.broadcast_to(row, (8, width)), lax.rem(width - mine * part, width), 1)
        plain(
            row[0:1, :part], gains_ref, gain_moment_ref, scalars[:, 27 + norm : 28 + norm] / width,
            gains_grad, new_gains, new_gain_moment, (slice(norm, norm + 1), slice(None)),
        )
    table = total_ref[starts[SMALL_AT] + 3 * one : starts[SMALL_AT + 1], 0 : table_ref.shape[1]]
    square = jnp.sum(jnp.sum(table_ref[...] * table_ref[...], axis=1, keepdims=True), axis=0, keepdims=True)
    plain(
        table, table_ref, table_moment_ref, square / (table_ref.shape[0] * table_ref.shape[1]),
        table_grad, new_table, new_table_moment, (slice(None), slice(None)),
    )
    quarters = range(4)
    for matrix in range(2):
        step(
            starts[IN_AT] + matrix * big, [in_held[at, matrix] for at in quarters], matrix,
            in_ref, in_grad, new_in, in_rows_ref, new_in_rows, in_cols_ref, new_in_cols, matrix, matrix,
        )
    step(
        starts[OUT_AT], [line_held[at, each + third :, :] for at in quarters], None,
        out_ref, out_grad, new_out, out_rows_ref, new_out_rows, out_cols_ref, new_out_cols, 0, 2,
    )
    for matrix in range(4):
        step(
            starts[CROSS_AT] + matrix * one, [line_held[matrix, 0:each, :]], matrix,
            cross_ref, cross_grad, new_cross, cross_rows_ref, new_cross_rows, cross_cols_ref, new_cross_cols,
            matrix, 3 + matrix,
        )
        if matrix < 3:
            at, pieces = starts[SELF_AT] + matrix * one, [self_held[at, matrix] for at in quarters]
        else:
            at, pieces = starts[PAST_AT], [line_held[at, each : each + third, :] for at in range(3)]
        step(
            at, pieces, matrix, self_ref, self_grad, new_self, self_rows_ref, new_self_rows,
            self_cols_ref, new_self_cols, matrix, 7 + matrix,
        )


def update_all(
    factor, starts, shards, where, total, in_near, line_near, self_near, weights, rows, cols, plain
):
    outs = (*weights, *weights, *rows, *cols, *plain[:2], *plain[:2], *plain[2:])
    out_shape = [jax.ShapeDtypeStruct(value.shape, WIDE) for value in outs]
    spec = pl.BlockSpec(memory_space=pltpu.VMEM)
    return pl.pallas_call(
        functools.partial(update_kernel, factor, starts, shards),
        in_specs=[pl.BlockSpec(memory_space=pltpu.SMEM)] + [spec] * 29,
        out_specs=[spec] * 22,
        out_shape=out_shape,
        scratch_shapes=[pltpu.VMEM((4, *near[0].shape), LOW) for near in (in_near, line_near, self_near)],
        cost_estimate=pl.CostEstimate(flops=int(8 * PEAK), bytes_accessed=16 << 20, transcendentals=0),
        compiler_params=pltpu.CompilerParams(vmem_limit_bytes=60 * MEGABYTE),
        name="update_all",
    )(where, total, *in_near, *line_near, *self_near, *weights, *rows, *cols, *plain)


def flat_permute(value, target):
    reps, shards = lax.axis_size("rep"), lax.axis_size("fsdp")
    pairs = []
    for rep in range(reps):
        for shard in range(shards):
            to_rep, to_shard = target(rep, shard)
            pairs.append((rep * shards + shard, to_rep * shards + to_shard))
    return lax.ppermute(value, ("rep", "fsdp"), pairs)


def from_rep(value, way):
    return flat_permute(value, lambda rep, shard: (rep ^ way, shard))


def from_shard(value, way):
    return flat_permute(value, lambda rep, shard: (rep, shard ^ way))


def from_line(value, hops):
    shards = lax.axis_size("fsdp")
    return flat_permute(value, lambda rep, shard: (rep, (shard + LINE_CORES * hops) % shards))


def along_line(piece):
    return jnp.stack([piece] + [from_line(piece, hop) for hop in range(1, LINE)])


def across_reps(line):
    return [line] + [from_rep(line, way) for way in range(1, 4)]


def with_partner(parts):
    return parts + [from_shard(part, 1) for part in parts]


def add_line(parts):
    return [parts[0]] + [from_line(parts[hop], hop) for hop in range(1, LINE)]


def assemble_kernel(place, where_ref, *refs):
    copies = piece_copies(refs[:8], where_ref, functools.partial(place, refs[8]), refs[9])
    for copy in copies:
        copy.start()
    for copy in copies:
        copy.wait()


def assemble(parts, where, shape, place, name):
    hops = parts[0].shape[0]
    return pl.pallas_call(
        functools.partial(assemble_kernel, place),
        in_specs=[pl.BlockSpec(memory_space=pltpu.SMEM)] + [pl.BlockSpec(memory_space=pl.ANY)] * 8,
        out_specs=pl.BlockSpec(memory_space=pltpu.VMEM),
        out_shape=jax.ShapeDtypeStruct(shape, LOW),
        scratch_shapes=[pltpu.SemaphoreType.DMA((8 * hops,))],
        cost_estimate=pl.CostEstimate(flops=int(4 * PEAK), bytes_accessed=8 << 20, transcendentals=0),
        compiler_params=pltpu.CompilerParams(vmem_limit_bytes=60 * MEGABYTE),
        name=name,
    )(where, *parts)


def rep_parts(parts, axis):
    rep = lax.axis_index("rep")
    pick = lambda at: lax.dynamic_index_in_dim(parts, at, axis, keepdims=False)
    return [pick(rep)] + [from_rep(pick(rep ^ way), way) for way in range(1, 4)]


def add_up(parts):
    return sum(part.astype(WIDE) for part in parts).astype(LOW)


def rep_near(piece):
    return [piece] + [from_rep(piece, way) for way in range(1, 4)]


def rep_order(near):
    rep = lax.axis_index("rep")
    return [lax.select_n(rep, *[near[at ^ own] for own in range(4)]) for at in range(4)]


def hold(*values):
    return lax.optimization_barrier(values)


def butterfly(vector, move, size):
    way = 1
    while way < size:
        vector = vector + move(vector, way)
        way *= 2
    return vector


def after(value, *earlier):
    return lax.optimization_barrier((value, *earlier))[0]


def row_moments(gradient, row_state):
    squares = gradient * gradient + TINY_TERM
    return DECAY_RATE * row_state + (1.0 - DECAY_RATE) * jnp.mean(squares, axis=-1)


def factored_sums(gradient, row_state):
    squares = gradient * gradient + TINY_TERM
    return jnp.sum(squares, axis=1), jnp.sum(row_moments(gradient, row_state), axis=1)


def pack(values):
    return jnp.concatenate([value.reshape(-1) for value in values])


def unpack(vector, values):
    out = []
    for value in values:
        out.append(vector[: value.size].reshape(value.shape))
        vector = vector[value.size :]
    return out


def factored_update(gradient, weight, row_moment, col_state, col_sum, row_sum, square):
    count, rows, cols = weight.shape
    whole_rows = rows * lax.axis_size("fsdp")
    col_moment = DECAY_RATE * col_state + (1.0 - DECAY_RATE) * col_sum / whole_rows
    scale = lax.rsqrt(row_moment / (row_sum[:, None] / whole_rows))
    step = STEP_RATE * jnp.sqrt(square / (whole_rows * cols) + 1e-06)
    direction = gradient * scale[:, :, None] * lax.rsqrt(col_moment)[:, None, :]
    return weight - step[:, None, None] * direction, col_moment


def plain_update(gradient, weight, moment, square):
    moment = DECAY_RATE * moment + (1.0 - DECAY_RATE) * (gradient * gradient + TINY_TERM)
    step = STEP_RATE * jnp.sqrt(square + 1e-06)
    return weight - step * gradient * lax.rsqrt(moment), moment


def per_device(
    dec_in,
    memory,
    out_grad,
    dec_len,
    enc_len,
    buckets,
    self_weight,
    cross_weight,
    ffn_in,
    ffn_out,
    gains,
    table,
    self_rows,
    self_cols,
    cross_rows,
    cross_cols,
    in_rows,
    in_cols,
    out_rows,
    out_cols,
    gain_moment,
    table_moment,
):
    seq_count, seq_length, model_width = dec_in.shape
    mem_length = memory.shape[1]
    row_count = seq_count * seq_length
    hidden_width = ffn_in.shape[2]
    reps, shards = lax.axis_size("rep"), lax.axis_size("fsdp")
    rep, shard = lax.axis_index("rep"), lax.axis_index("fsdp")
    quarters = reps == 4 and shards == 8
    part_rows = hidden_width // shards
    grad_factor = 1.0 / math.sqrt(row_count * reps * shards)
    where = jnp.stack([rep, shard // 2, shard % 2]).astype(jnp.int32) * int(quarters)
    w_self = lax.all_gather(self_weight.astype(LOW), "fsdp", axis=1, tiled=True)
    gain_full = lax.all_gather(gains.astype(LOW), "fsdp", axis=1, tiled=True).astype(WIDE)
    w_in = lax.all_gather(ffn_in.astype(LOW), "fsdp", axis=1, tiled=True)

    each = model_width // (LINE * LINE_CORES)
    if quarters:
        out_each = part_rows // 4
        cross_quarter = lax.dynamic_index_in_dim(cross_weight, rep, 0, keepdims=False).astype(LOW)
        out_quarter = lax.dynamic_index_in_dim(
            ffn_out.reshape(4, out_each, model_width), rep, 0, keepdims=False
        ).astype(LOW)
        cross_pieces = with_partner(across_reps(along_line(cross_quarter)))
    square = lambda value: jnp.sum(value * value, axis=(1, 2))
    squares = (
        square(ffn_in), square(ffn_out[None]), square(cross_weight), square(self_weight),
        jnp.sum(gains * gains, axis=1),
    )
    if quarters:
        state_sums = (
            jnp.sum(in_rows, axis=1), jnp.sum(out_rows)[None], jnp.sum(cross_rows, axis=1),
            jnp.sum(self_rows, axis=1),
        )
        blank = jnp.zeros((5,), WIDE)
        constants = pack([*state_sums, blank, *squares]) / reps
        constants = jnp.pad(constants, (0, LANES - constants.size)).reshape(1, LANES)
        gain_full, constants = hold(gain_full, constants)

    bucket_mask = (buckets[None, :] == jnp.arange(BUCKETS)[:, None]).astype(WIDE)
    by_distance = jnp.sum(table.T[:, :, None] * bucket_mask[None], axis=1)
    by_distance = jnp.pad(by_distance, ((0, 16 - H), (0, 0)))
    backwards = jnp.roll(by_distance[:, ::-1], 1, axis=1)
    no_bias = jnp.zeros((8, PAIR), WIDE)
    no_source = jnp.zeros((16, PAIR), LOW)

    dec_rows = dec_in.reshape(row_count, model_width)
    mem_rows = memory.reshape(seq_count * mem_length, model_width)
    grad_rows = out_grad.reshape(row_count, model_width)
    *kept_one, after_self = attention_forward(
        True, dec_rows, no_source, dec_len, gain_full[0:1], w_self, backwards
    )
    if quarters:
        w_cross = assemble(
            hold(*cross_pieces, after_self)[:-1],
            where,
            (4, model_width, model_width),
            lambda ref, quarter, at: ref.at[quarter, pl.ds(at * each, each)],
            "assemble_cross",
        )
        out_line = along_line(after(out_quarter, w_self))
        out_near = across_reps(after(out_line, after_self))
    else:
        w_cross = lax.all_gather(cross_weight.astype(LOW), "fsdp", axis=1, tiled=True)
        w_out = [lax.all_gather(ffn_out.astype(LOW), "fsdp", axis=0, tiled=True)]
    *kept_two, after_cross = attention_forward(
        False, after_self, mem_rows, enc_len, gain_full[1:2], w_cross, no_bias
    )
    if quarters:
        out_near = hold(*out_near, after_cross)[:-1]
        w_out = with_partner(list(out_near))
    layer_out, grad_cross, grad_gate, grad_up, *out_near, gain_three = feed_forward_both(
        after_cross, grad_rows, dec_len, where, gain_full[2:3], w_in, w_out
    )
    scatter = lambda value, at: lax.psum_scatter(value, "fsdp", scatter_dimension=at, tiled=True)
    if quarters:
        own_gate = scatter(grad_gate, 0)
        out_near = out_near[:1] + [from_rep(out_near[way], way) for way in range(1, 4)]
    grad_self, grad_k_two, grad_v_two, gain_two, *cross_near, cross_far = attention_backward(
        False, after_self, mem_rows, grad_cross, enc_len, where, gain_full[1:2], w_cross, no_bias, kept_two,
        kept_two[3], kept_one[3],
    )
    if quarters:
        cross_far, grad_k_two, *out_near = hold(cross_far, grad_k_two, *out_near)
        pair = from_shard(cross_far, 1)
        memory_grad = memory_gradient(grad_k_two, grad_v_two, w_cross)
        memory_grad, pair, own_gate = hold(memory_grad, pair, own_gate)
        own_up = scatter(grad_up, 0)
        cross_chip = [add_up([cross_near[way], pair[way]]) for way in range(4)]
        grad_self, *cross_chip = hold(grad_self, *cross_chip)
        cross_near = cross_chip[:1] + [from_rep(cross_chip[way], way) for way in range(1, 4)]
    else:
        memory_grad = memory_gradient(grad_k_two, grad_v_two, w_cross)
    *grads_one, grad_self_weights, dist_grad = attention_backward(
        True, dec_rows, no_source, grad_self, dec_len, where, gain_full[0:1], w_self, by_distance, kept_one,
        no_source, no_source,
    )
    if quarters:
        dist_grad, own_up, grad_self_weights, *rest = hold(
            dist_grad, own_up, grad_self_weights, *grads_one, *cross_near, *out_near
        )
        grads_one, cross_near, out_near = rest[:3], rest[3:7], rest[7:]
        own_self = scatter(grad_self_weights, 1)
        out_sum = add_up(out_near)
        out_pair = from_shard(out_sum[1], 1)
        in_parts = rep_parts(jnp.stack([own_gate, own_up]).reshape(2, 4, -1, hidden_width), 1)
        line = jnp.concatenate([add_up(cross_near), add_up([out_sum[0], out_pair])], axis=1)
        in_piece, in_columns = gated_sums(grad_factor, in_parts)
        in_near = rep_near(in_piece)
        *line_parts, gate = hold(*add_line(line), grads_one[0])
        grads_one = [gate, *grads_one[1:]]
        input_grad, gain_one = input_gradient(grads_one, w_self, dec_rows, grad_self, gain_full[0:1])
    else:
        input_grad, gain_one = input_gradient(grads_one, w_self, dec_rows, grad_self, gain_full[0:1])
    layer_out = layer_out.reshape(dec_in.shape)
    input_grad = input_grad.reshape(dec_in.shape)
    memory_grad = memory_grad.reshape(memory.shape)
    table_part = jnp.sum(dist_grad[:H, None, :] * bucket_mask[None], axis=2)
    wide = lambda value: value.astype(WIDE) * grad_factor
    gain_parts = jnp.concatenate([gain_one, gain_two, gain_three]) * grad_factor
    table_part = table_part * grad_factor
    if quarters:
        starts = vector_rows(model_width, hidden_width, 3 * model_width + H * LANES)
        small = jnp.concatenate(
            [gain_parts.reshape(-1, LANES), jnp.pad(table_part, ((0, 0), (0, LANES - BUCKETS)))]
        )
        line_piece, early = early_sums(grad_factor, starts, where, line_parts, in_columns, constants)
        line_near = rep_near(line_piece)
        own_self, early, *near = hold(own_self, early, *in_near, *line_near[:3])
        in_near, line_near = near[:4], near[4:] + line_near[3:]
        self_parts = rep_parts(own_self.reshape(3, 4, -1, model_width), 1)
        self_piece, vector = late_sums(grad_factor, starts, self_parts, small, early)
        vector, *self_near = hold(butterfly(vector, from_shard, shards), *rep_near(self_piece))
        total = butterfly(vector, from_rep, reps)
        (
            ffn_in_grad, feedforward_output_gradient, cross_grad, self_grad,
            new_ffn_in, new_ffn_out, new_cross, new_self,
            new_in_rows, new_out_rows, new_cross_rows, new_self_rows,
            new_in_cols, new_out_cols, new_cross_cols, new_self_cols,
            gains_grad, table_grad, new_gains, new_table, new_gain_moment, new_table_moment,
        ) = update_all(
            grad_factor, starts, shards, where, total, in_near, line_near, self_near,
            (ffn_in, ffn_out, cross_weight, self_weight),
            (in_rows, out_rows[None], cross_rows, self_rows),
            (in_cols, out_cols[None], cross_cols, self_cols),
            (gains, table.T, gain_moment, table_moment.T),
        )
        table_grad, new_table, new_table_moment = table_grad.T, new_table.T, new_table_moment.T
        new_out_rows, new_out_cols = new_out_rows.reshape(-1), new_out_cols.reshape(-1)
    else:
        over_reps = lambda value: lax.psum(value, "rep")
        own_in = over_reps(scatter(jnp.stack([grad_gate, grad_up]), 1))
        grad_out = jnp.stack(out_near)
        grad_out = grad_out.transpose(2, 1, 0, 3, 4).reshape(hidden_width, model_width)
        own_out = over_reps(scatter(grad_out, 0))
        packed = jnp.stack([jnp.stack(cross_near), cross_far]).transpose(1, 2, 0, 3, 4)
        cross_parts = packed[..., :each, :].reshape(4, model_width, model_width)
        past = packed[:3, ..., each:, :].transpose(1, 2, 0, 3, 4).reshape(1, model_width, model_width)
        own_cross = over_reps(scatter(cross_parts, 1))
        own_self = over_reps(scatter(jnp.concatenate([grad_self_weights, past]), 1))
        self_grad, cross_grad, ffn_in_grad, feedforward_output_gradient = [
            wide(member) for member in (own_self, own_cross, own_in, own_out)
        ]
        local = (
            *factored_sums(ffn_in_grad, in_rows),
            *factored_sums(feedforward_output_gradient[None], out_rows[None]),
            *factored_sums(cross_grad, cross_rows),
            *factored_sums(self_grad, self_rows),
            *squares,
        )
        found = unpack(lax.psum(pack(local), "fsdp"), local)
        in_sums, out_sums, cross_sums, self_sums, squares = (
            found[0:2], found[2:4], found[4:6], found[6:8], found[8:],
        )
        gain_total, table_grad = lax.psum((gain_parts, table_part.T), ("rep", "fsdp"))
        gains_grad = lax.dynamic_slice_in_dim(gain_total, shard * gains.shape[1], gains.shape[1], axis=1)
        new_gains, new_gain_moment = plain_update(
            gains_grad, gains, gain_moment, (squares[4] / model_width)[:, None]
        )
        new_table, new_table_moment = plain_update(
            table_grad, table, table_moment, jnp.mean(table * table)
        )
        new_in_rows = row_moments(ffn_in_grad, in_rows)
        new_out_rows = row_moments(feedforward_output_gradient, out_rows)
        new_cross_rows = row_moments(cross_grad, cross_rows)
        new_self_rows = row_moments(self_grad, self_rows)
        new_ffn_in, new_in_cols = factored_update(
            ffn_in_grad, ffn_in, new_in_rows, in_cols, *in_sums, squares[0]
        )
        new_ffn_out, new_out_cols = [
            member[0]
            for member in factored_update(
                feedforward_output_gradient[None], ffn_out[None], new_out_rows[None], out_cols[None],
                *out_sums, squares[1],
            )
        ]
        new_cross, new_cross_cols = factored_update(
            cross_grad, cross_weight, new_cross_rows, cross_cols, *cross_sums, squares[2]
        )
        new_self, new_self_cols = factored_update(
            self_grad, self_weight, new_self_rows, self_cols, *self_sums, squares[3]
        )
    return (
        layer_out,
        input_grad,
        memory_grad,
        self_grad,
        cross_grad,
        ffn_in_grad,
        feedforward_output_gradient,
        gains_grad,
        table_grad,
        new_self,
        new_cross,
        new_ffn_in,
        new_ffn_out,
        new_gains,
        new_table,
        new_self_rows,
        new_self_cols,
        new_cross_rows,
        new_cross_cols,
        new_in_rows,
        new_in_cols,
        new_out_rows,
        new_out_cols,
        new_gain_moment,
        new_table_moment,
    )


def solution(mesh):
    placed = (
        P(("rep", "fsdp"), None, None),
        P(("rep", "fsdp"), None, None),
        P(("rep", "fsdp"), None, None),
        P(("rep", "fsdp")),
        P(("rep", "fsdp")),
        P(),
        P(None, "fsdp", None),
        P(None, "fsdp", None),
        P(None, "fsdp", None),
        P("fsdp", None),
        P(None, "fsdp"),
        P(),
        P(None, "fsdp"),
        P(),
        P(None, "fsdp"),
        P(),
        P(None, "fsdp"),
        P(),
        P("fsdp"),
        P(),
        P(None, "fsdp"),
        P(),
    )
    return jax.shard_map(
        per_device,
        mesh=mesh,
        in_specs=placed,
        out_specs=(
            P(("rep", "fsdp"), None, None),
            P(("rep", "fsdp"), None, None),
            P(("rep", "fsdp"), None, None),
            P(None, "fsdp", None),
            P(None, "fsdp", None),
            P(None, "fsdp", None),
            P("fsdp", None),
            P(None, "fsdp"),
            P(),
            P(None, "fsdp", None),
            P(None, "fsdp", None),
            P(None, "fsdp", None),
            P("fsdp", None),
            P(None, "fsdp"),
            P(),
            P(None, "fsdp"),
            P(),
            P(None, "fsdp"),
            P(),
            P(None, "fsdp"),
            P(),
            P("fsdp"),
            P(),
            P(None, "fsdp"),
            P(),
        ),
        check_vma=False,
    )
```

```python
import functools
import math

import jax
import jax.numpy as jnp
from jax import lax
from jax.experimental import pallas as pl
from jax.experimental.pallas import tpu as pltpu
from jax.sharding import PartitionSpec as P

H = 12
DH = 64
BUCKETS = 32
DECAY_RATE = 0.8
STEP_RATE = 0.2
TINY_TERM = 1e-30
PAIR = 2 * DH
GROUP = 4 * DH
HIDDEN = -1e30
MEGABYTE = 1024 * 1024
PEAK = 1.15e9
LINE = 4
LINE_CORES = 2
LOW = jnp.bfloat16
WIDE = jnp.float32


def nn(left, right):
    return lax.dot_general(left, right, (((1,), (0,)), ((), ())), preferred_element_type=WIDE)


def nt(left, right):
    return lax.dot_general(left, right, (((1,), (1,)), ((), ())), preferred_element_type=WIDE)


def tn(left, right):
    return lax.dot_general(left, right, (((0,), (0,)), ((), ())), preferred_element_type=WIDE)


def rms_rate(rows):
    return lax.rsqrt(jnp.mean(rows * rows, axis=-1, keepdims=True) + 1e-06)


def three_parts(column):
    high = column.astype(LOW)
    rest = column - high.astype(WIDE)
    middle = rest.astype(LOW)
    low = (rest - middle.astype(WIDE)).astype(LOW)
    return high, middle, low


def chunks(total, size):
    return [(at, min(size, total - at)) for at in range(0, total, size)]


def lanes(rows):
    return lax.broadcasted_iota(jnp.int32, (rows, PAIR), 1)


def own_lanes(rows, side):
    lane = lanes(rows)
    return (lane >= DH * side) & (lane < DH * (side + 1))


def key_extras(rows, side, length):
    lane = lanes(rows) - DH * (1 - side)
    dead = lax.broadcasted_iota(jnp.int32, (rows, PAIR), 0) >= length
    mask = jnp.where(dead, HIDDEN, 0.0)
    return jnp.where(
        (lane >= 0) & (lane < 3), 1.0, jnp.where(lane == 3, mask, 0.0)
    ).astype(LOW)


def row_extras(rows, side, column, last):
    lane = lanes(rows) - DH * (1 - side)
    high, middle, low = three_parts(column)
    wide = lambda part: jnp.broadcast_to(part.astype(WIDE), (rows, PAIR))
    return jnp.where(
        lane == 0,
        wide(high),
        jnp.where(
            lane == 1, wide(middle), jnp.where(lane == 2, wide(low), jnp.where(lane == 3, last, 0.0))
        ),
    ).astype(LOW)


def piece_copies(parts, where_ref, place, sems):
    rep, line, core = where_ref[0], where_ref[1], where_ref[2]
    copies = []
    for other in range(LINE_CORES):
        for way in range(4):
            for hop in range(LINE):
                shard = lax.rem(line - hop + LINE, LINE) * LINE_CORES + (core ^ other)
                source = parts[4 * other + way].at[hop]
                copies.append(pltpu.make_async_copy(source, place(rep ^ way, shard), sems.at[len(copies)]))
    return copies


def forward_body(causal, seq_count, length_ref, wave_ref, bias_ref, q_ref, k_ref, v_ref, mix_ref, total_ref, group):
    rows = q_ref.shape[0] // seq_count
    keys = k_ref.shape[0] // seq_count
    block = rows
    for pair in range(2):
        at = pair * PAIR
        for side in range(2):
            head = 2 * pair + side
            if causal:
                wave = wave_ref[pl.ds(group * 4 + head, 1), :]
                spread = pltpu.roll(
                    jnp.broadcast_to(wave, (rows, keys)), 0, 1, stride=1, stride_axis=0
                )
                row = lax.broadcasted_iota(jnp.int32, (rows, keys), 0)
                column = lax.broadcasted_iota(jnp.int32, (rows, keys), 1)
                bias_ref[side] = jnp.where(column <= row, spread, HIDDEN)
        for seq in range(seq_count):
            outs = []
            for side in range(2):
                own_q = own_lanes(rows, side)
                own_k = own_lanes(keys, side)
                query = jnp.where(
                    own_q,
                    q_ref[seq * rows : (seq + 1) * rows, at : at + PAIR],
                    (lanes(rows) == DH * (1 - side) + 3).astype(LOW),
                )
                key = jnp.where(
                    own_k,
                    k_ref[seq * keys : (seq + 1) * keys, at : at + PAIR],
                    key_extras(keys, side, length_ref[seq]),
                )
                value = jnp.where(
                    own_k,
                    v_ref[seq * keys : (seq + 1) * keys, at : at + PAIR],
                    jnp.ones((), LOW),
                )
                parts = []
                for start in range(0, rows, block):
                    span = start + block if causal else keys
                    scores = nt(query[start : start + block], key[:span])
                    if causal:
                        scores = scores + bias_ref[side, start : start + block, :span]
                    top = jnp.max(scores, axis=1, keepdims=True)
                    weight = jnp.exp(scores - top)
                    out = nn(weight.astype(LOW), value[:span])
                    total = out[:, DH * (1 - side) : DH * (1 - side) + 1]
                    parts.append(out * (1.0 / total))
                    spot = pl.ds(seq * rows + start, block)
                    lane = lanes(block)
                    seen = total_ref[spot, :] if (pair or side) else jnp.zeros((block, PAIR), WIDE)
                    total_ref[spot, :] = jnp.where(
                        lane == 2 * pair + side, top + jnp.log(total), seen
                    )
                outs.append(jnp.concatenate(parts, axis=0))
            mix_ref[seq * rows : (seq + 1) * rows, at : at + PAIR] = jnp.where(
                own_lanes(rows, 0), outs[0], outs[1]
            ).astype(LOW)


def forward_kernel(causal, seq_count, pieces, length_ref, where_ref, x_ref, source_ref, gain_ref, *refs):
    group = pl.program_id(0)
    if pieces:
        w_refs, wave_ref, refs = refs[:8], refs[8], refs[9:]
        q_ref, k_ref, v_ref, mix_ref, total_ref, after_ref, whole_ref = refs[:7]
        normed, bias, held, sems, whole_sem = refs[7:]
        each = held.shape[1] // (LINE * LINE_CORES)
        place = lambda quarter, at: held.at[quarter, pl.ds(at * each, each)]
        copies = piece_copies(w_refs, where_ref, place, sems)
        keep = pltpu.make_async_copy(held, whole_ref, whole_sem)
        across = pl.ds(pl.multiple_of(group * GROUP, GROUP), GROUP)
        wq_ref, wk_ref, wv_ref = [held.at[at, :, across] for at in range(3)]
        wo_ref = held.at[3, across, :]
    else:
        wq_ref, wk_ref, wv_ref, wo_ref, wave_ref = refs[:5]
        q_ref, k_ref, v_ref, mix_ref, total_ref, after_ref, normed, bias = refs[5:]

    @pl.when(group == 0)
    def _():
        if pieces:
            for copy in copies:
                copy.start()
        for at, size in chunks(x_ref.shape[0], 256):
            rows = x_ref[at : at + size, :].astype(WIDE)
            normed[at : at + size, :] = (rows * rms_rate(rows) * gain_ref[...]).astype(LOW)
            after_ref[at : at + size, :] = rows
        if pieces:
            for copy in copies:
                copy.wait()
            keep.start()

    source = normed if causal else source_ref
    q_ref[...] = nn(normed[...], wq_ref[...]).astype(LOW)
    k_ref[...] = nn(source[...], wk_ref[...]).astype(LOW)
    v_ref[...] = nn(source[...], wv_ref[...]).astype(LOW)
    forward_body(causal, seq_count, length_ref, wave_ref, bias, q_ref, k_ref, v_ref, mix_ref, total_ref, group)
    after_ref[...] += nn(mix_ref[...], wo_ref[...])

    @pl.when(group == pl.num_programs(0) - 1)
    def _():
        if pieces:
            keep.wait()


def weight_specs(width):
    across = lambda at: pl.BlockSpec((None, width, GROUP), lambda g, at=at: (at, 0, g))
    return [across(0), across(1), across(2), pl.BlockSpec((None, GROUP, width), lambda g: (3, g, 0))]


def whole(shape):
    return pl.BlockSpec(shape, lambda g: (0,) * len(shape), pipeline_mode=pl.Buffered(1))


def columns(rows):
    return pl.BlockSpec((rows, GROUP), lambda g: (0, g))


def attention_forward(causal, x, source, lengths, where, gain, weights, wave):
    row_count, width = x.shape
    seq_count = lengths.shape[0]
    source_rows = row_count if causal else source.shape[0]
    length = row_count // seq_count
    groups = width // GROUP
    low = lambda rows: jax.ShapeDtypeStruct((rows, width), LOW)
    pieces = isinstance(weights, list)
    everything = jax.ShapeDtypeStruct((4, width, width), LOW)
    anywhere = pl.BlockSpec(memory_space=pl.ANY)
    return pl.pallas_call(
        functools.partial(forward_kernel, causal, seq_count, pieces),
        grid=(groups,),
        in_specs=[
            pl.BlockSpec(memory_space=pltpu.SMEM),
            pl.BlockSpec(memory_space=pltpu.SMEM),
            whole(x.shape),
            whole(source.shape),
            whole(gain.shape),
            *([anywhere] * 8 if pieces else weight_specs(width)),
            whole(wave.shape),
        ],
        out_specs=[
            columns(row_count),
            columns(source_rows),
            columns(source_rows),
            columns(row_count),
            pl.BlockSpec((None, row_count, PAIR), lambda g: (g, 0, 0)),
            whole((row_count, width)),
            *([anywhere] if pieces else []),
        ],
        out_shape=[
            low(row_count),
            low(source_rows),
            low(source_rows),
            low(row_count),
            jax.ShapeDtypeStruct((groups, row_count, PAIR), WIDE),
            jax.ShapeDtypeStruct((row_count, width), WIDE),
            *([everything] if pieces else []),
        ],
        scratch_shapes=[
            pltpu.VMEM((row_count, width), LOW),
            pltpu.VMEM((2, length, length) if causal else (1, 8, PAIR), WIDE),
            *(
                [
                    pltpu.VMEM(everything.shape, LOW),
                    pltpu.SemaphoreType.DMA((8 * LINE,)),
                    pltpu.SemaphoreType.DMA(()),
                ]
                if pieces
                else []
            ),
        ],
        cost_estimate=pl.CostEstimate(flops=int(27 * PEAK), bytes_accessed=20 << 20, transcendentals=0),
        compiler_params=pltpu.CompilerParams(vmem_limit_bytes=60 * MEGABYTE),
        name="self_forward" if causal else "cross_forward",
    )(lengths, where, x, source, gain, *(weights if pieces else [weights] * 4), wave)


def gelu_parts(gate):
    root = 0.7978845608028654
    square = gate * gate
    inner = jnp.tanh(root * gate * (1.0 + 0.044715 * square))
    half = 0.5 * (1.0 + inner)
    value = gate * half
    slope = half + 0.5 * gate * (1.0 - inner * inner) * (root * (1.0 + 3 * 0.044715 * square))
    return value, slope


def rms_back(rows, gain, grad):
    rate = rms_rate(rows)
    scaled = rows * rate
    low = grad * gain
    grad_rows = rate * (low - scaled * jnp.mean(scaled * low, axis=-1, keepdims=True))
    return grad_rows, jnp.sum(grad * scaled, axis=0, keepdims=True)


def shard_slot(where_ref, shard):
    return (shard % LINE_CORES) ^ where_ref[2], lax.rem(shard // LINE_CORES - where_ref[1] + LINE, LINE)


def feed_kernel(
    seq_count, pieces, length_ref, where_ref, after_ref, out_grad_ref, gain_ref, wg_ref, wu_ref, *refs,
):
    wd_refs, (layer_ref, grad_cross_ref, dwg_ref, dwu_ref) = refs[:pieces], refs[pieces : pieces + 4]
    near_refs = refs[pieces + 4 : pieces + 8]
    dgain_ref, normed, normed_t, down, out_total, grad_total, cut, *held = refs[pieces + 8 :]
    step = pl.program_id(0)
    row_count = after_ref.shape[0]
    length = row_count // seq_count

    def live(at, size):
        position = lax.broadcasted_iota(jnp.int32, (size, 1), 0) + (at % length)
        return (position < length_ref[at // length]).astype(WIDE)

    @pl.when(step == 0)
    def _():
        if pieces > 1:
            place = lambda quarter, at: held[0].at[pl.ds((at * 4 + quarter) * cut.shape[2], cut.shape[2])]
            copies = piece_copies(wd_refs, where_ref, place, held[1])
            for copy in copies:
                copy.start()
        for at, size in chunks(row_count, 256):
            rows = after_ref[at : at + size, :]
            low = (rows * rms_rate(rows) * gain_ref[...]).astype(LOW)
            normed[at : at + size, :] = low
            normed_t[:, at : at + size] = low.T
            down[at : at + size, :] = (
                out_grad_ref[at : at + size, :].astype(WIDE) * live(at, size)
            ).astype(LOW)
            out_total[at : at + size, :] = rows
            grad_total[at : at + size, :] = jnp.zeros((size, rows.shape[1]), WIDE)
        if pieces > 1:
            for copy in copies:
                copy.wait()

    block = wg_ref.shape[1]
    if pieces > 1:
        wd_ref = held[0].at[pl.ds(pl.multiple_of(step * block, block), block)]
    else:
        wd_ref = wd_refs[0]
    gate = nn(normed[...], wg_ref[...])
    up = nn(normed[...], wu_ref[...])
    value, slope = gelu_parts(gate)
    hidden = (value * up).astype(LOW)
    out_total[...] += nn(hidden, wd_ref[...])
    grad_hidden = nt(down[...], wd_ref[...])
    cut[...] = tn(hidden, down[...]).astype(LOW).reshape(cut.shape)
    for part in range(cut.shape[0]):
        core, hop = shard_slot(where_ref, step * cut.shape[0] + part)
        for way in range(4):
            near_refs[way][core, hop] = cut[part, where_ref[0] ^ way]
    grad_gate = (grad_hidden * up * slope).astype(LOW)
    grad_up = (grad_hidden * value).astype(LOW)
    dwg_ref[...] = nn(normed_t[...], grad_gate).astype(LOW)
    dwu_ref[...] = nn(normed_t[...], grad_up).astype(LOW)
    grad_total[...] += nt(grad_gate, wg_ref[...]) + nt(grad_up, wu_ref[...])

    @pl.when(step == pl.num_programs(0) - 1)
    def _():
        dgain = jnp.zeros(dgain_ref.shape, WIDE)
        for at, size in chunks(row_count, 256):
            part = slice(at, at + size)
            layer_ref[part, :] = (out_total[part, :] * live(at, size)).astype(LOW)
            grad_rows, gain_part = rms_back(after_ref[part, :], gain_ref[...], grad_total[part, :])
            dgain = dgain + gain_part
            grad_cross_ref[part, :] = (
                out_grad_ref[part, :].astype(WIDE) * live(at, size) + grad_rows
            )
        dgain_ref[...] = dgain


def feed_forward_both(after, out_grad, lengths, where, gain, w_in, w_out):
    row_count, width = after.shape
    hidden = w_in.shape[2]
    each = hidden // (LINE * LINE_CORES)
    block = 2 * each
    seq_count = lengths.shape[0]
    wide = pl.BlockSpec((None, width, block), lambda g: (0, 0, g))
    wide_up = pl.BlockSpec((None, width, block), lambda g: (1, 0, g))
    tall = pl.BlockSpec((block, width), lambda g: (g, 0))
    flat = pl.BlockSpec((width, block), lambda g: (0, g))
    near = (LINE_CORES, LINE, each // 4, width)
    pieces = len(w_out)
    held = [pltpu.VMEM((hidden, width), LOW), pltpu.SemaphoreType.DMA((pieces * LINE,))] if pieces > 1 else []
    return pl.pallas_call(
        functools.partial(feed_kernel, seq_count, pieces),
        grid=(hidden // block,),
        in_specs=[
            pl.BlockSpec(memory_space=pltpu.SMEM),
            pl.BlockSpec(memory_space=pltpu.SMEM),
            whole(after.shape),
            whole(out_grad.shape),
            whole(gain.shape),
            wide,
            wide_up,
            *([pl.BlockSpec(memory_space=pl.ANY)] * pieces if pieces > 1 else [tall]),
        ],
        out_specs=[whole(after.shape), whole(after.shape), flat, flat, *[whole(near)] * 4, whole((1, width))],
        out_shape=[
            jax.ShapeDtypeStruct((row_count, width), LOW),
            jax.ShapeDtypeStruct((row_count, width), WIDE),
            jax.ShapeDtypeStruct((width, hidden), LOW),
            jax.ShapeDtypeStruct((width, hidden), LOW),
            *[jax.ShapeDtypeStruct(near, LOW)] * 4,
            jax.ShapeDtypeStruct((1, width), WIDE),
        ],
        scratch_shapes=[
            pltpu.VMEM((row_count, width), LOW),
            pltpu.VMEM((width, row_count), LOW),
            pltpu.VMEM((row_count, width), LOW),
            pltpu.VMEM((row_count, width), WIDE),
            pltpu.VMEM((row_count, width), WIDE),
            pltpu.VMEM((2, 4, each // 4, width), LOW),
            *held,
        ],
        cost_estimate=pl.CostEstimate(flops=int(46 * PEAK), bytes_accessed=40 << 20, transcendentals=0),
        compiler_params=pltpu.CompilerParams(vmem_limit_bytes=60 * MEGABYTE),
        name="feed_forward_both",
    )(lengths, where, after, out_grad, gain, w_in, w_in, *w_out)


def backward_kernel(
    causal, seq_count, length_ref, where_ref, x_ref, source_ref, grad_ref, gain_ref, wq_ref, wo_ref, wave_ref,
    q_ref, k_ref, v_ref, mix_ref, total_ref, mix_all_ref, mix_past_ref, *refs,
):
    if causal:
        gq, gk_out_ref, gv_out_ref, dw_ref, dist_ref = refs[:5]
        normed_t, branch, grad_mix, bias, score_sum = refs[5:]
        source_t = normed_t
    else:
        grad_x_ref, gk_out_ref, gv_out_ref, dgain_ref = refs[:4]
        near_refs, far_ref = refs[4:8], refs[8]
        normed_t, branch, grad_mix, gq, source_t, mix_t, grad_total, dw_ref, past = refs[9:]
    group = pl.program_id(0)
    row_count = x_ref.shape[0]
    rows = q_ref.shape[0] // seq_count
    keys = k_ref.shape[0] // seq_count
    block = rows

    @pl.when(group == 0)
    def _():
        for at, size in chunks(row_count, 256):
            value = x_ref[at : at + size, :].astype(WIDE)
            low = (value * rms_rate(value) * gain_ref[...]).astype(LOW)
            normed_t[:, at : at + size] = low.T
            branch[at : at + size, :] = grad_ref[at : at + size, :].astype(LOW)
            if not causal:
                mix_t[:, at : at + size] = mix_all_ref[at : at + size, :].T
                grad_total[at : at + size, :] = jnp.zeros((size, value.shape[1]), WIDE)
        if not causal:
            for at, size in chunks(source_ref.shape[0], 256):
                source_t[:, at : at + size] = source_ref[at : at + size, :].T

    grad_mix[...] = nt(branch[...], wo_ref[...]).astype(LOW)
    if not causal:
        across = pl.ds(pl.multiple_of(group * GROUP, GROUP), GROUP)
        put = lambda at, value: dw_ref.__setitem__(at, value.astype(LOW).reshape(dw_ref.shape[1:]))
        put(3, nn(mix_t[...], branch[:, across]))

    for pair in range(2):
        at = pair * PAIR
        if causal:
            for side in range(2):
                head = 2 * pair + side
                wave = wave_ref[pl.ds(group * 4 + head, 1), :]
                spread = pltpu.roll(
                    jnp.broadcast_to(wave, (keys, rows)), 0, 1, stride=1, stride_axis=0
                )
                row = lax.broadcasted_iota(jnp.int32, (keys, rows), 0)
                column = lax.broadcasted_iota(jnp.int32, (keys, rows), 1)
                bias[side] = jnp.where(column >= row, spread, HIDDEN)
        for seq in range(seq_count):
            span_q = slice(seq * rows, (seq + 1) * rows)
            span_k = slice(seq * keys, (seq + 1) * keys)
            sides = []
            for side in range(2):
                head = 2 * pair + side
                own_q = own_lanes(rows, side)
                own_k = own_lanes(keys, side)
                total = jnp.sum(
                    jnp.where(lanes(rows) == head, total_ref[span_q, :], 0.0), axis=1, keepdims=True
                )
                grad_low = grad_mix[span_q, at : at + PAIR]
                product = grad_low.astype(WIDE) * mix_ref[span_q, at : at + PAIR].astype(WIDE)
                delta = jnp.sum(jnp.where(own_q, product, 0.0), axis=1, keepdims=True)
                query = jnp.where(
                    own_q, q_ref[span_q, at : at + PAIR], row_extras(rows, side, -total, 1.0)
                )
                grad_out = jnp.where(own_q, grad_low, row_extras(rows, side, -delta, 0.0))
                key = jnp.where(
                    own_k,
                    k_ref[span_k, at : at + PAIR],
                    key_extras(keys, side, length_ref[seq]),
                )
                value = jnp.where(own_k, v_ref[span_k, at : at + PAIR], jnp.ones((), LOW))
                grad_query = []
                grad_key = None
                grad_value = None
                for start in range(0, rows, block):
                    span = start + block if causal else keys
                    scores = nt(key[:span], query[start : start + block])
                    if causal:
                        scores = scores + bias[side, :span, start : start + block]
                    weight = jnp.exp(scores)
                    low = weight.astype(LOW)
                    grad_weight = nt(value[:span], grad_out[start : start + block])
                    grad_score = (weight * grad_weight).astype(LOW)
                    if causal:
                        if seq == 0:
                            score_sum[side, :span, start : start + block] = grad_score.astype(WIDE)
                        else:
                            score_sum[side, :span, start : start + block] += grad_score.astype(WIDE)
                    key_part = nn(grad_score, query[start : start + block])
                    value_part = nn(low, grad_out[start : start + block])
                    grad_query.append(tn(grad_score, key[:span]))
                    if causal and start == 0 and rows > block:
                        rest = jnp.zeros((keys - span, PAIR), WIDE)
                        key_part = jnp.concatenate([key_part, rest], axis=0)
                        value_part = jnp.concatenate([value_part, rest], axis=0)
                    grad_key = key_part if grad_key is None else grad_key + key_part
                    grad_value = value_part if grad_value is None else grad_value + value_part
                sides.append((jnp.concatenate(grad_query, axis=0), grad_key, grad_value))
            pick_q = own_lanes(rows, 0)
            pick_k = own_lanes(keys, 0)
            gq[span_q, at : at + PAIR] = jnp.where(pick_q, sides[0][0], sides[1][0]).astype(LOW)
            gk_out_ref[span_k, at : at + PAIR] = jnp.where(pick_k, sides[0][1], sides[1][1]).astype(LOW)
            gv_out_ref[span_k, at : at + PAIR] = jnp.where(pick_k, sides[0][2], sides[1][2]).astype(LOW)
        if causal:
            for side in range(2):
                head = 2 * pair + side
                row = lax.broadcasted_iota(jnp.int32, (keys, rows), 0)
                column = lax.broadcasted_iota(jnp.int32, (keys, rows), 1)
                held = jnp.where(column >= row, score_sum[side], 0.0)
                while held.shape[0] > 1:
                    half = held.shape[0] // 2
                    held = held[:half] + pltpu.roll(held[half:], rows - half, 1)
                dist_ref[pl.ds(group * 4 + head, 1), :] = held

    if causal:
        dw_ref[0] = nn(normed_t[...], gq[...]).astype(LOW)
        dw_ref[1] = nn(source_t[...], gk_out_ref[...]).astype(LOW)
        dw_ref[2] = nn(source_t[...], gv_out_ref[...]).astype(LOW)
        return
    put(0, nn(normed_t[...], gq[...]))
    put(1, nn(source_t[...], gk_out_ref[...]))
    put(2, nn(source_t[...], gv_out_ref[...]))
    grad_total[...] += nt(gq[...], wq_ref[...])
    rep, line, core = where_ref[0], where_ref[1], where_ref[2]
    held = dw_ref.shape[2]
    slots = []
    for way in range(4):
        for hop in range(LINE):
            at = lax.rem(line + hop, LINE) * LINE_CORES
            slots.append((near_refs[way].at[hop], rep ^ way, at + core))
            slots.append((far_ref.at[way, hop], rep ^ way, at + (core ^ 1)))
    for slot, quarter, shard in slots:
        slot[0:held, across] = dw_ref[quarter, shard]

    @pl.when(group == pl.num_programs(0) - 1)
    def _():
        dgain = jnp.zeros(dgain_ref.shape, WIDE)
        for at, size in chunks(row_count, 256):
            part = slice(at, at + size)
            grad_rows, gain_part = rms_back(
                x_ref[part, :].astype(WIDE), gain_ref[...], grad_total[part, :]
            )
            dgain = dgain + gain_part
            grad_rows = grad_ref[part, :] + grad_rows
            grad_x_ref[part, :] = grad_rows
            branch[part, :] = grad_rows.astype(LOW)
            mix_t[:, part] = mix_past_ref[part, :].T
        dgain_ref[...] = dgain
        thirds = nn(mix_t[...], branch[...]).astype(LOW)
        past[:, 0:3] = thirds.reshape(past.shape[0], 3, *past.shape[2:])
        past[:, 3] = jnp.zeros_like(past[:, 3])
        for slot, quarter, shard in slots:
            slot[held:, :] = past[shard, quarter]


def attention_backward(causal, x, source, grad, lengths, where, gain, weights, wave, kept, mix, past):
    row_count, width = x.shape
    seq_count = lengths.shape[0]
    source_rows = row_count if causal else source.shape[0]
    length = row_count // seq_count
    groups = width // GROUP
    low = lambda rows: jax.ShapeDtypeStruct((rows, width), LOW)
    if causal:
        out_specs = [
            columns(row_count), columns(source_rows), columns(source_rows),
            pl.BlockSpec((3, width, GROUP), lambda g: (0, 0, g)), whole(wave.shape),
        ]
        out_shape = [
            low(row_count), low(source_rows), low(source_rows),
            jax.ShapeDtypeStruct((3, width, width), LOW), jax.ShapeDtypeStruct(wave.shape, WIDE),
        ]
        scratch = [pltpu.VMEM((2, length, length), WIDE)] * 2
    else:
        shards = LINE * LINE_CORES
        each, third = width // shards, width // shards // 3
        near = (LINE, each + third, width)
        out_specs = [
            whole((row_count, width)), columns(source_rows), columns(source_rows), whole((1, width)),
            *[whole(near)] * 4, whole((4, *near)),
        ]
        out_shape = [
            jax.ShapeDtypeStruct((row_count, width), WIDE), low(source_rows), low(source_rows),
            jax.ShapeDtypeStruct((1, width), WIDE), *[jax.ShapeDtypeStruct(near, LOW)] * 4,
            jax.ShapeDtypeStruct((4, *near), LOW),
        ]
        scratch = [
            pltpu.VMEM((row_count, GROUP), LOW),
            pltpu.VMEM((width, source_rows), LOW),
            pltpu.VMEM((width, row_count), LOW),
            pltpu.VMEM((row_count, width), WIDE),
            pltpu.VMEM((4, shards, each, GROUP), LOW),
            pltpu.VMEM((shards, 4, third, width), LOW),
        ]
    return pl.pallas_call(
        functools.partial(backward_kernel, causal, seq_count),
        grid=(groups,),
        in_specs=[
            pl.BlockSpec(memory_space=pltpu.SMEM),
            pl.BlockSpec(memory_space=pltpu.SMEM),
            whole(x.shape),
            whole(source.shape),
            whole(grad.shape),
            whole(gain.shape),
            weight_specs(width)[0],
            weight_specs(width)[3],
            whole(wave.shape),
            columns(row_count),
            columns(source_rows),
            columns(source_rows),
            columns(row_count),
            pl.BlockSpec((None, row_count, PAIR), lambda g: (g, 0, 0)),
            whole(mix.shape),
            whole(past.shape),
        ],
        out_specs=out_specs,
        out_shape=out_shape,
        scratch_shapes=[
            pltpu.VMEM((width, row_count), LOW),
            pltpu.VMEM((row_count, width), LOW),
            pltpu.VMEM((row_count, GROUP), LOW),
            *scratch,
        ],
        cost_estimate=pl.CostEstimate(flops=int(45 * PEAK), bytes_accessed=40 << 20, transcendentals=0),
        compiler_params=pltpu.CompilerParams(vmem_limit_bytes=60 * MEGABYTE),
        name="self_backward" if causal else "cross_backward",
    )(lengths, where, x, source, grad, gain, weights, weights, wave, *kept, mix, past)


def input_kernel(gq_ref, gk_ref, gv_ref, wq_ref, wk_ref, wv_ref, x_ref, grad_ref, gain_ref, out_ref, dgain_ref):
    total = nt(gq_ref[...], wq_ref[...]) + nt(gk_ref[...], wk_ref[...]) + nt(gv_ref[...], wv_ref[...])
    grad_rows, dgain = rms_back(x_ref[...].astype(WIDE), gain_ref[...], total)
    out_ref[...] = grad_ref[...] + grad_rows

    @pl.when(pl.program_id(0) == 0)
    def _():
        dgain_ref[...] = jnp.zeros_like(dgain_ref)

    dgain_ref[...] += dgain


def input_gradient(grads, weights, x, grad, gain):
    rows, width = x.shape
    block = 256
    rowwise = pl.BlockSpec((block, width), lambda g: (g, 0))
    matrix = lambda at: pl.BlockSpec((None, width, width), lambda g: (at, 0, 0))
    return pl.pallas_call(
        input_kernel,
        grid=(rows // block,),
        in_specs=[rowwise, rowwise, rowwise, matrix(0), matrix(1), matrix(2), rowwise, rowwise, whole((1, width))],
        out_specs=[rowwise, whole((1, width))],
        out_shape=[jax.ShapeDtypeStruct((rows, width), WIDE), jax.ShapeDtypeStruct((1, width), WIDE)],
        cost_estimate=pl.CostEstimate(flops=int(8 * PEAK), bytes_accessed=12 << 20, transcendentals=0),
        compiler_params=pltpu.CompilerParams(vmem_limit_bytes=60 * MEGABYTE),
        name="input_gradient",
    )(*grads, weights, weights, weights, x, grad, gain)


def memory_kernel(gk_ref, gv_ref, wk_ref, wv_ref, out_ref):
    out_ref[...] = nt(gk_ref[...], wk_ref[...]) + nt(gv_ref[...], wv_ref[...])


def memory_gradient(grad_key, grad_value, weights):
    rows, width = grad_key.shape
    block = 256
    rowwise = pl.BlockSpec((block, width), lambda g: (g, 0))
    matrix = lambda at: pl.BlockSpec((None, width, width), lambda g: (at, 0, 0))
    return pl.pallas_call(
        memory_kernel,
        grid=(rows // block,),
        in_specs=[rowwise, rowwise, matrix(1), matrix(2)],
        out_specs=rowwise,
        out_shape=jax.ShapeDtypeStruct((rows, width), WIDE),
        cost_estimate=pl.CostEstimate(flops=int(7 * PEAK), bytes_accessed=10 << 20, transcendentals=0),
        compiler_params=pltpu.CompilerParams(vmem_limit_bytes=60 * MEGABYTE),
        name="memory_gradient",
    )(grad_key, grad_value, weights, weights)


LANES = 128
IN_AT, OUT_AT, CROSS_AT, PAST_AT, SELF_AT, SMALL_AT = 0, 1, 2, 3, 4, 5


def vector_rows(width, hidden, small):
    one, big = width // LANES, hidden // LANES
    starts = [0]
    for size in (2 * big, one, 4 * one, one, 3 * one, small // LANES):
        starts.append(starts[-1] + size)
    return starts


def spill(ref, at, row):
    for part in range(row.shape[1] // LANES):
        ref[pl.ds(at + part, 1), :] = row[:, part * LANES : (part + 1) * LANES]


def fetch(ref, at, width):
    return jnp.concatenate([ref[at + part : at + part + 1, :] for part in range(width // LANES)], axis=1)


def column_sums(rows):
    return jnp.sum(rows * rows + TINY_TERM, axis=0, keepdims=True)


def in_kernel(factor, *refs):
    in_refs, in_ref, sums_ref = refs[:4], refs[4], refs[5]
    big = in_ref.shape[2] // LANES
    for matrix in range(2):
        piece = sum(ref[matrix].astype(WIDE) for ref in in_refs).astype(LOW)
        in_ref[matrix] = piece
        spill(sums_ref, matrix * big, column_sums(piece.astype(WIDE) * factor))


def gated_sums(factor, in_parts):
    shape = in_parts[0].shape
    return pl.pallas_call(
        functools.partial(in_kernel, factor),
        in_specs=[pl.BlockSpec(memory_space=pltpu.VMEM)] * 4,
        out_specs=[pl.BlockSpec(memory_space=pltpu.VMEM)] * 2,
        out_shape=[
            jax.ShapeDtypeStruct(shape, LOW),
            jax.ShapeDtypeStruct((2 * shape[2] // LANES, LANES), WIDE),
        ],
        cost_estimate=pl.CostEstimate(flops=int(2 * PEAK), bytes_accessed=2 << 20, transcendentals=0),
        compiler_params=pltpu.CompilerParams(vmem_limit_bytes=60 * MEGABYTE),
        name="gated_sums",
    )(*in_parts)


def early_kernel(factor, starts, where_ref, *refs):
    line_refs, sums_ref, constant_ref, line_ref, vector_ref = refs[0:4], *refs[4:]
    rep = where_ref[0]
    one = line_ref.shape[1] // LANES
    each = line_ref.shape[0] // 2
    third = each // 3
    line = sum(ref[...].astype(WIDE) for ref in line_refs).astype(LOW)
    line_ref[...] = line
    vector_ref[...] = jnp.zeros_like(vector_ref)
    vector_ref[starts[IN_AT] : starts[OUT_AT], :] = sums_ref[...]
    line = line.astype(WIDE) * factor
    spill(vector_ref, starts[OUT_AT], column_sums(line[each + third :]))
    spill(vector_ref, starts[CROSS_AT] + rep * one, column_sums(line[:each]))
    past = column_sums(line[each : each + third])
    spill(vector_ref, starts[PAST_AT], past * (rep < 3).astype(WIDE))
    vector_ref[starts[-1] : starts[-1] + 1, :] = constant_ref[...]


def early_sums(factor, starts, where, line_parts, sums, constants):
    rows = -(-(starts[-1] + 1) // 8) * 8
    return pl.pallas_call(
        functools.partial(early_kernel, factor, starts),
        in_specs=[pl.BlockSpec(memory_space=pltpu.SMEM)] + [pl.BlockSpec(memory_space=pltpu.VMEM)] * 6,
        out_specs=[pl.BlockSpec(memory_space=pltpu.VMEM)] * 2,
        out_shape=[
            jax.ShapeDtypeStruct(line_parts[0].shape, LOW),
            jax.ShapeDtypeStruct((rows, LANES), WIDE),
        ],
        cost_estimate=pl.CostEstimate(flops=int(2 * PEAK), bytes_accessed=2 << 20, transcendentals=0),
        compiler_params=pltpu.CompilerParams(vmem_limit_bytes=60 * MEGABYTE),
        name="early_sums",
    )(where, *line_parts, sums, constants)


def late_kernel(factor, starts, *refs):
    part_refs, small_ref, early_ref, piece_ref, vector_ref = refs[0:4], refs[4], refs[5], refs[6], refs[7]
    vector_ref[...] = early_ref[...]
    one = piece_ref.shape[2] // LANES
    for matrix in range(3):
        piece = sum(ref[matrix].astype(WIDE) for ref in part_refs).astype(LOW)
        piece_ref[matrix] = piece
        spill(vector_ref, starts[SELF_AT] + matrix * one, column_sums(piece.astype(WIDE) * factor))
    vector_ref[starts[SMALL_AT] : starts[SMALL_AT + 1], :] = small_ref[...]


def late_sums(factor, starts, self_parts, small, early):
    return pl.pallas_call(
        functools.partial(late_kernel, factor, starts),
        in_specs=[pl.BlockSpec(memory_space=pltpu.VMEM)] * 6,
        out_specs=[pl.BlockSpec(memory_space=pltpu.VMEM)] * 2,
        out_shape=[
            jax.ShapeDtypeStruct(self_parts[0].shape, LOW),
            jax.ShapeDtypeStruct(early.shape, WIDE),
        ],
        cost_estimate=pl.CostEstimate(flops=int(2 * PEAK), bytes_accessed=1 << 20, transcendentals=0),
        compiler_params=pltpu.CompilerParams(vmem_limit_bytes=60 * MEGABYTE),
        name="late_sums",
    )(*self_parts, small, early)


def to_column(row):
    size = row.shape[1]
    same = lax.broadcasted_iota(jnp.int32, (size, size), 0) == lax.broadcasted_iota(jnp.int32, (size, size), 1)
    return jnp.sum(jnp.where(same, jnp.broadcast_to(row, (size, size)), 0.0), axis=1, keepdims=True)


def to_row(column):
    size = column.shape[0]
    same = lax.broadcasted_iota(jnp.int32, (size, size), 0) == lax.broadcasted_iota(jnp.int32, (size, size), 1)
    return jnp.sum(jnp.where(same, jnp.broadcast_to(column, (size, size)), 0.0), axis=0, keepdims=True)


def update_kernel(factor, starts, shards, where_ref, total_ref, *refs):
    in_near, line_near, self_near = refs[0:4], refs[4:8], refs[8:12]
    (
        in_ref, out_ref, cross_ref, self_ref, in_rows_ref, out_rows_ref, cross_rows_ref, self_rows_ref,
        in_cols_ref, out_cols_ref, cross_cols_ref, self_cols_ref,
    ) = refs[12:24]
    (
        in_grad, out_grad, cross_grad, self_grad, new_in, new_out, new_cross, new_self,
        new_in_rows, new_out_rows, new_cross_rows, new_self_rows,
        new_in_cols, new_out_cols, new_cross_cols, new_self_cols,
        gains_grad, table_grad, new_gains, new_table, new_gain_moment, new_table_moment,
    ) = refs[28:50]
    gains_ref, table_ref, gain_moment_ref, table_moment_ref = refs[24:28]
    in_held, line_held, self_held = refs[50:]
    rep = where_ref[0]
    for way in range(4):
        in_held[rep ^ way] = in_near[way][...]
        line_held[rep ^ way] = line_near[way][...]
        self_held[rep ^ way] = self_near[way][...]
    width = cross_ref.shape[2]
    one, big = width // LANES, in_ref.shape[2] // LANES
    each = cross_ref.shape[1]
    third = each // 3
    scalars = total_ref[starts[-1] : starts[-1] + 1, :]

    def step(at, pieces, index, weight, grad, new, rows_ref, new_rows, cols_ref, new_cols, row_at, scalar):
        rows, cols = weight.shape[-2:]
        spans = []
        start = 0
        for piece in pieces:
            spans.append(slice(start, start + piece.shape[0]))
            start += piece.shape[0]
        whole_rows = rows * shards
        col_sum = fetch(total_ref, at, cols)
        state_sum = scalars[:, scalar : scalar + 1]
        square = scalars[:, 16 + scalar : 17 + scalar]
        col_moment = DECAY_RATE * cols_ref[row_at : row_at + 1, :] + (1.0 - DECAY_RATE) * col_sum / whole_rows
        new_cols[row_at : row_at + 1, :] = col_moment
        row_mean = (
            DECAY_RATE * state_sum
            + (1.0 - DECAY_RATE) / cols * jnp.sum(col_sum, axis=1, keepdims=True)
        ) / whole_rows
        blocks = [piece.astype(WIDE) * factor for piece in pieces]
        means = jnp.concatenate(
            [jnp.mean(block * block + TINY_TERM, axis=1, keepdims=True) for block in blocks], axis=0
        )
        row_moment = DECAY_RATE * to_column(rows_ref[row_at : row_at + 1, :]) + (1.0 - DECAY_RATE) * means
        new_rows[row_at : row_at + 1, :] = to_row(row_moment)
        size = STEP_RATE * jnp.sqrt(square / (whole_rows * cols) + 1e-06)
        scale = size * lax.rsqrt(row_moment / row_mean)
        across = lax.rsqrt(col_moment)
        for block, span in zip(blocks, spans):
            place = (span, slice(None)) if index is None else (index, span, slice(None))
            grad[place] = block
            new[place] = weight[place] - scale[span] * block * across

    def plain(grad, ref, moment_ref, square, out, new, new_moment, spot):
        moment = DECAY_RATE * moment_ref[spot] + (1.0 - DECAY_RATE) * (grad * grad + TINY_TERM)
        out[spot] = grad
        new_moment[spot] = moment
        new[spot] = ref[spot] - STEP_RATE * jnp.sqrt(square + 1e-06) * grad * lax.rsqrt(moment)

    part = gains_ref.shape[1]
    for norm in range(3):
        row = fetch(total_ref, starts[SMALL_AT] + norm * one, width)
        mine = where_ref[1] * LINE_CORES + where_ref[2]
        row = pltpu.roll(jnp.broadcast_to(row, (8, width)), lax.rem(width - mine * part, width), 1)
        plain(
            row[0:1, :part], gains_ref, gain_moment_ref, scalars[:, 27 + norm : 28 + norm] / width,
            gains_grad, new_gains, new_gain_moment, (slice(norm, norm + 1), slice(None)),
        )
    table = total_ref[starts[SMALL_AT] + 3 * one : starts[SMALL_AT + 1], 0 : table_ref.shape[1]]
    square = jnp.sum(jnp.sum(table_ref[...] * table_ref[...], axis=1, keepdims=True), axis=0, keepdims=True)
    plain(
        table, table_ref, table_moment_ref, square / (table_ref.shape[0] * table_ref.shape[1]),
        table_grad, new_table, new_table_moment, (slice(None), slice(None)),
    )
    quarters = range(4)
    for matrix in range(2):
        step(
            starts[IN_AT] + matrix * big, [in_held[at, matrix] for at in quarters], matrix,
            in_ref, in_grad, new_in, in_rows_ref, new_in_rows, in_cols_ref, new_in_cols, matrix, matrix,
        )
    step(
        starts[OUT_AT], [line_held[at, each + third :, :] for at in quarters], None,
        out_ref, out_grad, new_out, out_rows_ref, new_out_rows, out_cols_ref, new_out_cols, 0, 2,
    )
    for matrix in range(4):
        step(
            starts[CROSS_AT] + matrix * one, [line_held[matrix, 0:each, :]], matrix,
            cross_ref, cross_grad, new_cross, cross_rows_ref, new_cross_rows, cross_cols_ref, new_cross_cols,
            matrix, 3 + matrix,
        )
        if matrix < 3:
            at, pieces = starts[SELF_AT] + matrix * one, [self_held[at, matrix] for at in quarters]
        else:
            at, pieces = starts[PAST_AT], [line_held[at, each : each + third, :] for at in range(3)]
        step(
            at, pieces, matrix, self_ref, self_grad, new_self, self_rows_ref, new_self_rows,
            self_cols_ref, new_self_cols, matrix, 7 + matrix,
        )


def update_all(
    factor, starts, shards, where, total, in_near, line_near, self_near, weights, rows, cols, plain
):
    outs = (*weights, *weights, *rows, *cols, *plain[:2], *plain[:2], *plain[2:])
    out_shape = [jax.ShapeDtypeStruct(value.shape, WIDE) for value in outs]
    spec = pl.BlockSpec(memory_space=pltpu.VMEM)
    return pl.pallas_call(
        functools.partial(update_kernel, factor, starts, shards),
        in_specs=[pl.BlockSpec(memory_space=pltpu.SMEM)] + [spec] * 29,
        out_specs=[spec] * 22,
        out_shape=out_shape,
        scratch_shapes=[pltpu.VMEM((4, *near[0].shape), LOW) for near in (in_near, line_near, self_near)],
        cost_estimate=pl.CostEstimate(flops=int(8 * PEAK), bytes_accessed=16 << 20, transcendentals=0),
        compiler_params=pltpu.CompilerParams(vmem_limit_bytes=60 * MEGABYTE),
        name="update_all",
    )(where, total, *in_near, *line_near, *self_near, *weights, *rows, *cols, *plain)


def flat_permute(value, target):
    reps, shards = lax.axis_size("rep"), lax.axis_size("fsdp")
    pairs = []
    for rep in range(reps):
        for shard in range(shards):
            to_rep, to_shard = target(rep, shard)
            pairs.append((rep * shards + shard, to_rep * shards + to_shard))
    return lax.ppermute(value, ("rep", "fsdp"), pairs)


def from_rep(value, way):
    return flat_permute(value, lambda rep, shard: (rep ^ way, shard))


def from_shard(value, way):
    return flat_permute(value, lambda rep, shard: (rep, shard ^ way))


def from_line(value, hops):
    shards = lax.axis_size("fsdp")
    return flat_permute(value, lambda rep, shard: (rep, (shard + LINE_CORES * hops) % shards))


def along_line(piece):
    return jnp.stack([piece] + [from_line(piece, hop) for hop in range(1, LINE)])


def across_reps(line):
    return [line] + [from_rep(line, way) for way in range(1, 4)]


def with_partner(parts):
    return parts + [from_shard(part, 1) for part in parts]


def add_line(parts):
    return [parts[0]] + [from_line(parts[hop], hop) for hop in range(1, LINE)]


def rep_parts(parts, axis):
    rep = lax.axis_index("rep")
    pick = lambda at: lax.dynamic_index_in_dim(parts, at, axis, keepdims=False)
    return [pick(rep)] + [from_rep(pick(rep ^ way), way) for way in range(1, 4)]


def add_up(parts):
    return sum(part.astype(WIDE) for part in parts).astype(LOW)


def rep_near(piece):
    return [piece] + [from_rep(piece, way) for way in range(1, 4)]


def rep_order(near):
    rep = lax.axis_index("rep")
    return [lax.select_n(rep, *[near[at ^ own] for own in range(4)]) for at in range(4)]


def hold(*values):
    return lax.optimization_barrier(values)


def butterfly(vector, move, size):
    way = 1
    while way < size:
        vector = vector + move(vector, way)
        way *= 2
    return vector


def after(value, *earlier):
    return lax.optimization_barrier((value, *earlier))[0]


def row_moments(gradient, row_state):
    squares = gradient * gradient + TINY_TERM
    return DECAY_RATE * row_state + (1.0 - DECAY_RATE) * jnp.mean(squares, axis=-1)


def factored_sums(gradient, row_state):
    squares = gradient * gradient + TINY_TERM
    return jnp.sum(squares, axis=1), jnp.sum(row_moments(gradient, row_state), axis=1)


def pack(values):
    return jnp.concatenate([value.reshape(-1) for value in values])


def unpack(vector, values):
    out = []
    for value in values:
        out.append(vector[: value.size].reshape(value.shape))
        vector = vector[value.size :]
    return out


def factored_update(gradient, weight, row_moment, col_state, col_sum, row_sum, square):
    count, rows, cols = weight.shape
    whole_rows = rows * lax.axis_size("fsdp")
    col_moment = DECAY_RATE * col_state + (1.0 - DECAY_RATE) * col_sum / whole_rows
    scale = lax.rsqrt(row_moment / (row_sum[:, None] / whole_rows))
    step = STEP_RATE * jnp.sqrt(square / (whole_rows * cols) + 1e-06)
    direction = gradient * scale[:, :, None] * lax.rsqrt(col_moment)[:, None, :]
    return weight - step[:, None, None] * direction, col_moment


def plain_update(gradient, weight, moment, square):
    moment = DECAY_RATE * moment + (1.0 - DECAY_RATE) * (gradient * gradient + TINY_TERM)
    step = STEP_RATE * jnp.sqrt(square + 1e-06)
    return weight - step * gradient * lax.rsqrt(moment), moment


def per_device(
    dec_in,
    memory,
    out_grad,
    dec_len,
    enc_len,
    buckets,
    self_weight,
    cross_weight,
    ffn_in,
    ffn_out,
    gains,
    table,
    self_rows,
    self_cols,
    cross_rows,
    cross_cols,
    in_rows,
    in_cols,
    out_rows,
    out_cols,
    gain_moment,
    table_moment,
):
    seq_count, seq_length, model_width = dec_in.shape
    mem_length = memory.shape[1]
    row_count = seq_count * seq_length
    hidden_width = ffn_in.shape[2]
    reps, shards = lax.axis_size("rep"), lax.axis_size("fsdp")
    rep, shard = lax.axis_index("rep"), lax.axis_index("fsdp")
    quarters = reps == 4 and shards == 8
    part_rows = hidden_width // shards
    grad_factor = 1.0 / math.sqrt(row_count * reps * shards)
    where = jnp.stack([rep, shard // 2, shard % 2]).astype(jnp.int32) * int(quarters)
    w_self = lax.all_gather(self_weight.astype(LOW), "fsdp", axis=1, tiled=True)
    gain_full = lax.all_gather(gains.astype(LOW), "fsdp", axis=1, tiled=True).astype(WIDE)
    w_in = lax.all_gather(ffn_in.astype(LOW), "fsdp", axis=1, tiled=True)

    each = model_width // (LINE * LINE_CORES)
    if quarters:
        out_each = part_rows // 4
        cross_quarter = lax.dynamic_index_in_dim(cross_weight, rep, 0, keepdims=False).astype(LOW)
        out_quarter = lax.dynamic_index_in_dim(
            ffn_out.reshape(4, out_each, model_width), rep, 0, keepdims=False
        ).astype(LOW)
        cross_pieces = with_partner(across_reps(along_line(cross_quarter)))
    square = lambda value: jnp.sum(value * value, axis=(1, 2))
    squares = (
        square(ffn_in), square(ffn_out[None]), square(cross_weight), square(self_weight),
        jnp.sum(gains * gains, axis=1),
    )
    if quarters:
        state_sums = (
            jnp.sum(in_rows, axis=1), jnp.sum(out_rows)[None], jnp.sum(cross_rows, axis=1),
            jnp.sum(self_rows, axis=1),
        )
        blank = jnp.zeros((5,), WIDE)
        constants = pack([*state_sums, blank, *squares]) / reps
        constants = jnp.pad(constants, (0, LANES - constants.size)).reshape(1, LANES)
        gain_full, constants = hold(gain_full, constants)

    bucket_mask = (buckets[None, :] == jnp.arange(BUCKETS)[:, None]).astype(WIDE)
    by_distance = jnp.sum(table.T[:, :, None] * bucket_mask[None], axis=1)
    by_distance = jnp.pad(by_distance, ((0, 16 - H), (0, 0)))
    backwards = jnp.roll(by_distance[:, ::-1], 1, axis=1)
    no_bias = jnp.zeros((8, PAIR), WIDE)
    no_source = jnp.zeros((16, PAIR), LOW)

    dec_rows = dec_in.reshape(row_count, model_width)
    mem_rows = memory.reshape(seq_count * mem_length, model_width)
    grad_rows = out_grad.reshape(row_count, model_width)
    *kept_one, after_self = attention_forward(
        True, dec_rows, no_source, dec_len, where, gain_full[0:1], w_self, backwards
    )
    if quarters:
        w_cross = list(hold(*cross_pieces, after_self)[:-1])
        out_line = along_line(after(out_quarter, w_self))
        out_near = across_reps(after(out_line, after_self))
    else:
        w_cross = lax.all_gather(cross_weight.astype(LOW), "fsdp", axis=1, tiled=True)
        w_out = [lax.all_gather(ffn_out.astype(LOW), "fsdp", axis=0, tiled=True)]
    *kept_two, after_cross = attention_forward(
        False, after_self, mem_rows, enc_len, where, gain_full[1:2], w_cross, no_bias
    )
    if quarters:
        *kept_two, after_cross, w_cross = (*kept_two, after_cross)
    if quarters:
        out_near = hold(*out_near, after_cross)[:-1]
        w_out = with_partner(list(out_near))
    layer_out, grad_cross, grad_gate, grad_up, *out_near, gain_three = feed_forward_both(
        after_cross, grad_rows, dec_len, where, gain_full[2:3], w_in, w_out
    )
    scatter = lambda value, at: lax.psum_scatter(value, "fsdp", scatter_dimension=at, tiled=True)
    if quarters:
        own_gate = scatter(grad_gate, 0)
        out_near = out_near[:1] + [from_rep(out_near[way], way) for way in range(1, 4)]
    grad_self, grad_k_two, grad_v_two, gain_two, *cross_near, cross_far = attention_backward(
        False, after_self, mem_rows, grad_cross, enc_len, where, gain_full[1:2], w_cross, no_bias, kept_two,
        kept_two[3], kept_one[3],
    )
    if quarters:
        cross_far, grad_k_two, *out_near = hold(cross_far, grad_k_two, *out_near)
        pair = from_shard(cross_far, 1)
        memory_grad = memory_gradient(grad_k_two, grad_v_two, w_cross)
        memory_grad, pair, own_gate = hold(memory_grad, pair, own_gate)
        own_up = scatter(grad_up, 0)
        cross_chip = [add_up([cross_near[way], pair[way]]) for way in range(4)]
        grad_self, *cross_chip = hold(grad_self, *cross_chip)
        cross_near = cross_chip[:1] + [from_rep(cross_chip[way], way) for way in range(1, 4)]
    else:
        memory_grad = memory_gradient(grad_k_two, grad_v_two, w_cross)
    *grads_one, grad_self_weights, dist_grad = attention_backward(
        True, dec_rows, no_source, grad_self, dec_len, where, gain_full[0:1], w_self, by_distance, kept_one,
        no_source, no_source,
    )
    if quarters:
        dist_grad, own_up, grad_self_weights, *rest = hold(
            dist_grad, own_up, grad_self_weights, *grads_one, *cross_near, *out_near
        )
        grads_one, cross_near, out_near = rest[:3], rest[3:7], rest[7:]
        own_self = scatter(grad_self_weights, 1)
        out_sum = add_up(out_near)
        out_pair = from_shard(out_sum[1], 1)
        in_parts = rep_parts(jnp.stack([own_gate, own_up]).reshape(2, 4, -1, hidden_width), 1)
        line = jnp.concatenate([add_up(cross_near), add_up([out_sum[0], out_pair])], axis=1)
        in_piece, in_columns = gated_sums(grad_factor, in_parts)
        in_near = rep_near(in_piece)
        *line_parts, gate = hold(*add_line(line), grads_one[0])
        grads_one = [gate, *grads_one[1:]]
        input_grad, gain_one = input_gradient(grads_one, w_self, dec_rows, grad_self, gain_full[0:1])
    else:
        input_grad, gain_one = input_gradient(grads_one, w_self, dec_rows, grad_self, gain_full[0:1])
    layer_out = layer_out.reshape(dec_in.shape)
    input_grad = input_grad.reshape(dec_in.shape)
    memory_grad = memory_grad.reshape(memory.shape)
    table_part = jnp.sum(dist_grad[:H, None, :] * bucket_mask[None], axis=2)
    wide = lambda value: value.astype(WIDE) * grad_factor
    gain_parts = jnp.concatenate([gain_one, gain_two, gain_three]) * grad_factor
    table_part = table_part * grad_factor
    if quarters:
        starts = vector_rows(model_width, hidden_width, 3 * model_width + H * LANES)
        small = jnp.concatenate(
            [gain_parts.reshape(-1, LANES), jnp.pad(table_part, ((0, 0), (0, LANES - BUCKETS)))]
        )
        line_piece, early = early_sums(grad_factor, starts, where, line_parts, in_columns, constants)
        line_near = rep_near(line_piece)
        own_self, early, *near = hold(own_self, early, *in_near, *line_near[:3])
        in_near, line_near = near[:4], near[4:] + line_near[3:]
        self_parts = rep_parts(own_self.reshape(3, 4, -1, model_width), 1)
        self_piece, vector = late_sums(grad_factor, starts, self_parts, small, early)
        vector, *self_near = hold(butterfly(vector, from_shard, shards), *rep_near(self_piece))
        total = butterfly(vector, from_rep, reps)
        (
            ffn_in_grad, feedforward_output_gradient, cross_grad, self_grad,
            new_ffn_in, new_ffn_out, new_cross, new_self,
            new_in_rows, new_out_rows, new_cross_rows, new_self_rows,
            new_in_cols, new_out_cols, new_cross_cols, new_self_cols,
            gains_grad, table_grad, new_gains, new_table, new_gain_moment, new_table_moment,
        ) = update_all(
            grad_factor, starts, shards, where, total, in_near, line_near, self_near,
            (ffn_in, ffn_out, cross_weight, self_weight),
            (in_rows, out_rows[None], cross_rows, self_rows),
            (in_cols, out_cols[None], cross_cols, self_cols),
            (gains, table.T, gain_moment, table_moment.T),
        )
        table_grad, new_table, new_table_moment = table_grad.T, new_table.T, new_table_moment.T
        new_out_rows, new_out_cols = new_out_rows.reshape(-1), new_out_cols.reshape(-1)
    else:
        over_reps = lambda value: lax.psum(value, "rep")
        own_in = over_reps(scatter(jnp.stack([grad_gate, grad_up]), 1))
        grad_out = jnp.stack(out_near)
        grad_out = grad_out.transpose(2, 1, 0, 3, 4).reshape(hidden_width, model_width)
        own_out = over_reps(scatter(grad_out, 0))
        packed = jnp.stack([jnp.stack(cross_near), cross_far]).transpose(1, 2, 0, 3, 4)
        cross_parts = packed[..., :each, :].reshape(4, model_width, model_width)
        past = packed[:3, ..., each:, :].transpose(1, 2, 0, 3, 4).reshape(1, model_width, model_width)
        own_cross = over_reps(scatter(cross_parts, 1))
        own_self = over_reps(scatter(jnp.concatenate([grad_self_weights, past]), 1))
        self_grad, cross_grad, ffn_in_grad, feedforward_output_gradient = [
            wide(member) for member in (own_self, own_cross, own_in, own_out)
        ]
        local = (
            *factored_sums(ffn_in_grad, in_rows),
            *factored_sums(feedforward_output_gradient[None], out_rows[None]),
            *factored_sums(cross_grad, cross_rows),
            *factored_sums(self_grad, self_rows),
            *squares,
        )
        found = unpack(lax.psum(pack(local), "fsdp"), local)
        in_sums, out_sums, cross_sums, self_sums, squares = (
            found[0:2], found[2:4], found[4:6], found[6:8], found[8:],
        )
        gain_total, table_grad = lax.psum((gain_parts, table_part.T), ("rep", "fsdp"))
        gains_grad = lax.dynamic_slice_in_dim(gain_total, shard * gains.shape[1], gains.shape[1], axis=1)
        new_gains, new_gain_moment = plain_update(
            gains_grad, gains, gain_moment, (squares[4] / model_width)[:, None]
        )
        new_table, new_table_moment = plain_update(
            table_grad, table, table_moment, jnp.mean(table * table)
        )
        new_in_rows = row_moments(ffn_in_grad, in_rows)
        new_out_rows = row_moments(feedforward_output_gradient, out_rows)
        new_cross_rows = row_moments(cross_grad, cross_rows)
        new_self_rows = row_moments(self_grad, self_rows)
        new_ffn_in, new_in_cols = factored_update(
            ffn_in_grad, ffn_in, new_in_rows, in_cols, *in_sums, squares[0]
        )
        new_ffn_out, new_out_cols = [
            member[0]
            for member in factored_update(
                feedforward_output_gradient[None], ffn_out[None], new_out_rows[None], out_cols[None],
                *out_sums, squares[1],
            )
        ]
        new_cross, new_cross_cols = factored_update(
            cross_grad, cross_weight, new_cross_rows, cross_cols, *cross_sums, squares[2]
        )
        new_self, new_self_cols = factored_update(
            self_grad, self_weight, new_self_rows, self_cols, *self_sums, squares[3]
        )
    return (
        layer_out,
        input_grad,
        memory_grad,
        self_grad,
        cross_grad,
        ffn_in_grad,
        feedforward_output_gradient,
        gains_grad,
        table_grad,
        new_self,
        new_cross,
        new_ffn_in,
        new_ffn_out,
        new_gains,
        new_table,
        new_self_rows,
        new_self_cols,
        new_cross_rows,
        new_cross_cols,
        new_in_rows,
        new_in_cols,
        new_out_rows,
        new_out_cols,
        new_gain_moment,
        new_table_moment,
    )


def solution(mesh):
    placed = (
        P(("rep", "fsdp"), None, None),
        P(("rep", "fsdp"), None, None),
        P(("rep", "fsdp"), None, None),
        P(("rep", "fsdp")),
        P(("rep", "fsdp")),
        P(),
        P(None, "fsdp", None),
        P(None, "fsdp", None),
        P(None, "fsdp", None),
        P("fsdp", None),
        P(None, "fsdp"),
        P(),
        P(None, "fsdp"),
        P(),
        P(None, "fsdp"),
        P(),
        P(None, "fsdp"),
        P(),
        P("fsdp"),
        P(),
        P(None, "fsdp"),
        P(),
    )
    return jax.shard_map(
        per_device,
        mesh=mesh,
        in_specs=placed,
        out_specs=(
            P(("rep", "fsdp"), None, None),
            P(("rep", "fsdp"), None, None),
            P(("rep", "fsdp"), None, None),
            P(None, "fsdp", None),
            P(None, "fsdp", None),
            P(None, "fsdp", None),
            P("fsdp", None),
            P(None, "fsdp"),
            P(),
            P(None, "fsdp", None),
            P(None, "fsdp", None),
            P(None, "fsdp", None),
            P("fsdp", None),
            P(None, "fsdp"),
            P(),
            P(None, "fsdp"),
            P(),
            P(None, "fsdp"),
            P(),
            P(None, "fsdp"),
            P(),
            P("fsdp"),
            P(),
            P(None, "fsdp"),
            P(),
        ),
        check_vma=False,
    )
```

```python
import functools
import math

import jax
import jax.numpy as jnp
from jax import lax
from jax.experimental import pallas as pl
from jax.experimental.pallas import tpu as pltpu
from jax.sharding import PartitionSpec as P

H = 12
DH = 64
BUCKETS = 32
DECAY_RATE = 0.8
STEP_RATE = 0.2
TINY_TERM = 1e-30
PAIR = 2 * DH
GROUP = 4 * DH
HIDDEN = -1e30
MEGABYTE = 1024 * 1024
PEAK = 1.15e9
LINE = 4
LINE_CORES = 2
LOW = jnp.bfloat16
WIDE = jnp.float32


def nn(left, right):
    return lax.dot_general(left, right, (((1,), (0,)), ((), ())), preferred_element_type=WIDE)


def nt(left, right):
    return lax.dot_general(left, right, (((1,), (1,)), ((), ())), preferred_element_type=WIDE)


def tn(left, right):
    return lax.dot_general(left, right, (((0,), (0,)), ((), ())), preferred_element_type=WIDE)


def rms_rate(rows):
    return lax.rsqrt(jnp.mean(rows * rows, axis=-1, keepdims=True) + 1e-06)


def three_parts(column):
    high = column.astype(LOW)
    rest = column - high.astype(WIDE)
    middle = rest.astype(LOW)
    low = (rest - middle.astype(WIDE)).astype(LOW)
    return high, middle, low


def chunks(total, size):
    return [(at, min(size, total - at)) for at in range(0, total, size)]


def lanes(rows):
    return lax.broadcasted_iota(jnp.int32, (rows, PAIR), 1)


def own_lanes(rows, side):
    lane = lanes(rows)
    return (lane >= DH * side) & (lane < DH * (side + 1))


def key_extras(rows, side, length):
    lane = lanes(rows) - DH * (1 - side)
    dead = lax.broadcasted_iota(jnp.int32, (rows, PAIR), 0) >= length
    mask = jnp.where(dead, HIDDEN, 0.0)
    return jnp.where(
        (lane >= 0) & (lane < 3), 1.0, jnp.where(lane == 3, mask, 0.0)
    ).astype(LOW)


def row_extras(rows, side, column, last):
    lane = lanes(rows) - DH * (1 - side)
    high, middle, low = three_parts(column)
    wide = lambda part: jnp.broadcast_to(part.astype(WIDE), (rows, PAIR))
    return jnp.where(
        lane == 0,
        wide(high),
        jnp.where(
            lane == 1, wide(middle), jnp.where(lane == 2, wide(low), jnp.where(lane == 3, last, 0.0))
        ),
    ).astype(LOW)


def piece_copies(parts, where_ref, place, sems):
    rep, line, core = where_ref[0], where_ref[1], where_ref[2]
    copies = []
    for other in range(LINE_CORES):
        for way in range(4):
            for hop in range(LINE):
                shard = lax.rem(line - hop + LINE, LINE) * LINE_CORES + (core ^ other)
                source = parts[4 * other + way].at[hop]
                copies.append(pltpu.make_async_copy(source, place(rep ^ way, shard), sems.at[len(copies)]))
    return copies


def forward_body(causal, seq_count, length_ref, wave_ref, bias_ref, q_ref, k_ref, v_ref, mix_ref, total_ref, group):
    rows = q_ref.shape[0] // seq_count
    keys = k_ref.shape[0] // seq_count
    block = rows
    for pair in range(2):
        at = pair * PAIR
        for side in range(2):
            head = 2 * pair + side
            if causal:
                wave = wave_ref[pl.ds(group * 4 + head, 1), :]
                spread = pltpu.roll(
                    jnp.broadcast_to(wave, (rows, keys)), 0, 1, stride=1, stride_axis=0
                )
                row = lax.broadcasted_iota(jnp.int32, (rows, keys), 0)
                column = lax.broadcasted_iota(jnp.int32, (rows, keys), 1)
                bias_ref[side] = jnp.where(column <= row, spread, HIDDEN)
        for seq in range(seq_count):
            outs = []
            for side in range(2):
                own_q = own_lanes(rows, side)
                own_k = own_lanes(keys, side)
                query = jnp.where(
                    own_q,
                    q_ref[seq * rows : (seq + 1) * rows, at : at + PAIR],
                    (lanes(rows) == DH * (1 - side) + 3).astype(LOW),
                )
                key = jnp.where(
                    own_k,
                    k_ref[seq * keys : (seq + 1) * keys, at : at + PAIR],
                    key_extras(keys, side, length_ref[seq]),
                )
                value = jnp.where(
                    own_k,
                    v_ref[seq * keys : (seq + 1) * keys, at : at + PAIR],
                    jnp.ones((), LOW),
                )
                parts = []
                for start in range(0, rows, block):
                    span = start + block if causal else keys
                    scores = nt(query[start : start + block], key[:span])
                    if causal:
                        scores = scores + bias_ref[side, start : start + block, :span]
                    top = jnp.max(scores, axis=1, keepdims=True)
                    weight = jnp.exp(scores - top)
                    out = nn(weight.astype(LOW), value[:span])
                    total = out[:, DH * (1 - side) : DH * (1 - side) + 1]
                    parts.append(out * (1.0 / total))
                    spot = pl.ds(seq * rows + start, block)
                    lane = lanes(block)
                    seen = total_ref[spot, :] if (pair or side) else jnp.zeros((block, PAIR), WIDE)
                    total_ref[spot, :] = jnp.where(
                        lane == 2 * pair + side, top + jnp.log(total), seen
                    )
                outs.append(jnp.concatenate(parts, axis=0))
            mix_ref[seq * rows : (seq + 1) * rows, at : at + PAIR] = jnp.where(
                own_lanes(rows, 0), outs[0], outs[1]
            ).astype(LOW)


def forward_kernel(causal, seq_count, pieces, length_ref, where_ref, x_ref, source_ref, gain_ref, *refs):
    group = pl.program_id(0)
    if pieces:
        w_refs, wave_ref, refs = refs[:8], refs[8], refs[9:]
        q_ref, k_ref, v_ref, mix_ref, total_ref, after_ref, whole_ref = refs[:7]
        normed, bias, held, sems, whole_sem = refs[7:]
        each = held.shape[1] // (LINE * LINE_CORES)
        place = lambda quarter, at: held.at[quarter, pl.ds(at * each, each)]
        copies = piece_copies(w_refs, where_ref, place, sems)
        keep = pltpu.make_async_copy(held, whole_ref, whole_sem)
        across = pl.ds(pl.multiple_of(group * GROUP, GROUP), GROUP)
        wq_ref, wk_ref, wv_ref = [held.at[at, :, across] for at in range(3)]
        wo_ref = held.at[3, across, :]
    else:
        wq_ref, wk_ref, wv_ref, wo_ref, wave_ref = refs[:5]
        q_ref, k_ref, v_ref, mix_ref, total_ref, after_ref, normed, bias = refs[5:]

    @pl.when(group == 0)
    def _():
        if pieces:
            for copy in copies:
                copy.start()
        for at, size in chunks(x_ref.shape[0], 256):
            rows = x_ref[at : at + size, :].astype(WIDE)
            normed[at : at + size, :] = (rows * rms_rate(rows) * gain_ref[...]).astype(LOW)
            after_ref[at : at + size, :] = rows
        if pieces:
            for copy in copies:
                copy.wait()
            keep.start()

    source = normed if causal else source_ref
    q_ref[...] = nn(normed[...], wq_ref[...]).astype(LOW)
    k_ref[...] = nn(source[...], wk_ref[...]).astype(LOW)
    v_ref[...] = nn(source[...], wv_ref[...]).astype(LOW)
    forward_body(causal, seq_count, length_ref, wave_ref, bias, q_ref, k_ref, v_ref, mix_ref, total_ref, group)
    after_ref[...] += nn(mix_ref[...], wo_ref[...])

    @pl.when(group == pl.num_programs(0) - 1)
    def _():
        if pieces:
            keep.wait()


def weight_specs(width):
    across = lambda at: pl.BlockSpec((None, width, GROUP), lambda g, at=at: (at, 0, g))
    return [across(0), across(1), across(2), pl.BlockSpec((None, GROUP, width), lambda g: (3, g, 0))]


def whole(shape):
    return pl.BlockSpec(shape, lambda g: (0,) * len(shape), pipeline_mode=pl.Buffered(1))


def columns(rows):
    return pl.BlockSpec((rows, GROUP), lambda g: (0, g))


def attention_forward(causal, x, source, lengths, where, gain, weights, wave):
    row_count, width = x.shape
    seq_count = lengths.shape[0]
    source_rows = row_count if causal else source.shape[0]
    length = row_count // seq_count
    groups = width // GROUP
    low = lambda rows: jax.ShapeDtypeStruct((rows, width), LOW)
    pieces = isinstance(weights, list)
    everything = jax.ShapeDtypeStruct((4, width, width), LOW)
    anywhere = pl.BlockSpec(memory_space=pl.ANY)
    return pl.pallas_call(
        functools.partial(forward_kernel, causal, seq_count, pieces),
        grid=(groups,),
        in_specs=[
            pl.BlockSpec(memory_space=pltpu.SMEM),
            pl.BlockSpec(memory_space=pltpu.SMEM),
            whole(x.shape),
            whole(source.shape),
            whole(gain.shape),
            *([anywhere] * 8 if pieces else weight_specs(width)),
            whole(wave.shape),
        ],
        out_specs=[
            columns(row_count),
            columns(source_rows),
            columns(source_rows),
            columns(row_count),
            pl.BlockSpec((None, row_count, PAIR), lambda g: (g, 0, 0)),
            whole((row_count, width)),
            *([anywhere] if pieces else []),
        ],
        out_shape=[
            low(row_count),
            low(source_rows),
            low(source_rows),
            low(row_count),
            jax.ShapeDtypeStruct((groups, row_count, PAIR), WIDE),
            jax.ShapeDtypeStruct((row_count, width), WIDE),
            *([everything] if pieces else []),
        ],
        scratch_shapes=[
            pltpu.VMEM((row_count, width), LOW),
            pltpu.VMEM((2, length, length) if causal else (1, 8, PAIR), WIDE),
            *(
                [
                    pltpu.VMEM(everything.shape, LOW),
                    pltpu.SemaphoreType.DMA((8 * LINE,)),
                    pltpu.SemaphoreType.DMA(()),
                ]
                if pieces
                else []
            ),
        ],
        cost_estimate=pl.CostEstimate(flops=int(27 * PEAK), bytes_accessed=20 << 20, transcendentals=0),
        compiler_params=pltpu.CompilerParams(vmem_limit_bytes=60 * MEGABYTE),
        name="self_forward" if causal else "cross_forward",
    )(lengths, where, x, source, gain, *(weights if pieces else [weights] * 4), wave)


def gelu_parts(gate):
    root = 0.7978845608028654
    square = gate * gate
    inner = jnp.tanh(root * gate * (1.0 + 0.044715 * square))
    half = 0.5 * (1.0 + inner)
    value = gate * half
    slope = half + 0.5 * gate * (1.0 - inner * inner) * (root * (1.0 + 3 * 0.044715 * square))
    return value, slope


def rms_back(rows, gain, grad):
    rate = rms_rate(rows)
    scaled = rows * rate
    low = grad * gain
    grad_rows = rate * (low - scaled * jnp.mean(scaled * low, axis=-1, keepdims=True))
    return grad_rows, jnp.sum(grad * scaled, axis=0, keepdims=True)


def shard_slot(where_ref, shard):
    return (shard % LINE_CORES) ^ where_ref[2], lax.rem(shard // LINE_CORES - where_ref[1] + LINE, LINE)


def feed_kernel(
    seq_count, pieces, length_ref, where_ref, after_ref, out_grad_ref, gain_ref, wg_ref, wu_ref, *refs,
):
    wd_refs, (layer_ref, grad_cross_ref, dwg_ref, dwu_ref) = refs[:pieces], refs[pieces : pieces + 4]
    near_refs = refs[pieces + 4 : pieces + 8]
    dgain_ref, normed, normed_t, down, out_total, grad_total, cut, *held = refs[pieces + 8 :]
    step = pl.program_id(0)
    row_count = after_ref.shape[0]
    length = row_count // seq_count

    def live(at, size):
        position = lax.broadcasted_iota(jnp.int32, (size, 1), 0) + (at % length)
        return (position < length_ref[at // length]).astype(WIDE)

    @pl.when(step == 0)
    def _():
        if pieces > 1:
            place = lambda quarter, at: held[0].at[pl.ds((at * 4 + quarter) * cut.shape[2], cut.shape[2])]
            copies = piece_copies(wd_refs, where_ref, place, held[1])
            for copy in copies:
                copy.start()
        for at, size in chunks(row_count, 256):
            rows = after_ref[at : at + size, :]
            low = (rows * rms_rate(rows) * gain_ref[...]).astype(LOW)
            normed[at : at + size, :] = low
            normed_t[:, at : at + size] = low.T
            down[at : at + size, :] = (
                out_grad_ref[at : at + size, :].astype(WIDE) * live(at, size)
            ).astype(LOW)
            out_total[at : at + size, :] = rows
            grad_total[at : at + size, :] = jnp.zeros((size, rows.shape[1]), WIDE)
        if pieces > 1:
            for copy in copies:
                copy.wait()

    block = wg_ref.shape[1]
    if pieces > 1:
        wd_ref = held[0].at[pl.ds(pl.multiple_of(step * block, block), block)]
    else:
        wd_ref = wd_refs[0]
    gate = nn(normed[...], wg_ref[...])
    up = nn(normed[...], wu_ref[...])
    value, slope = gelu_parts(gate)
    hidden = (value * up).astype(LOW)
    out_total[...] += nn(hidden, wd_ref[...])
    grad_hidden = nt(down[...], wd_ref[...])
    cut[...] = tn(hidden, down[...]).astype(LOW).reshape(cut.shape)
    for part in range(cut.shape[0]):
        core, hop = shard_slot(where_ref, step * cut.shape[0] + part)
        for way in range(4):
            near_refs[way][core, hop] = cut[part, where_ref[0] ^ way]
    grad_gate = (grad_hidden * up * slope).astype(LOW)
    grad_up = (grad_hidden * value).astype(LOW)
    dwg_ref[...] = nn(normed_t[...], grad_gate).astype(LOW)
    dwu_ref[...] = nn(normed_t[...], grad_up).astype(LOW)
    grad_total[...] += nt(grad_gate, wg_ref[...]) + nt(grad_up, wu_ref[...])

    @pl.when(step == pl.num_programs(0) - 1)
    def _():
        dgain = jnp.zeros(dgain_ref.shape, WIDE)
        for at, size in chunks(row_count, 256):
            part = slice(at, at + size)
            layer_ref[part, :] = (out_total[part, :] * live(at, size)).astype(LOW)
            grad_rows, gain_part = rms_back(after_ref[part, :], gain_ref[...], grad_total[part, :])
            dgain = dgain + gain_part
            grad_cross_ref[part, :] = (
                out_grad_ref[part, :].astype(WIDE) * live(at, size) + grad_rows
            )
        dgain_ref[...] = dgain


def feed_forward_both(after, out_grad, lengths, where, gain, w_in, w_out):
    row_count, width = after.shape
    hidden = w_in.shape[2]
    each = hidden // (LINE * LINE_CORES)
    block = 2 * each
    seq_count = lengths.shape[0]
    wide = pl.BlockSpec((None, width, block), lambda g: (0, 0, g))
    wide_up = pl.BlockSpec((None, width, block), lambda g: (1, 0, g))
    tall = pl.BlockSpec((block, width), lambda g: (g, 0))
    flat = pl.BlockSpec((width, block), lambda g: (0, g))
    near = (LINE_CORES, LINE, each // 4, width)
    pieces = len(w_out)
    held = [pltpu.VMEM((hidden, width), LOW), pltpu.SemaphoreType.DMA((pieces * LINE,))] if pieces > 1 else []
    return pl.pallas_call(
        functools.partial(feed_kernel, seq_count, pieces),
        grid=(hidden // block,),
        in_specs=[
            pl.BlockSpec(memory_space=pltpu.SMEM),
            pl.BlockSpec(memory_space=pltpu.SMEM),
            whole(after.shape),
            whole(out_grad.shape),
            whole(gain.shape),
            wide,
            wide_up,
            *([pl.BlockSpec(memory_space=pl.ANY)] * pieces if pieces > 1 else [tall]),
        ],
        out_specs=[whole(after.shape), whole(after.shape), flat, flat, *[whole(near)] * 4, whole((1, width))],
        out_shape=[
            jax.ShapeDtypeStruct((row_count, width), LOW),
            jax.ShapeDtypeStruct((row_count, width), WIDE),
            jax.ShapeDtypeStruct((width, hidden), LOW),
            jax.ShapeDtypeStruct((width, hidden), LOW),
            *[jax.ShapeDtypeStruct(near, LOW)] * 4,
            jax.ShapeDtypeStruct((1, width), WIDE),
        ],
        scratch_shapes=[
            pltpu.VMEM((row_count, width), LOW),
            pltpu.VMEM((width, row_count), LOW),
            pltpu.VMEM((row_count, width), LOW),
            pltpu.VMEM((row_count, width), WIDE),
            pltpu.VMEM((row_count, width), WIDE),
            pltpu.VMEM((2, 4, each // 4, width), LOW),
            *held,
        ],
        cost_estimate=pl.CostEstimate(flops=int(46 * PEAK), bytes_accessed=40 << 20, transcendentals=0),
        compiler_params=pltpu.CompilerParams(vmem_limit_bytes=60 * MEGABYTE),
        name="feed_forward_both",
    )(lengths, where, after, out_grad, gain, w_in, w_in, *w_out)


def backward_kernel(
    causal, seq_count, length_ref, where_ref, x_ref, source_ref, grad_ref, gain_ref, wq_ref, wo_ref, wave_ref,
    q_ref, k_ref, v_ref, mix_ref, total_ref, mix_all_ref, mix_past_ref, *refs,
):
    if causal:
        gq, gk_out_ref, gv_out_ref, dw_ref, dist_ref = refs[:5]
        normed_t, branch, grad_mix, bias, score_sum = refs[5:]
        source_t = normed_t
    else:
        grad_x_ref, gk_out_ref, gv_out_ref, dgain_ref = refs[:4]
        near_refs, far_ref = refs[4:8], refs[8]
        normed_t, branch, grad_mix, gq, source_t, mix_t, grad_total, dw_ref, past = refs[9:]
    group = pl.program_id(0)
    row_count = x_ref.shape[0]
    rows = q_ref.shape[0] // seq_count
    keys = k_ref.shape[0] // seq_count
    block = rows

    @pl.when(group == 0)
    def _():
        for at, size in chunks(row_count, 256):
            value = x_ref[at : at + size, :].astype(WIDE)
            low = (value * rms_rate(value) * gain_ref[...]).astype(LOW)
            normed_t[:, at : at + size] = low.T
            branch[at : at + size, :] = grad_ref[at : at + size, :].astype(LOW)
            if not causal:
                mix_t[:, at : at + size] = mix_all_ref[at : at + size, :].T
                grad_total[at : at + size, :] = jnp.zeros((size, value.shape[1]), WIDE)
        if not causal:
            for at, size in chunks(source_ref.shape[0], 256):
                source_t[:, at : at + size] = source_ref[at : at + size, :].T

    grad_mix[...] = nt(branch[...], wo_ref[...]).astype(LOW)
    if not causal:
        across = pl.ds(pl.multiple_of(group * GROUP, GROUP), GROUP)
        put = lambda at, value: dw_ref.__setitem__(at, value.astype(LOW).reshape(dw_ref.shape[1:]))
        put(3, nn(mix_t[...], branch[:, across]))

    for pair in range(2):
        at = pair * PAIR
        if causal:
            for side in range(2):
                head = 2 * pair + side
                wave = wave_ref[pl.ds(group * 4 + head, 1), :]
                spread = pltpu.roll(
                    jnp.broadcast_to(wave, (keys, rows)), 0, 1, stride=1, stride_axis=0
                )
                row = lax.broadcasted_iota(jnp.int32, (keys, rows), 0)
                column = lax.broadcasted_iota(jnp.int32, (keys, rows), 1)
                bias[side] = jnp.where(column >= row, spread, HIDDEN)
        for seq in range(seq_count):
            span_q = slice(seq * rows, (seq + 1) * rows)
            span_k = slice(seq * keys, (seq + 1) * keys)
            sides = []
            for side in range(2):
                head = 2 * pair + side
                own_q = own_lanes(rows, side)
                own_k = own_lanes(keys, side)
                total = jnp.sum(
                    jnp.where(lanes(rows) == head, total_ref[span_q, :], 0.0), axis=1, keepdims=True
                )
                grad_low = grad_mix[span_q, at : at + PAIR]
                product = grad_low.astype(WIDE) * mix_ref[span_q, at : at + PAIR].astype(WIDE)
                delta = jnp.sum(jnp.where(own_q, product, 0.0), axis=1, keepdims=True)
                query = jnp.where(
                    own_q, q_ref[span_q, at : at + PAIR], row_extras(rows, side, -total, 1.0)
                )
                grad_out = jnp.where(own_q, grad_low, row_extras(rows, side, -delta, 0.0))
                key = jnp.where(
                    own_k,
                    k_ref[span_k, at : at + PAIR],
                    key_extras(keys, side, length_ref[seq]),
                )
                value = jnp.where(own_k, v_ref[span_k, at : at + PAIR], jnp.ones((), LOW))
                grad_query = []
                grad_key = None
                grad_value = None
                for start in range(0, rows, block):
                    span = start + block if causal else keys
                    scores = nt(key[:span], query[start : start + block])
                    if causal:
                        scores = scores + bias[side, :span, start : start + block]
                    weight = jnp.exp(scores)
                    low = weight.astype(LOW)
                    grad_weight = nt(value[:span], grad_out[start : start + block])
                    grad_score = (weight * grad_weight).astype(LOW)
                    if causal:
                        if seq == 0:
                            score_sum[side, :span, start : start + block] = grad_score.astype(WIDE)
                        else:
                            score_sum[side, :span, start : start + block] += grad_score.astype(WIDE)
                    key_part = nn(grad_score, query[start : start + block])
                    value_part = nn(low, grad_out[start : start + block])
                    grad_query.append(tn(grad_score, key[:span]))
                    if causal and start == 0 and rows > block:
                        rest = jnp.zeros((keys - span, PAIR), WIDE)
                        key_part = jnp.concatenate([key_part, rest], axis=0)
                        value_part = jnp.concatenate([value_part, rest], axis=0)
                    grad_key = key_part if grad_key is None else grad_key + key_part
                    grad_value = value_part if grad_value is None else grad_value + value_part
                sides.append((jnp.concatenate(grad_query, axis=0), grad_key, grad_value))
            pick_q = own_lanes(rows, 0)
            pick_k = own_lanes(keys, 0)
            gq[span_q, at : at + PAIR] = jnp.where(pick_q, sides[0][0], sides[1][0]).astype(LOW)
            gk_out_ref[span_k, at : at + PAIR] = jnp.where(pick_k, sides[0][1], sides[1][1]).astype(LOW)
            gv_out_ref[span_k, at : at + PAIR] = jnp.where(pick_k, sides[0][2], sides[1][2]).astype(LOW)
        if causal:
            for side in range(2):
                head = 2 * pair + side
                row = lax.broadcasted_iota(jnp.int32, (keys, rows), 0)
                column = lax.broadcasted_iota(jnp.int32, (keys, rows), 1)
                held = jnp.where(column >= row, score_sum[side], 0.0)
                while held.shape[0] > 1:
                    half = held.shape[0] // 2
                    held = held[:half] + pltpu.roll(held[half:], rows - half, 1)
                dist_ref[pl.ds(group * 4 + head, 1), :] = held

    if causal:
        dw_ref[0] = nn(normed_t[...], gq[...]).astype(LOW)
        dw_ref[1] = nn(source_t[...], gk_out_ref[...]).astype(LOW)
        dw_ref[2] = nn(source_t[...], gv_out_ref[...]).astype(LOW)
        return
    put(0, nn(normed_t[...], gq[...]))
    put(1, nn(source_t[...], gk_out_ref[...]))
    put(2, nn(source_t[...], gv_out_ref[...]))
    grad_total[...] += nt(gq[...], wq_ref[...])
    rep, line, core = where_ref[0], where_ref[1], where_ref[2]
    held = dw_ref.shape[2]
    slots = []
    for way in range(4):
        for hop in range(LINE):
            at = lax.rem(line + hop, LINE) * LINE_CORES
            slots.append((near_refs[way].at[hop], rep ^ way, at + core))
            slots.append((far_ref.at[way, hop], rep ^ way, at + (core ^ 1)))
    for slot, quarter, shard in slots:
        slot[0:held, across] = dw_ref[quarter, shard]

    @pl.when(group == pl.num_programs(0) - 1)
    def _():
        dgain = jnp.zeros(dgain_ref.shape, WIDE)
        for at, size in chunks(row_count, 256):
            part = slice(at, at + size)
            grad_rows, gain_part = rms_back(
                x_ref[part, :].astype(WIDE), gain_ref[...], grad_total[part, :]
            )
            dgain = dgain + gain_part
            grad_rows = grad_ref[part, :] + grad_rows
            grad_x_ref[part, :] = grad_rows
            branch[part, :] = grad_rows.astype(LOW)
            mix_t[:, part] = mix_past_ref[part, :].T
        dgain_ref[...] = dgain
        thirds = nn(mix_t[...], branch[...]).astype(LOW)
        past[:, 0:3] = thirds.reshape(past.shape[0], 3, *past.shape[2:])
        past[:, 3] = jnp.zeros_like(past[:, 3])
        for slot, quarter, shard in slots:
            slot[held:, :] = past[shard, quarter]


def attention_backward(causal, x, source, grad, lengths, where, gain, weights, wave, kept, mix, past):
    row_count, width = x.shape
    seq_count = lengths.shape[0]
    source_rows = row_count if causal else source.shape[0]
    length = row_count // seq_count
    groups = width // GROUP
    low = lambda rows: jax.ShapeDtypeStruct((rows, width), LOW)
    if causal:
        out_specs = [
            columns(row_count), columns(source_rows), columns(source_rows),
            pl.BlockSpec((3, width, GROUP), lambda g: (0, 0, g)), whole(wave.shape),
        ]
        out_shape = [
            low(row_count), low(source_rows), low(source_rows),
            jax.ShapeDtypeStruct((3, width, width), LOW), jax.ShapeDtypeStruct(wave.shape, WIDE),
        ]
        scratch = [pltpu.VMEM((2, length, length), WIDE)] * 2
    else:
        shards = LINE * LINE_CORES
        each, third = width // shards, width // shards // 3
        near = (LINE, each + third, width)
        out_specs = [
            whole((row_count, width)), columns(source_rows), columns(source_rows), whole((1, width)),
            *[whole(near)] * 4, whole((4, *near)),
        ]
        out_shape = [
            jax.ShapeDtypeStruct((row_count, width), WIDE), low(source_rows), low(source_rows),
            jax.ShapeDtypeStruct((1, width), WIDE), *[jax.ShapeDtypeStruct(near, LOW)] * 4,
            jax.ShapeDtypeStruct((4, *near), LOW),
        ]
        scratch = [
            pltpu.VMEM((row_count, GROUP), LOW),
            pltpu.VMEM((width, source_rows), LOW),
            pltpu.VMEM((width, row_count), LOW),
            pltpu.VMEM((row_count, width), WIDE),
            pltpu.VMEM((4, shards, each, GROUP), LOW),
            pltpu.VMEM((shards, 4, third, width), LOW),
        ]
    return pl.pallas_call(
        functools.partial(backward_kernel, causal, seq_count),
        grid=(groups,),
        in_specs=[
            pl.BlockSpec(memory_space=pltpu.SMEM),
            pl.BlockSpec(memory_space=pltpu.SMEM),
            whole(x.shape),
            whole(source.shape),
            whole(grad.shape),
            whole(gain.shape),
            weight_specs(width)[0],
            weight_specs(width)[3],
            whole(wave.shape),
            columns(row_count),
            columns(source_rows),
            columns(source_rows),
            columns(row_count),
            pl.BlockSpec((None, row_count, PAIR), lambda g: (g, 0, 0)),
            whole(mix.shape),
            whole(past.shape),
        ],
        out_specs=out_specs,
        out_shape=out_shape,
        scratch_shapes=[
            pltpu.VMEM((width, row_count), LOW),
            pltpu.VMEM((row_count, width), LOW),
            pltpu.VMEM((row_count, GROUP), LOW),
            *scratch,
        ],
        cost_estimate=pl.CostEstimate(flops=int(45 * PEAK), bytes_accessed=40 << 20, transcendentals=0),
        compiler_params=pltpu.CompilerParams(vmem_limit_bytes=60 * MEGABYTE),
        name="self_backward" if causal else "cross_backward",
    )(lengths, where, x, source, grad, gain, weights, weights, wave, *kept, mix, past)


def input_kernel(gq_ref, gk_ref, gv_ref, wq_ref, wk_ref, wv_ref, x_ref, grad_ref, gain_ref, out_ref, dgain_ref):
    total = nt(gq_ref[...], wq_ref[...]) + nt(gk_ref[...], wk_ref[...]) + nt(gv_ref[...], wv_ref[...])
    grad_rows, dgain = rms_back(x_ref[...].astype(WIDE), gain_ref[...], total)
    out_ref[...] = grad_ref[...] + grad_rows

    @pl.when(pl.program_id(0) == 0)
    def _():
        dgain_ref[...] = jnp.zeros_like(dgain_ref)

    dgain_ref[...] += dgain


def input_gradient(grads, weights, x, grad, gain):
    rows, width = x.shape
    block = 256
    rowwise = pl.BlockSpec((block, width), lambda g: (g, 0))
    matrix = lambda at: pl.BlockSpec((None, width, width), lambda g: (at, 0, 0))
    return pl.pallas_call(
        input_kernel,
        grid=(rows // block,),
        in_specs=[rowwise, rowwise, rowwise, matrix(0), matrix(1), matrix(2), rowwise, rowwise, whole((1, width))],
        out_specs=[rowwise, whole((1, width))],
        out_shape=[jax.ShapeDtypeStruct((rows, width), WIDE), jax.ShapeDtypeStruct((1, width), WIDE)],
        cost_estimate=pl.CostEstimate(flops=int(8 * PEAK), bytes_accessed=12 << 20, transcendentals=0),
        compiler_params=pltpu.CompilerParams(vmem_limit_bytes=60 * MEGABYTE),
        name="input_gradient",
    )(*grads, weights, weights, weights, x, grad, gain)


def memory_kernel(gk_ref, gv_ref, wk_ref, wv_ref, out_ref):
    out_ref[...] = nt(gk_ref[...], wk_ref[...]) + nt(gv_ref[...], wv_ref[...])


def memory_gradient(grad_key, grad_value, weights):
    rows, width = grad_key.shape
    block = 256
    rowwise = pl.BlockSpec((block, width), lambda g: (g, 0))
    matrix = lambda at: pl.BlockSpec((None, width, width), lambda g: (at, 0, 0))
    return pl.pallas_call(
        memory_kernel,
        grid=(rows // block,),
        in_specs=[rowwise, rowwise, matrix(1), matrix(2)],
        out_specs=rowwise,
        out_shape=jax.ShapeDtypeStruct((rows, width), WIDE),
        cost_estimate=pl.CostEstimate(flops=int(7 * PEAK), bytes_accessed=10 << 20, transcendentals=0),
        compiler_params=pltpu.CompilerParams(vmem_limit_bytes=60 * MEGABYTE),
        name="memory_gradient",
    )(grad_key, grad_value, weights, weights)


LANES = 128
IN_AT, OUT_AT, CROSS_AT, PAST_AT, SELF_AT, SMALL_AT = 0, 1, 2, 3, 4, 5


def vector_rows(width, hidden, small):
    one, big = width // LANES, hidden // LANES
    starts = [0]
    for size in (2 * big, one, 4 * one, one, 3 * one, small // LANES):
        starts.append(starts[-1] + size)
    return starts


def spill(ref, at, row):
    for part in range(row.shape[1] // LANES):
        ref[pl.ds(at + part, 1), :] = row[:, part * LANES : (part + 1) * LANES]


def fetch(ref, at, width):
    return jnp.concatenate([ref[at + part : at + part + 1, :] for part in range(width // LANES)], axis=1)


def column_sums(rows):
    return jnp.sum(rows * rows + TINY_TERM, axis=0, keepdims=True)


def in_kernel(factor, *refs):
    in_refs, in_ref, sums_ref = refs[:4], refs[4], refs[5]
    big = in_ref.shape[2] // LANES
    for matrix in range(2):
        piece = sum(ref[matrix].astype(WIDE) for ref in in_refs).astype(LOW)
        in_ref[matrix] = piece
        spill(sums_ref, matrix * big, column_sums(piece.astype(WIDE) * factor))


def gated_sums(factor, in_parts):
    shape = in_parts[0].shape
    return pl.pallas_call(
        functools.partial(in_kernel, factor),
        in_specs=[pl.BlockSpec(memory_space=pltpu.VMEM)] * 4,
        out_specs=[pl.BlockSpec(memory_space=pltpu.VMEM)] * 2,
        out_shape=[
            jax.ShapeDtypeStruct(shape, LOW),
            jax.ShapeDtypeStruct((2 * shape[2] // LANES, LANES), WIDE),
        ],
        cost_estimate=pl.CostEstimate(flops=int(2 * PEAK), bytes_accessed=2 << 20, transcendentals=0),
        compiler_params=pltpu.CompilerParams(vmem_limit_bytes=60 * MEGABYTE),
        name="gated_sums",
    )(*in_parts)


def early_kernel(factor, starts, where_ref, *refs):
    line_refs, sums_ref, constant_ref, line_ref, vector_ref = refs[0:4], *refs[4:]
    rep = where_ref[0]
    one = line_ref.shape[1] // LANES
    each = line_ref.shape[0] // 2
    third = each // 3
    line = sum(ref[...].astype(WIDE) for ref in line_refs).astype(LOW)
    line_ref[...] = line
    vector_ref[...] = jnp.zeros_like(vector_ref)
    vector_ref[starts[IN_AT] : starts[OUT_AT], :] = sums_ref[...]
    line = line.astype(WIDE) * factor
    spill(vector_ref, starts[OUT_AT], column_sums(line[each + third :]))
    spill(vector_ref, starts[CROSS_AT] + rep * one, column_sums(line[:each]))
    past = column_sums(line[each : each + third])
    spill(vector_ref, starts[PAST_AT], past * (rep < 3).astype(WIDE))
    vector_ref[starts[-1] : starts[-1] + 1, :] = constant_ref[...]


def early_sums(factor, starts, where, line_parts, sums, constants):
    rows = -(-(starts[-1] + 1) // 8) * 8
    return pl.pallas_call(
        functools.partial(early_kernel, factor, starts),
        in_specs=[pl.BlockSpec(memory_space=pltpu.SMEM)] + [pl.BlockSpec(memory_space=pltpu.VMEM)] * 6,
        out_specs=[pl.BlockSpec(memory_space=pltpu.VMEM)] * 2,
        out_shape=[
            jax.ShapeDtypeStruct(line_parts[0].shape, LOW),
            jax.ShapeDtypeStruct((rows, LANES), WIDE),
        ],
        cost_estimate=pl.CostEstimate(flops=int(2 * PEAK), bytes_accessed=2 << 20, transcendentals=0),
        compiler_params=pltpu.CompilerParams(vmem_limit_bytes=60 * MEGABYTE),
        name="early_sums",
    )(where, *line_parts, sums, constants)


def late_kernel(factor, starts, *refs):
    part_refs, small_ref, early_ref, piece_ref, vector_ref = refs[0:4], refs[4], refs[5], refs[6], refs[7]
    vector_ref[...] = early_ref[...]
    one = piece_ref.shape[2] // LANES
    for matrix in range(3):
        piece = sum(ref[matrix].astype(WIDE) for ref in part_refs).astype(LOW)
        piece_ref[matrix] = piece
        spill(vector_ref, starts[SELF_AT] + matrix * one, column_sums(piece.astype(WIDE) * factor))
    vector_ref[starts[SMALL_AT] : starts[SMALL_AT + 1], :] = small_ref[...]


def late_sums(factor, starts, self_parts, small, early):
    return pl.pallas_call(
        functools.partial(late_kernel, factor, starts),
        in_specs=[pl.BlockSpec(memory_space=pltpu.VMEM)] * 6,
        out_specs=[pl.BlockSpec(memory_space=pltpu.VMEM)] * 2,
        out_shape=[
            jax.ShapeDtypeStruct(self_parts[0].shape, LOW),
            jax.ShapeDtypeStruct(early.shape, WIDE),
        ],
        cost_estimate=pl.CostEstimate(flops=int(2 * PEAK), bytes_accessed=1 << 20, transcendentals=0),
        compiler_params=pltpu.CompilerParams(vmem_limit_bytes=60 * MEGABYTE),
        name="late_sums",
    )(*self_parts, small, early)


def to_column(row):
    size = row.shape[1]
    same = lax.broadcasted_iota(jnp.int32, (size, size), 0) == lax.broadcasted_iota(jnp.int32, (size, size), 1)
    return jnp.sum(jnp.where(same, jnp.broadcast_to(row, (size, size)), 0.0), axis=1, keepdims=True)


def to_row(column):
    size = column.shape[0]
    same = lax.broadcasted_iota(jnp.int32, (size, size), 0) == lax.broadcasted_iota(jnp.int32, (size, size), 1)
    return jnp.sum(jnp.where(same, jnp.broadcast_to(column, (size, size)), 0.0), axis=0, keepdims=True)


def update_kernel(factor, starts, shards, where_ref, total_ref, *refs):
    in_near, line_near, self_near = refs[0:4], refs[4:8], refs[8:12]
    (
        in_ref, out_ref, cross_ref, self_ref, in_rows_ref, out_rows_ref, cross_rows_ref, self_rows_ref,
        in_cols_ref, out_cols_ref, cross_cols_ref, self_cols_ref,
    ) = refs[12:24]
    (
        in_grad, out_grad, cross_grad, self_grad, new_in, new_out, new_cross, new_self,
        new_in_rows, new_out_rows, new_cross_rows, new_self_rows,
        new_in_cols, new_out_cols, new_cross_cols, new_self_cols,
        gains_grad, table_grad, new_gains, new_table, new_gain_moment, new_table_moment,
    ) = refs[28:50]
    gains_ref, table_ref, gain_moment_ref, table_moment_ref = refs[24:28]
    in_held, line_held, self_held = refs[50:]
    rep = where_ref[0]
    for way in range(4):
        in_held[rep ^ way] = in_near[way][...]
        line_held[rep ^ way] = line_near[way][...]
        self_held[rep ^ way] = self_near[way][...]
    width = cross_ref.shape[2]
    one, big = width // LANES, in_ref.shape[2] // LANES
    each = cross_ref.shape[1]
    third = each // 3
    scalars = total_ref[starts[-1] : starts[-1] + 1, :]

    def step(at, pieces, index, weight, grad, new, rows_ref, new_rows, cols_ref, new_cols, row_at, scalar):
        rows, cols = weight.shape[-2:]
        spans = []
        start = 0
        for piece in pieces:
            spans.append(slice(start, start + piece.shape[0]))
            start += piece.shape[0]
        whole_rows = rows * shards
        col_sum = fetch(total_ref, at, cols)
        state_sum = scalars[:, scalar : scalar + 1]
        square = scalars[:, 16 + scalar : 17 + scalar]
        col_moment = DECAY_RATE * cols_ref[row_at : row_at + 1, :] + (1.0 - DECAY_RATE) * col_sum / whole_rows
        if index is None:
            spill(new_cols, 0, col_moment)
        else:
            new_cols[row_at : row_at + 1, :] = col_moment
        row_mean = (
            DECAY_RATE * state_sum
            + (1.0 - DECAY_RATE) / cols * jnp.sum(col_sum, axis=1, keepdims=True)
        ) / whole_rows
        blocks = [piece.astype(WIDE) * factor for piece in pieces]
        means = jnp.concatenate(
            [jnp.mean(block * block + TINY_TERM, axis=1, keepdims=True) for block in blocks], axis=0
        )
        row_moment = DECAY_RATE * to_column(rows_ref[row_at : row_at + 1, :]) + (1.0 - DECAY_RATE) * means
        new_rows[row_at : row_at + 1, :] = to_row(row_moment)
        size = STEP_RATE * jnp.sqrt(square / (whole_rows * cols) + 1e-06)
        scale = size * lax.rsqrt(row_moment / row_mean)
        across = lax.rsqrt(col_moment)
        for block, span in zip(blocks, spans):
            place = (span, slice(None)) if index is None else (index, span, slice(None))
            grad[place] = block
            new[place] = weight[place] - scale[span] * block * across

    def plain(grad, ref, moment_ref, square, out, new, new_moment, spot):
        moment = DECAY_RATE * moment_ref[spot] + (1.0 - DECAY_RATE) * (grad * grad + TINY_TERM)
        out[spot] = grad
        new_moment[spot] = moment
        new[spot] = ref[spot] - STEP_RATE * jnp.sqrt(square + 1e-06) * grad * lax.rsqrt(moment)

    part = gains_ref.shape[1]
    for norm in range(3):
        row = fetch(total_ref, starts[SMALL_AT] + norm * one, width)
        mine = where_ref[1] * LINE_CORES + where_ref[2]
        row = pltpu.roll(jnp.broadcast_to(row, (8, width)), lax.rem(width - mine * part, width), 1)
        plain(
            row[0:1, :part], gains_ref, gain_moment_ref, scalars[:, 27 + norm : 28 + norm] / width,
            gains_grad, new_gains, new_gain_moment, (slice(norm, norm + 1), slice(None)),
        )
    table = total_ref[starts[SMALL_AT] + 3 * one : starts[SMALL_AT + 1], 0 : table_ref.shape[1]]
    square = jnp.sum(jnp.sum(table_ref[...] * table_ref[...], axis=1, keepdims=True), axis=0, keepdims=True)
    plain(
        table, table_ref, table_moment_ref, square / (table_ref.shape[0] * table_ref.shape[1]),
        table_grad, new_table, new_table_moment, (slice(None), slice(None)),
    )
    quarters = range(4)
    for matrix in range(2):
        step(
            starts[IN_AT] + matrix * big, [in_held[at, matrix] for at in quarters], matrix,
            in_ref, in_grad, new_in, in_rows_ref, new_in_rows, in_cols_ref, new_in_cols, matrix, matrix,
        )
    step(
        starts[OUT_AT], [line_held[at, each + third :, :] for at in quarters], None,
        out_ref, out_grad, new_out, out_rows_ref, new_out_rows, out_cols_ref, new_out_cols, 0, 2,
    )
    for matrix in range(4):
        step(
            starts[CROSS_AT] + matrix * one, [line_held[matrix, 0:each, :]], matrix,
            cross_ref, cross_grad, new_cross, cross_rows_ref, new_cross_rows, cross_cols_ref, new_cross_cols,
            matrix, 3 + matrix,
        )
        if matrix < 3:
            at, pieces = starts[SELF_AT] + matrix * one, [self_held[at, matrix] for at in quarters]
        else:
            at, pieces = starts[PAST_AT], [line_held[at, each : each + third, :] for at in range(3)]
        step(
            at, pieces, matrix, self_ref, self_grad, new_self, self_rows_ref, new_self_rows,
            self_cols_ref, new_self_cols, matrix, 7 + matrix,
        )


def update_all(
    factor, starts, shards, where, total, in_near, line_near, self_near, weights, rows, cols, plain
):
    outs = (*weights, *weights, *rows, *cols, *plain[:2], *plain[:2], *plain[2:])
    out_shape = [jax.ShapeDtypeStruct(value.shape, WIDE) for value in outs]
    flat_cols = 2 * len(weights) + len(rows) + 1
    out_shape[flat_cols] = jax.ShapeDtypeStruct((cols[1].size // LANES, LANES), WIDE)
    spec = pl.BlockSpec(memory_space=pltpu.VMEM)
    return pl.pallas_call(
        functools.partial(update_kernel, factor, starts, shards),
        in_specs=[pl.BlockSpec(memory_space=pltpu.SMEM)] + [spec] * 29,
        out_specs=[spec] * 22,
        out_shape=out_shape,
        scratch_shapes=[pltpu.VMEM((4, *near[0].shape), LOW) for near in (in_near, line_near, self_near)],
        cost_estimate=pl.CostEstimate(flops=int(8 * PEAK), bytes_accessed=16 << 20, transcendentals=0),
        compiler_params=pltpu.CompilerParams(vmem_limit_bytes=60 * MEGABYTE),
        name="update_all",
    )(where, total, *in_near, *line_near, *self_near, *weights, *rows, *cols, *plain)


def flat_permute(value, target):
    reps, shards = lax.axis_size("rep"), lax.axis_size("fsdp")
    pairs = []
    for rep in range(reps):
        for shard in range(shards):
            to_rep, to_shard = target(rep, shard)
            pairs.append((rep * shards + shard, to_rep * shards + to_shard))
    return lax.ppermute(value, ("rep", "fsdp"), pairs)


def from_rep(value, way):
    return flat_permute(value, lambda rep, shard: (rep ^ way, shard))


def from_shard(value, way):
    return flat_permute(value, lambda rep, shard: (rep, shard ^ way))


def from_line(value, hops):
    shards = lax.axis_size("fsdp")
    return flat_permute(value, lambda rep, shard: (rep, (shard + LINE_CORES * hops) % shards))


def along_line(piece):
    return jnp.stack([piece] + [from_line(piece, hop) for hop in range(1, LINE)])


def across_reps(line):
    return [line] + [from_rep(line, way) for way in range(1, 4)]


def with_partner(parts):
    return parts + [from_shard(part, 1) for part in parts]


def add_line(parts):
    return [parts[0]] + [from_line(parts[hop], hop) for hop in range(1, LINE)]


def rep_parts(parts, axis):
    rep = lax.axis_index("rep")
    pick = lambda at: lax.dynamic_index_in_dim(parts, at, axis, keepdims=False)
    return [pick(rep)] + [from_rep(pick(rep ^ way), way) for way in range(1, 4)]


def add_up(parts):
    return sum(part.astype(WIDE) for part in parts).astype(LOW)


def rep_near(piece):
    return [piece] + [from_rep(piece, way) for way in range(1, 4)]


def rep_order(near):
    rep = lax.axis_index("rep")
    return [lax.select_n(rep, *[near[at ^ own] for own in range(4)]) for at in range(4)]


def hold(*values):
    return lax.optimization_barrier(values)


def butterfly(vector, move, size):
    way = 1
    while way < size:
        vector = vector + move(vector, way)
        way *= 2
    return vector


def after(value, *earlier):
    return lax.optimization_barrier((value, *earlier))[0]


def row_moments(gradient, row_state):
    squares = gradient * gradient + TINY_TERM
    return DECAY_RATE * row_state + (1.0 - DECAY_RATE) * jnp.mean(squares, axis=-1)


def factored_sums(gradient, row_state):
    squares = gradient * gradient + TINY_TERM
    return jnp.sum(squares, axis=1), jnp.sum(row_moments(gradient, row_state), axis=1)


def pack(values):
    return jnp.concatenate([value.reshape(-1) for value in values])


def unpack(vector, values):
    out = []
    for value in values:
        out.append(vector[: value.size].reshape(value.shape))
        vector = vector[value.size :]
    return out


def factored_update(gradient, weight, row_moment, col_state, col_sum, row_sum, square):
    count, rows, cols = weight.shape
    whole_rows = rows * lax.axis_size("fsdp")
    col_moment = DECAY_RATE * col_state + (1.0 - DECAY_RATE) * col_sum / whole_rows
    scale = lax.rsqrt(row_moment / (row_sum[:, None] / whole_rows))
    step = STEP_RATE * jnp.sqrt(square / (whole_rows * cols) + 1e-06)
    direction = gradient * scale[:, :, None] * lax.rsqrt(col_moment)[:, None, :]
    return weight - step[:, None, None] * direction, col_moment


def plain_update(gradient, weight, moment, square):
    moment = DECAY_RATE * moment + (1.0 - DECAY_RATE) * (gradient * gradient + TINY_TERM)
    step = STEP_RATE * jnp.sqrt(square + 1e-06)
    return weight - step * gradient * lax.rsqrt(moment), moment


def per_device(
    dec_in,
    memory,
    out_grad,
    dec_len,
    enc_len,
    buckets,
    self_weight,
    cross_weight,
    ffn_in,
    ffn_out,
    gains,
    table,
    self_rows,
    self_cols,
    cross_rows,
    cross_cols,
    in_rows,
    in_cols,
    out_rows,
    out_cols,
    gain_moment,
    table_moment,
):
    seq_count, seq_length, model_width = dec_in.shape
    mem_length = memory.shape[1]
    row_count = seq_count * seq_length
    hidden_width = ffn_in.shape[2]
    reps, shards = lax.axis_size("rep"), lax.axis_size("fsdp")
    rep, shard = lax.axis_index("rep"), lax.axis_index("fsdp")
    quarters = reps == 4 and shards == 8
    part_rows = hidden_width // shards
    grad_factor = 1.0 / math.sqrt(row_count * reps * shards)
    where = jnp.stack([rep, shard // 2, shard % 2]).astype(jnp.int32) * int(quarters)
    w_self = lax.all_gather(self_weight.astype(LOW), "fsdp", axis=1, tiled=True)
    gain_full = lax.all_gather(gains.astype(LOW), "fsdp", axis=1, tiled=True).astype(WIDE)
    w_in = lax.all_gather(ffn_in.astype(LOW), "fsdp", axis=1, tiled=True)

    each = model_width // (LINE * LINE_CORES)
    if quarters:
        out_each = part_rows // 4
        cross_quarter = lax.dynamic_index_in_dim(cross_weight, rep, 0, keepdims=False).astype(LOW)
        out_quarter = lax.dynamic_index_in_dim(
            ffn_out.reshape(4, out_each, model_width), rep, 0, keepdims=False
        ).astype(LOW)
        cross_pieces = with_partner(across_reps(along_line(cross_quarter)))
    square = lambda value: jnp.sum(value * value, axis=(1, 2))
    squares = (
        square(ffn_in), square(ffn_out[None]), square(cross_weight), square(self_weight),
        jnp.sum(gains * gains, axis=1),
    )
    if quarters:
        state_sums = (
            jnp.sum(in_rows, axis=1), jnp.sum(out_rows)[None], jnp.sum(cross_rows, axis=1),
            jnp.sum(self_rows, axis=1),
        )
        blank = jnp.zeros((5,), WIDE)
        constants = pack([*state_sums, blank, *squares]) / reps
        constants = jnp.pad(constants, (0, LANES - constants.size)).reshape(1, LANES)
        gain_full, constants = hold(gain_full, constants)

    bucket_mask = (buckets[None, :] == jnp.arange(BUCKETS)[:, None]).astype(WIDE)
    by_distance = jnp.sum(table.T[:, :, None] * bucket_mask[None], axis=1)
    by_distance = jnp.pad(by_distance, ((0, 16 - H), (0, 0)))
    backwards = jnp.roll(by_distance[:, ::-1], 1, axis=1)
    no_bias = jnp.zeros((8, PAIR), WIDE)
    no_source = jnp.zeros((16, PAIR), LOW)
    if quarters:
        gain_full, by_distance, backwards, no_bias, no_source = hold(
            gain_full, by_distance, backwards, no_bias, no_source
        )

    dec_rows = dec_in.reshape(row_count, model_width)
    mem_rows = memory.reshape(seq_count * mem_length, model_width)
    grad_rows = out_grad.reshape(row_count, model_width)
    *kept_one, after_self = attention_forward(
        True, dec_rows, no_source, dec_len, where, gain_full[0:1], w_self, backwards
    )
    if quarters:
        w_cross = list(hold(*cross_pieces, after_self)[:-1])
        out_line = along_line(after(out_quarter, w_self))
        out_near = across_reps(after(out_line, after_self))
    else:
        w_cross = lax.all_gather(cross_weight.astype(LOW), "fsdp", axis=1, tiled=True)
        w_out = [lax.all_gather(ffn_out.astype(LOW), "fsdp", axis=0, tiled=True)]
    *kept_two, after_cross = attention_forward(
        False, after_self, mem_rows, enc_len, where, gain_full[1:2], w_cross, no_bias
    )
    if quarters:
        *kept_two, after_cross, w_cross = (*kept_two, after_cross)
    if quarters:
        out_near = hold(*out_near, after_cross)[:-1]
        w_out = with_partner(list(out_near))
    layer_out, grad_cross, grad_gate, grad_up, *out_near, gain_three = feed_forward_both(
        after_cross, grad_rows, dec_len, where, gain_full[2:3], w_in, w_out
    )
    scatter = lambda value, at: lax.psum_scatter(value, "fsdp", scatter_dimension=at, tiled=True)
    if quarters:
        own_gate = scatter(grad_gate, 0)
        out_near = out_near[:1] + [from_rep(out_near[way], way) for way in range(1, 4)]
    grad_self, grad_k_two, grad_v_two, gain_two, *cross_near, cross_far = attention_backward(
        False, after_self, mem_rows, grad_cross, enc_len, where, gain_full[1:2], w_cross, no_bias, kept_two,
        kept_two[3], kept_one[3],
    )
    if quarters:
        cross_far, grad_k_two, *out_near = hold(cross_far, grad_k_two, *out_near)
        pair = from_shard(cross_far, 1)
        memory_grad = memory_gradient(grad_k_two, grad_v_two, w_cross)
        memory_grad, pair, own_gate = hold(memory_grad, pair, own_gate)
        own_up = scatter(grad_up, 0)
        cross_chip = [add_up([cross_near[way], pair[way]]) for way in range(4)]
        grad_self, *cross_chip = hold(grad_self, *cross_chip)
        cross_near = cross_chip[:1] + [from_rep(cross_chip[way], way) for way in range(1, 4)]
    else:
        memory_grad = memory_gradient(grad_k_two, grad_v_two, w_cross)
    *grads_one, grad_self_weights, dist_grad = attention_backward(
        True, dec_rows, no_source, grad_self, dec_len, where, gain_full[0:1], w_self, by_distance, kept_one,
        no_source, no_source,
    )
    if quarters:
        dist_grad, own_up, grad_self_weights, *rest = hold(
            dist_grad, own_up, grad_self_weights, *grads_one, *cross_near, *out_near
        )
        grads_one, cross_near, out_near = rest[:3], rest[3:7], rest[7:]
        own_self = scatter(grad_self_weights, 1)
        out_sum = add_up(out_near)
        out_pair = from_shard(out_sum[1], 1)
        in_parts = rep_parts(jnp.stack([own_gate, own_up]).reshape(2, 4, -1, hidden_width), 1)
        line = jnp.concatenate([add_up(cross_near), add_up([out_sum[0], out_pair])], axis=1)
        in_piece, in_columns = gated_sums(grad_factor, in_parts)
        in_near = rep_near(in_piece)
        *line_parts, gate = hold(*add_line(line), grads_one[0])
        grads_one = [gate, *grads_one[1:]]
        input_grad, gain_one = input_gradient(grads_one, w_self, dec_rows, grad_self, gain_full[0:1])
    else:
        input_grad, gain_one = input_gradient(grads_one, w_self, dec_rows, grad_self, gain_full[0:1])
    layer_out = layer_out.reshape(dec_in.shape)
    input_grad = input_grad.reshape(dec_in.shape)
    memory_grad = memory_grad.reshape(memory.shape)
    table_part = jnp.sum(dist_grad[:H, None, :] * bucket_mask[None], axis=2)
    wide = lambda value: value.astype(WIDE) * grad_factor
    gain_parts = jnp.concatenate([gain_one, gain_two, gain_three]) * grad_factor
    table_part = table_part * grad_factor
    if quarters:
        starts = vector_rows(model_width, hidden_width, 3 * model_width + H * LANES)
        small = jnp.concatenate(
            [gain_parts.reshape(-1, LANES), jnp.pad(table_part, ((0, 0), (0, LANES - BUCKETS)))]
        )
        line_piece, early = early_sums(grad_factor, starts, where, line_parts, in_columns, constants)
        line_near = rep_near(line_piece)
        own_self, early, *near = hold(own_self, early, *in_near, *line_near[:3])
        in_near, line_near = near[:4], near[4:] + line_near[3:]
        self_parts = rep_parts(own_self.reshape(3, 4, -1, model_width), 1)
        self_piece, vector = late_sums(grad_factor, starts, self_parts, small, early)
        vector, *self_near = hold(butterfly(vector, from_shard, shards), *rep_near(self_piece))
        total = butterfly(vector, from_rep, reps)
        (
            ffn_in_grad, feedforward_output_gradient, cross_grad, self_grad,
            new_ffn_in, new_ffn_out, new_cross, new_self,
            new_in_rows, new_out_rows, new_cross_rows, new_self_rows,
            new_in_cols, new_out_cols, new_cross_cols, new_self_cols,
            gains_grad, table_grad, new_gains, new_table, new_gain_moment, new_table_moment,
        ) = update_all(
            grad_factor, starts, shards, where, total, in_near, line_near, self_near,
            (ffn_in, ffn_out, cross_weight, self_weight),
            (in_rows, out_rows[None], cross_rows, self_rows),
            (in_cols, out_cols[None], cross_cols, self_cols),
            (gains, table.T, gain_moment, table_moment.T),
        )
        table_grad, new_table, new_table_moment = table_grad.T, new_table.T, new_table_moment.T
        new_out_rows, new_out_cols = new_out_rows.reshape(-1), new_out_cols.reshape(-1)
    else:
        over_reps = lambda value: lax.psum(value, "rep")
        own_in = over_reps(scatter(jnp.stack([grad_gate, grad_up]), 1))
        grad_out = jnp.stack(out_near)
        grad_out = grad_out.transpose(2, 1, 0, 3, 4).reshape(hidden_width, model_width)
        own_out = over_reps(scatter(grad_out, 0))
        packed = jnp.stack([jnp.stack(cross_near), cross_far]).transpose(1, 2, 0, 3, 4)
        cross_parts = packed[..., :each, :].reshape(4, model_width, model_width)
        past = packed[:3, ..., each:, :].transpose(1, 2, 0, 3, 4).reshape(1, model_width, model_width)
        own_cross = over_reps(scatter(cross_parts, 1))
        own_self = over_reps(scatter(jnp.concatenate([grad_self_weights, past]), 1))
        self_grad, cross_grad, ffn_in_grad, feedforward_output_gradient = [
            wide(member) for member in (own_self, own_cross, own_in, own_out)
        ]
        local = (
            *factored_sums(ffn_in_grad, in_rows),
            *factored_sums(feedforward_output_gradient[None], out_rows[None]),
            *factored_sums(cross_grad, cross_rows),
            *factored_sums(self_grad, self_rows),
            *squares,
        )
        found = unpack(lax.psum(pack(local), "fsdp"), local)
        in_sums, out_sums, cross_sums, self_sums, squares = (
            found[0:2], found[2:4], found[4:6], found[6:8], found[8:],
        )
        gain_total, table_grad = lax.psum((gain_parts, table_part.T), ("rep", "fsdp"))
        gains_grad = lax.dynamic_slice_in_dim(gain_total, shard * gains.shape[1], gains.shape[1], axis=1)
        new_gains, new_gain_moment = plain_update(
            gains_grad, gains, gain_moment, (squares[4] / model_width)[:, None]
        )
        new_table, new_table_moment = plain_update(
            table_grad, table, table_moment, jnp.mean(table * table)
        )
        new_in_rows = row_moments(ffn_in_grad, in_rows)
        new_out_rows = row_moments(feedforward_output_gradient, out_rows)
        new_cross_rows = row_moments(cross_grad, cross_rows)
        new_self_rows = row_moments(self_grad, self_rows)
        new_ffn_in, new_in_cols = factored_update(
            ffn_in_grad, ffn_in, new_in_rows, in_cols, *in_sums, squares[0]
        )
        new_ffn_out, new_out_cols = [
            member[0]
            for member in factored_update(
                feedforward_output_gradient[None], ffn_out[None], new_out_rows[None], out_cols[None],
                *out_sums, squares[1],
            )
        ]
        new_cross, new_cross_cols = factored_update(
            cross_grad, cross_weight, new_cross_rows, cross_cols, *cross_sums, squares[2]
        )
        new_self, new_self_cols = factored_update(
            self_grad, self_weight, new_self_rows, self_cols, *self_sums, squares[3]
        )
    return (
        layer_out,
        input_grad,
        memory_grad,
        self_grad,
        cross_grad,
        ffn_in_grad,
        feedforward_output_gradient,
        gains_grad,
        table_grad,
        new_self,
        new_cross,
        new_ffn_in,
        new_ffn_out,
        new_gains,
        new_table,
        new_self_rows,
        new_self_cols,
        new_cross_rows,
        new_cross_cols,
        new_in_rows,
        new_in_cols,
        new_out_rows,
        new_out_cols,
        new_gain_moment,
        new_table_moment,
    )


def solution(mesh):
    placed = (
        P(("rep", "fsdp"), None, None),
        P(("rep", "fsdp"), None, None),
        P(("rep", "fsdp"), None, None),
        P(("rep", "fsdp")),
        P(("rep", "fsdp")),
        P(),
        P(None, "fsdp", None),
        P(None, "fsdp", None),
        P(None, "fsdp", None),
        P("fsdp", None),
        P(None, "fsdp"),
        P(),
        P(None, "fsdp"),
        P(),
        P(None, "fsdp"),
        P(),
        P(None, "fsdp"),
        P(),
        P("fsdp"),
        P(),
        P(None, "fsdp"),
        P(),
    )
    return jax.shard_map(
        per_device,
        mesh=mesh,
        in_specs=placed,
        out_specs=(
            P(("rep", "fsdp"), None, None),
            P(("rep", "fsdp"), None, None),
            P(("rep", "fsdp"), None, None),
            P(None, "fsdp", None),
            P(None, "fsdp", None),
            P(None, "fsdp", None),
            P("fsdp", None),
            P(None, "fsdp"),
            P(),
            P(None, "fsdp", None),
            P(None, "fsdp", None),
            P(None, "fsdp", None),
            P("fsdp", None),
            P(None, "fsdp"),
            P(),
            P(None, "fsdp"),
            P(),
            P(None, "fsdp"),
            P(),
            P(None, "fsdp"),
            P(),
            P("fsdp"),
            P(),
            P(None, "fsdp"),
            P(),
        ),
        check_vma=False,
    )
```
